32 devices in a mesh: groups: 2 (over y), tm: 4 (over z), head: 2 (over x), rep: 2 (over core).
Axes of the slice: x: 2, y: 2, z: 4, core: 2. Of those that a mesh axis runs over, the one named last changes fastest.
Arguments:
- frozen_query: bfloat16 [2048, 2560], P(('groups', 'tm', 'rep'), 'head'), parts along dimension 0, may hold values from -144 to 144
- frozen_key: bfloat16 [2048, 2560], P(('groups', 'tm'), 'head'), parts along dimension 0, may hold values from -8 to 8
- frozen_value: bfloat16 [2048, 2560], P(('groups', 'tm'), 'head'), parts along dimension 0, may hold values from -6 to 6
- token_adapter_input: bfloat16 [2048, 128], P(('groups', 'tm')), parts along dimension 0, may hold values from -6 to 6
- query_adapter_out: bfloat16 [128, 2560], P(None, 'head'), may hold values from -0.5 to 0.5
- key_adapter_out: bfloat16 [128, 2560], P(None, 'head'), may hold values from -0.5 to 0.5
- value_adapter_out: bfloat16 [128, 2560], P(None, 'head'), may hold values from -0.5 to 0.5
- out_grad: bfloat16 [2048, 2560], P(('groups', 'tm', 'rep'), 'head'), parts along dimension 0, may hold values from -6 to 6
- band_width: int32 [4, 4], replicated, may hold values from 0 to 2, as said below
Outputs:
- grad_query: float32 [256, 2560], P('groups', 'head'), parts along dimension 0
- grad_key: float32 [256, 2560], P('groups', 'head'), parts along dimension 0
- grad_value: float32 [256, 2560], P('groups', 'head'), parts along dimension 0
- low_grad: float32 [2048, 128], P(('groups', 'tm')), parts along dimension 0
The draws below stay inside these ranges and needn't reach their ends.
There are 2 independent parts, one for each index of `groups`. The reference program is written for one: setup_inputs(seed, part) draws one part's arguments, and reference() takes and returns one part's arrays. A program takes and returns all parts, laid end to end along the dimension named above; an argument that names none is the same for every part. Nothing has to cross between parts.
Inputs may be any that keep to these rules, and one draw needn't show every extreme that they name: band_width[i, j] is 2 where i equals j, 1 or 2 where |i - j| is at most 1, 0 or 1 where |i - j| is at most 4, and 0 beyond.
All inputs are finite; a program needn't handle non-finite values.
Results may differ from the reference program's by a relative error of at most 0.013.
The reference program's roundings to bfloat16 on the way count: a program that leaves them out, or rounds other values in their place, can miss the bound.
Values may be sent and summed in bfloat16 or wider, within the bound.
No kernel may reach another device: no remote copies, remote signals or barrier semaphores. Data moves between devices by JAX's collectives and lax.ppermute only.
A program may use at most 64 MiB of HBM per device.

```python
import jax
import jax.numpy as jnp
from jax import lax

HEADS = 20
DH = 128
RANK = 128
TILE = 128
NEAR = 1
REACH = 4
FRAMES = 4
SEQ = 1024
WIDTH = 2560


def normal_rows(key):
    return jax.random.normal(key, (FRAMES * 2 * TILE, HEADS * DH), jnp.float32)


def draw_frozen_key(key, part):
    shared = normal_rows(key)
    return jnp.clip(shared, -8.0, 8.0).astype(jnp.bfloat16)


def draw_frozen_query(key, part):
    shared = normal_rows(key)
    key = jax.random.fold_in(key, 12)
    fresh_rows = jax.random.normal(key, shared.shape, jnp.float32)
    return jnp.clip(fresh_rows, -144.0, 144.0).astype(jnp.bfloat16)


def draw_band_width(key, part):
    key = jax.random.fold_in(key, 13)
    key_near, key_far = jax.random.split(key)
    frame_ids = jnp.arange(FRAMES)
    distance = jnp.abs(frame_ids[:, None] - frame_ids[None, :])
    near_band = jax.random.randint(key_near, (FRAMES, FRAMES), 1, 3)
    far_band = jax.random.randint(key_far, (FRAMES, FRAMES), 0, 2)
    return jnp.where(distance == 0, 2, jnp.where(distance <= NEAR, near_band, jnp.where(distance <= REACH, far_band, 0))).astype(jnp.int32)


def block_levels(own_key, dims, cuts, low, top_value):
    level, own = 1.0, jax.random.fold_in(own_key, 6)
    for position, blocks in cuts:
        steps = jnp.exp(jax.random.uniform(jax.random.fold_in(own, position), (blocks,), jnp.float32, low / len(cuts), top_value / len(cuts)))
        level = level * jnp.repeat(steps, dims[position] // blocks).reshape([-1 if axis == position else 1 for axis in range(len(dims))])
    return level


def centred(own_key, shape, width, bound, shards=(), kind=jnp.bfloat16):
    result = width * jax.random.normal(own_key, shape, jnp.float32)
    if shards:
        result = result * block_levels(own_key, shape, shards, -0.22, 0.18)
    return jnp.clip(result, -bound, bound).astype(kind)


def setup_inputs(seed: int = 0, part: int = 0) -> dict:
    seeds = jax.random.split(jax.random.key(seed), 10)
    own_keys = jax.random.split(jax.random.fold_in(seeds[9], part), 10)
    frozen_query = draw_frozen_query(jax.random.fold_in(jax.random.fold_in(seeds[9], part), 71), part)
    frozen_key = draw_frozen_key(jax.random.fold_in(jax.random.fold_in(seeds[9], part), 71), part)
    frozen_value = centred(own_keys[2], (SEQ, WIDTH), 1.0, 6.0, ((0, 4), (1, 2)))
    token_adapter_input = centred(own_keys[3], (SEQ, RANK), 1.0, 6.0, ((0, 4),))
    query_adapter_out = centred(seeds[4], (RANK, WIDTH), RANK ** -0.5, 0.5, ((1, 2),))
    key_adapter_out = centred(seeds[5], (RANK, WIDTH), RANK ** -0.5, 0.5, ((1, 2),))
    value_adapter_out = centred(seeds[6], (RANK, WIDTH), RANK ** -0.5, 0.5, ((1, 2),))
    out_grad = centred(own_keys[7], (SEQ, WIDTH), 1.0, 6.0, ((0, 8), (1, 2)))
    band_width = draw_band_width(jax.random.fold_in(seeds[9], 71), part)
    return dict(frozen_query=frozen_query, frozen_key=frozen_key, frozen_value=frozen_value, token_adapter_input=token_adapter_input, query_adapter_out=query_adapter_out, key_adapter_out=key_adapter_out, value_adapter_out=value_adapter_out, out_grad=out_grad, band_width=band_width)


def adapter_rows(frozen_rows, reduced_rows, adapter_map):
    return (frozen_rows.astype(jnp.float32) + jnp.dot(reduced_rows, adapter_map, preferred_element_type=jnp.float32)).astype(jnp.bfloat16)


def rounded(values):
    return lax.optimization_barrier(values.astype(jnp.bfloat16)).astype(jnp.float32)


def reference(frozen_query, frozen_key, frozen_value, token_adapter_input, query_adapter_out, key_adapter_out, value_adapter_out, out_grad, band_width):
    frame_count = band_width.shape[0]
    frame_rows = 2 * TILE
    col_width = HEADS * DH
    window = (2 * REACH + 1) * frame_rows
    margin = REACH * frame_rows
    score_scale = DH ** -0.5
    highest = lax.Precision.HIGHEST
    query_rows = adapter_rows(frozen_query, token_adapter_input, query_adapter_out)
    key_row_block = adapter_rows(frozen_key, token_adapter_input, key_adapter_out)
    value_row_block = adapter_rows(frozen_value, token_adapter_input, value_adapter_out)
    key_pad = jnp.pad(key_row_block, ((margin, margin), (0, 0)))
    value_pad = jnp.pad(value_row_block, ((margin, margin), (0, 0)))
    band_pad = jnp.pad(band_width, ((0, 0), (REACH, REACH)))
    col_pos = jnp.arange(window)
    col_tile = (col_pos // TILE) % 2
    col_frame = col_pos // frame_rows
    row_tile = jnp.arange(frame_rows) // TILE

    def one_frame(carry, frame_idx):
        key_acc, value_acc = carry
        row_start = (frame_idx * frame_rows).astype(jnp.int32)
        head_q = lax.dynamic_slice_in_dim(query_rows, row_start, frame_rows, 0).reshape(frame_rows, HEADS, DH).astype(jnp.float32)
        head_do = lax.dynamic_slice_in_dim(out_grad, row_start, frame_rows, 0).reshape(frame_rows, HEADS, DH).astype(jnp.float32)
        head_k = lax.dynamic_slice_in_dim(key_pad, row_start, window, 0).reshape(window, HEADS, DH).astype(jnp.float32)
        head_v = lax.dynamic_slice_in_dim(value_pad, row_start, window, 0).reshape(window, HEADS, DH).astype(jnp.float32)
        reach_band = lax.dynamic_slice(band_pad, (frame_idx.astype(jnp.int32), frame_idx.astype(jnp.int32)), (1, 2 * REACH + 1))[0]
        allowed = jnp.abs(row_tile[:, None] - col_tile[None, :]) < reach_band[col_frame][None, :]
        scores = jnp.einsum("qhd,khd->hqk", head_q, head_k, precision=highest) * score_scale
        scores = jnp.where(allowed[None], scores, -jnp.inf)
        shifted = jnp.exp(scores - jnp.max(scores, axis=2, keepdims=True))
        attn_prob = shifted / jnp.sum(shifted, axis=2, keepdims=True)
        prob_low = rounded(attn_prob)
        attended = rounded(jnp.einsum("hqk,khd->qhd", prob_low, head_v, precision=highest))
        row_delta = jnp.sum(head_do * attended, axis=2)
        prob_grad = jnp.einsum("qhd,khd->hqk", head_do, head_v, precision=highest)
        score_grad = rounded(attn_prob * (prob_grad - jnp.transpose(row_delta)[:, :, None]))
        query_grad = (jnp.einsum("hqk,khd->qhd", score_grad, head_k, precision=highest) * score_scale).astype(jnp.bfloat16)
        split_grad = score_grad.reshape(HEADS, 2, TILE, window)
        split_q = head_q.reshape(2, TILE, HEADS, DH)
        key_part = rounded(jnp.einsum("hrqk,rqhd->rkhd", split_grad, split_q, precision=highest) * score_scale)
        split_prob = prob_low.reshape(HEADS, 2, TILE, window)
        split_do = head_do.reshape(2, TILE, HEADS, DH)
        value_part = rounded(jnp.einsum("hrqk,rqhd->rkhd", split_prob, split_do, precision=highest))
        key_acc = lax.dynamic_update_slice_in_dim(key_acc, lax.dynamic_slice_in_dim(key_acc, row_start, window, 0) + jnp.sum(key_part, axis=0).reshape(window, col_width), row_start, 0)
        value_acc = lax.dynamic_update_slice_in_dim(value_acc, lax.dynamic_slice_in_dim(value_acc, row_start, window, 0) + jnp.sum(value_part, axis=0).reshape(window, col_width), row_start, 0)
        return (key_acc, value_acc), query_grad.reshape(frame_rows, col_width)

    padded_rows = frame_count * frame_rows + 2 * margin
    start_acc = (jnp.zeros((padded_rows, col_width), jnp.float32), jnp.zeros((padded_rows, col_width), jnp.float32))
    (key_acc, value_acc), query_blocks = lax.scan(one_frame, start_acc, jnp.arange(frame_count, dtype=jnp.int32))
    query_grad = query_blocks.reshape(frame_count * frame_rows, col_width)
    key_half = key_acc[margin:margin + frame_count * frame_rows]
    value_half = value_acc[margin:margin + frame_count * frame_rows]
    low_trans = jnp.transpose(token_adapter_input)
    low_wide = low_trans.astype(jnp.float32)
    grad_query = jnp.dot(low_trans, query_grad, preferred_element_type=jnp.float32)
    grad_key = jnp.dot(low_wide, key_half, precision=highest)
    grad_value = jnp.dot(low_wide, value_half, precision=highest)
    low_grad = jnp.dot(query_grad, jnp.transpose(query_adapter_out), preferred_element_type=jnp.float32)
    low_grad = low_grad + jnp.dot(key_half, jnp.transpose(key_adapter_out).astype(jnp.float32), precision=highest)
    low_grad = low_grad + jnp.dot(value_half, jnp.transpose(value_adapter_out).astype(jnp.float32), precision=highest)
    return (grad_query, grad_key, grad_value, low_grad)
```

```python
import functools

import jax
import jax.numpy as jnp
from jax import lax
from jax.experimental import pallas as pl
from jax.experimental.pallas import tpu as pltpu
from jax.sharding import PartitionSpec as P

DH = 128
NEAR = 1
REACH = 4
SCALE = DH ** (-0.5)
F32 = jnp.float32
BF16 = jnp.bfloat16


def dot_nn(left, right):
    return lax.dot_general(left, right, (((1,), (0,)), ((), ())), preferred_element_type=F32)


def dot_nt(left, right):
    return lax.dot_general(left, right, (((1,), (1,)), ((), ())), preferred_element_type=F32)


def dot_tn(left, right):
    return lax.dot_general(left, right, (((0,), (0,)), ((), ())), preferred_element_type=F32)


def routes(count):
    found = []
    for d in range(1, min(REACH, count - 1) + 1):
        if 2 * d >= count:
            found.append((d, (-d, d)))
        else:
            found.append((d, (-d,)))
            found.append((d, (d,)))
    return found


def pairs(count, offsets):
    return [(i + o, i) for o in offsets for i in range(count) if 0 <= i + o < count]


def swap(block, axis):
    return lax.ppermute(block, axis, [(0, 1), (1, 0)])


def attention_kernel(
    blocks, bias_ref, fq_ref, do_ref, fk_ref, fv_ref, t_ref, tr_ref, tt_ref, aq_ref, ak_ref, av_ref, *refs
):
    k_refs = refs[:blocks]
    v_refs = refs[blocks : 2 * blocks]
    gq_ref, gk_ref, gv_ref, lowq_ref, low_ref = refs[2 * blocks :]
    rows = fq_ref.shape[0]

    @pl.when(pl.program_id(0) == 0)
    def _():
        lowq_ref[...] = jnp.zeros_like(lowq_ref)
        low_ref[...] = jnp.zeros_like(low_ref)

    aq, ak, av = aq_ref[...], ak_ref[...], av_ref[...]
    query = (fq_ref[...].astype(F32) + dot_nn(tr_ref[...], aq)).astype(BF16)
    do = do_ref[...]
    own_k = (fk_ref[...].astype(F32) + dot_nn(t_ref[...], ak)).astype(BF16)
    own_v = (fv_ref[...].astype(F32) + dot_nn(t_ref[...], av)).astype(BF16)
    keys = [own_k[:rows], own_k[rows:]] + [ref[...] for ref in k_refs]
    values = [own_v[:rows], own_v[rows:]] + [ref[...] for ref in v_refs]
    count = len(keys)
    scores = [dot_nt(keys[b], query) * SCALE + bias_ref[b] for b in range(count)]
    top = functools.reduce(jnp.maximum, scores)
    top = jnp.max(top, axis=0, keepdims=True)
    shifted = [jnp.exp(s - top) for s in scores]
    total = jnp.sum(functools.reduce(jnp.add, shifted), axis=0, keepdims=True)
    inverse = 1.0 / total
    probs = [s * inverse for s in shifted]
    lows = [p.astype(BF16) for p in probs]
    attended = functools.reduce(jnp.add, [dot_tn(lows[b], values[b]) for b in range(count)])
    attended = attended.astype(BF16).astype(F32)
    delta = jnp.sum((do.astype(F32) * attended).T, axis=0, keepdims=True)
    grads = [
        (probs[b] * (dot_nt(values[b], do) - delta)).astype(BF16) for b in range(count)
    ]
    dq = functools.reduce(jnp.add, [dot_tn(grads[b], keys[b]) for b in range(count)])
    dq = (dq * SCALE).astype(BF16)
    gq_ref[...] = dot_tn(tr_ref[...], dq)
    lowq_ref[...] += dot_nt(dq, aq)
    both = jnp.concatenate([ak, av], axis=1)
    for b in range(count):
        dk = (dot_nn(grads[b], query) * SCALE).astype(BF16)
        dv = dot_nn(lows[b], do).astype(BF16)
        part = jnp.concatenate([dk, dv], axis=1)
        low_ref[b * rows : (b + 1) * rows, :] += dot_nt(part, both)
        out = dot_nn(tt_ref[:, b * rows : (b + 1) * rows], part)
        if b == 0:
            total_part = out
        else:
            total_part += out
    gk_ref[...] = total_part[:, :DH]
    gv_ref[...] = total_part[:, DH:]


def attention(bias, fq, do, fk, fv, t, tr, tt, aq, ak, av, payloads):
    rows, width = fq.shape
    heads = width // DH
    rank = t.shape[1]
    blocks = len(payloads)
    count = blocks + 2

    def col(r):
        return pl.BlockSpec((r, DH), lambda h: (0, h))

    def whole(shape):
        return pl.BlockSpec(shape, lambda h: (0, 0))

    return pl.pallas_call(
        functools.partial(attention_kernel, blocks),
        grid=(heads,),
        out_shape=[
            jax.ShapeDtypeStruct((rank, width), F32),
            jax.ShapeDtypeStruct((rank, width), F32),
            jax.ShapeDtypeStruct((rank, width), F32),
            jax.ShapeDtypeStruct((rows, rank), F32),
            jax.ShapeDtypeStruct((count * rows, rank), F32),
        ],
        in_specs=[pl.BlockSpec(memory_space=pltpu.SMEM)]
        + [col(rows), col(rows), col(2 * rows), col(2 * rows)]
        + [whole(t.shape), whole(tr.shape), whole(tt.shape)]
        + [col(rank)] * 3
        + [col(rows)] * blocks
        + [pl.BlockSpec((rows, DH), lambda h: (0, heads + h))] * blocks,
        out_specs=[col(rank)] * 3 + [whole((rows, rank)), whole((count * rows, rank))],
        compiler_params=pltpu.CompilerParams(vmem_limit_bytes=32 * 1024 * 1024),
    )(bias, fq, do, fk, fv, t, tr, tt, aq, ak, av, *payloads, *payloads)


def sum_rows(part, frame_idx, half_idx, frames):
    rows, width = part.shape
    half = width // 2
    keep = lax.dynamic_slice_in_dim(part, half_idx * half, half, 1)
    give = lax.dynamic_slice_in_dim(part, (1 - half_idx) * half, half, 1)
    mine = keep + swap(give, "rep")
    if frames & (frames - 1) or rows % frames or frames > REACH + 1:
        total = lax.psum(mine, "tm").astype(BF16)
    else:
        chunk = rows // frames
        low = mine.astype(BF16)
        acc = lax.dynamic_slice_in_dim(mine, frame_idx * chunk, chunk, 0)
        for m in range(1, frames):
            give = lax.dynamic_slice_in_dim(low, (frame_idx ^ m) * chunk, chunk, 0)
            acc = acc + lax.ppermute(give, "tm", [(i, i ^ m) for i in range(frames)]).astype(F32)
        acc = acc.astype(BF16)
        total = jnp.zeros((rows, half), BF16)
        total = lax.dynamic_update_slice_in_dim(total, acc, frame_idx * chunk, 0)
        for m in range(1, frames):
            got = lax.ppermute(acc, "tm", [(i, i ^ m) for i in range(frames)])
            total = lax.dynamic_update_slice_in_dim(total, got, (frame_idx ^ m) * chunk, 0)
    other = swap(total, "rep")
    first = jnp.where(half_idx == 0, total, other)
    second = jnp.where(half_idx == 0, other, total)
    return jnp.concatenate([first, second], axis=1).astype(F32)


def on_device(
    frozen_query,
    frozen_key,
    frozen_value,
    token_adapter_input,
    query_adapter_out,
    key_adapter_out,
    value_adapter_out,
    out_grad,
    band_width,
):
    rows, width = frozen_query.shape
    rank = token_adapter_input.shape[1]
    frames = band_width.shape[0]
    frame_idx = lax.axis_index("tm")
    half_idx = lax.axis_index("rep")
    t = token_adapter_input
    tr = lax.dynamic_slice_in_dim(t, half_idx * rows, rows, 0)

    def tile_rows_of(frozen, adapter):
        own = lax.dynamic_slice_in_dim(frozen, half_idx * rows, rows, 0)
        return (own.astype(F32) + dot_nn(tr, adapter)).astype(BF16)

    payload = jnp.concatenate(
        [tile_rows_of(frozen_key, key_adapter_out), tile_rows_of(frozen_value, value_adapter_out), tr],
        axis=1,
    )

    frame_ids = jnp.arange(frames)
    band_row = jnp.sum(jnp.where((frame_ids == frame_idx)[:, None], band_width, 0), axis=0)

    def band_at(offsets):
        seen = functools.reduce(jnp.logical_or, [frame_ids == frame_idx + o for o in offsets])
        return jnp.sum(jnp.where(seen, band_row, 0))

    own_band = band_at((0,))
    allowed = [jnp.abs(half_idx - tile) < own_band for tile in range(2)]
    payloads = []
    plan = routes(frames)
    for d, offsets in plan:
        got = lax.ppermute(payload, "tm", pairs(frames, offsets))
        band = band_at(offsets)
        payloads.append(got)
        allowed.append(band > 0)
        if d <= NEAR:
            payloads.append(swap(got, "rep"))
            allowed.append(band > 1)
    bias = jnp.where(jnp.stack(allowed), 0.0, -jnp.inf).astype(F32)
    tt = jnp.concatenate([t] + [p[:, 2 * width :] for p in payloads], axis=0).T

    gq, gk, gv, low_q, low_b = attention(
        bias, frozen_query, out_grad, frozen_key, frozen_value, t, tr, tt,
        query_adapter_out, key_adapter_out, value_adapter_out, payloads,
    )

    own = low_b[: 2 * rows]
    same = lax.dynamic_slice_in_dim(own, half_idx * rows, rows, 0) + low_q
    other = lax.dynamic_slice_in_dim(own, (1 - half_idx) * rows, rows, 0)
    start = 2 * rows
    for d, offsets in plan:
        size = 2 * rows if d <= NEAR else rows
        back = [(target, source) for source, target in pairs(frames, offsets)]
        got = lax.ppermute(low_b[start : start + size], "tm", back)
        start += size
        same = same + got[:rows]
        if d <= NEAR:
            other = other + got[rows:]
    low = jnp.where(
        half_idx == 0,
        jnp.concatenate([same, other], axis=0),
        jnp.concatenate([other, same], axis=0),
    )
    low = low + swap(low, "rep")
    low = low + swap(low, "head")

    grads = sum_rows(jnp.concatenate([gq, gk, gv], axis=0), frame_idx, half_idx, frames)
    return grads[:rank], grads[rank : 2 * rank], grads[2 * rank :], low


def solution(mesh):
    in_specs = (
        P(("groups", "tm", "rep"), "head"),
        P(("groups", "tm"), "head"),
        P(("groups", "tm"), "head"),
        P(("groups", "tm"), None),
        P(None, "head"),
        P(None, "head"),
        P(None, "head"),
        P(("groups", "tm", "rep"), "head"),
        P(),
    )
    out_specs = (
        P("groups", "head"),
        P("groups", "head"),
        P("groups", "head"),
        P(("groups", "tm"), None),
    )
    return jax.shard_map(
        on_device, mesh=mesh, in_specs=in_specs, out_specs=out_specs, check_vma=False
    )
```

```python
import functools

import jax
import jax.numpy as jnp
from jax import lax
from jax.experimental import pallas as pl
from jax.experimental.pallas import tpu as pltpu
from jax.sharding import PartitionSpec as P

DH = 128
NEAR = 1
REACH = 4
SCALE = DH ** (-0.5)
F32 = jnp.float32
BF16 = jnp.bfloat16


def dot_nn(left, right):
    return lax.dot_general(left, right, (((1,), (0,)), ((), ())), preferred_element_type=F32)


def dot_nt(left, right):
    return lax.dot_general(left, right, (((1,), (1,)), ((), ())), preferred_element_type=F32)


def dot_tn(left, right):
    return lax.dot_general(left, right, (((0,), (0,)), ((), ())), preferred_element_type=F32)


def routes(count):
    found = []
    for d in range(1, min(REACH, count - 1) + 1):
        if 2 * d >= count:
            found.append((d, (-d, d)))
        else:
            found.append((d, (-d,)))
            found.append((d, (d,)))
    return found


def pairs(count, offsets):
    return [(i + o, i) for o in offsets for i in range(count) if 0 <= i + o < count]


def swap(block, axis):
    return lax.ppermute(block, axis, [(0, 1), (1, 0)])


def attention_kernel(
    blocks, bias_ref, fq_ref, do_ref, fk_ref, fv_ref, t_ref, tr_ref, tt_ref, aq_ref, ak_ref, av_ref, *refs
):
    k_refs = refs[:blocks]
    v_refs = refs[blocks : 2 * blocks]
    gq_ref, gk_ref, gv_ref, lowq_ref, low_ref = refs[2 * blocks :]
    rows = fq_ref.shape[0]

    @pl.when(pl.program_id(0) == 0)
    def _():
        lowq_ref[...] = jnp.zeros_like(lowq_ref)
        low_ref[...] = jnp.zeros_like(low_ref)

    aq, ak, av = aq_ref[...], ak_ref[...], av_ref[...]
    query = (fq_ref[...].astype(F32) + dot_nn(tr_ref[...], aq)).astype(BF16)
    do = do_ref[...]
    own_k = (fk_ref[...].astype(F32) + dot_nn(t_ref[...], ak)).astype(BF16)
    own_v = (fv_ref[...].astype(F32) + dot_nn(t_ref[...], av)).astype(BF16)
    keys = [own_k[:rows], own_k[rows:]] + [ref[...] for ref in k_refs]
    values = [own_v[:rows], own_v[rows:]] + [ref[...] for ref in v_refs]
    count = len(keys)
    scores = [dot_nt(keys[b], query) * SCALE + bias_ref[b] for b in range(count)]
    top = functools.reduce(jnp.maximum, scores)
    top = jnp.max(top, axis=0, keepdims=True)
    shifted = [jnp.exp(s - top) for s in scores]
    total = jnp.sum(functools.reduce(jnp.add, shifted), axis=0, keepdims=True)
    inverse = 1.0 / total
    probs = [s * inverse for s in shifted]
    lows = [p.astype(BF16) for p in probs]
    attended = functools.reduce(jnp.add, [dot_tn(lows[b], values[b]) for b in range(count)])
    attended = attended.astype(BF16).astype(F32)
    delta = jnp.sum((do.astype(F32) * attended).T, axis=0, keepdims=True)
    grads = [
        (probs[b] * (dot_nt(values[b], do) - delta)).astype(BF16) for b in range(count)
    ]
    dq = functools.reduce(jnp.add, [dot_tn(grads[b], keys[b]) for b in range(count)])
    dq = (dq * SCALE).astype(BF16)
    gq_ref[...] = dot_tn(tr_ref[...], dq)
    lowq_ref[...] += dot_nt(dq, aq)
    both = jnp.concatenate([ak, av], axis=1)
    for b in range(count):
        dk = (dot_nn(grads[b], query) * SCALE).astype(BF16)
        dv = dot_nn(lows[b], do).astype(BF16)
        part = jnp.concatenate([dk, dv], axis=1)
        low_ref[b * rows : (b + 1) * rows, :] += dot_nt(part, both)
        out = dot_nn(tt_ref[:, b * rows : (b + 1) * rows], part)
        if b == 0:
            total_part = out
        else:
            total_part += out
    gk_ref[...] = total_part[:, :DH]
    gv_ref[...] = total_part[:, DH:]


def attention(bias, fq, do, fk, fv, t, tr, tt, aq, ak, av, payloads):
    rows, width = fq.shape
    heads = width // DH
    rank = t.shape[1]
    blocks = len(payloads)
    count = blocks + 2

    def col(r):
        return pl.BlockSpec((r, DH), lambda h: (0, h))

    def whole(shape):
        return pl.BlockSpec(shape, lambda h: (0, 0))

    return pl.pallas_call(
        functools.partial(attention_kernel, blocks),
        grid=(heads,),
        out_shape=[
            jax.ShapeDtypeStruct((rank, width), F32),
            jax.ShapeDtypeStruct((rank, width), F32),
            jax.ShapeDtypeStruct((rank, width), F32),
            jax.ShapeDtypeStruct((rows, rank), F32),
            jax.ShapeDtypeStruct((count * rows, rank), F32),
        ],
        in_specs=[pl.BlockSpec(memory_space=pltpu.SMEM)]
        + [col(rows), col(rows), col(2 * rows), col(2 * rows)]
        + [whole(t.shape), whole(tr.shape), whole(tt.shape)]
        + [col(rank)] * 3
        + [col(rows)] * blocks
        + [pl.BlockSpec((rows, DH), lambda h: (0, heads + h))] * blocks,
        out_specs=[col(rank)] * 3 + [whole((rows, rank)), whole((count * rows, rank))],
        compiler_params=pltpu.CompilerParams(vmem_limit_bytes=32 * 1024 * 1024),
    )(bias, fq, do, fk, fv, t, tr, tt, aq, ak, av, *payloads, *payloads)


def sum_rows(part, frame_idx, half_idx, frames):
    rows, width = part.shape
    half = width // 2
    keep = lax.dynamic_slice_in_dim(part, half_idx * half, half, 1)
    give = lax.dynamic_slice_in_dim(part, (1 - half_idx) * half, half, 1)
    mine = keep + swap(give, "rep")
    if frames & (frames - 1) or rows % frames or frames > REACH + 1:
        total = lax.psum(mine, "tm").astype(BF16)
    else:
        chunk = rows // frames
        low = mine.astype(BF16)
        acc = lax.dynamic_slice_in_dim(mine, frame_idx * chunk, chunk, 0)
        for m in range(1, frames):
            give = lax.dynamic_slice_in_dim(low, (frame_idx ^ m) * chunk, chunk, 0)
            acc = acc + lax.ppermute(give, "tm", [(i, i ^ m) for i in range(frames)]).astype(F32)
        acc = acc.astype(BF16)
        total = jnp.zeros((rows, half), BF16)
        total = lax.dynamic_update_slice_in_dim(total, acc, frame_idx * chunk, 0)
        for m in range(1, frames):
            got = lax.ppermute(acc, "tm", [(i, i ^ m) for i in range(frames)])
            total = lax.dynamic_update_slice_in_dim(total, got, (frame_idx ^ m) * chunk, 0)
    other = swap(total, "rep")
    first = jnp.where(half_idx == 0, total, other)
    second = jnp.where(half_idx == 0, other, total)
    return jnp.concatenate([first, second], axis=1).astype(F32)


def window_plan(
    frozen_query,
    frozen_key,
    frozen_value,
    token_adapter_input,
    query_adapter_out,
    key_adapter_out,
    value_adapter_out,
    out_grad,
    band_width,
):
    rows, width = frozen_query.shape
    rank = token_adapter_input.shape[1]
    frames = band_width.shape[0]
    frame_idx = lax.axis_index("tm")
    half_idx = lax.axis_index("rep")
    t = token_adapter_input
    tr = lax.dynamic_slice_in_dim(t, half_idx * rows, rows, 0)

    def tile_rows_of(frozen, adapter):
        own = lax.dynamic_slice_in_dim(frozen, half_idx * rows, rows, 0)
        return (own.astype(F32) + dot_nn(tr, adapter)).astype(BF16)

    payload = jnp.concatenate(
        [tile_rows_of(frozen_key, key_adapter_out), tile_rows_of(frozen_value, value_adapter_out), tr],
        axis=1,
    )

    frame_ids = jnp.arange(frames)
    band_row = jnp.sum(jnp.where((frame_ids == frame_idx)[:, None], band_width, 0), axis=0)

    def band_at(offsets):
        seen = functools.reduce(jnp.logical_or, [frame_ids == frame_idx + o for o in offsets])
        return jnp.sum(jnp.where(seen, band_row, 0))

    own_band = band_at((0,))
    allowed = [jnp.abs(half_idx - tile) < own_band for tile in range(2)]
    payloads = []
    plan = routes(frames)
    for d, offsets in plan:
        got = lax.ppermute(payload, "tm", pairs(frames, offsets))
        band = band_at(offsets)
        payloads.append(got)
        allowed.append(band > 0)
        if d <= NEAR:
            payloads.append(swap(got, "rep"))
            allowed.append(band > 1)
    bias = jnp.where(jnp.stack(allowed), 0.0, -jnp.inf).astype(F32)
    tt = jnp.concatenate([t] + [p[:, 2 * width :] for p in payloads], axis=0).T

    gq, gk, gv, low_q, low_b = attention(
        bias, frozen_query, out_grad, frozen_key, frozen_value, t, tr, tt,
        query_adapter_out, key_adapter_out, value_adapter_out, payloads,
    )

    own = low_b[: 2 * rows]
    same = lax.dynamic_slice_in_dim(own, half_idx * rows, rows, 0) + low_q
    other = lax.dynamic_slice_in_dim(own, (1 - half_idx) * rows, rows, 0)
    start = 2 * rows
    for d, offsets in plan:
        size = 2 * rows if d <= NEAR else rows
        back = [(target, source) for source, target in pairs(frames, offsets)]
        got = lax.ppermute(low_b[start : start + size], "tm", back)
        start += size
        same = same + got[:rows]
        if d <= NEAR:
            other = other + got[rows:]
    low = jnp.where(
        half_idx == 0,
        jnp.concatenate([same, other], axis=0),
        jnp.concatenate([other, same], axis=0),
    )
    low = low + swap(low, "rep")
    low = low + swap(low, "head")

    grads = sum_rows(jnp.concatenate([gq, gk, gv], axis=0), frame_idx, half_idx, frames)
    return grads[:rank], grads[rank : 2 * rank], grads[2 * rank :], low


def head_table(heads, frames):
    base, extra = divmod(heads, frames)
    lead = (frames - extra) // 2
    counts = [base + (1 if lead <= j < lead + extra else 0) for j in range(frames)]
    return [sum(counts[:j]) for j in range(frames)], counts


def pick(table, index):
    ids = jnp.arange(len(table))
    return jnp.sum(jnp.where(ids == index, jnp.array(table, jnp.int32), 0))


def pack_kernel(slots, heads_ref, *refs):
    full = slots[0]
    ins, t_ref, outs = refs[: -1 - len(slots)], refs[-1 - len(slots)], refs[-len(slots) :]
    for s in range(sum(slots)):
        out, at = (outs[0], s) if s < full else (outs[1], s - full)
        for a in range(4):
            col = (4 * at + a) * DH
            out[0, :, col : col + DH] = ins[4 * s + a][...]
    outs[0][0, :, 4 * full * DH :] = t_ref[...]


def pack(heads, half_idx, fq, do, fk, fv, t, slots, frames):
    rows, rank = fq.shape[0], t.shape[1]
    total = sum(slots)
    scalars = jnp.concatenate([heads, half_idx[None]]).astype(jnp.int32)

    def spec(s, tile):
        def index(j, ref):
            return (ref[frames * total] if tile else 0, ref[j * total + s])

        return pl.BlockSpec((rows, DH), index)

    specs, args = [], []
    for s in range(total):
        specs += [spec(s, False), spec(s, False), spec(s, True), spec(s, True)]
        args += [fq, do, fk, fv]
    specs.append(pl.BlockSpec((rows, rank), lambda j, ref: (ref[frames * total], 0)))
    widths = [4 * n * DH for n in slots]
    widths[0] += rank
    return pl.pallas_call(
        functools.partial(pack_kernel, slots),
        grid_spec=pltpu.PrefetchScalarGridSpec(
            num_scalar_prefetch=1,
            grid=(frames,),
            in_specs=specs,
            out_specs=[pl.BlockSpec((1, rows, w), lambda j, ref: (j, 0, 0)) for w in widths],
        ),
        out_shape=[jax.ShapeDtypeStruct((frames, rows, w), BF16) for w in widths],
    )(scalars, *args, t)


def head_kernel(frames, scalar_ref, *refs):
    grad_ref, low_ref = refs[-2:]
    live = scalar_ref[frames * frames + pl.num_programs(0) + pl.program_id(0)] > 0

    @pl.when(pl.program_id(0) == 0)
    def _():
        low_ref[...] = jnp.zeros_like(low_ref)

    @pl.when(live)
    def _():
        one_head(frames, scalar_ref, *refs)

    @pl.when(jnp.logical_not(live))
    def _():
        grad_ref[...] = jnp.zeros_like(grad_ref)


def one_head(frames, bands, q_ref, do_ref, k_ref, v_ref, k2_ref, v2_ref, t_ref, t2_ref,
             aq_ref, ak_ref, av_ref, grad_ref, low_ref):
    rows = q_ref.shape[1]
    flat = frames * rows

    def load(ref):
        return ref[...].reshape(flat, ref.shape[2])

    def adapted(ref, tokens, adapter):
        return (load(ref).astype(F32) + dot_nn(tokens, adapter)).astype(BF16)

    aq, ak, av = aq_ref[...], ak_ref[...], av_ref[...]
    t_same, t_other = load(t_ref), load(t2_ref)
    query = adapted(q_ref, t_same, aq)
    do = load(do_ref)
    do_t = do.T
    keys = jnp.concatenate([adapted(k_ref, t_same, ak), adapted(k2_ref, t_other, ak)], axis=0)
    values = jnp.concatenate([adapted(v_ref, t_same, av), adapted(v2_ref, t_other, av)], axis=0)
    keys_t, values_t = keys.T, values.T

    def bias(i, b):
        j, need = (b, 0) if b < frames else (b - frames, 1)
        value = jnp.where(bands[i * frames + j] > need, 0.0, -jnp.inf).astype(F32)
        return jnp.full((1, rows), value, F32)

    span = 2 if frames % 2 == 0 else 1
    wide = span * rows
    dks, dvs, dqs = [None] * (2 * frames), [None] * (2 * frames), []
    for first in range(0, frames, span):
        mine = range(first, first + span)
        blocks = list(range(frames)) + [
            frames + j for j in range(frames) if any(abs(i - j) <= NEAR for i in mine)
        ]
        here = slice(first * rows, first * rows + wide)
        q_p, do_p = query[here], do[here]

        def gather(whole, axis):
            parts = [
                whole[b * rows : (b + 1) * rows] if axis == 0 else whole[:, b * rows : (b + 1) * rows]
                for b in blocks
            ]
            return jnp.concatenate(parts, axis=axis)

        raw = dot_nt(gather(keys, 0), q_p)
        scores = [
            raw[n * rows : (n + 1) * rows] * SCALE + jnp.concatenate([bias(i, b) for i in mine], axis=1)
            for n, b in enumerate(blocks)
        ]
        top = jnp.max(functools.reduce(jnp.maximum, scores), axis=0, keepdims=True)
        shifted = [jnp.exp(s - top) for s in scores]
        inverse = 1.0 / jnp.sum(functools.reduce(jnp.add, shifted), axis=0, keepdims=True)
        probs = [s * inverse for s in shifted]
        low = jnp.concatenate([p.astype(BF16) for p in probs], axis=0)
        attended = dot_nn(gather(values_t, 1), low).astype(BF16).astype(F32)
        delta = jnp.sum(do_t[:, here].astype(F32) * attended, axis=0, keepdims=True)
        prob_grad = dot_nt(gather(values, 0), do_p)
        grad = jnp.concatenate(
            [
                (probs[n] * (prob_grad[n * rows : (n + 1) * rows] - delta)).astype(BF16)
                for n in range(len(blocks))
            ],
            axis=0,
        )
        dqs.append((dot_nn(gather(keys_t, 1), grad) * SCALE).astype(BF16).T)
        dk, dv = dot_nn(grad, q_p), dot_nn(low, do_p)
        for n, b in enumerate(blocks):
            part = slice(n * rows, (n + 1) * rows)
            dks[b] = dk[part] if dks[b] is None else dks[b] + dk[part]
            dvs[b] = dv[part] if dvs[b] is None else dvs[b] + dv[part]
    dq = jnp.concatenate(dqs, axis=0)
    grad_ref[0, :, :] = dot_tn(t_same, dq)
    dk = (jnp.concatenate(dks, axis=0) * SCALE).astype(BF16)
    dv = jnp.concatenate(dvs, axis=0).astype(BF16)
    both = jnp.concatenate([dk, dv], axis=1)
    sums = dot_tn(jnp.concatenate([t_same, t_other], axis=0), both)
    grad_ref[1, :, :] = sums[:, :DH]
    grad_ref[2, :, :] = sums[:, DH:]
    lows = dot_nt(both, jnp.concatenate([ak, av], axis=1))
    low_ref[:flat] += lows[:flat] + dot_nt(dq, aq)
    low_ref[flat:] += lows[flat:]


def head_group(band_width, heads, live, mine, other, tokens, tokens2, token_col, aq, ak, av):
    frames, rows = mine.shape[:2]
    rank = aq.shape[0]
    slots = heads.shape[0]
    scalars = jnp.concatenate([band_width.reshape(-1), heads, live]).astype(jnp.int32)

    def spec(a):
        return pl.BlockSpec((frames, rows, DH), lambda s, ref: (0, 0, 4 * s + a))

    adapter = pl.BlockSpec((rank, DH), lambda s, ref: (0, ref[frames * frames + s]))
    token = pl.BlockSpec((frames, rows, rank), lambda s, ref: (0, 0, token_col))
    return pl.pallas_call(
        functools.partial(head_kernel, frames),
        grid_spec=pltpu.PrefetchScalarGridSpec(
            num_scalar_prefetch=1,
            grid=(slots,),
            in_specs=[spec(0), spec(1), spec(2), spec(3), spec(2), spec(3), token, token] + [adapter] * 3,
            out_specs=[
                pl.BlockSpec((3, rank, DH), lambda s, ref: (0, 0, s)),
                pl.BlockSpec((2 * frames * rows, rank), lambda s, ref: (0, 0)),
            ],
        ),
        out_shape=[
            jax.ShapeDtypeStruct((3, rank, slots * DH), F32),
            jax.ShapeDtypeStruct((2 * frames * rows, rank), F32),
        ],
        compiler_params=pltpu.CompilerParams(vmem_limit_bytes=48 * 1024 * 1024),
    )(scalars, mine, mine, mine, mine, other, other, tokens, tokens2, aq, ak, av)


def place_kernel(slots, scalar_ref, mine_ref, other_ref, *refs):
    half = scalar_ref[0]
    count = mine_ref.shape[0]
    outs = refs
    total = sum(slots)
    rank = outs[0].shape[0]
    rows = mine_ref.shape[1]
    for m in range(count):
        a = mine_ref[m].astype(F32)
        b = other_ref[m].astype(F32)
        both = jnp.where(half == 0, jnp.concatenate([a, b], axis=0), jnp.concatenate([b, a], axis=0))
        for s in range(total):
            col = pl.multiple_of(scalar_ref[1 + m * total + s] * DH, DH)
            live = scalar_ref[1 + count * total + m * total + s] > 0

            @pl.when(live)
            def _():
                for o in range(3):
                    outs[o][:, pl.ds(col, DH)] = both[o * rank : (o + 1) * rank, s * DH : (s + 1) * DH]


def place(scalars, mine, other, rank, width, slots):
    return pl.pallas_call(
        functools.partial(place_kernel, slots),
        in_specs=[pl.BlockSpec(memory_space=pltpu.SMEM)] + [pl.BlockSpec(memory_space=pltpu.VMEM)] * 2,
        out_specs=[pl.BlockSpec(memory_space=pltpu.VMEM)] * 3,
        out_shape=[jax.ShapeDtypeStruct((rank, width), F32)] * 3,
        compiler_params=pltpu.CompilerParams(vmem_limit_bytes=32 * 1024 * 1024),
    )(scalars, mine, other)


def exchange_plan(
    frozen_query,
    frozen_key,
    frozen_value,
    token_adapter_input,
    query_adapter_out,
    key_adapter_out,
    value_adapter_out,
    out_grad,
    band_width,
):
    rows, width = frozen_query.shape
    rank = token_adapter_input.shape[1]
    frames = band_width.shape[0]
    heads = width // DH
    frame_idx = lax.axis_index("tm")
    half_idx = lax.axis_index("rep")
    starts, counts = head_table(heads, frames)
    full, most = min(counts), max(counts)
    slots = (full, most - full) if most > full else (full,)
    table = [[min(starts[j] + s, heads - 1) for s in range(most)] for j in range(frames)]
    wide = [j for j in range(frames) if counts[j] == most]

    def meet(block, m, targets=range(frames)):
        return lax.ppermute(block, "tm", [(j ^ m, j) for j in targets])

    flat_heads = jnp.array([h for row in table for h in row], jnp.int32)
    packed = pack(
        flat_heads, half_idx, frozen_query, out_grad, frozen_key, frozen_value,
        token_adapter_input, slots, frames,
    )
    my_heads = jnp.stack([pick([row[s] for row in table], frame_idx) for s in range(most)])
    my_live = (jnp.arange(most) < pick(counts, frame_idx)).astype(jnp.int32)
    adapters = (query_adapter_out, key_adapter_out, value_adapter_out)
    got = lax.all_to_all(packed[0], "tm", 0, 0, tiled=True)
    got2 = swap(got, "rep")
    token_col = 4 * full
    grads, low = head_group(
        band_width, my_heads[:full], my_live[:full], got, got2, got, got2, token_col, *adapters
    )
    grads = [grads]
    if most > full:
        extra = jnp.zeros_like(packed[1])
        for m in range(frames):
            part = lax.dynamic_slice_in_dim(packed[1], frame_idx ^ m, 1, 0)
            part = part if m == 0 else meet(part, m, wide)
            extra = lax.dynamic_update_slice_in_dim(extra, part, frame_idx ^ m, 0)
        extra2 = swap(extra, "rep")
        more, low2 = head_group(
            band_width, my_heads[full:], my_live[full:], extra, extra2, got, got2, token_col, *adapters
        )
        grads.append(more)
        low = low + low2

    low = low.reshape(2, frames, rows, rank)
    mine = lax.dynamic_slice_in_dim(low, frame_idx, 1, 1)
    for m in range(1, frames):
        give = lax.dynamic_slice_in_dim(low, frame_idx ^ m, 1, 1).astype(BF16)
        mine = mine + meet(give, m).astype(F32)
    same, other = mine[0, 0], mine[1, 0]
    low = jnp.where(
        half_idx == 0,
        jnp.concatenate([same, other], axis=0),
        jnp.concatenate([other, same], axis=0),
    )
    low = low + swap(low, "rep")
    low = low + swap(low, "head")

    total = jnp.concatenate(grads, axis=2).reshape(3 * rank, most * DH)
    half = 3 * rank // 2
    keep = lax.dynamic_slice_in_dim(total, half_idx * half, half, 0)
    give = lax.dynamic_slice_in_dim(total, (1 - half_idx) * half, half, 0)
    piece = (keep + swap(give, "rep")).astype(BF16)
    pieces = jnp.stack([piece] + [meet(piece, m) for m in range(1, frames)])
    scalars = [half_idx[None]]
    for values in (table, [[int(s < counts[j]) for s in range(most)] for j in range(frames)]):
        for m in range(frames):
            scalars.append(
                jnp.stack([pick([row[s] for row in values], frame_idx ^ m) for s in range(most)])
            )
    scalars = jnp.concatenate(scalars).astype(jnp.int32)
    outs = place(scalars, pieces, swap(pieces, "rep"), rank, width, slots)
    return outs[0], outs[1], outs[2], low


def on_device(frozen_query, *rest):
    frames = rest[-1].shape[0]
    heads = frozen_query.shape[1] // DH
    whole_reach = frames <= REACH + 1 and frames & (frames - 1) == 0 and heads >= frames
    return (exchange_plan if whole_reach else window_plan)(frozen_query, *rest)


def solution(mesh):
    in_specs = (
        P(("groups", "tm", "rep"), "head"),
        P(("groups", "tm"), "head"),
        P(("groups", "tm"), "head"),
        P(("groups", "tm"), None),
        P(None, "head"),
        P(None, "head"),
        P(None, "head"),
        P(("groups", "tm", "rep"), "head"),
        P(),
    )
    out_specs = (
        P("groups", "head"),
        P("groups", "head"),
        P("groups", "head"),
        P(("groups", "tm"), None),
    )
    return jax.shard_map(
        on_device, mesh=mesh, in_specs=in_specs, out_specs=out_specs, check_vma=False
    )
```

```python
import functools

import jax
import jax.numpy as jnp
from jax import lax
from jax.experimental import pallas as pl
from jax.experimental.pallas import tpu as pltpu
from jax.sharding import PartitionSpec as P

DH = 128
NEAR = 1
REACH = 4
SCALE = DH ** (-0.5)
F32 = jnp.float32
BF16 = jnp.bfloat16


def dot_nn(left, right):
    return lax.dot_general(left, right, (((1,), (0,)), ((), ())), preferred_element_type=F32)


def dot_nt(left, right):
    return lax.dot_general(left, right, (((1,), (1,)), ((), ())), preferred_element_type=F32)


def dot_tn(left, right):
    return lax.dot_general(left, right, (((0,), (0,)), ((), ())), preferred_element_type=F32)


def routes(count):
    found = []
    for d in range(1, min(REACH, count - 1) + 1):
        if 2 * d >= count:
            found.append((d, (-d, d)))
        else:
            found.append((d, (-d,)))
            found.append((d, (d,)))
    return found


def pairs(count, offsets):
    return [(i + o, i) for o in offsets for i in range(count) if 0 <= i + o < count]


def swap(block, axis):
    return lax.ppermute(block, axis, [(0, 1), (1, 0)])


def attention_kernel(
    blocks, bias_ref, fq_ref, do_ref, fk_ref, fv_ref, t_ref, tr_ref, tt_ref, aq_ref, ak_ref, av_ref, *refs
):
    k_refs = refs[:blocks]
    v_refs = refs[blocks : 2 * blocks]
    gq_ref, gk_ref, gv_ref, lowq_ref, low_ref = refs[2 * blocks :]
    rows = fq_ref.shape[0]

    @pl.when(pl.program_id(0) == 0)
    def _():
        lowq_ref[...] = jnp.zeros_like(lowq_ref)
        low_ref[...] = jnp.zeros_like(low_ref)

    aq, ak, av = aq_ref[...], ak_ref[...], av_ref[...]
    query = (fq_ref[...].astype(F32) + dot_nn(tr_ref[...], aq)).astype(BF16)
    do = do_ref[...]
    own_k = (fk_ref[...].astype(F32) + dot_nn(t_ref[...], ak)).astype(BF16)
    own_v = (fv_ref[...].astype(F32) + dot_nn(t_ref[...], av)).astype(BF16)
    keys = [own_k[:rows], own_k[rows:]] + [ref[...] for ref in k_refs]
    values = [own_v[:rows], own_v[rows:]] + [ref[...] for ref in v_refs]
    count = len(keys)
    scores = [dot_nt(keys[b], query) * SCALE + bias_ref[b] for b in range(count)]
    top = functools.reduce(jnp.maximum, scores)
    top = jnp.max(top, axis=0, keepdims=True)
    shifted = [jnp.exp(s - top) for s in scores]
    total = jnp.sum(functools.reduce(jnp.add, shifted), axis=0, keepdims=True)
    inverse = 1.0 / total
    probs = [s * inverse for s in shifted]
    lows = [p.astype(BF16) for p in probs]
    attended = functools.reduce(jnp.add, [dot_tn(lows[b], values[b]) for b in range(count)])
    attended = attended.astype(BF16).astype(F32)
    delta = jnp.sum((do.astype(F32) * attended).T, axis=0, keepdims=True)
    grads = [
        (probs[b] * (dot_nt(values[b], do) - delta)).astype(BF16) for b in range(count)
    ]
    dq = functools.reduce(jnp.add, [dot_tn(grads[b], keys[b]) for b in range(count)])
    dq = (dq * SCALE).astype(BF16)
    gq_ref[...] = dot_tn(tr_ref[...], dq)
    lowq_ref[...] += dot_nt(dq, aq)
    both = jnp.concatenate([ak, av], axis=1)
    for b in range(count):
        dk = (dot_nn(grads[b], query) * SCALE).astype(BF16)
        dv = dot_nn(lows[b], do).astype(BF16)
        part = jnp.concatenate([dk, dv], axis=1)
        low_ref[b * rows : (b + 1) * rows, :] += dot_nt(part, both)
        out = dot_nn(tt_ref[:, b * rows : (b + 1) * rows], part)
        if b == 0:
            total_part = out
        else:
            total_part += out
    gk_ref[...] = total_part[:, :DH]
    gv_ref[...] = total_part[:, DH:]


def attention(bias, fq, do, fk, fv, t, tr, tt, aq, ak, av, payloads):
    rows, width = fq.shape
    heads = width // DH
    rank = t.shape[1]
    blocks = len(payloads)
    count = blocks + 2

    def col(r):
        return pl.BlockSpec((r, DH), lambda h: (0, h))

    def whole(shape):
        return pl.BlockSpec(shape, lambda h: (0, 0))

    return pl.pallas_call(
        functools.partial(attention_kernel, blocks),
        grid=(heads,),
        out_shape=[
            jax.ShapeDtypeStruct((rank, width), F32),
            jax.ShapeDtypeStruct((rank, width), F32),
            jax.ShapeDtypeStruct((rank, width), F32),
            jax.ShapeDtypeStruct((rows, rank), F32),
            jax.ShapeDtypeStruct((count * rows, rank), F32),
        ],
        in_specs=[pl.BlockSpec(memory_space=pltpu.SMEM)]
        + [col(rows), col(rows), col(2 * rows), col(2 * rows)]
        + [whole(t.shape), whole(tr.shape), whole(tt.shape)]
        + [col(rank)] * 3
        + [col(rows)] * blocks
        + [pl.BlockSpec((rows, DH), lambda h: (0, heads + h))] * blocks,
        out_specs=[col(rank)] * 3 + [whole((rows, rank)), whole((count * rows, rank))],
        compiler_params=pltpu.CompilerParams(vmem_limit_bytes=32 * 1024 * 1024),
    )(bias, fq, do, fk, fv, t, tr, tt, aq, ak, av, *payloads, *payloads)


def sum_rows(part, frame_idx, half_idx, frames):
    rows, width = part.shape
    half = width // 2
    keep = lax.dynamic_slice_in_dim(part, half_idx * half, half, 1)
    give = lax.dynamic_slice_in_dim(part, (1 - half_idx) * half, half, 1)
    mine = keep + swap(give, "rep")
    if frames & (frames - 1) or rows % frames or frames > REACH + 1:
        total = lax.psum(mine, "tm").astype(BF16)
    else:
        chunk = rows // frames
        low = mine.astype(BF16)
        acc = lax.dynamic_slice_in_dim(mine, frame_idx * chunk, chunk, 0)
        for m in range(1, frames):
            give = lax.dynamic_slice_in_dim(low, (frame_idx ^ m) * chunk, chunk, 0)
            acc = acc + lax.ppermute(give, "tm", [(i, i ^ m) for i in range(frames)]).astype(F32)
        acc = acc.astype(BF16)
        total = jnp.zeros((rows, half), BF16)
        total = lax.dynamic_update_slice_in_dim(total, acc, frame_idx * chunk, 0)
        for m in range(1, frames):
            got = lax.ppermute(acc, "tm", [(i, i ^ m) for i in range(frames)])
            total = lax.dynamic_update_slice_in_dim(total, got, (frame_idx ^ m) * chunk, 0)
    other = swap(total, "rep")
    first = jnp.where(half_idx == 0, total, other)
    second = jnp.where(half_idx == 0, other, total)
    return jnp.concatenate([first, second], axis=1).astype(F32)


def window_plan(
    frozen_query,
    frozen_key,
    frozen_value,
    token_adapter_input,
    query_adapter_out,
    key_adapter_out,
    value_adapter_out,
    out_grad,
    band_width,
):
    rows, width = frozen_query.shape
    rank = token_adapter_input.shape[1]
    frames = band_width.shape[0]
    frame_idx = lax.axis_index("tm")
    half_idx = lax.axis_index("rep")
    t = token_adapter_input
    tr = lax.dynamic_slice_in_dim(t, half_idx * rows, rows, 0)

    def tile_rows_of(frozen, adapter):
        own = lax.dynamic_slice_in_dim(frozen, half_idx * rows, rows, 0)
        return (own.astype(F32) + dot_nn(tr, adapter)).astype(BF16)

    payload = jnp.concatenate(
        [tile_rows_of(frozen_key, key_adapter_out), tile_rows_of(frozen_value, value_adapter_out), tr],
        axis=1,
    )

    frame_ids = jnp.arange(frames)
    band_row = jnp.sum(jnp.where((frame_ids == frame_idx)[:, None], band_width, 0), axis=0)

    def band_at(offsets):
        seen = functools.reduce(jnp.logical_or, [frame_ids == frame_idx + o for o in offsets])
        return jnp.sum(jnp.where(seen, band_row, 0))

    own_band = band_at((0,))
    allowed = [jnp.abs(half_idx - tile) < own_band for tile in range(2)]
    payloads = []
    plan = routes(frames)
    for d, offsets in plan:
        got = lax.ppermute(payload, "tm", pairs(frames, offsets))
        band = band_at(offsets)
        payloads.append(got)
        allowed.append(band > 0)
        if d <= NEAR:
            payloads.append(swap(got, "rep"))
            allowed.append(band > 1)
    bias = jnp.where(jnp.stack(allowed), 0.0, -jnp.inf).astype(F32)
    tt = jnp.concatenate([t] + [p[:, 2 * width :] for p in payloads], axis=0).T

    gq, gk, gv, low_q, low_b = attention(
        bias, frozen_query, out_grad, frozen_key, frozen_value, t, tr, tt,
        query_adapter_out, key_adapter_out, value_adapter_out, payloads,
    )

    own = low_b[: 2 * rows]
    same = lax.dynamic_slice_in_dim(own, half_idx * rows, rows, 0) + low_q
    other = lax.dynamic_slice_in_dim(own, (1 - half_idx) * rows, rows, 0)
    start = 2 * rows
    for d, offsets in plan:
        size = 2 * rows if d <= NEAR else rows
        back = [(target, source) for source, target in pairs(frames, offsets)]
        got = lax.ppermute(low_b[start : start + size], "tm", back)
        start += size
        same = same + got[:rows]
        if d <= NEAR:
            other = other + got[rows:]
    low = jnp.where(
        half_idx == 0,
        jnp.concatenate([same, other], axis=0),
        jnp.concatenate([other, same], axis=0),
    )
    low = low + swap(low, "rep")
    low = low + swap(low, "head")

    grads = sum_rows(jnp.concatenate([gq, gk, gv], axis=0), frame_idx, half_idx, frames)
    return grads[:rank], grads[rank : 2 * rank], grads[2 * rank :], low


def head_table(heads, frames):
    base, extra = divmod(heads, frames)
    lead = (frames - extra) // 2
    counts = [base + (1 if lead <= j < lead + extra else 0) for j in range(frames)]
    return [sum(counts[:j]) for j in range(frames)], counts


def lookup(table, index):
    value = jnp.int32(table[0])
    for j in range(1, len(table)):
        value = jnp.where(index == j, jnp.int32(table[j]), value)
    return value


def column(head):
    return pl.ds(pl.multiple_of(head * DH, DH), DH)


def vmem(count):
    return [pl.BlockSpec(memory_space=pltpu.VMEM)] * count


def pack_kernel(tables, frames, with_t, fq_ref, do_ref, fk_ref, fv_ref, t_ref, *outs):
    me, half = lax.axis_index("tm"), lax.axis_index("rep")
    rows = fq_ref.shape[0]
    for m in range(frames + 1):
        out = outs[m]
        tile = half if m < frames else 1 - half
        own = pl.ds(pl.multiple_of(tile * rows, rows), rows)
        for s, table in enumerate(tables):
            cols = column(lookup(table, me ^ m if m < frames else me))
            at = 4 * s * DH
            if m < frames:
                out[:, at : at + DH] = fq_ref[:, cols]
                out[:, at + DH : at + 2 * DH] = do_ref[:, cols]
            out[:, at + 2 * DH : at + 3 * DH] = fk_ref[own, cols]
            out[:, at + 3 * DH : at + 4 * DH] = fv_ref[own, cols]
        if with_t:
            out[:, 4 * len(tables) * DH :] = t_ref[own, :]


def pack(tables, frames, with_t, fq, do, fk, fv, t):
    rows = fq.shape[0]
    width = 4 * DH * len(tables) + (t.shape[1] if with_t else 0)
    return pl.pallas_call(
        functools.partial(pack_kernel, tables, frames, with_t),
        in_specs=vmem(5),
        out_specs=vmem(frames + 1),
        out_shape=[jax.ShapeDtypeStruct((rows, width), BF16)] * (frames + 1),
        compiler_params=pltpu.CompilerParams(vmem_limit_bytes=32 * 1024 * 1024),
    )(fq, do, fk, fv, t)


def one_head(frames, bands, q, do, frozen_k, frozen_v, t_same, t_other, aq, ak, av):
    flat = t_same.shape[0]
    rows = flat // frames
    tokens = jnp.concatenate([t_same, t_other], axis=0)

    def adapted(frozen, rows_of, adapter):
        return (frozen.astype(F32) + dot_nn(rows_of, adapter)).astype(BF16)

    query = adapted(q, t_same, aq)
    keys, values = adapted(frozen_k, tokens, ak), adapted(frozen_v, tokens, av)
    do_t, keys_t, values_t = do.T, keys.T, values.T

    def bias(i, b):
        j, need = (b, 0) if b < frames else (b - frames, 1)
        value = jnp.where(bands[i, j] > need, 0.0, -jnp.inf).astype(F32)
        return jnp.full((1, rows), value, F32)

    span = 2 if frames % 2 == 0 else 1
    wide = span * rows
    dks, dvs, dqs = [None] * (2 * frames), [None] * (2 * frames), []
    for first in range(0, frames, span):
        mine = range(first, first + span)
        blocks = list(range(frames)) + [
            frames + j for j in range(frames) if any(abs(i - j) <= NEAR for i in mine)
        ]
        here = slice(first * rows, first * rows + wide)
        q_p, do_p = query[here], do[here]

        def gather(whole, axis):
            parts = [
                whole[b * rows : (b + 1) * rows] if axis == 0 else whole[:, b * rows : (b + 1) * rows]
                for b in blocks
            ]
            return jnp.concatenate(parts, axis=axis)

        raw = dot_nt(gather(keys, 0), q_p)
        scores = [
            raw[n * rows : (n + 1) * rows] * SCALE + jnp.concatenate([bias(i, b) for i in mine], axis=1)
            for n, b in enumerate(blocks)
        ]
        top = jnp.max(functools.reduce(jnp.maximum, scores), axis=0, keepdims=True)
        shifted = [jnp.exp(s - top) for s in scores]
        inverse = 1.0 / jnp.sum(functools.reduce(jnp.add, shifted), axis=0, keepdims=True)
        probs = [s * inverse for s in shifted]
        low = jnp.concatenate([p.astype(BF16) for p in probs], axis=0)
        attended = dot_nn(gather(values_t, 1), low).astype(BF16).astype(F32)
        delta = jnp.sum(do_t[:, here].astype(F32) * attended, axis=0, keepdims=True)
        prob_grad = dot_nt(gather(values, 0), do_p)
        grad = jnp.concatenate(
            [
                (probs[n] * (prob_grad[n * rows : (n + 1) * rows] - delta)).astype(BF16)
                for n in range(len(blocks))
            ],
            axis=0,
        )
        dqs.append((dot_nn(gather(keys_t, 1), grad) * SCALE).astype(BF16).T)
        dk, dv = dot_nn(grad, q_p), dot_nn(low, do_p)
        for n, b in enumerate(blocks):
            part = slice(n * rows, (n + 1) * rows)
            dks[b] = dk[part] if dks[b] is None else dks[b] + dk[part]
            dvs[b] = dv[part] if dvs[b] is None else dvs[b] + dv[part]
    dq = jnp.concatenate(dqs, axis=0)
    dk = (jnp.concatenate(dks, axis=0) * SCALE).astype(BF16)
    dv = jnp.concatenate(dvs, axis=0).astype(BF16)
    both = jnp.concatenate([dk, dv], axis=1)
    sums = dot_tn(tokens, both)
    grads = jnp.concatenate([dot_tn(t_same, dq), sums[:, :DH], sums[:, DH:]], axis=0)
    lows = dot_nt(both, jnp.concatenate([ak, av], axis=1))
    return grads, lows[:flat] + dot_nt(dq, aq), lows[flat:]


def group_kernel(tables, frames, counts, t_col, chained, last, *refs):
    refs = list(refs)
    bands = refs.pop(0)
    mine, others = [refs.pop(0) for _ in range(frames)], [refs.pop(0) for _ in range(frames)]
    if t_col is None:
        t_mine, t_others = [refs.pop(0) for _ in range(frames)], [refs.pop(0) for _ in range(frames)]
    adapters = [refs.pop(0) for _ in range(3)]
    before = [refs.pop(0) for _ in range(2)] if chained else None
    keep_ref, give_ref = refs.pop(0), refs.pop(0)
    low_refs = None if last else [refs.pop(0) for _ in range(2)]
    same, other = refs.pop(0), refs.pop(0)
    t_same, t_other = refs.pop(0), refs.pop(0)
    me, half = lax.axis_index("tm"), lax.axis_index("rep")
    rows = mine[0].shape[0]
    flat = frames * rows
    rank = t_same.shape[1]
    cut = 3 * rank // 2
    slots = len(tables)
    main = 4 * slots * DH
    for m in range(frames):
        at = pl.ds(pl.multiple_of((me ^ m) * rows, rows), rows)
        same[at, :] = mine[m][:, :main]
        other[at, :] = others[m][:, :main]
        t_same[at, :] = t_mine[m][...] if t_col is None else mine[m][:, main:]
        t_other[at, :] = t_others[m][...] if t_col is None else others[m][:, main:]

    def body():
        total_same = before[0][...] if chained else None
        total_other = before[1][...] if chained else None
        for s, table in enumerate(tables):
            cols = column(lookup(table, me))
            at = 4 * s * DH
            kv = [
                jnp.concatenate([ref[:, at + c * DH : at + (c + 1) * DH] for ref in (same, other)], axis=0)
                for c in (2, 3)
            ]
            grads, low_same, low_other = one_head(
                frames, bands, same[:, at : at + DH], same[:, at + DH : at + 2 * DH], *kv,
                t_same[...], t_other[...], *[ref[:, cols] for ref in adapters],
            )
            first = half == 0
            keep_ref[s * cut : (s + 1) * cut, :] = jnp.where(first, grads[:cut], grads[cut:])
            give_ref[s * cut : (s + 1) * cut, :] = jnp.where(first, grads[cut:], grads[:cut])
            total_same = low_same if total_same is None else total_same + low_same
            total_other = low_other if total_other is None else total_other + low_other
        if last:
            keep_ref[slots * cut :, :] = total_same
            give_ref[slots * cut :, :] = total_other
        else:
            low_refs[0][...] = total_same
            low_refs[1][...] = total_other

    if min(counts) > 0:
        body()
    else:
        live = lookup(counts, me) > 0
        pl.when(live)(body)

        @pl.when(jnp.logical_not(live))
        def _():
            zeros = jnp.zeros((slots * cut, DH), F32)
            keep_ref[: slots * cut, :] = zeros
            give_ref[: slots * cut, :] = zeros
            keep_ref[slots * cut :, :] = before[0][...]
            give_ref[slots * cut :, :] = before[1][...]


def head_group(tables, counts, bands, mine, others, t_mine, t_others, adapters, before, last):
    frames, rows = len(mine), mine[0].shape[0]
    rank = adapters[0].shape[0]
    slots = len(tables)
    flat = frames * rows
    size = slots * 3 * rank // 2
    low = jax.ShapeDtypeStruct((flat, rank), F32)
    main = 4 * slots * DH
    inline = t_mine is None
    args = [bands, *mine, *others]
    specs = [pl.BlockSpec(memory_space=pltpu.SMEM)] + vmem(2 * frames)
    if not inline:
        col = t_mine[0].shape[1] // rank - 1
        args += [*t_mine, *t_others]
        specs += [pl.BlockSpec((rows, rank), lambda n: (0, col))] * (2 * frames)
    args += adapters
    specs += vmem(3)
    if before is not None:
        args += before
        specs += vmem(2)
    edge = jax.ShapeDtypeStruct((size + (flat if last else 0), rank), F32)
    shapes = [edge, edge] + ([] if last else [low, low])
    return pl.pallas_call(
        functools.partial(
            group_kernel, tables, frames, counts, main if inline else None, before is not None, last
        ),
        grid=(1,),
        in_specs=specs,
        out_specs=vmem(len(shapes)),
        out_shape=shapes,
        scratch_shapes=[
            pltpu.VMEM((flat, main), BF16),
            pltpu.VMEM((flat, main), BF16),
            pltpu.VMEM((flat, rank), BF16),
            pltpu.VMEM((flat, rank), BF16),
        ],
        compiler_params=pltpu.CompilerParams(vmem_limit_bytes=48 * 1024 * 1024),
    )(*args)


def hand_out_kernel(frames, size, keep_ref, got_ref, own_ref, *sends):
    me = lax.axis_index("tm")
    rows = own_ref.shape[0]
    grads = (keep_ref[:size, :] + got_ref[:size, :]).astype(BF16)
    for m in range(frames):
        at = pl.ds(pl.multiple_of(size + (me ^ m) * rows, 8), rows)
        low = keep_ref[at, :] + got_ref[at, :]
        if m == 0:
            own_ref[...] = low
        sends[m][:rows, :] = low.astype(BF16)
        sends[m][rows:, :] = grads


def hand_out(frames, rows, keep, got):
    size, rank = keep.shape[0] - frames * rows, keep.shape[1]
    send = jax.ShapeDtypeStruct((rows + size, rank), BF16)
    return pl.pallas_call(
        functools.partial(hand_out_kernel, frames, size),
        in_specs=vmem(2),
        out_specs=vmem(frames + 1),
        out_shape=[jax.ShapeDtypeStruct((rows, rank), F32)] + [send] * frames,
    )(keep, got)


def collect_kernel(frames, own_ref, *refs):
    gots, out_ref = refs[:-1], refs[-1]
    rows = own_ref.shape[0]
    size = gots[0].shape[0] - rows
    low = own_ref[...]
    for m in range(1, frames):
        low = low + gots[m][:rows, :].astype(F32)
    out_ref[:rows, :] = low.astype(BF16)
    for m in range(frames):
        out_ref[rows + m * size : rows + (m + 1) * size, :] = gots[m][rows:, :]


def collect(own, gots):
    frames, (rows, rank) = len(gots), own.shape
    size = gots[0].shape[0] - rows
    return pl.pallas_call(
        functools.partial(collect_kernel, frames),
        in_specs=vmem(frames + 1),
        out_specs=pl.BlockSpec(memory_space=pltpu.VMEM),
        out_shape=jax.ShapeDtypeStruct((rows + frames * size, rank), BF16),
    )(own, *gots)


def place_kernel(table, counts, full, *refs):
    frames = len(table)
    mine, others = refs[:frames], refs[frames : 2 * frames]
    tail, tail2, low_head, low_diag = refs[2 * frames : 2 * frames + 4]
    outs = refs[2 * frames + 4 :]
    me, half = lax.axis_index("tm"), lax.axis_index("rep")
    first = half == 0
    rank = outs[0].shape[0]
    cut = 3 * rank // 2
    rows = low_head.shape[0]
    same = tail[:rows, :].astype(F32) + low_head[...].astype(F32)
    other = tail2[:rows, :].astype(F32) + low_diag[...].astype(F32)
    outs[3][:rows, :] = jnp.where(first, same, other)
    outs[3][rows:, :] = jnp.where(first, other, same)
    for m in range(frames):
        chip = me ^ m
        for s in range(len(table[0])):
            if s < full:
                a, b = mine[m][s * cut : (s + 1) * cut, :], others[m][s * cut : (s + 1) * cut, :]
            else:
                at = rows + (m * (len(table[0]) - full) + s - full) * cut
                a, b = tail[at : at + cut, :], tail2[at : at + cut, :]
            a, b = a.astype(F32), b.astype(F32)

            def write():
                cols = column(lookup([row[s] for row in table], chip))
                both = jnp.concatenate([jnp.where(first, a, b), jnp.where(first, b, a)], axis=0)
                for o in range(3):
                    outs[o][:, cols] = both[o * rank : (o + 1) * rank]

            if s < full:
                write()
            else:
                pl.when(lookup(counts, chip) > s)(write)


def place(table, counts, mine, others, tail, tail2, low_head, low_diag, rank, width):
    rows = low_head.shape[0]
    full = min(counts)
    return pl.pallas_call(
        functools.partial(place_kernel, table, counts, full),
        in_specs=vmem(2 * len(table) + 4),
        out_specs=vmem(4),
        out_shape=[jax.ShapeDtypeStruct((rank, width), F32)] * 3
        + [jax.ShapeDtypeStruct((2 * rows, rank), F32)],
        compiler_params=pltpu.CompilerParams(vmem_limit_bytes=32 * 1024 * 1024),
    )(*mine, *others, tail, tail2, low_head, low_diag)


def exchange_plan(
    frozen_query,
    frozen_key,
    frozen_value,
    token_adapter_input,
    query_adapter_out,
    key_adapter_out,
    value_adapter_out,
    out_grad,
    band_width,
):
    rows, width = frozen_query.shape
    rank = token_adapter_input.shape[1]
    frames = band_width.shape[0]
    heads = width // DH
    starts, counts = head_table(heads, frames)
    full, most = min(counts), max(counts)
    table = [[min(starts[j] + s, heads - 1) for s in range(most)] for j in range(frames)]
    columns = [[row[s] for row in table] for s in range(most)]
    wide = [j for j in range(frames) if counts[j] == most]
    adapters = [query_adapter_out, key_adapter_out, value_adapter_out]
    arrays = (frozen_query, out_grad, frozen_key, frozen_value, token_adapter_input)

    def meet(block, m, targets=range(frames)):
        return lax.ppermute(block, "tm", [(j ^ m, j) for j in targets])

    packed = pack(columns[:full], frames, True, *arrays)
    mine = [packed[0]] + [meet(packed[m], m) for m in range(1, frames)]
    packed2 = pack(columns[full:], frames, False, *arrays)
    mine2 = [packed2[0]] + [meet(packed2[m], m, wide) for m in range(1, frames)]
    others = [packed[frames]] + [swap(block, "rep") for block in mine[1:]]
    others2 = [packed2[frames]] + [swap(block, "rep") for block in mine2[1:]]
    keep, give, *low = head_group(
        columns[:full], counts, band_width, mine, others, None, None, adapters, None, False
    )
    piece = (keep + swap(give, "rep")).astype(BF16)
    pieces = [piece] + [meet(piece, m) for m in range(1, frames)]
    pieces2 = [swap(block, "rep") for block in pieces]
    keep, give = head_group(
        columns[full:], [c - full for c in counts], band_width, mine2, others2, mine, others,
        adapters, low, True,
    )
    own, *sends = hand_out(frames, rows, keep, swap(give, "rep"))
    gots = [sends[0]] + [meet(sends[m], m) for m in range(1, frames)]
    tail = collect(own, gots)
    low = tail[:rows]
    diag = [(0, 3), (1, 2), (2, 1), (3, 0)]
    outs = place(
        table, counts, pieces, pieces2, tail, swap(tail, "rep"), swap(low, "head"),
        lax.ppermute(low, ("head", "rep"), diag), rank, width,
    )
    return tuple(outs)


def on_device(frozen_query, *rest):
    frames = rest[-1].shape[0]
    heads = frozen_query.shape[1] // DH
    whole_reach = frames <= REACH + 1 and frames & (frames - 1) == 0 and heads > frames and heads % frames
    return (exchange_plan if whole_reach else window_plan)(frozen_query, *rest)


def solution(mesh):
    in_specs = (
        P(("groups", "tm", "rep"), "head"),
        P(("groups", "tm"), "head"),
        P(("groups", "tm"), "head"),
        P(("groups", "tm"), None),
        P(None, "head"),
        P(None, "head"),
        P(None, "head"),
        P(("groups", "tm", "rep"), "head"),
        P(),
    )
    out_specs = (
        P("groups", "head"),
        P("groups", "head"),
        P("groups", "head"),
        P(("groups", "tm"), None),
    )
    return jax.shard_map(
        on_device, mesh=mesh, in_specs=in_specs, out_specs=out_specs, check_vma=False
    )
```

```python
import functools

import jax
import jax.numpy as jnp
from jax import lax
from jax.experimental import pallas as pl
from jax.experimental.pallas import tpu as pltpu
from jax.sharding import PartitionSpec as P

DH = 128
NEAR = 1
REACH = 4
SCALE = DH ** (-0.5)
F32 = jnp.float32
BF16 = jnp.bfloat16
SMALL = pltpu.CompilerParams(vmem_limit_bytes=16 * 1024 * 1024)


def dot_nn(left, right):
    return lax.dot_general(left, right, (((1,), (0,)), ((), ())), preferred_element_type=F32)


def dot_nt(left, right):
    return lax.dot_general(left, right, (((1,), (1,)), ((), ())), preferred_element_type=F32)


def dot_tn(left, right):
    return lax.dot_general(left, right, (((0,), (0,)), ((), ())), preferred_element_type=F32)


def routes(count):
    found = []
    for d in range(1, min(REACH, count - 1) + 1):
        if 2 * d >= count:
            found.append((d, (-d, d)))
        else:
            found.append((d, (-d,)))
            found.append((d, (d,)))
    return found


def pairs(count, offsets):
    return [(i + o, i) for o in offsets for i in range(count) if 0 <= i + o < count]


def swap(block, axis):
    return lax.ppermute(block, axis, [(0, 1), (1, 0)])


def attention_kernel(
    blocks, bias_ref, fq_ref, do_ref, fk_ref, fv_ref, t_ref, tr_ref, tt_ref, aq_ref, ak_ref, av_ref, *refs
):
    k_refs = refs[:blocks]
    v_refs = refs[blocks : 2 * blocks]
    gq_ref, gk_ref, gv_ref, lowq_ref, low_ref = refs[2 * blocks :]
    rows = fq_ref.shape[0]

    @pl.when(pl.program_id(0) == 0)
    def _():
        lowq_ref[...] = jnp.zeros_like(lowq_ref)
        low_ref[...] = jnp.zeros_like(low_ref)

    aq, ak, av = aq_ref[...], ak_ref[...], av_ref[...]
    query = (fq_ref[...].astype(F32) + dot_nn(tr_ref[...], aq)).astype(BF16)
    do = do_ref[...]
    own_k = (fk_ref[...].astype(F32) + dot_nn(t_ref[...], ak)).astype(BF16)
    own_v = (fv_ref[...].astype(F32) + dot_nn(t_ref[...], av)).astype(BF16)
    keys = [own_k[:rows], own_k[rows:]] + [ref[...] for ref in k_refs]
    values = [own_v[:rows], own_v[rows:]] + [ref[...] for ref in v_refs]
    count = len(keys)
    scores = [dot_nt(keys[b], query) * SCALE + bias_ref[b] for b in range(count)]
    top = functools.reduce(jnp.maximum, scores)
    top = jnp.max(top, axis=0, keepdims=True)
    shifted = [jnp.exp(s - top) for s in scores]
    total = jnp.sum(functools.reduce(jnp.add, shifted), axis=0, keepdims=True)
    inverse = 1.0 / total
    probs = [s * inverse for s in shifted]
    lows = [p.astype(BF16) for p in probs]
    attended = functools.reduce(jnp.add, [dot_tn(lows[b], values[b]) for b in range(count)])
    attended = attended.astype(BF16).astype(F32)
    delta = jnp.sum((do.astype(F32) * attended).T, axis=0, keepdims=True)
    grads = [
        (probs[b] * (dot_nt(values[b], do) - delta)).astype(BF16) for b in range(count)
    ]
    dq = functools.reduce(jnp.add, [dot_tn(grads[b], keys[b]) for b in range(count)])
    dq = (dq * SCALE).astype(BF16)
    gq_ref[...] = dot_tn(tr_ref[...], dq)
    lowq_ref[...] += dot_nt(dq, aq)
    both = jnp.concatenate([ak, av], axis=1)
    for b in range(count):
        dk = (dot_nn(grads[b], query) * SCALE).astype(BF16)
        dv = dot_nn(lows[b], do).astype(BF16)
        part = jnp.concatenate([dk, dv], axis=1)
        low_ref[b * rows : (b + 1) * rows, :] += dot_nt(part, both)
        out = dot_nn(tt_ref[:, b * rows : (b + 1) * rows], part)
        if b == 0:
            total_part = out
        else:
            total_part += out
    gk_ref[...] = total_part[:, :DH]
    gv_ref[...] = total_part[:, DH:]


def attention(bias, fq, do, fk, fv, t, tr, tt, aq, ak, av, payloads):
    rows, width = fq.shape
    heads = width // DH
    rank = t.shape[1]
    blocks = len(payloads)
    count = blocks + 2

    def col(r):
        return pl.BlockSpec((r, DH), lambda h: (0, h))

    def whole(shape):
        return pl.BlockSpec(shape, lambda h: (0, 0))

    return pl.pallas_call(
        functools.partial(attention_kernel, blocks),
        grid=(heads,),
        out_shape=[
            jax.ShapeDtypeStruct((rank, width), F32),
            jax.ShapeDtypeStruct((rank, width), F32),
            jax.ShapeDtypeStruct((rank, width), F32),
            jax.ShapeDtypeStruct((rows, rank), F32),
            jax.ShapeDtypeStruct((count * rows, rank), F32),
        ],
        in_specs=[pl.BlockSpec(memory_space=pltpu.SMEM)]
        + [col(rows), col(rows), col(2 * rows), col(2 * rows)]
        + [whole(t.shape), whole(tr.shape), whole(tt.shape)]
        + [col(rank)] * 3
        + [col(rows)] * blocks
        + [pl.BlockSpec((rows, DH), lambda h: (0, heads + h))] * blocks,
        out_specs=[col(rank)] * 3 + [whole((rows, rank)), whole((count * rows, rank))],
        compiler_params=pltpu.CompilerParams(vmem_limit_bytes=32 * 1024 * 1024),
    )(bias, fq, do, fk, fv, t, tr, tt, aq, ak, av, *payloads, *payloads)


def sum_rows(part, frame_idx, half_idx, frames):
    rows, width = part.shape
    half = width // 2
    keep = lax.dynamic_slice_in_dim(part, half_idx * half, half, 1)
    give = lax.dynamic_slice_in_dim(part, (1 - half_idx) * half, half, 1)
    mine = keep + swap(give, "rep")
    if frames & (frames - 1) or rows % frames or frames > REACH + 1:
        total = lax.psum(mine, "tm").astype(BF16)
    else:
        chunk = rows // frames
        low = mine.astype(BF16)
        acc = lax.dynamic_slice_in_dim(mine, frame_idx * chunk, chunk, 0)
        for m in range(1, frames):
            give = lax.dynamic_slice_in_dim(low, (frame_idx ^ m) * chunk, chunk, 0)
            acc = acc + lax.ppermute(give, "tm", [(i, i ^ m) for i in range(frames)]).astype(F32)
        acc = acc.astype(BF16)
        total = jnp.zeros((rows, half), BF16)
        total = lax.dynamic_update_slice_in_dim(total, acc, frame_idx * chunk, 0)
        for m in range(1, frames):
            got = lax.ppermute(acc, "tm", [(i, i ^ m) for i in range(frames)])
            total = lax.dynamic_update_slice_in_dim(total, got, (frame_idx ^ m) * chunk, 0)
    other = swap(total, "rep")
    first = jnp.where(half_idx == 0, total, other)
    second = jnp.where(half_idx == 0, other, total)
    return jnp.concatenate([first, second], axis=1).astype(F32)


def window_plan(
    frozen_query,
    frozen_key,
    frozen_value,
    token_adapter_input,
    query_adapter_out,
    key_adapter_out,
    value_adapter_out,
    out_grad,
    band_width,
):
    rows, width = frozen_query.shape
    rank = token_adapter_input.shape[1]
    frames = band_width.shape[0]
    frame_idx = lax.axis_index("tm")
    half_idx = lax.axis_index("rep")
    t = token_adapter_input
    tr = lax.dynamic_slice_in_dim(t, half_idx * rows, rows, 0)

    def tile_rows_of(frozen, adapter):
        own = lax.dynamic_slice_in_dim(frozen, half_idx * rows, rows, 0)
        return (own.astype(F32) + dot_nn(tr, adapter)).astype(BF16)

    payload = jnp.concatenate(
        [tile_rows_of(frozen_key, key_adapter_out), tile_rows_of(frozen_value, value_adapter_out), tr],
        axis=1,
    )

    frame_ids = jnp.arange(frames)
    band_row = jnp.sum(jnp.where((frame_ids == frame_idx)[:, None], band_width, 0), axis=0)

    def band_at(offsets):
        seen = functools.reduce(jnp.logical_or, [frame_ids == frame_idx + o for o in offsets])
        return jnp.sum(jnp.where(seen, band_row, 0))

    own_band = band_at((0,))
    allowed = [jnp.abs(half_idx - tile) < own_band for tile in range(2)]
    payloads = []
    plan = routes(frames)
    for d, offsets in plan:
        got = lax.ppermute(payload, "tm", pairs(frames, offsets))
        band = band_at(offsets)
        payloads.append(got)
        allowed.append(band > 0)
        if d <= NEAR:
            payloads.append(swap(got, "rep"))
            allowed.append(band > 1)
    bias = jnp.where(jnp.stack(allowed), 0.0, -jnp.inf).astype(F32)
    tt = jnp.concatenate([t] + [p[:, 2 * width :] for p in payloads], axis=0).T

    gq, gk, gv, low_q, low_b = attention(
        bias, frozen_query, out_grad, frozen_key, frozen_value, t, tr, tt,
        query_adapter_out, key_adapter_out, value_adapter_out, payloads,
    )

    own = low_b[: 2 * rows]
    same = lax.dynamic_slice_in_dim(own, half_idx * rows, rows, 0) + low_q
    other = lax.dynamic_slice_in_dim(own, (1 - half_idx) * rows, rows, 0)
    start = 2 * rows
    for d, offsets in plan:
        size = 2 * rows if d <= NEAR else rows
        back = [(target, source) for source, target in pairs(frames, offsets)]
        got = lax.ppermute(low_b[start : start + size], "tm", back)
        start += size
        same = same + got[:rows]
        if d <= NEAR:
            other = other + got[rows:]
    low = jnp.where(
        half_idx == 0,
        jnp.concatenate([same, other], axis=0),
        jnp.concatenate([other, same], axis=0),
    )
    low = low + swap(low, "rep")
    low = low + swap(low, "head")

    grads = sum_rows(jnp.concatenate([gq, gk, gv], axis=0), frame_idx, half_idx, frames)
    return grads[:rank], grads[rank : 2 * rank], grads[2 * rank :], low


def head_table(heads, frames):
    base, extra = divmod(heads, frames)
    lead = (frames - extra) // 2
    counts = [base + (1 if lead <= j < lead + extra else 0) for j in range(frames)]
    return [sum(counts[:j]) for j in range(frames)], counts


def lookup(table, index):
    value = jnp.int32(table[0])
    for j in range(1, len(table)):
        value = jnp.where(index == j, jnp.int32(table[j]), value)
    return value


def column(head):
    return pl.ds(pl.multiple_of(head * DH, DH), DH)


def vmem(count):
    return [pl.BlockSpec(memory_space=pltpu.VMEM)] * count


def pack_kernel(table, slots, frames, both, fq_ref, do_ref, fk_ref, fv_ref, t_ref, *refs):
    outs, sems = refs[:-1], refs[-1]
    me, half = lax.axis_index("tm"), lax.axis_index("rep")
    rows = fq_ref.shape[0]
    wide = slots * DH
    copies = []

    def copy(source, target):
        copies.append(pltpu.make_async_copy(source, target, sems.at[len(copies)]))
        copies[-1].start()

    def tile_rows_at(tile):
        return pl.ds(pl.multiple_of(tile * rows, rows), rows)

    for m in range(len(outs)):
        mine = m < frames
        own = tile_rows_at(half if mine else 1 - half)
        head = lookup(table, me ^ m if mine else me)
        cols = pl.ds(pl.multiple_of(head * DH, DH), wide)
        sources = [(2, fk_ref.at[own, cols]), (3, fv_ref.at[own, cols])]
        if mine:
            sources += [(0, fq_ref.at[:, cols]), (1, do_ref.at[:, cols])]
        if both:
            rest = tile_rows_at(1 - half)
            sources += [(4, fk_ref.at[rest, cols]), (5, fv_ref.at[rest, cols])]
        for place_in, source in sources:
            copy(source, outs[m].at[:, pl.ds(place_in * wide, wide)])
        if not both:
            copy(t_ref.at[own, :], outs[m].at[:, pl.ds(4 * wide, t_ref.shape[1])])
    for started in copies:
        started.wait()


def pack(table, slots, frames, both, fq, do, fk, fv, t):
    rows = fq.shape[0]
    width = 6 * DH * slots if both else 4 * DH * slots + t.shape[1]
    count = frames if both else frames + 1
    anywhere = pl.BlockSpec(memory_space=pl.ANY)
    return pl.pallas_call(
        functools.partial(pack_kernel, table, slots, frames, both),
        in_specs=[anywhere] * 5,
        out_specs=[anywhere] * count,
        out_shape=[jax.ShapeDtypeStruct((rows, width), BF16)] * count,
        scratch_shapes=[pltpu.SemaphoreType.DMA((6 * count,))],
    )(fq, do, fk, fv, t)


def one_head(frames, bands, q, do, frozen_k, frozen_v, t_same, t_other, aq, ak, av):
    flat = t_same.shape[0]
    rows = flat // frames
    tokens = jnp.concatenate([t_same, t_other], axis=0)

    def adapted(frozen, rows_of, adapter):
        return (frozen.astype(F32) + dot_nn(rows_of, adapter)).astype(BF16)

    query = adapted(q, t_same, aq)
    keys, values = adapted(frozen_k, tokens, ak), adapted(frozen_v, tokens, av)
    do_t, keys_t, values_t = do.T, keys.T, values.T

    def bias(i, b):
        j, need = (b, 0) if b < frames else (b - frames, 1)
        value = jnp.where(bands[i, j] > need, 0.0, -jnp.inf).astype(F32)
        return jnp.full((1, rows), value, F32)

    span = 2 if frames % 2 == 0 else 1
    wide = span * rows
    dks, dvs, dqs = [None] * (2 * frames), [None] * (2 * frames), []
    for first in range(0, frames, span):
        mine = range(first, first + span)
        blocks = list(range(frames)) + [
            frames + j for j in range(frames) if any(abs(i - j) <= NEAR for i in mine)
        ]
        here = slice(first * rows, first * rows + wide)
        q_p, do_p = query[here], do[here]

        def gather(whole, axis):
            parts = [
                whole[b * rows : (b + 1) * rows] if axis == 0 else whole[:, b * rows : (b + 1) * rows]
                for b in blocks
            ]
            return jnp.concatenate(parts, axis=axis)

        raw = dot_nt(gather(keys, 0), q_p)
        scores = [
            raw[n * rows : (n + 1) * rows] * SCALE + jnp.concatenate([bias(i, b) for i in mine], axis=1)
            for n, b in enumerate(blocks)
        ]
        top = jnp.max(functools.reduce(jnp.maximum, scores), axis=0, keepdims=True)
        shifted = [jnp.exp(s - top) for s in scores]
        inverse = 1.0 / jnp.sum(functools.reduce(jnp.add, shifted), axis=0, keepdims=True)
        probs = [s * inverse for s in shifted]
        low = jnp.concatenate([p.astype(BF16) for p in probs], axis=0)
        attended = dot_nn(gather(values_t, 1), low).astype(BF16).astype(F32)
        delta = jnp.sum(do_t[:, here].astype(F32) * attended, axis=0, keepdims=True)
        prob_grad = dot_nt(gather(values, 0), do_p)
        grad = jnp.concatenate(
            [
                (probs[n] * (prob_grad[n * rows : (n + 1) * rows] - delta)).astype(BF16)
                for n in range(len(blocks))
            ],
            axis=0,
        )
        dqs.append((dot_nn(gather(keys_t, 1), grad) * SCALE).astype(BF16).T)
        dk, dv = dot_nn(grad, q_p), dot_nn(low, do_p)
        for n, b in enumerate(blocks):
            part = slice(n * rows, (n + 1) * rows)
            dks[b] = dk[part] if dks[b] is None else dks[b] + dk[part]
            dvs[b] = dv[part] if dvs[b] is None else dvs[b] + dv[part]
    dq = jnp.concatenate(dqs, axis=0)
    dk = (jnp.concatenate(dks, axis=0) * SCALE).astype(BF16)
    dv = jnp.concatenate(dvs, axis=0).astype(BF16)
    both = jnp.concatenate([dk, dv], axis=1)
    sums = dot_tn(tokens, both)
    grads = jnp.concatenate([dot_tn(t_same, dq), sums[:, :DH], sums[:, DH:]], axis=0)
    lows = dot_nt(both, jnp.concatenate([ak, av], axis=1))
    return grads, lows[:flat] + dot_nt(dq, aq), lows[flat:]


def group_kernel(tables, frames, counts, chained, *refs):
    refs = list(refs)

    def take(count):
        taken = refs[:count]
        del refs[:count]
        return taken

    (bands,) = take(1)
    mine = take(frames)
    others = mine if chained else take(frames)
    if chained:
        t_mine, t_others = take(frames), take(frames)
    adapters = take(3)
    before = take(2) if chained else [None, None]
    keep_ref, give_ref = take(2)
    low_refs = [] if chained else take(2)
    same, other, t_same, t_other = refs
    me, half = lax.axis_index("tm"), lax.axis_index("rep")
    rows = mine[0].shape[0]
    cut = 3 * t_same.shape[1] // 2
    slots = len(tables)
    main = 4 * slots * DH
    wide = slots * DH

    def body():
        for m in range(frames):
            at = pl.ds(pl.multiple_of((me ^ m) * rows, rows), rows)
            same[at, :] = mine[m][:, :main]
            start = main if chained else main // 2
            other[at, :] = others[m][:, start : start + main // 2]
            t_same[at, :] = t_mine[m][...] if chained else mine[m][:, main:]
            t_other[at, :] = t_others[m][...] if chained else others[m][:, main:]
        total_same, total_other = [None if ref is None else ref[...] for ref in before]
        for s, table in enumerate(tables):
            cols = column(lookup(table, me))

            def part(c):
                return slice(c * wide + s * DH, c * wide + (s + 1) * DH)

            grads, low_same, low_other = one_head(
                frames, bands, same[:, part(0)], same[:, part(1)],
                jnp.concatenate([same[:, part(2)], other[:, part(0)]], axis=0),
                jnp.concatenate([same[:, part(3)], other[:, part(1)]], axis=0),
                t_same[...], t_other[...], *[ref[:, cols] for ref in adapters],
            )
            first = half == 0
            keep_ref[s * cut : (s + 1) * cut, :] = jnp.where(first, grads[:cut], grads[cut:])
            give_ref[s * cut : (s + 1) * cut, :] = jnp.where(first, grads[cut:], grads[:cut])
            total_same = low_same if total_same is None else total_same + low_same
            total_other = low_other if total_other is None else total_other + low_other
        if chained:
            keep_ref[slots * cut :, :] = total_same
            give_ref[slots * cut :, :] = total_other
        else:
            low_refs[0][...] = total_same
            low_refs[1][...] = total_other

    if min(counts) > 0:
        body()
    else:
        live = lookup(counts, me) > 0
        pl.when(live)(body)

        @pl.when(jnp.logical_not(live))
        def _():
            zeros = jnp.zeros((slots * cut, DH), F32)
            keep_ref[: slots * cut, :] = zeros
            give_ref[: slots * cut, :] = zeros
            keep_ref[slots * cut :, :] = before[0][...]
            give_ref[slots * cut :, :] = before[1][...]


def head_group(tables, counts, bands, mine, others, adapters, before=None):
    frames, rows = len(mine), mine[0].shape[0]
    rank = adapters[0].shape[0]
    slots = len(tables)
    flat = frames * rows
    size = slots * 3 * rank // 2
    main = 4 * slots * DH
    chained = before is not None
    args = [bands, *mine, *others, *adapters]
    specs = [pl.BlockSpec(memory_space=pltpu.SMEM)] + vmem(frames)
    if chained:
        col = others[0].shape[1] // rank - 1
        specs += [pl.BlockSpec((rows, rank), lambda n: (0, col))] * len(others) + vmem(3 + len(before))
        args += before
    else:
        specs += vmem(len(others) + 3)
    low = jax.ShapeDtypeStruct((flat, rank), F32)
    edge = jax.ShapeDtypeStruct((size + (flat if chained else 0), rank), F32)
    shapes = [edge, edge] + ([] if chained else [low, low])
    return pl.pallas_call(
        functools.partial(group_kernel, tables, frames, counts, chained),
        grid=(1,),
        in_specs=specs,
        out_specs=vmem(len(shapes)),
        out_shape=shapes,
        scratch_shapes=[
            pltpu.VMEM((flat, main), BF16),
            pltpu.VMEM((flat, main // 2), BF16),
            pltpu.VMEM((flat, rank), BF16),
            pltpu.VMEM((flat, rank), BF16),
        ],
        compiler_params=pltpu.CompilerParams(vmem_limit_bytes=40 * 1024 * 1024),
        cost_estimate=pl.CostEstimate(
            flops=4 * slots * 16 * 2 * DH * flat * 2 * flat,
            transcendentals=slots * flat * 2 * flat,
            bytes_accessed=8 * slots * flat * DH * 2,
        ),
    )(*args)


def hand_out_kernel(frames, size, waits, keep_ref, got_ref, *refs):
    own_ref, *sends = refs[waits:]
    me = lax.axis_index("tm")
    rows = own_ref.shape[0]
    grads = (keep_ref[:size, :] + got_ref[:size, :]).astype(BF16)
    for m in range(frames):
        at = pl.ds(pl.multiple_of(size + (me ^ m) * rows, 8), rows)
        low = keep_ref[at, :] + got_ref[at, :]
        if m == 0:
            own_ref[...] = low
        sends[m][:rows, :] = low.astype(BF16)
        sends[m][rows:, :] = grads


def hand_out(frames, rows, keep, got, after):
    size, rank = keep.shape[0] - frames * rows, keep.shape[1]
    send = jax.ShapeDtypeStruct((rows + size, rank), BF16)
    return pl.pallas_call(
        functools.partial(hand_out_kernel, frames, size, len(after)),
        in_specs=vmem(2) + [pl.BlockSpec(memory_space=pl.ANY)] * len(after),
        out_specs=vmem(frames + 1),
        out_shape=[jax.ShapeDtypeStruct((rows, rank), F32)] + [send] * frames,
        compiler_params=SMALL,
    )(keep, got, *after)


def collect_kernel(frames, own_ref, *refs):
    gots, out_ref = refs[:-1], refs[-1]
    rows = own_ref.shape[0]
    size = gots[0].shape[0] - rows
    low = own_ref[...]
    for m in range(1, frames):
        low = low + gots[m][:rows, :].astype(F32)
    out_ref[:rows, :] = low.astype(BF16)
    for m in range(frames):
        out_ref[rows + m * size : rows + (m + 1) * size, :] = gots[m][rows:, :]


def collect(own, gots):
    frames, (rows, rank) = len(gots), own.shape
    size = gots[0].shape[0] - rows
    return pl.pallas_call(
        functools.partial(collect_kernel, frames),
        in_specs=vmem(frames + 1),
        out_specs=pl.BlockSpec(memory_space=pltpu.VMEM),
        out_shape=jax.ShapeDtypeStruct((rows + frames * size, rank), BF16),
        compiler_params=SMALL,
    )(own, *gots)


def place_kernel(table, counts, full, *refs):
    frames = len(table)
    mine, others = refs[:frames], refs[frames : 2 * frames]
    tail, tail2, low_head, low_diag = refs[2 * frames : 2 * frames + 4]
    outs = refs[2 * frames + 4 :]
    me, half = lax.axis_index("tm"), lax.axis_index("rep")
    first = half == 0
    rank = outs[0].shape[0]
    cut = 3 * rank // 2
    rows = low_head.shape[0]
    same = tail[:rows, :].astype(F32) + low_head[...].astype(F32)
    other = tail2[:rows, :].astype(F32) + low_diag[...].astype(F32)
    outs[3][:rows, :] = jnp.where(first, same, other)
    outs[3][rows:, :] = jnp.where(first, other, same)
    for m in range(frames):
        chip = me ^ m
        for s in range(len(table[0])):
            if s < full:
                a, b = mine[m][s * cut : (s + 1) * cut, :], others[m][s * cut : (s + 1) * cut, :]
            else:
                at = rows + (m * (len(table[0]) - full) + s - full) * cut
                a, b = tail[at : at + cut, :], tail2[at : at + cut, :]
            a, b = a.astype(F32), b.astype(F32)

            def write():
                cols = column(lookup([row[s] for row in table], chip))
                both = jnp.concatenate([jnp.where(first, a, b), jnp.where(first, b, a)], axis=0)
                for o in range(3):
                    outs[o][:, cols] = both[o * rank : (o + 1) * rank]

            if s < full:
                write()
            else:
                pl.when(lookup(counts, chip) > s)(write)


def place(table, counts, mine, others, tail, tail2, low_head, low_diag, rank, width):
    rows = low_head.shape[0]
    full = min(counts)
    return pl.pallas_call(
        functools.partial(place_kernel, table, counts, full),
        in_specs=vmem(2 * len(table) + 4),
        out_specs=vmem(4),
        out_shape=[jax.ShapeDtypeStruct((rank, width), F32)] * 3
        + [jax.ShapeDtypeStruct((2 * rows, rank), F32)],
        compiler_params=SMALL,
    )(*mine, *others, tail, tail2, low_head, low_diag)


def exchange_plan(
    frozen_query,
    frozen_key,
    frozen_value,
    token_adapter_input,
    query_adapter_out,
    key_adapter_out,
    value_adapter_out,
    out_grad,
    band_width,
):
    rows, width = frozen_query.shape
    rank = token_adapter_input.shape[1]
    frames = band_width.shape[0]
    heads = width // DH
    starts, counts = head_table(heads, frames)
    full, most = min(counts), max(counts)
    table = [[min(starts[j] + s, heads - 1) for s in range(most)] for j in range(frames)]
    columns = [[row[s] for row in table] for s in range(most)]
    wide = [j for j in range(frames) if counts[j] == most]
    adapters = [query_adapter_out, key_adapter_out, value_adapter_out]
    arrays = (frozen_query, out_grad, frozen_key, frozen_value, token_adapter_input)

    def meet(block, m, targets=range(frames)):
        return lax.ppermute(block, "tm", [(j ^ m, j) for j in targets])

    packed = pack(columns[0], full, frames, False, *arrays)
    mine = [packed[0]] + [meet(packed[m], m) for m in range(1, frames)]
    packed2 = pack(columns[full], most - full, frames, True, *arrays)
    mine2 = [packed2[0]] + [meet(packed2[m], m, wide) for m in range(1, frames)]
    others = [packed[frames]] + [swap(block, "rep") for block in mine[1:]]
    keep, give, *low = head_group(columns[:full], counts, band_width, mine, others, adapters)
    piece = (keep + swap(give, "rep")).astype(BF16)
    pieces = [piece] + [meet(piece, m) for m in range(1, frames)]
    pieces2 = [swap(block, "rep") for block in pieces]
    keep, give = head_group(
        columns[full:], [c - full for c in counts], band_width, mine2, mine + others, adapters,
        low,
    )
    own, *sends = hand_out(frames, rows, keep, swap(give, "rep"), pieces[1:])
    gots = [sends[0]] + [meet(sends[m], m) for m in range(1, frames)]
    tail = collect(own, gots)
    low = tail[:rows]
    diag = [(0, 3), (1, 2), (2, 1), (3, 0)]
    outs = place(
        table, counts, pieces, pieces2, tail, swap(tail, "rep"), swap(low, "head"),
        lax.ppermute(low, ("head", "rep"), diag), rank, width,
    )
    return tuple(outs)


def on_device(frozen_query, *rest):
    frames = rest[-1].shape[0]
    heads = frozen_query.shape[1] // DH
    whole_reach = frames <= REACH + 1 and frames & (frames - 1) == 0 and heads > frames and heads % frames
    return (exchange_plan if whole_reach else window_plan)(frozen_query, *rest)


def solution(mesh):
    in_specs = (
        P(("groups", "tm", "rep"), "head"),
        P(("groups", "tm"), "head"),
        P(("groups", "tm"), "head"),
        P(("groups", "tm"), None),
        P(None, "head"),
        P(None, "head"),
        P(None, "head"),
        P(("groups", "tm", "rep"), "head"),
        P(),
    )
    out_specs = (
        P("groups", "head"),
        P("groups", "head"),
        P("groups", "head"),
        P(("groups", "tm"), None),
    )
    return jax.shard_map(
        on_device, mesh=mesh, in_specs=in_specs, out_specs=out_specs, check_vma=False
    )
```

```python
import functools

import jax
import jax.numpy as jnp
from jax import lax
from jax.experimental import pallas as pl
from jax.experimental.pallas import tpu as pltpu
from jax.sharding import PartitionSpec as P

DH = 128
NEAR = 1
REACH = 4
SCALE = DH ** (-0.5)
F32 = jnp.float32
BF16 = jnp.bfloat16
SMALL = pltpu.CompilerParams(vmem_limit_bytes=16 * 1024 * 1024)


def dot_nn(left, right):
    return lax.dot_general(left, right, (((1,), (0,)), ((), ())), preferred_element_type=F32)


def dot_nt(left, right):
    return lax.dot_general(left, right, (((1,), (1,)), ((), ())), preferred_element_type=F32)


def dot_tn(left, right):
    return lax.dot_general(left, right, (((0,), (0,)), ((), ())), preferred_element_type=F32)


def routes(count):
    found = []
    for d in range(1, min(REACH, count - 1) + 1):
        if 2 * d >= count:
            found.append((d, (-d, d)))
        else:
            found.append((d, (-d,)))
            found.append((d, (d,)))
    return found


def pairs(count, offsets):
    return [(i + o, i) for o in offsets for i in range(count) if 0 <= i + o < count]


def swap(block, axis):
    return lax.ppermute(block, axis, [(0, 1), (1, 0)])


def attention_kernel(
    blocks, bias_ref, fq_ref, do_ref, fk_ref, fv_ref, t_ref, tr_ref, tt_ref, aq_ref, ak_ref, av_ref, *refs
):
    k_refs = refs[:blocks]
    v_refs = refs[blocks : 2 * blocks]
    gq_ref, gk_ref, gv_ref, lowq_ref, low_ref = refs[2 * blocks :]
    rows = fq_ref.shape[0]

    @pl.when(pl.program_id(0) == 0)
    def _():
        lowq_ref[...] = jnp.zeros_like(lowq_ref)
        low_ref[...] = jnp.zeros_like(low_ref)

    aq, ak, av = aq_ref[...], ak_ref[...], av_ref[...]
    query = (fq_ref[...].astype(F32) + dot_nn(tr_ref[...], aq)).astype(BF16)
    do = do_ref[...]
    own_k = (fk_ref[...].astype(F32) + dot_nn(t_ref[...], ak)).astype(BF16)
    own_v = (fv_ref[...].astype(F32) + dot_nn(t_ref[...], av)).astype(BF16)
    keys = [own_k[:rows], own_k[rows:]] + [ref[...] for ref in k_refs]
    values = [own_v[:rows], own_v[rows:]] + [ref[...] for ref in v_refs]
    count = len(keys)
    scores = [dot_nt(keys[b], query) * SCALE + bias_ref[b] for b in range(count)]
    top = functools.reduce(jnp.maximum, scores)
    top = jnp.max(top, axis=0, keepdims=True)
    shifted = [jnp.exp(s - top) for s in scores]
    total = jnp.sum(functools.reduce(jnp.add, shifted), axis=0, keepdims=True)
    inverse = 1.0 / total
    probs = [s * inverse for s in shifted]
    lows = [p.astype(BF16) for p in probs]
    attended = functools.reduce(jnp.add, [dot_tn(lows[b], values[b]) for b in range(count)])
    attended = attended.astype(BF16).astype(F32)
    delta = jnp.sum((do.astype(F32) * attended).T, axis=0, keepdims=True)
    grads = [
        (probs[b] * (dot_nt(values[b], do) - delta)).astype(BF16) for b in range(count)
    ]
    dq = functools.reduce(jnp.add, [dot_tn(grads[b], keys[b]) for b in range(count)])
    dq = (dq * SCALE).astype(BF16)
    gq_ref[...] = dot_tn(tr_ref[...], dq)
    lowq_ref[...] += dot_nt(dq, aq)
    both = jnp.concatenate([ak, av], axis=1)
    for b in range(count):
        dk = (dot_nn(grads[b], query) * SCALE).astype(BF16)
        dv = dot_nn(lows[b], do).astype(BF16)
        part = jnp.concatenate([dk, dv], axis=1)
        low_ref[b * rows : (b + 1) * rows, :] += dot_nt(part, both)
        out = dot_nn(tt_ref[:, b * rows : (b + 1) * rows], part)
        if b == 0:
            total_part = out
        else:
            total_part += out
    gk_ref[...] = total_part[:, :DH]
    gv_ref[...] = total_part[:, DH:]


def attention(bias, fq, do, fk, fv, t, tr, tt, aq, ak, av, payloads):
    rows, width = fq.shape
    heads = width // DH
    rank = t.shape[1]
    blocks = len(payloads)
    count = blocks + 2

    def col(r):
        return pl.BlockSpec((r, DH), lambda h: (0, h))

    def whole(shape):
        return pl.BlockSpec(shape, lambda h: (0, 0))

    return pl.pallas_call(
        functools.partial(attention_kernel, blocks),
        grid=(heads,),
        out_shape=[
            jax.ShapeDtypeStruct((rank, width), F32),
            jax.ShapeDtypeStruct((rank, width), F32),
            jax.ShapeDtypeStruct((rank, width), F32),
            jax.ShapeDtypeStruct((rows, rank), F32),
            jax.ShapeDtypeStruct((count * rows, rank), F32),
        ],
        in_specs=[pl.BlockSpec(memory_space=pltpu.SMEM)]
        + [col(rows), col(rows), col(2 * rows), col(2 * rows)]
        + [whole(t.shape), whole(tr.shape), whole(tt.shape)]
        + [col(rank)] * 3
        + [col(rows)] * blocks
        + [pl.BlockSpec((rows, DH), lambda h: (0, heads + h))] * blocks,
        out_specs=[col(rank)] * 3 + [whole((rows, rank)), whole((count * rows, rank))],
        compiler_params=pltpu.CompilerParams(vmem_limit_bytes=32 * 1024 * 1024),
    )(bias, fq, do, fk, fv, t, tr, tt, aq, ak, av, *payloads, *payloads)


def sum_rows(part, frame_idx, half_idx, frames):
    rows, width = part.shape
    half = width // 2
    keep = lax.dynamic_slice_in_dim(part, half_idx * half, half, 1)
    give = lax.dynamic_slice_in_dim(part, (1 - half_idx) * half, half, 1)
    mine = keep + swap(give, "rep")
    if frames & (frames - 1) or rows % frames or frames > REACH + 1:
        total = lax.psum(mine, "tm").astype(BF16)
    else:
        chunk = rows // frames
        low = mine.astype(BF16)
        acc = lax.dynamic_slice_in_dim(mine, frame_idx * chunk, chunk, 0)
        for m in range(1, frames):
            give = lax.dynamic_slice_in_dim(low, (frame_idx ^ m) * chunk, chunk, 0)
            acc = acc + lax.ppermute(give, "tm", [(i, i ^ m) for i in range(frames)]).astype(F32)
        acc = acc.astype(BF16)
        total = jnp.zeros((rows, half), BF16)
        total = lax.dynamic_update_slice_in_dim(total, acc, frame_idx * chunk, 0)
        for m in range(1, frames):
            got = lax.ppermute(acc, "tm", [(i, i ^ m) for i in range(frames)])
            total = lax.dynamic_update_slice_in_dim(total, got, (frame_idx ^ m) * chunk, 0)
    other = swap(total, "rep")
    first = jnp.where(half_idx == 0, total, other)
    second = jnp.where(half_idx == 0, other, total)
    return jnp.concatenate([first, second], axis=1).astype(F32)


def window_plan(
    frozen_query,
    frozen_key,
    frozen_value,
    token_adapter_input,
    query_adapter_out,
    key_adapter_out,
    value_adapter_out,
    out_grad,
    band_width,
):
    rows, width = frozen_query.shape
    rank = token_adapter_input.shape[1]
    frames = band_width.shape[0]
    frame_idx = lax.axis_index("tm")
    half_idx = lax.axis_index("rep")
    t = token_adapter_input
    tr = lax.dynamic_slice_in_dim(t, half_idx * rows, rows, 0)

    def tile_rows_of(frozen, adapter):
        own = lax.dynamic_slice_in_dim(frozen, half_idx * rows, rows, 0)
        return (own.astype(F32) + dot_nn(tr, adapter)).astype(BF16)

    payload = jnp.concatenate(
        [tile_rows_of(frozen_key, key_adapter_out), tile_rows_of(frozen_value, value_adapter_out), tr],
        axis=1,
    )

    frame_ids = jnp.arange(frames)
    band_row = jnp.sum(jnp.where((frame_ids == frame_idx)[:, None], band_width, 0), axis=0)

    def band_at(offsets):
        seen = functools.reduce(jnp.logical_or, [frame_ids == frame_idx + o for o in offsets])
        return jnp.sum(jnp.where(seen, band_row, 0))

    own_band = band_at((0,))
    allowed = [jnp.abs(half_idx - tile) < own_band for tile in range(2)]
    payloads = []
    plan = routes(frames)
    for d, offsets in plan:
        got = lax.ppermute(payload, "tm", pairs(frames, offsets))
        band = band_at(offsets)
        payloads.append(got)
        allowed.append(band > 0)
        if d <= NEAR:
            payloads.append(swap(got, "rep"))
            allowed.append(band > 1)
    bias = jnp.where(jnp.stack(allowed), 0.0, -jnp.inf).astype(F32)
    tt = jnp.concatenate([t] + [p[:, 2 * width :] for p in payloads], axis=0).T

    gq, gk, gv, low_q, low_b = attention(
        bias, frozen_query, out_grad, frozen_key, frozen_value, t, tr, tt,
        query_adapter_out, key_adapter_out, value_adapter_out, payloads,
    )

    own = low_b[: 2 * rows]
    same = lax.dynamic_slice_in_dim(own, half_idx * rows, rows, 0) + low_q
    other = lax.dynamic_slice_in_dim(own, (1 - half_idx) * rows, rows, 0)
    start = 2 * rows
    for d, offsets in plan:
        size = 2 * rows if d <= NEAR else rows
        back = [(target, source) for source, target in pairs(frames, offsets)]
        got = lax.ppermute(low_b[start : start + size], "tm", back)
        start += size
        same = same + got[:rows]
        if d <= NEAR:
            other = other + got[rows:]
    low = jnp.where(
        half_idx == 0,
        jnp.concatenate([same, other], axis=0),
        jnp.concatenate([other, same], axis=0),
    )
    low = low + swap(low, "rep")
    low = low + swap(low, "head")

    grads = sum_rows(jnp.concatenate([gq, gk, gv], axis=0), frame_idx, half_idx, frames)
    return grads[:rank], grads[rank : 2 * rank], grads[2 * rank :], low


def head_table(heads, frames):
    base, extra = divmod(heads, frames)
    lead = (frames - extra) // 2
    counts = [base + (1 if lead <= j < lead + extra else 0) for j in range(frames)]
    return [sum(counts[:j]) for j in range(frames)], counts


def lookup(table, index):
    value = jnp.int32(table[0])
    for j in range(1, len(table)):
        value = jnp.where(index == j, jnp.int32(table[j]), value)
    return value


def column(head):
    return pl.ds(pl.multiple_of(head * DH, DH), DH)


def vmem(count):
    return [pl.BlockSpec(memory_space=pltpu.VMEM)] * count


def pack_kernel(tables, frames, full, extra, fq_ref, do_ref, fk_ref, fv_ref, t_ref, *refs):
    count = 2 * frames + 1
    outs, (q_in, do_in, k_in, v_in, k2_in, v2_in, sems) = refs[:count], refs[count:]
    me, half = lax.axis_index("tm"), lax.axis_index("rep")
    rows = fq_ref.shape[0]
    mine = pl.ds(pl.multiple_of(half * rows, rows), rows)
    rest = pl.ds(pl.multiple_of((1 - half) * rows, rows), rows)
    moves = [
        (fq_ref, q_in), (do_ref, do_in), (fk_ref.at[mine, :], k_in), (fv_ref.at[mine, :], v_in),
        (fk_ref.at[rest, :], k2_in), (fv_ref.at[rest, :], v2_in),
    ]
    copies = [pltpu.make_async_copy(a, b, sems.at[n]) for n, (a, b) in enumerate(moves)]
    for copy in copies:
        copy.start()
    for copy in copies:
        copy.wait()

    def fill(out, refs, chip, group, heads):
        wide = heads * DH
        cols = pl.ds(pl.multiple_of(lookup(tables[group], chip) * DH, DH), wide)
        for n, ref in enumerate(refs):
            if ref is not None:
                out[:, n * wide : (n + 1) * wide] = ref[:, cols]

    for m in range(frames):
        fill(outs[m], (q_in, do_in, k_in, v_in), me ^ m, 0, full)
        outs[m][:, 4 * full * DH :] = t_ref[mine, :]
        fill(outs[frames + 1 + m], (q_in, do_in, k_in, v_in, k2_in, v2_in), me ^ m, 1, extra)
    fill(outs[frames], (None, None, k2_in, v2_in), me, 0, full)
    outs[frames][:, 4 * full * DH :] = t_ref[rest, :]


def pack(tables, frames, full, extra, fq, do, fk, fv, t):
    rows, width = fq.shape
    first = jax.ShapeDtypeStruct((rows, 4 * DH * full + t.shape[1]), BF16)
    second = jax.ShapeDtypeStruct((rows, 6 * DH * extra), BF16)
    anywhere = pl.BlockSpec(memory_space=pl.ANY)
    return pl.pallas_call(
        functools.partial(pack_kernel, tables, frames, full, extra),
        in_specs=[anywhere] * 4 + vmem(1),
        out_specs=vmem(2 * frames + 1),
        out_shape=[first] * (frames + 1) + [second] * frames,
        scratch_shapes=[pltpu.VMEM((rows, width), BF16)] * 6 + [pltpu.SemaphoreType.DMA((6,))],
        compiler_params=pltpu.CompilerParams(vmem_limit_bytes=56 * 1024 * 1024),
    )(fq, do, fk, fv, t)


def one_head(frames, bands, q, do, frozen_k, frozen_v, t_same, t_other, aq, ak, av):
    flat = t_same.shape[0]
    rows = flat // frames
    tokens = jnp.concatenate([t_same, t_other], axis=0)

    def adapted(frozen, rows_of, adapter):
        return (frozen.astype(F32) + dot_nn(rows_of, adapter)).astype(BF16)

    query = adapted(q, t_same, aq)
    keys, values = adapted(frozen_k, tokens, ak), adapted(frozen_v, tokens, av)
    do_t, keys_t, values_t = do.T, keys.T, values.T

    def bias(i, b):
        j, need = (b, 0) if b < frames else (b - frames, 1)
        value = jnp.where(bands[i, j] > need, 0.0, -jnp.inf).astype(F32)
        return jnp.full((1, rows), value, F32)

    span = 2 if frames % 2 == 0 else 1
    wide = span * rows
    dks, dvs, dqs = [None] * (2 * frames), [None] * (2 * frames), []
    for first in range(0, frames, span):
        mine = range(first, first + span)
        blocks = list(range(frames)) + [
            frames + j for j in range(frames) if any(abs(i - j) <= NEAR for i in mine)
        ]
        here = slice(first * rows, first * rows + wide)
        q_p, do_p = query[here], do[here]

        def gather(whole, axis):
            parts = [
                whole[b * rows : (b + 1) * rows] if axis == 0 else whole[:, b * rows : (b + 1) * rows]
                for b in blocks
            ]
            return jnp.concatenate(parts, axis=axis)

        raw = dot_nt(gather(keys, 0), q_p)
        scores = [
            raw[n * rows : (n + 1) * rows] * SCALE + jnp.concatenate([bias(i, b) for i in mine], axis=1)
            for n, b in enumerate(blocks)
        ]
        top = jnp.max(functools.reduce(jnp.maximum, scores), axis=0, keepdims=True)
        shifted = [jnp.exp(s - top) for s in scores]
        inverse = 1.0 / jnp.sum(functools.reduce(jnp.add, shifted), axis=0, keepdims=True)
        probs = [s * inverse for s in shifted]
        low = jnp.concatenate([p.astype(BF16) for p in probs], axis=0)
        attended = dot_nn(gather(values_t, 1), low).astype(BF16).astype(F32)
        delta = jnp.sum(do_t[:, here].astype(F32) * attended, axis=0, keepdims=True)
        prob_grad = dot_nt(gather(values, 0), do_p)
        grad = jnp.concatenate(
            [
                (probs[n] * (prob_grad[n * rows : (n + 1) * rows] - delta)).astype(BF16)
                for n in range(len(blocks))
            ],
            axis=0,
        )
        dqs.append((dot_nn(gather(keys_t, 1), grad) * SCALE).astype(BF16).T)
        dk, dv = dot_nn(grad, q_p), dot_nn(low, do_p)
        for n, b in enumerate(blocks):
            part = slice(n * rows, (n + 1) * rows)
            dks[b] = dk[part] if dks[b] is None else dks[b] + dk[part]
            dvs[b] = dv[part] if dvs[b] is None else dvs[b] + dv[part]
    dq = jnp.concatenate(dqs, axis=0)
    dk = (jnp.concatenate(dks, axis=0) * SCALE).astype(BF16)
    dv = jnp.concatenate(dvs, axis=0).astype(BF16)
    both = jnp.concatenate([dk, dv], axis=1)
    sums = dot_tn(tokens, both)
    grads = jnp.concatenate([dot_tn(t_same, dq), sums[:, :DH], sums[:, DH:]], axis=0)
    lows = dot_nt(both, jnp.concatenate([ak, av], axis=1))
    return grads, lows[:flat] + dot_nt(dq, aq), lows[flat:]


def group_kernel(tables, frames, counts, chained, *refs):
    refs = list(refs)

    def take(count):
        taken = refs[:count]
        del refs[:count]
        return taken

    (bands,) = take(1)
    mine = take(frames)
    others = mine if chained else take(frames)
    if chained:
        take(1)
        t_mine, t_others = take(frames), take(frames)
    adapters = take(3)
    before = take(2) if chained else [None, None]
    keep_ref, *give_refs = take(3 if chained else 2)
    low_refs = [] if chained else take(2)
    same, other, t_same, t_other = refs
    me, half = lax.axis_index("tm"), lax.axis_index("rep")
    rows = mine[0].shape[0]
    cut = 3 * t_same.shape[1] // 2
    slots = len(tables)
    main = 4 * slots * DH
    wide = slots * DH

    def give_out(gives):
        whole = jnp.concatenate(gives, axis=0)
        size = whole.shape[0] // len(give_refs)
        for n, ref in enumerate(give_refs):
            ref[...] = whole[n * size : (n + 1) * size].astype(ref.dtype)

    def body():
        for m in range(frames):
            at = pl.ds(pl.multiple_of((me ^ m) * rows, rows), rows)
            same[at, :] = mine[m][:, :main]
            start = main if chained else main // 2
            other[at, :] = others[m][:, start : start + main // 2]
            t_same[at, :] = t_mine[m][...] if chained else mine[m][:, main:]
            t_other[at, :] = t_others[m][...] if chained else others[m][:, main:]
        gives = []
        total_same, total_other = [None if ref is None else ref[...] for ref in before]
        for s, table in enumerate(tables):
            cols = column(lookup(table, me))

            def part(c):
                return slice(c * wide + s * DH, c * wide + (s + 1) * DH)

            grads, low_same, low_other = one_head(
                frames, bands, same[:, part(0)], same[:, part(1)],
                jnp.concatenate([same[:, part(2)], other[:, part(0)]], axis=0),
                jnp.concatenate([same[:, part(3)], other[:, part(1)]], axis=0),
                t_same[...], t_other[...], *[ref[:, cols] for ref in adapters],
            )
            first = half == 0
            keep_ref[s * cut : (s + 1) * cut, :] = jnp.where(first, grads[:cut], grads[cut:])
            gives.append(jnp.where(first, grads[cut:], grads[:cut]))
            total_same = low_same if total_same is None else total_same + low_same
            total_other = low_other if total_other is None else total_other + low_other
        if chained:
            keep_ref[slots * cut :, :] = total_same
            gives.append(total_other)
        give_out(gives)
        if not chained:
            low_refs[0][...] = total_same
            low_refs[1][...] = total_other

    if min(counts) > 0:
        body()
    else:
        live = lookup(counts, me) > 0
        pl.when(live)(body)

        @pl.when(jnp.logical_not(live))
        def _():
            zeros = jnp.zeros((slots * cut, DH), F32)
            keep_ref[: slots * cut, :] = zeros
            keep_ref[slots * cut :, :] = before[0][...]
            give_out([zeros, before[1][...]])


def head_group(tables, counts, bands, mine, others, adapters, before=None, after=None):
    frames, rows = len(mine), mine[0].shape[0]
    rank = adapters[0].shape[0]
    slots = len(tables)
    flat = frames * rows
    size = slots * 3 * rank // 2
    main = 4 * slots * DH
    chained = before is not None
    args = [bands, *mine, *([after] if chained else []), *others, *adapters]
    specs = [pl.BlockSpec(memory_space=pltpu.SMEM)] + vmem(frames)
    if chained:
        specs.append(pl.BlockSpec(memory_space=pl.ANY))
    if chained:
        col = others[0].shape[1] // rank - 1
        specs += [pl.BlockSpec((rows, rank), lambda n: (0, col))] * len(others) + vmem(3 + len(before))
        args += before
    else:
        specs += vmem(len(others) + 3)
    low = jax.ShapeDtypeStruct((flat, rank), F32)
    edge = jax.ShapeDtypeStruct((size + (flat if chained else 0), rank), F32)
    if chained:
        shapes = [edge] + [jax.ShapeDtypeStruct((edge.shape[0] // 2, rank), BF16)] * 2
    else:
        shapes = [edge, edge, low, low]
    return pl.pallas_call(
        functools.partial(group_kernel, tables, frames, counts, chained),
        grid=(1,),
        in_specs=specs,
        out_specs=vmem(len(shapes)),
        out_shape=shapes,
        scratch_shapes=[
            pltpu.VMEM((flat, main), BF16),
            pltpu.VMEM((flat, main // 2), BF16),
            pltpu.VMEM((flat, rank), BF16),
            pltpu.VMEM((flat, rank), BF16),
        ],
        compiler_params=pltpu.CompilerParams(vmem_limit_bytes=40 * 1024 * 1024),
        cost_estimate=pl.CostEstimate(
            flops=4 * slots * 16 * 2 * DH * flat * 2 * flat,
            transcendentals=slots * flat * 2 * flat,
            bytes_accessed=8 * slots * flat * DH * 2,
        ),
    )(*args)


def gate(block, after):
    anywhere = pl.BlockSpec(memory_space=pl.ANY)
    return pl.pallas_call(
        lambda *refs: None,
        in_specs=[anywhere] * (1 + len(after)),
        out_specs=anywhere,
        out_shape=jax.ShapeDtypeStruct(block.shape, block.dtype),
        input_output_aliases={0: 0},
        compiler_params=SMALL,
    )(block, *after)


def hand_out_kernel(frames, size, parts, waits, keep_ref, *refs):
    gots, (own_ref, *sends, total) = refs[:parts], refs[parts + waits :]
    me = lax.axis_index("tm")
    rows = own_ref.shape[0]
    total[...] = keep_ref[...] + jnp.concatenate([got[...].astype(F32) for got in gots], axis=0)
    grads = total[:size, :].astype(BF16)
    for m in range(frames):
        low = total[pl.ds(pl.multiple_of(size + (me ^ m) * rows, 8), rows), :]
        if m == 0:
            own_ref[...] = low
        sends[m][:rows, :] = low.astype(BF16)
        sends[m][rows:, :] = grads


def hand_out(frames, rows, keep, gots, after):
    size, rank = keep.shape[0] - frames * rows, keep.shape[1]
    send = jax.ShapeDtypeStruct((rows + size, rank), BF16)
    return pl.pallas_call(
        functools.partial(hand_out_kernel, frames, size, len(gots), len(after)),
        in_specs=vmem(1 + len(gots)) + [pl.BlockSpec(memory_space=pl.ANY)] * len(after),
        out_specs=vmem(frames + 1),
        out_shape=[jax.ShapeDtypeStruct((rows, rank), F32)] + [send] * frames,
        scratch_shapes=[pltpu.VMEM(keep.shape, F32)],
        compiler_params=SMALL,
    )(keep, *gots, *after)


def collect_kernel(frames, own_ref, *refs):
    gots, out_ref = refs[:-1], refs[-1]
    rows = own_ref.shape[0]
    size = gots[0].shape[0] - rows
    low = own_ref[...]
    for m in range(1, frames):
        low = low + gots[m][:rows, :].astype(F32)
    out_ref[:rows, :] = low.astype(BF16)
    for m in range(frames):
        out_ref[rows + m * size : rows + (m + 1) * size, :] = gots[m][rows:, :]


def collect(own, gots):
    frames, (rows, rank) = len(gots), own.shape
    size = gots[0].shape[0] - rows
    return pl.pallas_call(
        functools.partial(collect_kernel, frames),
        in_specs=vmem(frames + 1),
        out_specs=pl.BlockSpec(memory_space=pltpu.VMEM),
        out_shape=jax.ShapeDtypeStruct((rows + frames * size, rank), BF16),
        compiler_params=SMALL,
    )(own, *gots)


def place_kernel(table, counts, full, *refs):
    frames = len(table)
    mine, others = refs[:frames], refs[frames : 2 * frames]
    tail, tail2, low_head, low_diag = refs[2 * frames : 2 * frames + 4]
    outs = refs[2 * frames + 4 :]
    me, half = lax.axis_index("tm"), lax.axis_index("rep")
    first = half == 0
    rank = outs[0].shape[0]
    cut = 3 * rank // 2
    rows = low_head.shape[0]
    same = tail[:rows, :].astype(F32) + low_head[...].astype(F32)
    other = tail2[:rows, :].astype(F32) + low_diag[...].astype(F32)
    outs[3][:rows, :] = jnp.where(first, same, other)
    outs[3][rows:, :] = jnp.where(first, other, same)
    for m in range(frames):
        chip = me ^ m
        for s in range(len(table[0])):
            if s < full:
                a, b = mine[m][s * cut : (s + 1) * cut, :], others[m][s * cut : (s + 1) * cut, :]
            else:
                at = rows + (m * (len(table[0]) - full) + s - full) * cut
                a, b = tail[at : at + cut, :], tail2[at : at + cut, :]
            a, b = a.astype(F32), b.astype(F32)

            def write():
                cols = column(lookup([row[s] for row in table], chip))
                both = jnp.concatenate([jnp.where(first, a, b), jnp.where(first, b, a)], axis=0)
                for o in range(3):
                    outs[o][:, cols] = both[o * rank : (o + 1) * rank]

            if s < full:
                write()
            else:
                pl.when(lookup(counts, chip) > s)(write)


def place(table, counts, mine, others, tail, tail2, low_head, low_diag, rank, width):
    rows = low_head.shape[0]
    full = min(counts)
    return pl.pallas_call(
        functools.partial(place_kernel, table, counts, full),
        in_specs=vmem(2 * len(table) + 4),
        out_specs=vmem(4),
        out_shape=[jax.ShapeDtypeStruct((rank, width), F32)] * 3
        + [jax.ShapeDtypeStruct((2 * rows, rank), F32)],
        compiler_params=SMALL,
    )(*mine, *others, tail, tail2, low_head, low_diag)


def exchange_plan(
    frozen_query,
    frozen_key,
    frozen_value,
    token_adapter_input,
    query_adapter_out,
    key_adapter_out,
    value_adapter_out,
    out_grad,
    band_width,
):
    rows, width = frozen_query.shape
    rank = token_adapter_input.shape[1]
    frames = band_width.shape[0]
    heads = width // DH
    starts, counts = head_table(heads, frames)
    full, most = min(counts), max(counts)
    table = [[min(starts[j] + s, heads - 1) for s in range(most)] for j in range(frames)]
    columns = [[row[s] for row in table] for s in range(most)]
    wide = [j for j in range(frames) if counts[j] == most]
    adapters = [query_adapter_out, key_adapter_out, value_adapter_out]
    arrays = (frozen_query, out_grad, frozen_key, frozen_value, token_adapter_input)

    def meet(block, m, targets=range(frames)):
        return lax.ppermute(block, "tm", [(j ^ m, j) for j in targets])

    extra = most - full
    tables = (columns[0], [min(h, heads - extra) for h in columns[full]])
    packed = pack(tables, frames, full, extra, *arrays)
    mine = [packed[0]] + [meet(packed[m], m) for m in range(1, frames)]
    packed2 = packed[frames + 1 :]
    mine2 = [packed2[0]] + [meet(packed2[m], m, wide) for m in range(1, frames)]
    others = [packed[frames]] + [swap(block, "rep") for block in mine[1:]]
    keep, give, *low = head_group(columns[:full], counts, band_width, mine, others, adapters)
    piece = (keep + swap(gate(give, mine2[1:]), "rep")).astype(BF16)
    pieces = [piece] + [meet(piece, m) for m in range(1, frames)]
    pieces2 = [swap(block, "rep") for block in pieces]
    keep, *gives = head_group(
        columns[full:], [c - full for c in counts], band_width, mine2, mine + others, adapters,
        low, piece,
    )
    own, *sends = hand_out(frames, rows, keep, [swap(g, "rep") for g in gives], pieces[1:])
    gots = [sends[0]] + [meet(sends[m], m) for m in range(1, frames)]
    tail = collect(own, gots)
    low = tail[:rows]
    diag = [(0, 3), (1, 2), (2, 1), (3, 0)]
    outs = place(
        table, counts, pieces, pieces2, tail, swap(tail, "rep"), swap(low, "head"),
        lax.ppermute(low, ("head", "rep"), diag), rank, width,
    )
    return tuple(outs)


def on_device(frozen_query, *rest):
    frames = rest[-1].shape[0]
    heads = frozen_query.shape[1] // DH
    whole_reach = frames <= REACH + 1 and frames & (frames - 1) == 0 and heads > frames and heads % frames
    return (exchange_plan if whole_reach else window_plan)(frozen_query, *rest)


def solution(mesh):
    in_specs = (
        P(("groups", "tm", "rep"), "head"),
        P(("groups", "tm"), "head"),
        P(("groups", "tm"), "head"),
        P(("groups", "tm"), None),
        P(None, "head"),
        P(None, "head"),
        P(None, "head"),
        P(("groups", "tm", "rep"), "head"),
        P(),
    )
    out_specs = (
        P("groups", "head"),
        P("groups", "head"),
        P("groups", "head"),
        P(("groups", "tm"), None),
    )
    return jax.shard_map(
        on_device, mesh=mesh, in_specs=in_specs, out_specs=out_specs, check_vma=False
    )
```

```python
import functools

import jax
import jax.numpy as jnp
from jax import lax
from jax.experimental import pallas as pl
from jax.experimental.pallas import tpu as pltpu
from jax.sharding import PartitionSpec as P

DH = 128
NEAR = 1
REACH = 4
SCALE = DH ** (-0.5)
F32 = jnp.float32
BF16 = jnp.bfloat16
SMALL = pltpu.CompilerParams(vmem_limit_bytes=16 * 1024 * 1024)


def dot_nn(left, right):
    return lax.dot_general(left, right, (((1,), (0,)), ((), ())), preferred_element_type=F32)


def dot_nt(left, right):
    return lax.dot_general(left, right, (((1,), (1,)), ((), ())), preferred_element_type=F32)


def dot_tn(left, right):
    return lax.dot_general(left, right, (((0,), (0,)), ((), ())), preferred_element_type=F32)


def routes(count):
    found = []
    for d in range(1, min(REACH, count - 1) + 1):
        if 2 * d >= count:
            found.append((d, (-d, d)))
        else:
            found.append((d, (-d,)))
            found.append((d, (d,)))
    return found


def pairs(count, offsets):
    return [(i + o, i) for o in offsets for i in range(count) if 0 <= i + o < count]


def swap(block, axis):
    return lax.ppermute(block, axis, [(0, 1), (1, 0)])


def attention_kernel(
    blocks, bias_ref, fq_ref, do_ref, fk_ref, fv_ref, t_ref, tr_ref, tt_ref, aq_ref, ak_ref, av_ref, *refs
):
    k_refs = refs[:blocks]
    v_refs = refs[blocks : 2 * blocks]
    gq_ref, gk_ref, gv_ref, lowq_ref, low_ref = refs[2 * blocks :]
    rows = fq_ref.shape[0]

    @pl.when(pl.program_id(0) == 0)
    def _():
        lowq_ref[...] = jnp.zeros_like(lowq_ref)
        low_ref[...] = jnp.zeros_like(low_ref)

    aq, ak, av = aq_ref[...], ak_ref[...], av_ref[...]
    query = (fq_ref[...].astype(F32) + dot_nn(tr_ref[...], aq)).astype(BF16)
    do = do_ref[...]
    own_k = (fk_ref[...].astype(F32) + dot_nn(t_ref[...], ak)).astype(BF16)
    own_v = (fv_ref[...].astype(F32) + dot_nn(t_ref[...], av)).astype(BF16)
    keys = [own_k[:rows], own_k[rows:]] + [ref[...] for ref in k_refs]
    values = [own_v[:rows], own_v[rows:]] + [ref[...] for ref in v_refs]
    count = len(keys)
    scores = [dot_nt(keys[b], query) * SCALE + bias_ref[b] for b in range(count)]
    top = functools.reduce(jnp.maximum, scores)
    top = jnp.max(top, axis=0, keepdims=True)
    shifted = [jnp.exp(s - top) for s in scores]
    total = jnp.sum(functools.reduce(jnp.add, shifted), axis=0, keepdims=True)
    inverse = 1.0 / total
    probs = [s * inverse for s in shifted]
    lows = [p.astype(BF16) for p in probs]
    attended = functools.reduce(jnp.add, [dot_tn(lows[b], values[b]) for b in range(count)])
    attended = attended.astype(BF16).astype(F32)
    delta = jnp.sum((do.astype(F32) * attended).T, axis=0, keepdims=True)
    grads = [
        (probs[b] * (dot_nt(values[b], do) - delta)).astype(BF16) for b in range(count)
    ]
    dq = functools.reduce(jnp.add, [dot_tn(grads[b], keys[b]) for b in range(count)])
    dq = (dq * SCALE).astype(BF16)
    gq_ref[...] = dot_tn(tr_ref[...], dq)
    lowq_ref[...] += dot_nt(dq, aq)
    both = jnp.concatenate([ak, av], axis=1)
    for b in range(count):
        dk = (dot_nn(grads[b], query) * SCALE).astype(BF16)
        dv = dot_nn(lows[b], do).astype(BF16)
        part = jnp.concatenate([dk, dv], axis=1)
        low_ref[b * rows : (b + 1) * rows, :] += dot_nt(part, both)
        out = dot_nn(tt_ref[:, b * rows : (b + 1) * rows], part)
        if b == 0:
            total_part = out
        else:
            total_part += out
    gk_ref[...] = total_part[:, :DH]
    gv_ref[...] = total_part[:, DH:]


def attention(bias, fq, do, fk, fv, t, tr, tt, aq, ak, av, payloads):
    rows, width = fq.shape
    heads = width // DH
    rank = t.shape[1]
    blocks = len(payloads)
    count = blocks + 2

    def col(r):
        return pl.BlockSpec((r, DH), lambda h: (0, h))

    def whole(shape):
        return pl.BlockSpec(shape, lambda h: (0, 0))

    return pl.pallas_call(
        functools.partial(attention_kernel, blocks),
        grid=(heads,),
        out_shape=[
            jax.ShapeDtypeStruct((rank, width), F32),
            jax.ShapeDtypeStruct((rank, width), F32),
            jax.ShapeDtypeStruct((rank, width), F32),
            jax.ShapeDtypeStruct((rows, rank), F32),
            jax.ShapeDtypeStruct((count * rows, rank), F32),
        ],
        in_specs=[pl.BlockSpec(memory_space=pltpu.SMEM)]
        + [col(rows), col(rows), col(2 * rows), col(2 * rows)]
        + [whole(t.shape), whole(tr.shape), whole(tt.shape)]
        + [col(rank)] * 3
        + [col(rows)] * blocks
        + [pl.BlockSpec((rows, DH), lambda h: (0, heads + h))] * blocks,
        out_specs=[col(rank)] * 3 + [whole((rows, rank)), whole((count * rows, rank))],
        compiler_params=pltpu.CompilerParams(vmem_limit_bytes=32 * 1024 * 1024),
    )(bias, fq, do, fk, fv, t, tr, tt, aq, ak, av, *payloads, *payloads)


def sum_rows(part, frame_idx, half_idx, frames):
    rows, width = part.shape
    half = width // 2
    keep = lax.dynamic_slice_in_dim(part, half_idx * half, half, 1)
    give = lax.dynamic_slice_in_dim(part, (1 - half_idx) * half, half, 1)
    mine = keep + swap(give, "rep")
    if frames & (frames - 1) or rows % frames or frames > REACH + 1:
        total = lax.psum(mine, "tm").astype(BF16)
    else:
        chunk = rows // frames
        low = mine.astype(BF16)
        acc = lax.dynamic_slice_in_dim(mine, frame_idx * chunk, chunk, 0)
        for m in range(1, frames):
            give = lax.dynamic_slice_in_dim(low, (frame_idx ^ m) * chunk, chunk, 0)
            acc = acc + lax.ppermute(give, "tm", [(i, i ^ m) for i in range(frames)]).astype(F32)
        acc = acc.astype(BF16)
        total = jnp.zeros((rows, half), BF16)
        total = lax.dynamic_update_slice_in_dim(total, acc, frame_idx * chunk, 0)
        for m in range(1, frames):
            got = lax.ppermute(acc, "tm", [(i, i ^ m) for i in range(frames)])
            total = lax.dynamic_update_slice_in_dim(total, got, (frame_idx ^ m) * chunk, 0)
    other = swap(total, "rep")
    first = jnp.where(half_idx == 0, total, other)
    second = jnp.where(half_idx == 0, other, total)
    return jnp.concatenate([first, second], axis=1).astype(F32)


def window_plan(
    frozen_query,
    frozen_key,
    frozen_value,
    token_adapter_input,
    query_adapter_out,
    key_adapter_out,
    value_adapter_out,
    out_grad,
    band_width,
):
    rows, width = frozen_query.shape
    rank = token_adapter_input.shape[1]
    frames = band_width.shape[0]
    frame_idx = lax.axis_index("tm")
    half_idx = lax.axis_index("rep")
    t = token_adapter_input
    tr = lax.dynamic_slice_in_dim(t, half_idx * rows, rows, 0)

    def tile_rows_of(frozen, adapter):
        own = lax.dynamic_slice_in_dim(frozen, half_idx * rows, rows, 0)
        return (own.astype(F32) + dot_nn(tr, adapter)).astype(BF16)

    payload = jnp.concatenate(
        [tile_rows_of(frozen_key, key_adapter_out), tile_rows_of(frozen_value, value_adapter_out), tr],
        axis=1,
    )

    frame_ids = jnp.arange(frames)
    band_row = jnp.sum(jnp.where((frame_ids == frame_idx)[:, None], band_width, 0), axis=0)

    def band_at(offsets):
        seen = functools.reduce(jnp.logical_or, [frame_ids == frame_idx + o for o in offsets])
        return jnp.sum(jnp.where(seen, band_row, 0))

    own_band = band_at((0,))
    allowed = [jnp.abs(half_idx - tile) < own_band for tile in range(2)]
    payloads = []
    plan = routes(frames)
    for d, offsets in plan:
        got = lax.ppermute(payload, "tm", pairs(frames, offsets))
        band = band_at(offsets)
        payloads.append(got)
        allowed.append(band > 0)
        if d <= NEAR:
            payloads.append(swap(got, "rep"))
            allowed.append(band > 1)
    bias = jnp.where(jnp.stack(allowed), 0.0, -jnp.inf).astype(F32)
    tt = jnp.concatenate([t] + [p[:, 2 * width :] for p in payloads], axis=0).T

    gq, gk, gv, low_q, low_b = attention(
        bias, frozen_query, out_grad, frozen_key, frozen_value, t, tr, tt,
        query_adapter_out, key_adapter_out, value_adapter_out, payloads,
    )

    own = low_b[: 2 * rows]
    same = lax.dynamic_slice_in_dim(own, half_idx * rows, rows, 0) + low_q
    other = lax.dynamic_slice_in_dim(own, (1 - half_idx) * rows, rows, 0)
    start = 2 * rows
    for d, offsets in plan:
        size = 2 * rows if d <= NEAR else rows
        back = [(target, source) for source, target in pairs(frames, offsets)]
        got = lax.ppermute(low_b[start : start + size], "tm", back)
        start += size
        same = same + got[:rows]
        if d <= NEAR:
            other = other + got[rows:]
    low = jnp.where(
        half_idx == 0,
        jnp.concatenate([same, other], axis=0),
        jnp.concatenate([other, same], axis=0),
    )
    low = low + swap(low, "rep")
    low = low + swap(low, "head")

    grads = sum_rows(jnp.concatenate([gq, gk, gv], axis=0), frame_idx, half_idx, frames)
    return grads[:rank], grads[rank : 2 * rank], grads[2 * rank :], low


def head_table(heads, frames):
    base, extra = divmod(heads, frames)
    lead = (frames - extra) // 2
    counts = [base + (1 if lead <= j < lead + extra else 0) for j in range(frames)]
    return [sum(counts[:j]) for j in range(frames)], counts


def lookup(table, index):
    value = jnp.int32(table[0])
    for j in range(1, len(table)):
        value = jnp.where(index == j, jnp.int32(table[j]), value)
    return value


def column(head):
    return pl.ds(pl.multiple_of(head * DH, DH), DH)


def vmem(count):
    return [pl.BlockSpec(memory_space=pltpu.VMEM)] * count


def pack_kernel(frames, outputs, fq_ref, do_ref, fk_ref, fv_ref, t_ref, *refs):
    outs, (q_in, do_in, k_in, v_in, k2_in, v2_in, sems) = refs[:-7], refs[-7:]
    me, half = lax.axis_index("tm"), lax.axis_index("rep")
    rows = fq_ref.shape[0]
    mine = pl.ds(pl.multiple_of(half * rows, rows), rows)
    rest = pl.ds(pl.multiple_of((1 - half) * rows, rows), rows)
    moves = [
        (fq_ref, q_in), (do_ref, do_in), (fk_ref.at[mine, :], k_in), (fv_ref.at[mine, :], v_in),
        (fk_ref.at[rest, :], k2_in), (fv_ref.at[rest, :], v2_in),
    ]
    copies = [pltpu.make_async_copy(a, b, sems.at[n]) for n, (a, b) in enumerate(moves)]
    for copy in copies:
        copy.start()
    for copy in copies:
        copy.wait()
    for out, parts in zip(outs, outputs):
        at = 0
        for table, m, what in parts:
            if what in ("t", "other t"):
                blocks = [t_ref[mine if what == "t" else rest, :]]
            else:
                cols = column(lookup(table, me ^ m))
                sources = (q_in, do_in, k_in, v_in) if what == "mine" else (k2_in, v2_in)
                blocks = [ref[:, cols] for ref in sources]
            for block in blocks:
                out[:, at : at + block.shape[1]] = block
                at += block.shape[1]


def pack(frames, outputs, limit, fq, do, fk, fv, t):
    rows, width = fq.shape
    size = {"mine": 4 * DH, "other": 2 * DH, "t": t.shape[1], "other t": t.shape[1]}
    anywhere = pl.BlockSpec(memory_space=pl.ANY)
    return pl.pallas_call(
        functools.partial(pack_kernel, frames, outputs),
        in_specs=[anywhere] * 4 + vmem(1),
        out_specs=vmem(len(outputs)),
        out_shape=[
            jax.ShapeDtypeStruct((rows, sum(size[what] for _, _, what in parts)), BF16)
            for parts in outputs
        ],
        scratch_shapes=[pltpu.VMEM((rows, width), BF16)] * 6 + [pltpu.SemaphoreType.DMA((6,))],
        compiler_params=pltpu.CompilerParams(vmem_limit_bytes=limit * 1024 * 1024),
    )(fq, do, fk, fv, t)


def pick_kernel(spans, *refs):
    out, at = refs[-1], 0
    for n, (start, size) in enumerate(spans):
        out[:, at : at + size] = refs[n][:, start : start + size]
        at += size


def pick(parts, size, after=()):
    arrays = [array for array, _ in parts]
    return pl.pallas_call(
        functools.partial(pick_kernel, [(start, size) for _, start in parts]),
        in_specs=vmem(len(arrays)) + [pl.BlockSpec(memory_space=pl.ANY)] * len(after),
        out_specs=pl.BlockSpec(memory_space=pltpu.VMEM),
        out_shape=jax.ShapeDtypeStruct((arrays[0].shape[0], size * len(parts)), arrays[0].dtype),
        compiler_params=SMALL,
    )(*arrays, *after)


def one_head(frames, bands, q, do, frozen_k, frozen_v, tokens, aq, ak, av):
    flat = q.shape[0]
    rows = flat // frames
    t_same = tokens[:flat]

    def adapted(frozen, rows_of, adapter):
        return (frozen.astype(F32) + dot_nn(rows_of, adapter)).astype(BF16)

    query = adapted(q, t_same, aq)
    keys, values = adapted(frozen_k, tokens, ak), adapted(frozen_v, tokens, av)
    do_t, keys_t, values_t = do.T, keys.T, values.T

    def bias(i, b):
        j, need = (b, 0) if b < frames else (b - frames, 1)
        value = jnp.where(bands[i, j] > need, 0.0, -jnp.inf).astype(F32)
        return jnp.full((1, rows), value, F32)

    span = 2 if frames % 2 == 0 else 1
    wide = span * rows
    dks, dvs, dqs = [None] * (2 * frames), [None] * (2 * frames), []
    for first in range(0, frames, span):
        mine = range(first, first + span)
        blocks = list(range(frames)) + [
            frames + j for j in range(frames) if any(abs(i - j) <= NEAR for i in mine)
        ]
        here = slice(first * rows, first * rows + wide)
        q_p, do_p = query[here], do[here]

        def gather(whole, axis):
            parts = [
                whole[b * rows : (b + 1) * rows] if axis == 0 else whole[:, b * rows : (b + 1) * rows]
                for b in blocks
            ]
            return jnp.concatenate(parts, axis=axis)

        raw = dot_nt(gather(keys, 0), q_p)
        scores = [
            raw[n * rows : (n + 1) * rows] * SCALE + jnp.concatenate([bias(i, b) for i in mine], axis=1)
            for n, b in enumerate(blocks)
        ]
        top = jnp.max(functools.reduce(jnp.maximum, scores), axis=0, keepdims=True)
        shifted = [jnp.exp(s - top) for s in scores]
        inverse = 1.0 / jnp.sum(functools.reduce(jnp.add, shifted), axis=0, keepdims=True)
        probs = [s * inverse for s in shifted]
        low = jnp.concatenate([p.astype(BF16) for p in probs], axis=0)
        attended = dot_nn(gather(values_t, 1), low).astype(BF16).astype(F32)
        delta = jnp.sum(do_t[:, here].astype(F32) * attended, axis=0, keepdims=True)
        prob_grad = dot_nt(gather(values, 0), do_p)
        grad = jnp.concatenate(
            [
                (probs[n] * (prob_grad[n * rows : (n + 1) * rows] - delta)).astype(BF16)
                for n in range(len(blocks))
            ],
            axis=0,
        )
        dqs.append((dot_nn(gather(keys_t, 1), grad) * SCALE).astype(BF16).T)
        dk, dv = dot_nn(grad, q_p), dot_nn(low, do_p)
        for n, b in enumerate(blocks):
            part = slice(n * rows, (n + 1) * rows)
            dks[b] = dk[part] if dks[b] is None else dks[b] + dk[part]
            dvs[b] = dv[part] if dvs[b] is None else dvs[b] + dv[part]
    dq = jnp.concatenate(dqs, axis=0)
    dk = (jnp.concatenate(dks, axis=0) * SCALE).astype(BF16)
    dv = jnp.concatenate(dvs, axis=0).astype(BF16)
    both = jnp.concatenate([dk, dv], axis=1)
    sums = dot_tn(tokens, both)
    grads = jnp.concatenate([dot_tn(t_same, dq), sums[:, :DH], sums[:, DH:]], axis=0)
    lows = dot_nt(both, jnp.concatenate([ak, av], axis=1))
    return grads, lows[:flat] + dot_nt(dq, aq), lows[flat:]


def group_kernel(heads, frames, chained, waits, sides, count, *refs):
    refs = list(refs)

    def take(count):
        taken = refs[:count]
        del refs[:count]
        return taken

    (bands,) = take(1)
    arrays, adapters = take(count), take(3)
    before = take(2) if chained else None
    take(waits)
    keep_ref, *give_refs = take(3 if chained else 2)
    low_refs = [] if chained else take(2)
    q, do, k, v, tokens = refs
    me, half = lax.axis_index("tm"), lax.axis_index("rep")
    rows = arrays[0].shape[0]
    flat = frames * rows
    cut = 3 * tokens.shape[1] // 2
    first = half == 0
    same_at = [pl.ds(pl.multiple_of((me ^ m) * rows, rows), rows) for m in range(frames)]
    other_at = [pl.ds(pl.multiple_of(flat + (me ^ m) * rows, rows), rows) for m in range(frames)]

    def put(targets, places, rows_at):
        for m, (n, start) in enumerate(places):
            for c, target in enumerate(targets):
                target[rows_at[m], :] = arrays[n][:, start + c * DH : start + (c + 1) * DH]

    put([tokens], sides[0][0], same_at)
    put([tokens], sides[0][1], other_at)

    def run(n, table):
        put([q, do, k, v], sides[1 + n][0], same_at)
        put([k, v], sides[1 + n][1], other_at)
        cols = column(lookup(table, me))
        grads, low_same, low_other = one_head(
            frames, bands, q[...], do[...], k[...], v[...], tokens[...], *[a[:, cols] for a in adapters]
        )
        keep = jnp.where(first, grads[:cut], grads[cut:])
        give = jnp.where(first, grads[cut:], grads[:cut])
        return keep, give, low_same, low_other

    if chained:
        keep, give, low_same, low_other = run(0, heads[0][0])
        keep_ref[:cut, :] = keep
        keep_ref[cut:, :] = before[0][...] + low_same
        give = jnp.concatenate([give, before[1][...] + low_other], axis=0)
        size = give.shape[0] // 2
        for n, ref in enumerate(give_refs):
            ref[...] = give[n * size : (n + 1) * size].astype(ref.dtype)
        return
    for n, (table, counts) in enumerate(heads):
        here = slice(n * cut, (n + 1) * cut)

        def body():
            keep, give, low_same, low_other = run(n, table)
            keep_ref[here, :] = keep
            give_refs[0][here, :] = give.astype(BF16)
            if n == 0:
                low_refs[0][...] = low_same
                low_refs[1][...] = low_other
            else:
                low_refs[0][...] += low_same
                low_refs[1][...] += low_other

        if min(counts) > 0:
            body()
        else:
            live = lookup(counts, me) > 0
            pl.when(live)(body)

            @pl.when(jnp.logical_not(live))
            def _():
                keep_ref[here, :] = jnp.zeros((cut, DH), F32)
                give_refs[0][here, :] = jnp.zeros((cut, DH), BF16)


def head_group(heads, bands, sides, adapters, before=(), after=()):
    frames = len(sides[0][0])
    arrays, places = [], []
    for side in sides:
        found = []
        for pairs_of in side:
            found.append([])
            for array, start in pairs_of:
                known = [n for n, a in enumerate(arrays) if a is array]
                if not known:
                    arrays.append(array)
                found[-1].append((known[0] if known else len(arrays) - 1, start))
        places.append(found)
    rows, rank = arrays[0].shape[0], adapters[0].shape[0]
    flat = frames * rows
    size = len(heads) * 3 * rank // 2
    chained = len(before) > 0
    args = [bands, *arrays, *adapters, *before, *after]
    specs = [pl.BlockSpec(memory_space=pltpu.SMEM)] + vmem(len(arrays) + 3 + len(before))
    specs += [pl.BlockSpec(memory_space=pl.ANY)] * len(after)
    low = jax.ShapeDtypeStruct((flat, rank), F32)
    if chained:
        half = jax.ShapeDtypeStruct(((size + flat) // 2, rank), BF16)
        shapes = [jax.ShapeDtypeStruct((size + flat, rank), F32), half, half]
    else:
        edge = jax.ShapeDtypeStruct((size, rank), F32)
        shapes = [edge, jax.ShapeDtypeStruct((size, rank), BF16), low, low]
    return pl.pallas_call(
        functools.partial(
            group_kernel, heads, frames, chained, len(after), places, len(arrays)
        ),
        in_specs=specs,
        out_specs=vmem(len(shapes)),
        out_shape=shapes,
        scratch_shapes=[pltpu.VMEM((flat, DH), BF16)] * 2
        + [pltpu.VMEM((2 * flat, DH), BF16)] * 2
        + [pltpu.VMEM((2 * flat, rank), BF16)],
        compiler_params=pltpu.CompilerParams(vmem_limit_bytes=40 * 1024 * 1024),
    )(*args)


def hand_out_kernel(frames, size, parts, keep_ref, *refs):
    gots, pieces, (stack, own_ref, *sends, total) = refs[:parts], refs[parts : parts + frames], refs[parts + frames :]
    me = lax.axis_index("tm")
    rows = own_ref.shape[0]
    total[...] = keep_ref[...] + jnp.concatenate([got[...].astype(F32) for got in gots], axis=0)
    grads = total[:size, :].astype(BF16)
    for m in range(frames):
        low = total[pl.ds(pl.multiple_of(size + (me ^ m) * rows, 8), rows), :]
        if m == 0:
            own_ref[...] = low
        sends[m][:rows, :] = low.astype(BF16)
        sends[m][rows:, :] = grads
        high = pieces[m].shape[0]
        stack[m * high : (m + 1) * high, :] = pieces[m][...]


def hand_out(rows, keep, gots, pieces):
    frames = len(pieces)
    size, rank = keep.shape[0] - frames * rows, keep.shape[1]
    send = jax.ShapeDtypeStruct((rows + size, rank), BF16)
    return pl.pallas_call(
        functools.partial(hand_out_kernel, frames, size, len(gots)),
        in_specs=vmem(1 + len(gots) + frames),
        out_specs=vmem(frames + 2),
        out_shape=[
            jax.ShapeDtypeStruct((frames * pieces[0].shape[0], rank), BF16),
            jax.ShapeDtypeStruct((rows, rank), F32),
        ]
        + [send] * frames,
        scratch_shapes=[pltpu.VMEM(keep.shape, F32)],
        compiler_params=SMALL,
    )(keep, *gots, *pieces)


def collect_kernel(frames, own_ref, *refs):
    gots, (out_ref, low_ref) = refs[:frames], refs[-2:]
    rows = own_ref.shape[0]
    size = gots[0].shape[0] - rows
    low = own_ref[...]
    for m in range(1, frames):
        low = low + gots[m][:rows, :].astype(F32)
    out_ref[:rows, :] = low.astype(BF16)
    low_ref[...] = low.astype(BF16)
    for m in range(frames):
        out_ref[rows + m * size : rows + (m + 1) * size, :] = gots[m][rows:, :]


def collect(own, gots, after):
    frames, (rows, rank) = len(gots), own.shape
    size = gots[0].shape[0] - rows
    return pl.pallas_call(
        functools.partial(collect_kernel, frames),
        in_specs=vmem(frames + 1) + [pl.BlockSpec(memory_space=pl.ANY)] * len(after),
        out_specs=vmem(2),
        out_shape=[
            jax.ShapeDtypeStruct((rows + frames * size, rank), BF16),
            jax.ShapeDtypeStruct((rows, rank), BF16),
        ],
        compiler_params=SMALL,
    )(own, *gots, *after)


def place_kernel(early, late, *refs):
    frames = len(late[0])
    stack, stack2, tail, tail2, low_head, low_diag, *outs = refs
    me, half = lax.axis_index("tm"), lax.axis_index("rep")
    first = half == 0
    rank = outs[0].shape[0]
    cut = 3 * rank // 2
    rows = low_head.shape[0]
    same = tail[:rows, :].astype(F32) + low_head[...].astype(F32)
    other = tail2[:rows, :].astype(F32) + low_diag[...].astype(F32)
    outs[3][:rows, :] = jnp.where(first, same, other)
    outs[3][rows:, :] = jnp.where(first, other, same)
    for m in range(frames):
        chip = me ^ m

        def write(head, a_ref, b_ref, at):
            def body():
                a, b = a_ref[at : at + cut, :].astype(F32), b_ref[at : at + cut, :].astype(F32)
                cols = column(lookup(head[0], chip))
                both = jnp.concatenate([jnp.where(first, a, b), jnp.where(first, b, a)], axis=0)
                for o in range(3):
                    outs[o][:, cols] = both[o * rank : (o + 1) * rank]

            if min(head[1]) > 0:
                body()
            else:
                pl.when(lookup(head[1], chip) > 0)(body)

        for n, head in enumerate(early):
            write(head, stack, stack2, (m * len(early) + n) * cut)
        write(late, tail, tail2, rows + m * cut)


def place(early, late, stack, stack2, tail, tail2, low_head, low_diag, rank, width):
    rows = low_head.shape[0]
    return pl.pallas_call(
        functools.partial(place_kernel, early, late),
        in_specs=vmem(6),
        out_specs=vmem(4),
        out_shape=[jax.ShapeDtypeStruct((rank, width), F32)] * 3
        + [jax.ShapeDtypeStruct((2 * rows, rank), F32)],
        compiler_params=SMALL,
    )(stack, stack2, tail, tail2, low_head, low_diag)


def exchange_plan(
    frozen_query,
    frozen_key,
    frozen_value,
    token_adapter_input,
    query_adapter_out,
    key_adapter_out,
    value_adapter_out,
    out_grad,
    band_width,
):
    rows, width = frozen_query.shape
    rank = token_adapter_input.shape[1]
    frames = band_width.shape[0]
    heads = width // DH
    starts, counts = head_table(heads, frames)
    most = max(counts)
    columns = [[min(starts[j] + s, heads - 1) for j in range(frames)] for s in range(most)]
    numbers = [[int(s < counts[j]) for j in range(frames)] for s in range(most)]
    slots = list(zip(columns, numbers))
    lead, late, rest = slots[0], slots[1], slots[2]
    wide = [j for j in range(frames) if counts[j] == most]
    adapters = [query_adapter_out, key_adapter_out, value_adapter_out]
    arrays = (frozen_query, out_grad, frozen_key, frozen_value, token_adapter_input)

    def meet(block, m, targets=range(frames)):
        return lax.ppermute(block, "tm", [(j ^ m, j) for j in targets])

    def mine(slot, m):
        return (slot[0], m, "mine")

    sent, kept, sent_late = [], [], []
    for m in range(1, frames):
        first = [mine(lead, m), (None, m, "t")]
        if m == 1:
            sent.append(first + [mine(rest, m), mine(late, m)])
        else:
            sent += [first, [mine(rest, m)]]
            sent_late.append([mine(late, m)])
    for slot in (lead, rest, late):
        kept += [[mine(slot, 0)], [(slot[0], 0, "other")]]
    kept += [[(None, 0, "t")], [(None, 0, "other t")]]
    packed = pack(frames, sent, 56, *arrays)
    packed_late = pack(frames, sent_late + kept, 16, *arrays)
    kept = packed_late[len(sent_late) :]
    block = meet(packed[0], 1)
    lead_got, rest_got, late_got = [(block, 0)], [(block, 4 * DH + rank)], [(block, 8 * DH + rank)]
    for m in range(2, frames):
        lead_got.append((meet(packed[2 * m - 3], m), 0))
        rest_got.append((meet(packed[2 * m - 2], m, wide), 0))
        late_got.append((meet(packed_late[m - 2], m), 0))

    def sides(n, got, wide_t, after=()):
        size = 2 * DH + (rank if wide_t else 0)
        cross = swap(pick([(a, start + 2 * DH) for a, start in got], size, after), "rep")
        rows_here = [(kept[2 * n], 0)] + got
        rows_there = [(kept[2 * n + 1], 0)] + [(cross, m * size) for m in range(frames - 1)]
        return rows_here, rows_there, cross

    *lead_side, cross = sides(0, lead_got, True, kept[:1])
    t_side = (
        [(kept[6], 0)] + [(a, start + 4 * DH) for a, start in lead_got],
        [(kept[7], 0)] + [(cross, m * (2 * DH + rank) + 2 * DH) for m in range(frames - 1)],
    )
    *rest_side, _ = sides(1, rest_got, False)
    early = [lead, rest]
    keep, give, *low = head_group(early, band_width, [t_side, lead_side, rest_side], adapters)
    *late_side, _ = sides(2, late_got, False, [give])
    piece = (keep + swap(give, "rep").astype(F32)).astype(BF16)
    pieces = [piece] + [meet(piece, m) for m in range(1, frames)]
    keep, *gives = head_group([late], band_width, [t_side, late_side], adapters, low, [piece])
    stack, own, *sends = hand_out(rows, keep, [swap(g, "rep") for g in gives], pieces)
    stack2 = swap(stack, "rep")
    gots = [sends[0]] + [meet(sends[m], m) for m in range(1, frames)]
    tail, low = collect(own, gots, [stack2])
    diag = [(0, 3), (1, 2), (2, 1), (3, 0)]
    low_head, low_diag = swap(low, "head"), lax.ppermute(low, ("head", "rep"), diag)
    outs = place(
        early, late, stack, stack2, tail, swap(tail, "rep"), low_head, low_diag, rank, width
    )
    return tuple(outs)


def on_device(frozen_query, *rest):
    frames = rest[-1].shape[0]
    heads = frozen_query.shape[1] // DH
    whole_reach = frames <= REACH + 1 and frames & (frames - 1) == 0 and 2 * frames < heads < 3 * frames
    return (exchange_plan if whole_reach else window_plan)(frozen_query, *rest)


def solution(mesh):
    in_specs = (
        P(("groups", "tm", "rep"), "head"),
        P(("groups", "tm"), "head"),
        P(("groups", "tm"), "head"),
        P(("groups", "tm"), None),
        P(None, "head"),
        P(None, "head"),
        P(None, "head"),
        P(("groups", "tm", "rep"), "head"),
        P(),
    )
    out_specs = (
        P("groups", "head"),
        P("groups", "head"),
        P("groups", "head"),
        P(("groups", "tm"), None),
    )
    return jax.shard_map(
        on_device, mesh=mesh, in_specs=in_specs, out_specs=out_specs, check_vma=False
    )
```

```python
import functools

import jax
import jax.numpy as jnp
from jax import lax
from jax.experimental import pallas as pl
from jax.experimental.pallas import tpu as pltpu
from jax.sharding import PartitionSpec as P

DH = 128
NEAR = 1
REACH = 4
SCALE = DH ** (-0.5)
F32 = jnp.float32
BF16 = jnp.bfloat16
SMALL = pltpu.CompilerParams(vmem_limit_bytes=16 * 1024 * 1024)


def dot_nn(left, right):
    return lax.dot_general(left, right, (((1,), (0,)), ((), ())), preferred_element_type=F32)


def dot_nt(left, right):
    return lax.dot_general(left, right, (((1,), (1,)), ((), ())), preferred_element_type=F32)


def dot_tn(left, right):
    return lax.dot_general(left, right, (((0,), (0,)), ((), ())), preferred_element_type=F32)


def routes(count):
    found = []
    for d in range(1, min(REACH, count - 1) + 1):
        if 2 * d >= count:
            found.append((d, (-d, d)))
        else:
            found.append((d, (-d,)))
            found.append((d, (d,)))
    return found


def pairs(count, offsets):
    return [(i + o, i) for o in offsets for i in range(count) if 0 <= i + o < count]


def swap(block, axis):
    return lax.ppermute(block, axis, [(0, 1), (1, 0)])


def attention_kernel(
    blocks, bias_ref, fq_ref, do_ref, fk_ref, fv_ref, t_ref, tr_ref, tt_ref, aq_ref, ak_ref, av_ref, *refs
):
    k_refs = refs[:blocks]
    v_refs = refs[blocks : 2 * blocks]
    gq_ref, gk_ref, gv_ref, lowq_ref, low_ref = refs[2 * blocks :]
    rows = fq_ref.shape[0]

    @pl.when(pl.program_id(0) == 0)
    def _():
        lowq_ref[...] = jnp.zeros_like(lowq_ref)
        low_ref[...] = jnp.zeros_like(low_ref)

    aq, ak, av = aq_ref[...], ak_ref[...], av_ref[...]
    query = (fq_ref[...].astype(F32) + dot_nn(tr_ref[...], aq)).astype(BF16)
    do = do_ref[...]
    own_k = (fk_ref[...].astype(F32) + dot_nn(t_ref[...], ak)).astype(BF16)
    own_v = (fv_ref[...].astype(F32) + dot_nn(t_ref[...], av)).astype(BF16)
    keys = [own_k[:rows], own_k[rows:]] + [ref[...] for ref in k_refs]
    values = [own_v[:rows], own_v[rows:]] + [ref[...] for ref in v_refs]
    count = len(keys)
    scores = [dot_nt(keys[b], query) * SCALE + bias_ref[b] for b in range(count)]
    top = functools.reduce(jnp.maximum, scores)
    top = jnp.max(top, axis=0, keepdims=True)
    shifted = [jnp.exp(s - top) for s in scores]
    total = jnp.sum(functools.reduce(jnp.add, shifted), axis=0, keepdims=True)
    inverse = 1.0 / total
    probs = [s * inverse for s in shifted]
    lows = [p.astype(BF16) for p in probs]
    attended = functools.reduce(jnp.add, [dot_tn(lows[b], values[b]) for b in range(count)])
    attended = attended.astype(BF16).astype(F32)
    delta = jnp.sum((do.astype(F32) * attended).T, axis=0, keepdims=True)
    grads = [
        (probs[b] * (dot_nt(values[b], do) - delta)).astype(BF16) for b in range(count)
    ]
    dq = functools.reduce(jnp.add, [dot_tn(grads[b], keys[b]) for b in range(count)])
    dq = (dq * SCALE).astype(BF16)
    gq_ref[...] = dot_tn(tr_ref[...], dq)
    lowq_ref[...] += dot_nt(dq, aq)
    both = jnp.concatenate([ak, av], axis=1)
    for b in range(count):
        dk = (dot_nn(grads[b], query) * SCALE).astype(BF16)
        dv = dot_nn(lows[b], do).astype(BF16)
        part = jnp.concatenate([dk, dv], axis=1)
        low_ref[b * rows : (b + 1) * rows, :] += dot_nt(part, both)
        out = dot_nn(tt_ref[:, b * rows : (b + 1) * rows], part)
        if b == 0:
            total_part = out
        else:
            total_part += out
    gk_ref[...] = total_part[:, :DH]
    gv_ref[...] = total_part[:, DH:]


def attention(bias, fq, do, fk, fv, t, tr, tt, aq, ak, av, payloads):
    rows, width = fq.shape
    heads = width // DH
    rank = t.shape[1]
    blocks = len(payloads)
    count = blocks + 2

    def col(r):
        return pl.BlockSpec((r, DH), lambda h: (0, h))

    def whole(shape):
        return pl.BlockSpec(shape, lambda h: (0, 0))

    return pl.pallas_call(
        functools.partial(attention_kernel, blocks),
        grid=(heads,),
        out_shape=[
            jax.ShapeDtypeStruct((rank, width), F32),
            jax.ShapeDtypeStruct((rank, width), F32),
            jax.ShapeDtypeStruct((rank, width), F32),
            jax.ShapeDtypeStruct((rows, rank), F32),
            jax.ShapeDtypeStruct((count * rows, rank), F32),
        ],
        in_specs=[pl.BlockSpec(memory_space=pltpu.SMEM)]
        + [col(rows), col(rows), col(2 * rows), col(2 * rows)]
        + [whole(t.shape), whole(tr.shape), whole(tt.shape)]
        + [col(rank)] * 3
        + [col(rows)] * blocks
        + [pl.BlockSpec((rows, DH), lambda h: (0, heads + h))] * blocks,
        out_specs=[col(rank)] * 3 + [whole((rows, rank)), whole((count * rows, rank))],
        compiler_params=pltpu.CompilerParams(vmem_limit_bytes=32 * 1024 * 1024),
    )(bias, fq, do, fk, fv, t, tr, tt, aq, ak, av, *payloads, *payloads)


def sum_rows(part, frame_idx, half_idx, frames):
    rows, width = part.shape
    half = width // 2
    keep = lax.dynamic_slice_in_dim(part, half_idx * half, half, 1)
    give = lax.dynamic_slice_in_dim(part, (1 - half_idx) * half, half, 1)
    mine = keep + swap(give, "rep")
    if frames & (frames - 1) or rows % frames or frames > REACH + 1:
        total = lax.psum(mine, "tm").astype(BF16)
    else:
        chunk = rows // frames
        low = mine.astype(BF16)
        acc = lax.dynamic_slice_in_dim(mine, frame_idx * chunk, chunk, 0)
        for m in range(1, frames):
            give = lax.dynamic_slice_in_dim(low, (frame_idx ^ m) * chunk, chunk, 0)
            acc = acc + lax.ppermute(give, "tm", [(i, i ^ m) for i in range(frames)]).astype(F32)
        acc = acc.astype(BF16)
        total = jnp.zeros((rows, half), BF16)
        total = lax.dynamic_update_slice_in_dim(total, acc, frame_idx * chunk, 0)
        for m in range(1, frames):
            got = lax.ppermute(acc, "tm", [(i, i ^ m) for i in range(frames)])
            total = lax.dynamic_update_slice_in_dim(total, got, (frame_idx ^ m) * chunk, 0)
    other = swap(total, "rep")
    first = jnp.where(half_idx == 0, total, other)
    second = jnp.where(half_idx == 0, other, total)
    return jnp.concatenate([first, second], axis=1).astype(F32)


def window_plan(
    frozen_query,
    frozen_key,
    frozen_value,
    token_adapter_input,
    query_adapter_out,
    key_adapter_out,
    value_adapter_out,
    out_grad,
    band_width,
):
    rows, width = frozen_query.shape
    rank = token_adapter_input.shape[1]
    frames = band_width.shape[0]
    frame_idx = lax.axis_index("tm")
    half_idx = lax.axis_index("rep")
    t = token_adapter_input
    tr = lax.dynamic_slice_in_dim(t, half_idx * rows, rows, 0)

    def tile_rows_of(frozen, adapter):
        own = lax.dynamic_slice_in_dim(frozen, half_idx * rows, rows, 0)
        return (own.astype(F32) + dot_nn(tr, adapter)).astype(BF16)

    payload = jnp.concatenate(
        [tile_rows_of(frozen_key, key_adapter_out), tile_rows_of(frozen_value, value_adapter_out), tr],
        axis=1,
    )

    frame_ids = jnp.arange(frames)
    band_row = jnp.sum(jnp.where((frame_ids == frame_idx)[:, None], band_width, 0), axis=0)

    def band_at(offsets):
        seen = functools.reduce(jnp.logical_or, [frame_ids == frame_idx + o for o in offsets])
        return jnp.sum(jnp.where(seen, band_row, 0))

    own_band = band_at((0,))
    allowed = [jnp.abs(half_idx - tile) < own_band for tile in range(2)]
    payloads = []
    plan = routes(frames)
    for d, offsets in plan:
        got = lax.ppermute(payload, "tm", pairs(frames, offsets))
        band = band_at(offsets)
        payloads.append(got)
        allowed.append(band > 0)
        if d <= NEAR:
            payloads.append(swap(got, "rep"))
            allowed.append(band > 1)
    bias = jnp.where(jnp.stack(allowed), 0.0, -jnp.inf).astype(F32)
    tt = jnp.concatenate([t] + [p[:, 2 * width :] for p in payloads], axis=0).T

    gq, gk, gv, low_q, low_b = attention(
        bias, frozen_query, out_grad, frozen_key, frozen_value, t, tr, tt,
        query_adapter_out, key_adapter_out, value_adapter_out, payloads,
    )

    own = low_b[: 2 * rows]
    same = lax.dynamic_slice_in_dim(own, half_idx * rows, rows, 0) + low_q
    other = lax.dynamic_slice_in_dim(own, (1 - half_idx) * rows, rows, 0)
    start = 2 * rows
    for d, offsets in plan:
        size = 2 * rows if d <= NEAR else rows
        back = [(target, source) for source, target in pairs(frames, offsets)]
        got = lax.ppermute(low_b[start : start + size], "tm", back)
        start += size
        same = same + got[:rows]
        if d <= NEAR:
            other = other + got[rows:]
    low = jnp.where(
        half_idx == 0,
        jnp.concatenate([same, other], axis=0),
        jnp.concatenate([other, same], axis=0),
    )
    low = low + swap(low, "rep")
    low = low + swap(low, "head")

    grads = sum_rows(jnp.concatenate([gq, gk, gv], axis=0), frame_idx, half_idx, frames)
    return grads[:rank], grads[rank : 2 * rank], grads[2 * rank :], low


def head_table(heads, frames):
    base, extra = divmod(heads, frames)
    lead = (frames - extra) // 2
    counts = [base + (1 if lead <= j < lead + extra else 0) for j in range(frames)]
    return [sum(counts[:j]) for j in range(frames)], counts


def lookup(table, index):
    value = jnp.int32(table[0])
    for j in range(1, len(table)):
        value = jnp.where(index == j, jnp.int32(table[j]), value)
    return value


def column(head):
    return pl.ds(pl.multiple_of(head * DH, DH), DH)


def vmem(count):
    return [pl.BlockSpec(memory_space=pltpu.VMEM)] * count


def pack_kernel(frames, outputs, fq_ref, do_ref, fk_ref, fv_ref, t_ref, *refs):
    outs, (q_in, do_in, k_in, v_in, k2_in, v2_in, t_in, sems) = refs[:-8], refs[-8:]
    me, half = lax.axis_index("tm"), lax.axis_index("rep")
    rows = fq_ref.shape[0]
    mine = pl.ds(pl.multiple_of(half * rows, rows), rows)
    rest = pl.ds(pl.multiple_of((1 - half) * rows, rows), rows)
    moves = [
        (fq_ref, q_in), (do_ref, do_in), (fk_ref.at[mine, :], k_in), (fv_ref.at[mine, :], v_in),
        (fk_ref.at[rest, :], k2_in), (fv_ref.at[rest, :], v2_in), (t_ref, t_in),
    ]
    copies = [pltpu.make_async_copy(a, b, sems.at[n]) for n, (a, b) in enumerate(moves)]
    for copy in copies:
        copy.start()
    for copy in copies:
        copy.wait()
    for out, parts in zip(outs, outputs):
        at = 0
        for table, m, what in parts:
            if what in ("t", "other t"):
                blocks = [t_in[mine if what == "t" else rest, :]]
            else:
                cols = column(lookup(table, me ^ m))
                sources = (q_in, do_in, k_in, v_in) if what == "mine" else (k2_in, v2_in)
                blocks = [ref[:, cols] for ref in sources]
            for block in blocks:
                out[:, at : at + block.shape[1]] = block
                at += block.shape[1]


def pack(frames, outputs, limit, fq, do, fk, fv, t):
    rows, width = fq.shape
    size = {"mine": 4 * DH, "other": 2 * DH, "t": t.shape[1], "other t": t.shape[1]}
    return pl.pallas_call(
        functools.partial(pack_kernel, frames, outputs),
        in_specs=[pl.BlockSpec(memory_space=pltpu.HBM)] * 5,
        out_specs=vmem(len(outputs)),
        out_shape=[
            jax.ShapeDtypeStruct((rows, sum(size[what] for _, _, what in parts)), BF16)
            for parts in outputs
        ],
        scratch_shapes=[pltpu.VMEM((rows, width), BF16)] * 6
        + [pltpu.VMEM(t.shape, BF16), pltpu.SemaphoreType.DMA((7,))],
        compiler_params=pltpu.CompilerParams(vmem_limit_bytes=limit * 1024 * 1024),
    )(fq, do, fk, fv, t)


def pick_kernel(spans, apart, *refs):
    at = 0
    for n, (start, size) in enumerate(spans):
        out = refs[n - len(spans)] if apart else refs[-1].at[:, pl.ds(at, size)]
        out[...] = refs[n][:, start : start + size]
        at += size


def pick(parts, size, apart, after=()):
    arrays = [array for array, _ in parts]
    rows, dtype = arrays[0].shape[0], arrays[0].dtype
    shapes = [(rows, size)] * len(arrays) if apart else [(rows, size * len(arrays))]
    return pl.pallas_call(
        functools.partial(pick_kernel, [(start, size) for _, start in parts], apart),
        in_specs=vmem(len(arrays)) + [pl.BlockSpec(memory_space=pl.ANY)] * len(after),
        out_specs=vmem(len(shapes)),
        out_shape=[jax.ShapeDtypeStruct(shape, dtype) for shape in shapes],
        compiler_params=SMALL,
    )(*arrays, *after)


def one_head(frames, bands, q, do, frozen_k, frozen_v, tokens, aq, ak, av):
    flat = q.shape[0]
    rows = flat // frames
    t_same = tokens[:flat]

    def adapted(frozen, rows_of, adapter):
        return (frozen.astype(F32) + dot_nn(rows_of, adapter)).astype(BF16)

    query = adapted(q, t_same, aq)
    keys, values = adapted(frozen_k, tokens, ak), adapted(frozen_v, tokens, av)
    do_t, keys_t, values_t = do.T, keys.T, values.T

    def bias(i, b):
        j, need = (b, 0) if b < frames else (b - frames, 1)
        value = jnp.where(bands[i, j] > need, 0.0, -jnp.inf).astype(F32)
        return jnp.full((1, rows), value, F32)

    span = 2 if frames % 2 == 0 else 1
    wide = span * rows
    dks, dvs, dqs = [None] * (2 * frames), [None] * (2 * frames), []
    for first in range(0, frames, span):
        mine = range(first, first + span)
        blocks = list(range(frames)) + [
            frames + j for j in range(frames) if any(abs(i - j) <= NEAR for i in mine)
        ]
        here = slice(first * rows, first * rows + wide)
        q_p, do_p = query[here], do[here]

        def gather(whole, axis):
            parts = [
                whole[b * rows : (b + 1) * rows] if axis == 0 else whole[:, b * rows : (b + 1) * rows]
                for b in blocks
            ]
            return jnp.concatenate(parts, axis=axis)

        raw = dot_nt(gather(keys, 0), q_p)
        scores = [
            raw[n * rows : (n + 1) * rows] * SCALE + jnp.concatenate([bias(i, b) for i in mine], axis=1)
            for n, b in enumerate(blocks)
        ]
        top = jnp.max(functools.reduce(jnp.maximum, scores), axis=0, keepdims=True)
        shifted = [jnp.exp(s - top) for s in scores]
        inverse = 1.0 / jnp.sum(functools.reduce(jnp.add, shifted), axis=0, keepdims=True)
        probs = [s * inverse for s in shifted]
        low = jnp.concatenate([p.astype(BF16) for p in probs], axis=0)
        attended = dot_nn(gather(values_t, 1), low).astype(BF16).astype(F32)
        delta = jnp.sum(do_t[:, here].astype(F32) * attended, axis=0, keepdims=True)
        prob_grad = dot_nt(gather(values, 0), do_p)
        grad = jnp.concatenate(
            [
                (probs[n] * (prob_grad[n * rows : (n + 1) * rows] - delta)).astype(BF16)
                for n in range(len(blocks))
            ],
            axis=0,
        )
        dqs.append((dot_nn(gather(keys_t, 1), grad) * SCALE).astype(BF16).T)
        dk, dv = dot_nn(grad, q_p), dot_nn(low, do_p)
        for n, b in enumerate(blocks):
            part = slice(n * rows, (n + 1) * rows)
            dks[b] = dk[part] if dks[b] is None else dks[b] + dk[part]
            dvs[b] = dv[part] if dvs[b] is None else dvs[b] + dv[part]
    dq = jnp.concatenate(dqs, axis=0)
    dk = (jnp.concatenate(dks, axis=0) * SCALE).astype(BF16)
    dv = jnp.concatenate(dvs, axis=0).astype(BF16)
    both = jnp.concatenate([dk, dv], axis=1)
    sums = dot_tn(tokens, both)
    grads = jnp.concatenate([dot_tn(t_same, dq), sums[:, :DH], sums[:, DH:]], axis=0)
    lows = dot_nt(both, jnp.concatenate([ak, av], axis=1))
    return grads, lows[:flat] + dot_nt(dq, aq), lows[flat:]


def group_kernel(heads, frames, chained, waits, sides, count, *refs):
    refs = list(refs)

    def take(count):
        taken = refs[:count]
        del refs[:count]
        return taken

    (bands,) = take(1)
    arrays, adapters = take(count), take(3)
    before = take(2) if chained else None
    take(waits)
    keep_ref, *give_refs = take(3 if chained else 2)
    low_refs = [] if chained else take(2)
    q, do, k, v, tokens = refs
    me, half = lax.axis_index("tm"), lax.axis_index("rep")
    rows = arrays[0].shape[0]
    flat = frames * rows
    cut = 3 * tokens.shape[1] // 2
    first = half == 0
    same_at = [pl.ds(pl.multiple_of((me ^ m) * rows, rows), rows) for m in range(frames)]
    other_at = [pl.ds(pl.multiple_of(flat + (me ^ m) * rows, rows), rows) for m in range(frames)]

    def put(targets, places, rows_at):
        for m, (n, start) in enumerate(places):
            for c, target in enumerate(targets):
                target[rows_at[m], :] = arrays[n][:, start + c * DH : start + (c + 1) * DH]

    put([tokens], sides[0][0], same_at)
    put([tokens], sides[0][1], other_at)

    def run(n, table):
        put([q, do, k, v], sides[1 + n][0], same_at)
        put([k, v], sides[1 + n][1], other_at)
        cols = column(lookup(table, me))
        grads, low_same, low_other = one_head(
            frames, bands, q[...], do[...], k[...], v[...], tokens[...], *[a[:, cols] for a in adapters]
        )
        keep = jnp.where(first, grads[:cut], grads[cut:])
        give = jnp.where(first, grads[cut:], grads[:cut])
        return keep, give, low_same, low_other

    if chained:
        keep, give, low_same, low_other = run(0, heads[0][0])
        keep_ref[:cut, :] = keep
        keep_ref[cut:, :] = before[0][...] + low_same
        give = jnp.concatenate([give, before[1][...] + low_other], axis=0)
        size = give.shape[0] // 2
        for n, ref in enumerate(give_refs):
            ref[...] = give[n * size : (n + 1) * size].astype(ref.dtype)
        return
    for n, (table, counts) in enumerate(heads):
        here = slice(n * cut, (n + 1) * cut)

        def body():
            keep, give, low_same, low_other = run(n, table)
            keep_ref[here, :] = keep
            give_refs[0][here, :] = give.astype(BF16)
            if n == 0:
                low_refs[0][...] = low_same
                low_refs[1][...] = low_other
            else:
                low_refs[0][...] += low_same
                low_refs[1][...] += low_other

        if min(counts) > 0:
            body()
        else:
            live = lookup(counts, me) > 0
            pl.when(live)(body)

            @pl.when(jnp.logical_not(live))
            def _():
                keep_ref[here, :] = jnp.zeros((cut, DH), F32)
                give_refs[0][here, :] = jnp.zeros((cut, DH), BF16)


def head_group(heads, bands, sides, adapters, before=(), after=()):
    frames = len(sides[0][0])
    arrays, places = [], []
    for side in sides:
        found = []
        for pairs_of in side:
            found.append([])
            for array, start in pairs_of:
                known = [n for n, a in enumerate(arrays) if a is array]
                if not known:
                    arrays.append(array)
                found[-1].append((known[0] if known else len(arrays) - 1, start))
        places.append(found)
    rows, rank = arrays[0].shape[0], adapters[0].shape[0]
    flat = frames * rows
    size = len(heads) * 3 * rank // 2
    chained = len(before) > 0
    args = [bands, *arrays, *adapters, *before, *after]
    specs = [pl.BlockSpec(memory_space=pltpu.SMEM)] + vmem(len(arrays) + 3 + len(before))
    specs += [pl.BlockSpec(memory_space=pl.ANY)] * len(after)
    low = jax.ShapeDtypeStruct((flat, rank), F32)
    if chained:
        half = jax.ShapeDtypeStruct(((size + flat) // 2, rank), BF16)
        shapes = [jax.ShapeDtypeStruct((size + flat, rank), F32), half, half]
    else:
        edge = jax.ShapeDtypeStruct((size, rank), F32)
        shapes = [edge, jax.ShapeDtypeStruct((size, rank), BF16), low, low]
    return pl.pallas_call(
        functools.partial(
            group_kernel, heads, frames, chained, len(after), places, len(arrays)
        ),
        in_specs=specs,
        out_specs=vmem(len(shapes)),
        out_shape=shapes,
        scratch_shapes=[pltpu.VMEM((flat, DH), BF16)] * 2
        + [pltpu.VMEM((2 * flat, DH), BF16)] * 2
        + [pltpu.VMEM((2 * flat, rank), BF16)],
        compiler_params=pltpu.CompilerParams(vmem_limit_bytes=40 * 1024 * 1024),
    )(*args)


def hand_out_kernel(frames, size, parts, keep_ref, *refs):
    gots, (own_ref, *sends, total) = refs[:parts], refs[parts:]
    me = lax.axis_index("tm")
    rows = own_ref.shape[0]
    total[...] = keep_ref[...] + jnp.concatenate([got[...].astype(F32) for got in gots], axis=0)
    grads = total[:size, :].astype(BF16)
    for m in range(frames):
        low = total[pl.ds(pl.multiple_of(size + (me ^ m) * rows, 8), rows), :]
        if m == 0:
            own_ref[...] = low
        sends[m][:rows, :] = low.astype(BF16)
        sends[m][rows:, :] = grads


def hand_out(frames, rows, keep, gots):
    size, rank = keep.shape[0] - frames * rows, keep.shape[1]
    send = jax.ShapeDtypeStruct((rows + size, rank), BF16)
    return pl.pallas_call(
        functools.partial(hand_out_kernel, frames, size, len(gots)),
        in_specs=vmem(1 + len(gots)),
        out_specs=vmem(frames + 1),
        out_shape=[jax.ShapeDtypeStruct((rows, rank), F32)] + [send] * frames,
        scratch_shapes=[pltpu.VMEM(keep.shape, F32)],
        compiler_params=SMALL,
    )(keep, *gots)


def collect_kernel(frames, own_ref, *refs):
    gots, (out_ref, low_ref) = refs[:frames], refs[-2:]
    rows = own_ref.shape[0]
    size = gots[0].shape[0] - rows
    low = own_ref[...]
    for m in range(1, frames):
        low = low + gots[m][:rows, :].astype(F32)
    out_ref[:rows, :] = low.astype(BF16)
    low_ref[...] = low.astype(BF16)
    for m in range(frames):
        out_ref[rows + m * size : rows + (m + 1) * size, :] = gots[m][rows:, :]


def collect(own, gots):
    frames, (rows, rank) = len(gots), own.shape
    size = gots[0].shape[0] - rows
    return pl.pallas_call(
        functools.partial(collect_kernel, frames),
        in_specs=vmem(frames + 1),
        out_specs=vmem(2),
        out_shape=[
            jax.ShapeDtypeStruct((rows + frames * size, rank), BF16),
            jax.ShapeDtypeStruct((rows, rank), BF16),
        ],
        compiler_params=SMALL,
    )(own, *gots)


def place_kernel(early, late, *refs):
    frames = len(late[0])
    all_ref, tail, tail2, low_head, low_diag, *outs = refs
    me, half = lax.axis_index("tm"), lax.axis_index("rep")
    first = half == 0
    rank = outs[0].shape[0]
    cut = 3 * rank // 2
    rows = low_head.shape[0]
    same = tail[:rows, :].astype(F32) + low_head[...].astype(F32)
    other = tail2[:rows, :].astype(F32) + low_diag[...].astype(F32)
    outs[3][:rows, :] = jnp.where(first, same, other)
    outs[3][rows:, :] = jnp.where(first, other, same)
    def write(cols, a, b):
        both = jnp.concatenate([a.astype(F32), b.astype(F32)], axis=0)
        for o in range(3):
            outs[o][:, cols] = both[o * rank : (o + 1) * rank]

    for chip in range(frames):
        for n, (table, numbers) in enumerate(early):
            here = slice(n * cut, (n + 1) * cut)
            if numbers[chip]:
                cols = slice(table[chip] * DH, (table[chip] + 1) * DH)
                write(cols, all_ref[2 * chip, here, :], all_ref[2 * chip + 1, here, :])
    for m in range(frames):
        here = slice(rows + m * cut, rows + (m + 1) * cut)
        a, b = tail[here, :], tail2[here, :]
        write(column(lookup(late[0], me ^ m)), jnp.where(first, a, b), jnp.where(first, b, a))


def place(early, late, everything, tail, tail2, low_head, low_diag, rank, width):
    rows = low_head.shape[0]
    return pl.pallas_call(
        functools.partial(place_kernel, early, late),
        in_specs=vmem(5),
        out_specs=vmem(4),
        out_shape=[jax.ShapeDtypeStruct((rank, width), F32)] * 3
        + [jax.ShapeDtypeStruct((2 * rows, rank), F32)],
        compiler_params=SMALL,
    )(everything, tail, tail2, low_head, low_diag)


def exchange_plan(
    frozen_query,
    frozen_key,
    frozen_value,
    token_adapter_input,
    query_adapter_out,
    key_adapter_out,
    value_adapter_out,
    out_grad,
    band_width,
):
    rows, width = frozen_query.shape
    rank = token_adapter_input.shape[1]
    frames = band_width.shape[0]
    heads = width // DH
    starts, counts = head_table(heads, frames)
    most = max(counts)
    columns = [[min(starts[j] + s, heads - 1) for j in range(frames)] for s in range(most)]
    numbers = [[int(s < counts[j]) for j in range(frames)] for s in range(most)]
    slots = list(zip(columns, numbers))
    lead, late, rest = slots[0], slots[1], slots[2]
    wide = [j for j in range(frames) if counts[j] == most]
    adapters = [query_adapter_out, key_adapter_out, value_adapter_out]
    arrays = (frozen_query, out_grad, frozen_key, frozen_value, token_adapter_input)

    def meet(block, m, targets=range(frames)):
        return lax.ppermute(block, "tm", [(j ^ m, j) for j in targets])

    def mine(slot, m):
        return (slot[0], m, "mine")

    sent, kept, sent_late = [], [], []
    for m in range(1, frames):
        first = [mine(lead, m), (None, m, "t")]
        if m == 1:
            sent.append(first + [mine(rest, m), mine(late, m)])
        else:
            sent += [first, [mine(rest, m)]]
            sent_late.append([mine(late, m)])
    for slot in (lead, rest, late):
        kept += [[mine(slot, 0)], [(slot[0], 0, "other")]]
    kept += [[(None, 0, "t")], [(None, 0, "other t")]]
    packed = pack(frames, sent, 56, *arrays)
    packed_late = pack(frames, sent_late + kept, 16, *arrays)
    kept = packed_late[len(sent_late) :]
    block = meet(packed[0], 1)
    lead_got, rest_got, late_got = [(block, 0)], [(block, 4 * DH + rank)], [(block, 8 * DH + rank)]
    for m in range(2, frames):
        lead_got.append((meet(packed[2 * m - 3], m), 0))
        rest_got.append((meet(packed[2 * m - 2], m, wide), 0))
        late_got.append((meet(packed_late[m - 2], m), 0))

    def sides(n, got, wide_t, apart, after=()):
        skip = 0 if n == 2 else 2 * DH
        size = 4 * DH - skip + (rank if wide_t else 0)
        picked = pick([(a, start + skip) for a, start in got], size, apart, after)
        cross = [swap(block, "rep") for block in picked]
        cross = [(cross[m], 2 * DH - skip) if apart else (cross[0], m * size + 2 * DH - skip) for m in range(frames - 1)]
        rows_here = [(kept[2 * n], 0)] + got
        rows_there = [(kept[2 * n + 1], 0)] + cross
        return rows_here, rows_there, cross

    *lead_side, cross = sides(0, lead_got, True, False, kept[:1])
    t_side = (
        [(kept[6], 0)] + [(a, start + 4 * DH) for a, start in lead_got],
        [(kept[7], 0)] + [(block, start + 2 * DH) for block, start in cross],
    )
    *rest_side, _ = sides(1, rest_got, False, False)
    early = [lead, rest]
    keep, give, *low = head_group(early, band_width, [t_side, lead_side, rest_side], adapters)
    got = swap(give, "rep")
    *late_side, _ = sides(2, late_got, False, False, [got])
    piece = (keep + got.astype(F32)).astype(BF16)
    everything = lax.all_gather(piece, ("tm", "rep"))
    keep, *gives = head_group([late], band_width, [t_side, late_side], adapters, low)
    own, *sends = hand_out(frames, rows, keep, [swap(g, "rep") for g in gives])
    gots = [sends[0]] + [meet(sends[m], m) for m in range(1, frames)]
    tail, low = collect(own, gots)
    diag = [(0, 3), (1, 2), (2, 1), (3, 0)]
    low_head, low_diag = swap(low, "head"), lax.ppermute(low, ("head", "rep"), diag)
    outs = place(
        early, late, everything, tail, swap(tail, "rep"), low_head, low_diag, rank, width
    )
    return tuple(outs)


def on_device(frozen_query, *rest):
    frames = rest[-1].shape[0]
    heads = frozen_query.shape[1] // DH
    whole_reach = frames <= REACH + 1 and frames & (frames - 1) == 0 and 2 * frames < heads < 3 * frames
    return (exchange_plan if whole_reach else window_plan)(frozen_query, *rest)


def solution(mesh):
    in_specs = (
        P(("groups", "tm", "rep"), "head"),
        P(("groups", "tm"), "head"),
        P(("groups", "tm"), "head"),
        P(("groups", "tm"), None),
        P(None, "head"),
        P(None, "head"),
        P(None, "head"),
        P(("groups", "tm", "rep"), "head"),
        P(),
    )
    out_specs = (
        P("groups", "head"),
        P("groups", "head"),
        P("groups", "head"),
        P(("groups", "tm"), None),
    )
    return jax.shard_map(
        on_device, mesh=mesh, in_specs=in_specs, out_specs=out_specs, check_vma=False
    )
```

```python
import functools

import jax
import jax.numpy as jnp
from jax import lax
from jax.experimental import pallas as pl
from jax.experimental.pallas import tpu as pltpu
from jax.sharding import PartitionSpec as P

DH = 128
NEAR = 1
REACH = 4
SCALE = DH ** (-0.5)
F32 = jnp.float32
BF16 = jnp.bfloat16
GIVES = 4
SMALL = pltpu.CompilerParams(vmem_limit_bytes=16 * 1024 * 1024)


def dot_nn(left, right):
    return lax.dot_general(left, right, (((1,), (0,)), ((), ())), preferred_element_type=F32)


def dot_nt(left, right):
    return lax.dot_general(left, right, (((1,), (1,)), ((), ())), preferred_element_type=F32)


def dot_tn(left, right):
    return lax.dot_general(left, right, (((0,), (0,)), ((), ())), preferred_element_type=F32)


def routes(count):
    found = []
    for d in range(1, min(REACH, count - 1) + 1):
        if 2 * d >= count:
            found.append((d, (-d, d)))
        else:
            found.append((d, (-d,)))
            found.append((d, (d,)))
    return found


def pairs(count, offsets):
    return [(i + o, i) for o in offsets for i in range(count) if 0 <= i + o < count]


def swap(block, axis):
    return lax.ppermute(block, axis, [(0, 1), (1, 0)])


def attention_kernel(
    blocks, bias_ref, fq_ref, do_ref, fk_ref, fv_ref, t_ref, tr_ref, tt_ref, aq_ref, ak_ref, av_ref, *refs
):
    k_refs = refs[:blocks]
    v_refs = refs[blocks : 2 * blocks]
    gq_ref, gk_ref, gv_ref, lowq_ref, low_ref = refs[2 * blocks :]
    rows = fq_ref.shape[0]

    @pl.when(pl.program_id(0) == 0)
    def _():
        lowq_ref[...] = jnp.zeros_like(lowq_ref)
        low_ref[...] = jnp.zeros_like(low_ref)

    aq, ak, av = aq_ref[...], ak_ref[...], av_ref[...]
    query = (fq_ref[...].astype(F32) + dot_nn(tr_ref[...], aq)).astype(BF16)
    do = do_ref[...]
    own_k = (fk_ref[...].astype(F32) + dot_nn(t_ref[...], ak)).astype(BF16)
    own_v = (fv_ref[...].astype(F32) + dot_nn(t_ref[...], av)).astype(BF16)
    keys = [own_k[:rows], own_k[rows:]] + [ref[...] for ref in k_refs]
    values = [own_v[:rows], own_v[rows:]] + [ref[...] for ref in v_refs]
    count = len(keys)
    scores = [dot_nt(keys[b], query) * SCALE + bias_ref[b] for b in range(count)]
    top = functools.reduce(jnp.maximum, scores)
    top = jnp.max(top, axis=0, keepdims=True)
    shifted = [jnp.exp(s - top) for s in scores]
    total = jnp.sum(functools.reduce(jnp.add, shifted), axis=0, keepdims=True)
    inverse = 1.0 / total
    probs = [s * inverse for s in shifted]
    lows = [p.astype(BF16) for p in probs]
    attended = functools.reduce(jnp.add, [dot_tn(lows[b], values[b]) for b in range(count)])
    attended = attended.astype(BF16).astype(F32)
    delta = jnp.sum((do.astype(F32) * attended).T, axis=0, keepdims=True)
    grads = [
        (probs[b] * (dot_nt(values[b], do) - delta)).astype(BF16) for b in range(count)
    ]
    dq = functools.reduce(jnp.add, [dot_tn(grads[b], keys[b]) for b in range(count)])
    dq = (dq * SCALE).astype(BF16)
    gq_ref[...] = dot_tn(tr_ref[...], dq)
    lowq_ref[...] += dot_nt(dq, aq)
    both = jnp.concatenate([ak, av], axis=1)
    for b in range(count):
        dk = (dot_nn(grads[b], query) * SCALE).astype(BF16)
        dv = dot_nn(lows[b], do).astype(BF16)
        part = jnp.concatenate([dk, dv], axis=1)
        low_ref[b * rows : (b + 1) * rows, :] += dot_nt(part, both)
        out = dot_nn(tt_ref[:, b * rows : (b + 1) * rows], part)
        if b == 0:
            total_part = out
        else:
            total_part += out
    gk_ref[...] = total_part[:, :DH]
    gv_ref[...] = total_part[:, DH:]


def attention(bias, fq, do, fk, fv, t, tr, tt, aq, ak, av, payloads):
    rows, width = fq.shape
    heads = width // DH
    rank = t.shape[1]
    blocks = len(payloads)
    count = blocks + 2

    def col(r):
        return pl.BlockSpec((r, DH), lambda h: (0, h))

    def whole(shape):
        return pl.BlockSpec(shape, lambda h: (0, 0))

    return pl.pallas_call(
        functools.partial(attention_kernel, blocks),
        grid=(heads,),
        out_shape=[
            jax.ShapeDtypeStruct((rank, width), F32),
            jax.ShapeDtypeStruct((rank, width), F32),
            jax.ShapeDtypeStruct((rank, width), F32),
            jax.ShapeDtypeStruct((rows, rank), F32),
            jax.ShapeDtypeStruct((count * rows, rank), F32),
        ],
        in_specs=[pl.BlockSpec(memory_space=pltpu.SMEM)]
        + [col(rows), col(rows), col(2 * rows), col(2 * rows)]
        + [whole(t.shape), whole(tr.shape), whole(tt.shape)]
        + [col(rank)] * 3
        + [col(rows)] * blocks
        + [pl.BlockSpec((rows, DH), lambda h: (0, heads + h))] * blocks,
        out_specs=[col(rank)] * 3 + [whole((rows, rank)), whole((count * rows, rank))],
        compiler_params=pltpu.CompilerParams(vmem_limit_bytes=32 * 1024 * 1024),
    )(bias, fq, do, fk, fv, t, tr, tt, aq, ak, av, *payloads, *payloads)


def sum_rows(part, frame_idx, half_idx, frames):
    rows, width = part.shape
    half = width // 2
    keep = lax.dynamic_slice_in_dim(part, half_idx * half, half, 1)
    give = lax.dynamic_slice_in_dim(part, (1 - half_idx) * half, half, 1)
    mine = keep + swap(give, "rep")
    if frames & (frames - 1) or rows % frames or frames > REACH + 1:
        total = lax.psum(mine, "tm").astype(BF16)
    else:
        chunk = rows // frames
        low = mine.astype(BF16)
        acc = lax.dynamic_slice_in_dim(mine, frame_idx * chunk, chunk, 0)
        for m in range(1, frames):
            give = lax.dynamic_slice_in_dim(low, (frame_idx ^ m) * chunk, chunk, 0)
            acc = acc + lax.ppermute(give, "tm", [(i, i ^ m) for i in range(frames)]).astype(F32)
        acc = acc.astype(BF16)
        total = jnp.zeros((rows, half), BF16)
        total = lax.dynamic_update_slice_in_dim(total, acc, frame_idx * chunk, 0)
        for m in range(1, frames):
            got = lax.ppermute(acc, "tm", [(i, i ^ m) for i in range(frames)])
            total = lax.dynamic_update_slice_in_dim(total, got, (frame_idx ^ m) * chunk, 0)
    other = swap(total, "rep")
    first = jnp.where(half_idx == 0, total, other)
    second = jnp.where(half_idx == 0, other, total)
    return jnp.concatenate([first, second], axis=1).astype(F32)


def window_plan(
    frozen_query,
    frozen_key,
    frozen_value,
    token_adapter_input,
    query_adapter_out,
    key_adapter_out,
    value_adapter_out,
    out_grad,
    band_width,
):
    rows, width = frozen_query.shape
    rank = token_adapter_input.shape[1]
    frames = band_width.shape[0]
    frame_idx = lax.axis_index("tm")
    half_idx = lax.axis_index("rep")
    t = token_adapter_input
    tr = lax.dynamic_slice_in_dim(t, half_idx * rows, rows, 0)

    def tile_rows_of(frozen, adapter):
        own = lax.dynamic_slice_in_dim(frozen, half_idx * rows, rows, 0)
        return (own.astype(F32) + dot_nn(tr, adapter)).astype(BF16)

    payload = jnp.concatenate(
        [tile_rows_of(frozen_key, key_adapter_out), tile_rows_of(frozen_value, value_adapter_out), tr],
        axis=1,
    )

    frame_ids = jnp.arange(frames)
    band_row = jnp.sum(jnp.where((frame_ids == frame_idx)[:, None], band_width, 0), axis=0)

    def band_at(offsets):
        seen = functools.reduce(jnp.logical_or, [frame_ids == frame_idx + o for o in offsets])
        return jnp.sum(jnp.where(seen, band_row, 0))

    own_band = band_at((0,))
    allowed = [jnp.abs(half_idx - tile) < own_band for tile in range(2)]
    payloads = []
    plan = routes(frames)
    for d, offsets in plan:
        got = lax.ppermute(payload, "tm", pairs(frames, offsets))
        band = band_at(offsets)
        payloads.append(got)
        allowed.append(band > 0)
        if d <= NEAR:
            payloads.append(swap(got, "rep"))
            allowed.append(band > 1)
    bias = jnp.where(jnp.stack(allowed), 0.0, -jnp.inf).astype(F32)
    tt = jnp.concatenate([t] + [p[:, 2 * width :] for p in payloads], axis=0).T

    gq, gk, gv, low_q, low_b = attention(
        bias, frozen_query, out_grad, frozen_key, frozen_value, t, tr, tt,
        query_adapter_out, key_adapter_out, value_adapter_out, payloads,
    )

    own = low_b[: 2 * rows]
    same = lax.dynamic_slice_in_dim(own, half_idx * rows, rows, 0) + low_q
    other = lax.dynamic_slice_in_dim(own, (1 - half_idx) * rows, rows, 0)
    start = 2 * rows
    for d, offsets in plan:
        size = 2 * rows if d <= NEAR else rows
        back = [(target, source) for source, target in pairs(frames, offsets)]
        got = lax.ppermute(low_b[start : start + size], "tm", back)
        start += size
        same = same + got[:rows]
        if d <= NEAR:
            other = other + got[rows:]
    low = jnp.where(
        half_idx == 0,
        jnp.concatenate([same, other], axis=0),
        jnp.concatenate([other, same], axis=0),
    )
    low = low + swap(low, "rep")
    low = low + swap(low, "head")

    grads = sum_rows(jnp.concatenate([gq, gk, gv], axis=0), frame_idx, half_idx, frames)
    return grads[:rank], grads[rank : 2 * rank], grads[2 * rank :], low


def head_table(heads, frames):
    base, extra = divmod(heads, frames)
    lead = (frames - extra) // 2
    counts = [base + (1 if lead <= j < lead + extra else 0) for j in range(frames)]
    return [sum(counts[:j]) for j in range(frames)], counts


def lookup(table, index):
    value = jnp.int32(table[0])
    for j in range(1, len(table)):
        value = jnp.where(index == j, jnp.int32(table[j]), value)
    return value


def column(head):
    return pl.ds(pl.multiple_of(head * DH, DH), DH)


def vmem(count):
    return [pl.BlockSpec(memory_space=pltpu.VMEM)] * count


def pack_kernel(frames, outputs, fq_ref, do_ref, fk_ref, fv_ref, t_ref, *refs):
    outs, (q_in, do_in, k_in, v_in, k2_in, v2_in, t_in, sems) = refs[:-8], refs[-8:]
    wanted = {what for parts in outputs for _, _, what in parts}
    me, half = lax.axis_index("tm"), lax.axis_index("rep")
    rows = fq_ref.shape[0]
    mine = pl.ds(pl.multiple_of(half * rows, rows), rows)
    rest = pl.ds(pl.multiple_of((1 - half) * rows, rows), rows)
    moves = [
        (fq_ref, q_in), (do_ref, do_in), (fk_ref.at[mine, :], k_in), (fv_ref.at[mine, :], v_in), (t_ref, t_in)
    ]
    if "other" in wanted:
        moves += [(fk_ref.at[rest, :], k2_in), (fv_ref.at[rest, :], v2_in)]
    copies = [pltpu.make_async_copy(a, b, sems.at[n]) for n, (a, b) in enumerate(moves)]
    for copy in copies:
        copy.start()
    for copy in copies:
        copy.wait()
    for out, parts in zip(outs, outputs):
        at = 0
        for table, m, what in parts:
            if what in ("t", "other t"):
                blocks = [t_in[mine if what == "t" else rest, :]]
            else:
                cols = column(lookup(table, me ^ m))
                sources = (q_in, do_in, k_in, v_in) if what == "mine" else (k2_in, v2_in)
                blocks = [ref[:, cols] for ref in sources]
            for block in blocks:
                out[:, at : at + block.shape[1]] = block
                at += block.shape[1]


def pack(frames, outputs, limit, fq, do, fk, fv, t):
    rows, width = fq.shape
    size = {"mine": 4 * DH, "other": 2 * DH, "t": t.shape[1], "other t": t.shape[1]}
    return pl.pallas_call(
        functools.partial(pack_kernel, frames, outputs),
        in_specs=[pl.BlockSpec(memory_space=pltpu.HBM)] * 5,
        out_specs=vmem(len(outputs)),
        out_shape=[
            jax.ShapeDtypeStruct((rows, sum(size[what] for _, _, what in parts)), BF16)
            for parts in outputs
        ],
        scratch_shapes=[pltpu.VMEM((rows, width), BF16)] * 6
        + [pltpu.VMEM(t.shape, BF16), pltpu.SemaphoreType.DMA((7,))],
        compiler_params=pltpu.CompilerParams(vmem_limit_bytes=limit * 1024 * 1024),
    )(fq, do, fk, fv, t)


def pick_kernel(spans, apart, *refs):
    at = 0
    for n, (start, size) in enumerate(spans):
        out = refs[n - len(spans)] if apart else refs[-1].at[:, pl.ds(at, size)]
        out[...] = refs[n][:, start : start + size]
        at += size


def pick(parts, size, apart, after=()):
    arrays = [array for array, _ in parts]
    rows, dtype = arrays[0].shape[0], arrays[0].dtype
    shapes = [(rows, size)] * len(arrays) if apart else [(rows, size * len(arrays))]
    return pl.pallas_call(
        functools.partial(pick_kernel, [(start, size) for _, start in parts], apart),
        in_specs=vmem(len(arrays)) + [pl.BlockSpec(memory_space=pl.ANY)] * len(after),
        out_specs=vmem(len(shapes)),
        out_shape=[jax.ShapeDtypeStruct(shape, dtype) for shape in shapes],
        compiler_params=SMALL,
    )(*arrays, *after)


def one_head(frames, bands, q, do, frozen_k, frozen_v, tokens, aq, ak, av):
    flat = q.shape[0]
    rows = flat // frames
    t_same = tokens[:flat]

    def adapted(frozen, rows_of, adapter):
        return (frozen.astype(F32) + dot_nn(rows_of, adapter)).astype(BF16)

    query = adapted(q, t_same, aq)
    keys, values = adapted(frozen_k, tokens, ak), adapted(frozen_v, tokens, av)
    do_t, keys_t, values_t = do.T, keys.T, values.T

    def bias(i, b):
        j, need = (b, 0) if b < frames else (b - frames, 1)
        value = jnp.where(bands[i, j] > need, 0.0, -jnp.inf).astype(F32)
        return jnp.full((1, rows), value, F32)

    span = 2 if frames % 2 == 0 else 1
    wide = span * rows
    dks, dvs, dqs = [None] * (2 * frames), [None] * (2 * frames), []
    for first in range(0, frames, span):
        mine = range(first, first + span)
        blocks = list(range(frames)) + [
            frames + j for j in range(frames) if any(abs(i - j) <= NEAR for i in mine)
        ]
        here = slice(first * rows, first * rows + wide)
        q_p, do_p = query[here], do[here]

        def gather(whole, axis):
            parts = [
                whole[b * rows : (b + 1) * rows] if axis == 0 else whole[:, b * rows : (b + 1) * rows]
                for b in blocks
            ]
            return jnp.concatenate(parts, axis=axis)

        raw = dot_nt(gather(keys, 0), q_p)
        scores = [
            raw[n * rows : (n + 1) * rows] * SCALE + jnp.concatenate([bias(i, b) for i in mine], axis=1)
            for n, b in enumerate(blocks)
        ]
        top = jnp.max(functools.reduce(jnp.maximum, scores), axis=0, keepdims=True)
        shifted = [jnp.exp(s - top) for s in scores]
        inverse = 1.0 / jnp.sum(functools.reduce(jnp.add, shifted), axis=0, keepdims=True)
        probs = [s * inverse for s in shifted]
        low = jnp.concatenate([p.astype(BF16) for p in probs], axis=0)
        attended = dot_nn(gather(values_t, 1), low).astype(BF16).astype(F32)
        delta = jnp.sum(do_t[:, here].astype(F32) * attended, axis=0, keepdims=True)
        prob_grad = dot_nt(gather(values, 0), do_p)
        grad = jnp.concatenate(
            [
                (probs[n] * (prob_grad[n * rows : (n + 1) * rows] - delta)).astype(BF16)
                for n in range(len(blocks))
            ],
            axis=0,
        )
        dqs.append((dot_nn(gather(keys_t, 1), grad) * SCALE).astype(BF16).T)
        dk, dv = dot_nn(grad, q_p), dot_nn(low, do_p)
        for n, b in enumerate(blocks):
            part = slice(n * rows, (n + 1) * rows)
            dks[b] = dk[part] if dks[b] is None else dks[b] + dk[part]
            dvs[b] = dv[part] if dvs[b] is None else dvs[b] + dv[part]
    dq = jnp.concatenate(dqs, axis=0)
    dk = (jnp.concatenate(dks, axis=0) * SCALE).astype(BF16)
    dv = jnp.concatenate(dvs, axis=0).astype(BF16)
    both = jnp.concatenate([dk, dv], axis=1)
    sums = dot_tn(tokens, both)
    grads = jnp.concatenate([dot_tn(t_same, dq), sums[:, :DH], sums[:, DH:]], axis=0)
    lows = dot_nt(both, jnp.concatenate([ak, av], axis=1))
    return grads, lows[:flat] + dot_nt(dq, aq), lows[flat:]


def group_kernel(heads, frames, chained, waits, sides, count, *refs):
    refs = list(refs)

    def take(count):
        taken = refs[:count]
        del refs[:count]
        return taken

    (bands,) = take(1)
    arrays, adapters = take(count), take(3)
    before = take(2) if chained else None
    take(waits)
    keep_ref, *give_refs = take(1 + GIVES if chained else 2)
    low_refs = [] if chained else take(2)
    q, do, k, v, tokens = refs
    me, half = lax.axis_index("tm"), lax.axis_index("rep")
    rows = arrays[0].shape[0]
    flat = frames * rows
    cut = 3 * tokens.shape[1] // 2
    first = half == 0
    same_at = [pl.ds(pl.multiple_of((me ^ m) * rows, rows), rows) for m in range(frames)]
    other_at = [pl.ds(pl.multiple_of(flat + (me ^ m) * rows, rows), rows) for m in range(frames)]

    def put(targets, places, rows_at):
        for m, (n, start) in enumerate(places):
            for c, target in enumerate(targets):
                target[rows_at[m], :] = arrays[n][:, start + c * DH : start + (c + 1) * DH]

    put([tokens], sides[0][0], same_at)
    put([tokens], sides[0][1], other_at)

    def run(n, table):
        put([q, do, k, v], sides[1 + n][0], same_at)
        put([k, v], sides[1 + n][1], other_at)
        cols = column(lookup(table, me))
        grads, low_same, low_other = one_head(
            frames, bands, q[...], do[...], k[...], v[...], tokens[...], *[a[:, cols] for a in adapters]
        )
        keep = jnp.where(first, grads[:cut], grads[cut:])
        give = jnp.where(first, grads[cut:], grads[:cut])
        return keep, give, low_same, low_other

    if chained:
        keep, give, low_same, low_other = run(0, heads[0][0])
        keep_ref[:cut, :] = keep
        keep_ref[cut:, :] = before[0][...] + low_same
        give = jnp.concatenate([give, before[1][...] + low_other], axis=0)
        size = give.shape[0] // GIVES
        for n, ref in enumerate(give_refs):
            ref[...] = give[n * size : (n + 1) * size].astype(ref.dtype)
        return
    for n, (table, counts) in enumerate(heads):
        here = slice(n * cut, (n + 1) * cut)

        def body():
            keep, give, low_same, low_other = run(n, table)
            keep_ref[here, :] = keep
            give_refs[0][here, :] = give.astype(BF16)
            if n == 0:
                low_refs[0][...] = low_same
                low_refs[1][...] = low_other
            else:
                low_refs[0][...] += low_same
                low_refs[1][...] += low_other

        if min(counts) > 0:
            body()
        else:
            live = lookup(counts, me) > 0
            pl.when(live)(body)

            @pl.when(jnp.logical_not(live))
            def _():
                keep_ref[here, :] = jnp.zeros((cut, DH), F32)
                give_refs[0][here, :] = jnp.zeros((cut, DH), BF16)


def head_group(heads, bands, sides, adapters, before=(), after=()):
    frames = len(sides[0][0])
    arrays, places = [], []
    for side in sides:
        found = []
        for pairs_of in side:
            found.append([])
            for array, start in pairs_of:
                known = [n for n, a in enumerate(arrays) if a is array]
                if not known:
                    arrays.append(array)
                found[-1].append((known[0] if known else len(arrays) - 1, start))
        places.append(found)
    rows, rank = arrays[0].shape[0], adapters[0].shape[0]
    flat = frames * rows
    size = len(heads) * 3 * rank // 2
    chained = len(before) > 0
    args = [bands, *arrays, *adapters, *before, *after]
    specs = [pl.BlockSpec(memory_space=pltpu.SMEM)] + vmem(len(arrays) + 3 + len(before))
    specs += [pl.BlockSpec(memory_space=pl.ANY)] * len(after)
    low = jax.ShapeDtypeStruct((flat, rank), F32)
    if chained:
        part = jax.ShapeDtypeStruct(((size + flat) // GIVES, rank), BF16)
        shapes = [jax.ShapeDtypeStruct((size + flat, rank), F32)] + [part] * GIVES
    else:
        edge = jax.ShapeDtypeStruct((size, rank), F32)
        shapes = [edge, jax.ShapeDtypeStruct((size, rank), BF16), low, low]
    return pl.pallas_call(
        functools.partial(
            group_kernel, heads, frames, chained, len(after), places, len(arrays)
        ),
        in_specs=specs,
        out_specs=vmem(len(shapes)),
        out_shape=shapes,
        scratch_shapes=[pltpu.VMEM((flat, DH), BF16)] * 2
        + [pltpu.VMEM((2 * flat, DH), BF16)] * 2
        + [pltpu.VMEM((2 * flat, rank), BF16)],
        compiler_params=pltpu.CompilerParams(vmem_limit_bytes=40 * 1024 * 1024),
    )(*args)


def hand_out_kernel(frames, size, parts, keep_ref, *refs):
    gots, (piece, facing), (own_ref, *sends, total) = refs[:parts], refs[parts : parts + 2], refs[-frames - 2 :]
    me = lax.axis_index("tm")
    rows = own_ref.shape[0]
    total[...] = keep_ref[...] + jnp.concatenate([got[...].astype(F32) for got in gots], axis=0)
    grads = total[:size, :].astype(BF16)
    for m in range(frames):
        low = total[pl.ds(pl.multiple_of(size + (me ^ m) * rows, 8), rows), :]
        if m == 0:
            own_ref[...] = low
        sends[m][:rows, :] = low.astype(BF16)
        sends[m][rows : rows + size, :] = grads
    sends[1][rows + size : rows + 3 * size, :] = piece[...]
    sends[1][rows + 3 * size :, :] = facing[size:, :]


def hand_out(frames, rows, keep, gots, piece, facing, after):
    size, rank = keep.shape[0] - frames * rows, keep.shape[1]
    sends = [jax.ShapeDtypeStruct((rows + size * (4 if m == 1 else 1), rank), BF16) for m in range(frames)]
    return pl.pallas_call(
        functools.partial(hand_out_kernel, frames, size, len(gots)),
        in_specs=vmem(3 + len(gots)) + [pl.BlockSpec(memory_space=pl.ANY)] * len(after),
        out_specs=vmem(frames + 1),
        out_shape=[jax.ShapeDtypeStruct((rows, rank), F32)] + sends,
        scratch_shapes=[pltpu.VMEM(keep.shape, F32)],
        compiler_params=SMALL,
    )(keep, *gots, piece, facing, *after)


def collect_kernel(frames, wide, own_ref, *refs):
    gots, (piece, far, facing), (out_ref, low_ref) = refs[:frames], refs[frames : frames + 3], refs[-2:]
    rows = own_ref.shape[0]
    size = gots[0].shape[0] - rows
    low = own_ref[...]
    for m in range(1, frames):
        low = low + gots[m][:rows, :].astype(F32)
    out_ref[:rows, :] = low.astype(BF16)
    low_ref[...] = low.astype(BF16)
    near = rows + size
    middle = lookup(wide, lax.axis_index("tm")) > 0
    blocks = [got[rows:near, :] for got in gots]
    blocks += [piece[:size, :], gots[1][near : near + size, :], far[...], facing[:size, :]]
    blocks.append(jnp.where(middle, piece[size:, :], gots[1][near + size : near + 2 * size, :]))
    blocks.append(jnp.where(middle, facing[size:, :], gots[1][near + 2 * size :, :]))
    for n, block in enumerate(blocks):
        out_ref[rows + n * size : rows + (n + 1) * size, :] = block


def collect(wide, own, gots, piece, far, facing):
    frames, (rows, rank) = len(gots), own.shape
    size = gots[0].shape[0] - rows
    return pl.pallas_call(
        functools.partial(collect_kernel, frames, wide),
        in_specs=vmem(frames + 4),
        out_specs=vmem(2),
        out_shape=[
            jax.ShapeDtypeStruct((rows + (2 * frames + 2) * size, rank), BF16),
            jax.ShapeDtypeStruct((rows, rank), BF16),
        ],
        compiler_params=SMALL,
    )(own, *gots, piece, far, facing)


def place_kernel(frames, lead, late, rest, tail, tail2, low_head, low_diag, *outs):
    me, half = lax.axis_index("tm"), lax.axis_index("rep")
    first = half == 0
    rank = outs[0].shape[0]
    cut = 3 * rank // 2
    rows = low_head.shape[0]
    same = tail[:rows, :].astype(F32) + low_head[...].astype(F32)
    other = tail2[:rows, :].astype(F32) + low_diag[...].astype(F32)
    outs[3][:rows, :] = jnp.where(first, same, other)
    outs[3][rows:, :] = jnp.where(first, other, same)
    side = me // 2
    places = [lookup(late, me ^ m) for m in range(frames)] + [lookup(lead, me ^ m) for m in range(frames)]
    places += [lookup(rest, 1 + side), lookup(rest, 2 - side)]
    for n, head in enumerate(places):
        here = slice(rows + n * cut, rows + (n + 1) * cut)
        a, b = tail[here, :].astype(F32), tail2[here, :].astype(F32)
        both = jnp.concatenate([jnp.where(first, a, b), jnp.where(first, b, a)], axis=0)
        for o in range(3):
            outs[o][:, column(head)] = both[o * rank : (o + 1) * rank]


def place(frames, lead, late, rest, tail, tail2, low_head, low_diag, rank, width):
    rows = low_head.shape[0]
    return pl.pallas_call(
        functools.partial(place_kernel, frames, lead, late, rest),
        in_specs=vmem(4),
        out_specs=vmem(4),
        out_shape=[jax.ShapeDtypeStruct((rank, width), F32)] * 3
        + [jax.ShapeDtypeStruct((2 * rows, rank), F32)],
        compiler_params=SMALL,
    )(tail, tail2, low_head, low_diag)


def exchange_plan(
    frozen_query,
    frozen_key,
    frozen_value,
    token_adapter_input,
    query_adapter_out,
    key_adapter_out,
    value_adapter_out,
    out_grad,
    band_width,
):
    rows, width = frozen_query.shape
    rank = token_adapter_input.shape[1]
    frames = band_width.shape[0]
    heads = width // DH
    starts, counts = head_table(heads, frames)
    most = max(counts)
    columns = [[min(starts[j] + s, heads - 1) for j in range(frames)] for s in range(most)]
    numbers = [[int(s < counts[j]) for j in range(frames)] for s in range(most)]
    slots = list(zip(columns, numbers))
    lead, late, rest = slots[0], slots[1], slots[2]
    wide = [j for j in range(frames) if counts[j] == most]
    adapters = [query_adapter_out, key_adapter_out, value_adapter_out]
    arrays = (frozen_query, out_grad, frozen_key, frozen_value, token_adapter_input)

    def meet(name, block, m, targets=range(frames)):
        with jax.named_scope(f"{name}_over_tm"):
            return lax.ppermute(block, "tm", [(j ^ m, j) for j in targets])

    def swap_in_chip(name, block):
        with jax.named_scope(f"{name}_in_chip"):
            return swap(block, "rep")

    def mine(slot, m):
        return (slot[0], m, "mine")

    sent, kept, sent_late = [], [], []
    for m in range(1, frames):
        first = [mine(lead, m), (None, m, "t")]
        if m == 1:
            sent.append(first + [mine(rest, m), mine(late, m)])
        else:
            sent += [first, [mine(rest, m)]]
            sent_late.append([mine(late, m)])
    for slot in (lead, rest, late):
        kept += [[mine(slot, 0)], [(slot[0], 0, "other")]]
    kept += [[(None, 0, "t")], [(None, 0, "other t")]]
    packed = pack(frames, sent, 56, *arrays)
    packed_late = pack(frames, sent_late + kept, 16, *arrays)
    kept = packed_late[len(sent_late) :]
    block = meet("nearest", packed[0], 1)
    lead_got, rest_got, late_got = [(block, 0)], [(block, 4 * DH + rank)], [(block, 8 * DH + rank)]
    for m in range(2, frames):
        lead_got.append((meet("lead", packed[2 * m - 3], m), 0))
        rest_got.append((meet("rest", packed[2 * m - 2], m, wide), 0))
        late_got.append((meet("late", packed_late[m - 2], m), 0))

    def sides(name, n, got, wide_t, apart, skip, after=()):
        size = 4 * DH - skip + (rank if wide_t else 0)
        picked = pick([(a, start + skip) for a, start in got], size, apart, after)
        cross = [swap_in_chip(name, block) for block in picked]
        where = 2 * DH - skip
        cross = [(cross[m], where) if apart else (cross[0], m * size + where) for m in range(frames - 1)]
        rows_here = [(kept[2 * n], 0)] + got
        rows_there = [(kept[2 * n + 1], 0)] + cross
        return rows_here, rows_there, cross

    *lead_side, cross = sides("lead", 0, lead_got, True, False, 2 * DH, kept[:1])
    t_side = (
        [(kept[6], 0)] + [(a, start + 4 * DH) for a, start in lead_got],
        [(kept[7], 0)] + [(block, start + 2 * DH) for block, start in cross],
    )
    *rest_side, _ = sides("rest", 1, rest_got, False, False, 2 * DH)
    early = [lead, rest]
    keep, give, *low = head_group(early, band_width, [t_side, lead_side, rest_side], adapters)
    got = swap_in_chip("early_gradients", give)
    piece = (keep + got.astype(F32)).astype(BF16)
    *late_side, _ = sides("late", 2, late_got, False, False, 0, [got])
    cut = 3 * rank // 2
    far = meet("early_gradients", piece[:cut], 2)
    facing = meet("early_gradients", piece, 3)
    keep, *gives = head_group([late], band_width, [t_side, late_side], adapters, low, [piece])
    gives = [swap_in_chip("late_sums", g) for g in gives]
    own, *sends = hand_out(frames, rows, keep, gives, piece, facing, [far])
    gots = [sends[0]] + [meet("late_sums", sends[m], m) for m in range(1, frames)]
    tail, low = collect(rest[1], own, gots, piece, far, facing)
    diag = [(0, 3), (1, 2), (2, 1), (3, 0)]
    with jax.named_scope("low_over_head"):
        low_head, low_diag = swap(low, "head"), lax.ppermute(low, ("head", "rep"), diag)
    outs = place(
        frames, lead[0], late[0], rest[0], tail, swap_in_chip("tail", tail), low_head, low_diag, rank, width
    )
    return tuple(outs)


def on_device(frozen_query, *rest):
    frames = rest[-1].shape[0]
    heads = frozen_query.shape[1] // DH
    whole_reach = frames == 4 and heads == 2 * frames + 2
    return (exchange_plan if whole_reach else window_plan)(frozen_query, *rest)


def solution(mesh):
    in_specs = (
        P(("groups", "tm", "rep"), "head"),
        P(("groups", "tm"), "head"),
        P(("groups", "tm"), "head"),
        P(("groups", "tm"), None),
        P(None, "head"),
        P(None, "head"),
        P(None, "head"),
        P(("groups", "tm", "rep"), "head"),
        P(),
    )
    out_specs = (
        P("groups", "head"),
        P("groups", "head"),
        P("groups", "head"),
        P(("groups", "tm"), None),
    )
    return jax.shard_map(
        on_device, mesh=mesh, in_specs=in_specs, out_specs=out_specs, check_vma=False
    )
```

```python
import functools

import jax
import jax.numpy as jnp
from jax import lax
from jax.experimental import pallas as pl
from jax.experimental.pallas import tpu as pltpu
from jax.sharding import PartitionSpec as P

DH = 128
NEAR = 1
REACH = 4
SCALE = DH ** (-0.5)
F32 = jnp.float32
BF16 = jnp.bfloat16
GIVES = 2
SMALL = pltpu.CompilerParams(vmem_limit_bytes=16 * 1024 * 1024)


def dot_nn(left, right):
    return lax.dot_general(left, right, (((1,), (0,)), ((), ())), preferred_element_type=F32)


def dot_nt(left, right):
    return lax.dot_general(left, right, (((1,), (1,)), ((), ())), preferred_element_type=F32)


def dot_tn(left, right):
    return lax.dot_general(left, right, (((0,), (0,)), ((), ())), preferred_element_type=F32)


def routes(count):
    found = []
    for d in range(1, min(REACH, count - 1) + 1):
        if 2 * d >= count:
            found.append((d, (-d, d)))
        else:
            found.append((d, (-d,)))
            found.append((d, (d,)))
    return found


def pairs(count, offsets):
    return [(i + o, i) for o in offsets for i in range(count) if 0 <= i + o < count]


def swap(block, axis):
    return lax.ppermute(block, axis, [(0, 1), (1, 0)])


def attention_kernel(
    blocks, bias_ref, fq_ref, do_ref, fk_ref, fv_ref, t_ref, tr_ref, tt_ref, aq_ref, ak_ref, av_ref, *refs
):
    k_refs = refs[:blocks]
    v_refs = refs[blocks : 2 * blocks]
    gq_ref, gk_ref, gv_ref, lowq_ref, low_ref = refs[2 * blocks :]
    rows = fq_ref.shape[0]

    @pl.when(pl.program_id(0) == 0)
    def _():
        lowq_ref[...] = jnp.zeros_like(lowq_ref)
        low_ref[...] = jnp.zeros_like(low_ref)

    aq, ak, av = aq_ref[...], ak_ref[...], av_ref[...]
    query = (fq_ref[...].astype(F32) + dot_nn(tr_ref[...], aq)).astype(BF16)
    do = do_ref[...]
    own_k = (fk_ref[...].astype(F32) + dot_nn(t_ref[...], ak)).astype(BF16)
    own_v = (fv_ref[...].astype(F32) + dot_nn(t_ref[...], av)).astype(BF16)
    keys = [own_k[:rows], own_k[rows:]] + [ref[...] for ref in k_refs]
    values = [own_v[:rows], own_v[rows:]] + [ref[...] for ref in v_refs]
    count = len(keys)
    scores = [dot_nt(keys[b], query) * SCALE + bias_ref[b] for b in range(count)]
    top = functools.reduce(jnp.maximum, scores)
    top = jnp.max(top, axis=0, keepdims=True)
    shifted = [jnp.exp(s - top) for s in scores]
    total = jnp.sum(functools.reduce(jnp.add, shifted), axis=0, keepdims=True)
    inverse = 1.0 / total
    probs = [s * inverse for s in shifted]
    lows = [p.astype(BF16) for p in probs]
    attended = functools.reduce(jnp.add, [dot_tn(lows[b], values[b]) for b in range(count)])
    attended = attended.astype(BF16).astype(F32)
    delta = jnp.sum((do.astype(F32) * attended).T, axis=0, keepdims=True)
    grads = [
        (probs[b] * (dot_nt(values[b], do) - delta)).astype(BF16) for b in range(count)
    ]
    dq = functools.reduce(jnp.add, [dot_tn(grads[b], keys[b]) for b in range(count)])
    dq = (dq * SCALE).astype(BF16)
    gq_ref[...] = dot_tn(tr_ref[...], dq)
    lowq_ref[...] += dot_nt(dq, aq)
    both = jnp.concatenate([ak, av], axis=1)
    for b in range(count):
        dk = (dot_nn(grads[b], query) * SCALE).astype(BF16)
        dv = dot_nn(lows[b], do).astype(BF16)
        part = jnp.concatenate([dk, dv], axis=1)
        low_ref[b * rows : (b + 1) * rows, :] += dot_nt(part, both)
        out = dot_nn(tt_ref[:, b * rows : (b + 1) * rows], part)
        if b == 0:
            total_part = out
        else:
            total_part += out
    gk_ref[...] = total_part[:, :DH]
    gv_ref[...] = total_part[:, DH:]


def attention(bias, fq, do, fk, fv, t, tr, tt, aq, ak, av, payloads):
    rows, width = fq.shape
    heads = width // DH
    rank = t.shape[1]
    blocks = len(payloads)
    count = blocks + 2

    def col(r):
        return pl.BlockSpec((r, DH), lambda h: (0, h))

    def whole(shape):
        return pl.BlockSpec(shape, lambda h: (0, 0))

    return pl.pallas_call(
        functools.partial(attention_kernel, blocks),
        grid=(heads,),
        out_shape=[
            jax.ShapeDtypeStruct((rank, width), F32),
            jax.ShapeDtypeStruct((rank, width), F32),
            jax.ShapeDtypeStruct((rank, width), F32),
            jax.ShapeDtypeStruct((rows, rank), F32),
            jax.ShapeDtypeStruct((count * rows, rank), F32),
        ],
        in_specs=[pl.BlockSpec(memory_space=pltpu.SMEM)]
        + [col(rows), col(rows), col(2 * rows), col(2 * rows)]
        + [whole(t.shape), whole(tr.shape), whole(tt.shape)]
        + [col(rank)] * 3
        + [col(rows)] * blocks
        + [pl.BlockSpec((rows, DH), lambda h: (0, heads + h))] * blocks,
        out_specs=[col(rank)] * 3 + [whole((rows, rank)), whole((count * rows, rank))],
        compiler_params=pltpu.CompilerParams(vmem_limit_bytes=32 * 1024 * 1024),
    )(bias, fq, do, fk, fv, t, tr, tt, aq, ak, av, *payloads, *payloads)


def sum_rows(part, frame_idx, half_idx, frames):
    rows, width = part.shape
    half = width // 2
    keep = lax.dynamic_slice_in_dim(part, half_idx * half, half, 1)
    give = lax.dynamic_slice_in_dim(part, (1 - half_idx) * half, half, 1)
    mine = keep + swap(give, "rep")
    if frames & (frames - 1) or rows % frames or frames > REACH + 1:
        total = lax.psum(mine, "tm").astype(BF16)
    else:
        chunk = rows // frames
        low = mine.astype(BF16)
        acc = lax.dynamic_slice_in_dim(mine, frame_idx * chunk, chunk, 0)
        for m in range(1, frames):
            give = lax.dynamic_slice_in_dim(low, (frame_idx ^ m) * chunk, chunk, 0)
            acc = acc + lax.ppermute(give, "tm", [(i, i ^ m) for i in range(frames)]).astype(F32)
        acc = acc.astype(BF16)
        total = jnp.zeros((rows, half), BF16)
        total = lax.dynamic_update_slice_in_dim(total, acc, frame_idx * chunk, 0)
        for m in range(1, frames):
            got = lax.ppermute(acc, "tm", [(i, i ^ m) for i in range(frames)])
            total = lax.dynamic_update_slice_in_dim(total, got, (frame_idx ^ m) * chunk, 0)
    other = swap(total, "rep")
    first = jnp.where(half_idx == 0, total, other)
    second = jnp.where(half_idx == 0, other, total)
    return jnp.concatenate([first, second], axis=1).astype(F32)


def window_plan(
    frozen_query,
    frozen_key,
    frozen_value,
    token_adapter_input,
    query_adapter_out,
    key_adapter_out,
    value_adapter_out,
    out_grad,
    band_width,
):
    rows, width = frozen_query.shape
    rank = token_adapter_input.shape[1]
    frames = band_width.shape[0]
    frame_idx = lax.axis_index("tm")
    half_idx = lax.axis_index("rep")
    t = token_adapter_input
    tr = lax.dynamic_slice_in_dim(t, half_idx * rows, rows, 0)

    def tile_rows_of(frozen, adapter):
        own = lax.dynamic_slice_in_dim(frozen, half_idx * rows, rows, 0)
        return (own.astype(F32) + dot_nn(tr, adapter)).astype(BF16)

    payload = jnp.concatenate(
        [tile_rows_of(frozen_key, key_adapter_out), tile_rows_of(frozen_value, value_adapter_out), tr],
        axis=1,
    )

    frame_ids = jnp.arange(frames)
    band_row = jnp.sum(jnp.where((frame_ids == frame_idx)[:, None], band_width, 0), axis=0)

    def band_at(offsets):
        seen = functools.reduce(jnp.logical_or, [frame_ids == frame_idx + o for o in offsets])
        return jnp.sum(jnp.where(seen, band_row, 0))

    own_band = band_at((0,))
    allowed = [jnp.abs(half_idx - tile) < own_band for tile in range(2)]
    payloads = []
    plan = routes(frames)
    for d, offsets in plan:
        got = lax.ppermute(payload, "tm", pairs(frames, offsets))
        band = band_at(offsets)
        payloads.append(got)
        allowed.append(band > 0)
        if d <= NEAR:
            payloads.append(swap(got, "rep"))
            allowed.append(band > 1)
    bias = jnp.where(jnp.stack(allowed), 0.0, -jnp.inf).astype(F32)
    tt = jnp.concatenate([t] + [p[:, 2 * width :] for p in payloads], axis=0).T

    gq, gk, gv, low_q, low_b = attention(
        bias, frozen_query, out_grad, frozen_key, frozen_value, t, tr, tt,
        query_adapter_out, key_adapter_out, value_adapter_out, payloads,
    )

    own = low_b[: 2 * rows]
    same = lax.dynamic_slice_in_dim(own, half_idx * rows, rows, 0) + low_q
    other = lax.dynamic_slice_in_dim(own, (1 - half_idx) * rows, rows, 0)
    start = 2 * rows
    for d, offsets in plan:
        size = 2 * rows if d <= NEAR else rows
        back = [(target, source) for source, target in pairs(frames, offsets)]
        got = lax.ppermute(low_b[start : start + size], "tm", back)
        start += size
        same = same + got[:rows]
        if d <= NEAR:
            other = other + got[rows:]
    low = jnp.where(
        half_idx == 0,
        jnp.concatenate([same, other], axis=0),
        jnp.concatenate([other, same], axis=0),
    )
    low = low + swap(low, "rep")
    low = low + swap(low, "head")

    grads = sum_rows(jnp.concatenate([gq, gk, gv], axis=0), frame_idx, half_idx, frames)
    return grads[:rank], grads[rank : 2 * rank], grads[2 * rank :], low


def head_table(heads, frames):
    base, extra = divmod(heads, frames)
    lead = (frames - extra) // 2
    counts = [base + (1 if lead <= j < lead + extra else 0) for j in range(frames)]
    return [sum(counts[:j]) for j in range(frames)], counts


def lookup(table, index):
    value = jnp.int32(table[0])
    for j in range(1, len(table)):
        value = jnp.where(index == j, jnp.int32(table[j]), value)
    return value


def column(head):
    return pl.ds(pl.multiple_of(head * DH, DH), DH)


def vmem(count):
    return [pl.BlockSpec(memory_space=pltpu.VMEM)] * count


def pack_kernel(frames, outputs, fq_ref, do_ref, fk_ref, fv_ref, t_ref, *refs):
    outs, (q_in, do_in, k_in, v_in, k2_in, v2_in, t_in, sems) = refs[:-8], refs[-8:]
    wanted = {what for parts in outputs for _, _, what in parts}
    me, half = lax.axis_index("tm"), lax.axis_index("rep")
    rows = fq_ref.shape[0]
    mine = pl.ds(pl.multiple_of(half * rows, rows), rows)
    rest = pl.ds(pl.multiple_of((1 - half) * rows, rows), rows)
    moves = [
        (fq_ref, q_in), (do_ref, do_in), (fk_ref.at[mine, :], k_in), (fv_ref.at[mine, :], v_in), (t_ref, t_in)
    ]
    if "other" in wanted:
        moves += [(fk_ref.at[rest, :], k2_in), (fv_ref.at[rest, :], v2_in)]
    copies = [pltpu.make_async_copy(a, b, sems.at[n]) for n, (a, b) in enumerate(moves)]
    for copy in copies:
        copy.start()
    for copy in copies:
        copy.wait()
    for out, parts in zip(outs, outputs):
        at = 0
        for table, m, what in parts:
            if what in ("t", "other t"):
                blocks = [t_in[mine if what == "t" else rest, :]]
            else:
                cols = column(lookup(table, me ^ m))
                sources = (q_in, do_in, k_in, v_in) if what == "mine" else (k2_in, v2_in)
                blocks = [ref[:, cols] for ref in sources]
            for block in blocks:
                out[:, at : at + block.shape[1]] = block
                at += block.shape[1]


def pack(frames, outputs, limit, fq, do, fk, fv, t):
    rows, width = fq.shape
    size = {"mine": 4 * DH, "other": 2 * DH, "t": t.shape[1], "other t": t.shape[1]}
    return pl.pallas_call(
        functools.partial(pack_kernel, frames, outputs),
        in_specs=[pl.BlockSpec(memory_space=pltpu.HBM)] * 5,
        out_specs=vmem(len(outputs)),
        out_shape=[
            jax.ShapeDtypeStruct((rows, sum(size[what] for _, _, what in parts)), BF16)
            for parts in outputs
        ],
        scratch_shapes=[pltpu.VMEM((rows, width), BF16)] * 6
        + [pltpu.VMEM(t.shape, BF16), pltpu.SemaphoreType.DMA((7,))],
        compiler_params=pltpu.CompilerParams(vmem_limit_bytes=limit * 1024 * 1024),
    )(fq, do, fk, fv, t)


def pick_kernel(spans, apart, *refs):
    at = 0
    for n, (start, size) in enumerate(spans):
        out = refs[n - len(spans)] if apart else refs[-1].at[:, pl.ds(at, size)]
        out[...] = refs[n][:, start : start + size]
        at += size


def pick(parts, size, apart, after=()):
    arrays = [array for array, _ in parts]
    rows, dtype = arrays[0].shape[0], arrays[0].dtype
    shapes = [(rows, size)] * len(arrays) if apart else [(rows, size * len(arrays))]
    return pl.pallas_call(
        functools.partial(pick_kernel, [(start, size) for _, start in parts], apart),
        in_specs=vmem(len(arrays)) + [pl.BlockSpec(memory_space=pl.ANY)] * len(after),
        out_specs=vmem(len(shapes)),
        out_shape=[jax.ShapeDtypeStruct(shape, dtype) for shape in shapes],
        compiler_params=SMALL,
    )(*arrays, *after)


def one_head(frames, bands, q, do, frozen_k, frozen_v, tokens, aq, ak, av):
    flat = q.shape[0]
    rows = flat // frames
    t_same = tokens[:flat]

    def adapted(frozen, rows_of, adapter):
        return (frozen.astype(F32) + dot_nn(rows_of, adapter)).astype(BF16)

    query = adapted(q, t_same, aq)
    keys, values = adapted(frozen_k, tokens, ak), adapted(frozen_v, tokens, av)
    do_t, keys_t, values_t = do.T, keys.T, values.T

    def bias(i, b):
        j, need = (b, 0) if b < frames else (b - frames, 1)
        value = jnp.where(bands[i, j] > need, 0.0, -jnp.inf).astype(F32)
        return jnp.full((1, rows), value, F32)

    span = 2 if frames % 2 == 0 else 1
    wide = span * rows
    dks, dvs, dqs = [None] * (2 * frames), [None] * (2 * frames), []
    for first in range(0, frames, span):
        mine = range(first, first + span)
        blocks = list(range(frames)) + [
            frames + j for j in range(frames) if any(abs(i - j) <= NEAR for i in mine)
        ]
        here = slice(first * rows, first * rows + wide)
        q_p, do_p = query[here], do[here]

        def gather(whole, axis):
            parts = [
                whole[b * rows : (b + 1) * rows] if axis == 0 else whole[:, b * rows : (b + 1) * rows]
                for b in blocks
            ]
            return jnp.concatenate(parts, axis=axis)

        raw = dot_nt(gather(keys, 0), q_p)
        scores = [
            raw[n * rows : (n + 1) * rows] * SCALE + jnp.concatenate([bias(i, b) for i in mine], axis=1)
            for n, b in enumerate(blocks)
        ]
        top = jnp.max(functools.reduce(jnp.maximum, scores), axis=0, keepdims=True)
        shifted = [jnp.exp(s - top) for s in scores]
        inverse = 1.0 / jnp.sum(functools.reduce(jnp.add, shifted), axis=0, keepdims=True)
        probs = [s * inverse for s in shifted]
        low = jnp.concatenate([p.astype(BF16) for p in probs], axis=0)
        attended = dot_nn(gather(values_t, 1), low).astype(BF16).astype(F32)
        delta = jnp.sum(do_t[:, here].astype(F32) * attended, axis=0, keepdims=True)
        prob_grad = dot_nt(gather(values, 0), do_p)
        grad = jnp.concatenate(
            [
                (probs[n] * (prob_grad[n * rows : (n + 1) * rows] - delta)).astype(BF16)
                for n in range(len(blocks))
            ],
            axis=0,
        )
        dqs.append((dot_nn(gather(keys_t, 1), grad) * SCALE).astype(BF16).T)
        dk, dv = dot_nn(grad, q_p), dot_nn(low, do_p)
        for n, b in enumerate(blocks):
            part = slice(n * rows, (n + 1) * rows)
            dks[b] = dk[part] if dks[b] is None else dks[b] + dk[part]
            dvs[b] = dv[part] if dvs[b] is None else dvs[b] + dv[part]
    dq = jnp.concatenate(dqs, axis=0)
    dk = (jnp.concatenate(dks, axis=0) * SCALE).astype(BF16)
    dv = jnp.concatenate(dvs, axis=0).astype(BF16)
    both = jnp.concatenate([dk, dv], axis=1)
    sums = dot_tn(tokens, both)
    grads = jnp.concatenate([dot_tn(t_same, dq), sums[:, :DH], sums[:, DH:]], axis=0)
    lows = dot_nt(both, jnp.concatenate([ak, av], axis=1))
    return grads, lows[:flat] + dot_nt(dq, aq), lows[flat:]


def group_kernel(heads, frames, chained, waits, sides, count, *refs):
    refs = list(refs)

    def take(count):
        taken = refs[:count]
        del refs[:count]
        return taken

    (bands,) = take(1)
    arrays, adapters = take(count), take(3)
    before = take(2) if chained else None
    take(waits)
    keep_ref, *give_refs = take(1 + GIVES if chained else 2)
    low_refs = [] if chained else take(2)
    q, do, k, v, tokens = refs
    me, half = lax.axis_index("tm"), lax.axis_index("rep")
    rows = arrays[0].shape[0]
    flat = frames * rows
    cut = 3 * tokens.shape[1] // 2
    first = half == 0
    same_at = [pl.ds(pl.multiple_of((me ^ m) * rows, rows), rows) for m in range(frames)]
    other_at = [pl.ds(pl.multiple_of(flat + (me ^ m) * rows, rows), rows) for m in range(frames)]

    def put(targets, places, rows_at):
        for m, (n, start) in enumerate(places):
            for c, target in enumerate(targets):
                target[rows_at[m], :] = arrays[n][:, start + c * DH : start + (c + 1) * DH]

    put([tokens], sides[0][0], same_at)
    put([tokens], sides[0][1], other_at)

    def run(n, table):
        put([q, do, k, v], sides[1 + n][0], same_at)
        put([k, v], sides[1 + n][1], other_at)
        cols = column(lookup(table, me))
        grads, low_same, low_other = one_head(
            frames, bands, q[...], do[...], k[...], v[...], tokens[...], *[a[:, cols] for a in adapters]
        )
        keep = jnp.where(first, grads[:cut], grads[cut:])
        give = jnp.where(first, grads[cut:], grads[:cut])
        return keep, give, low_same, low_other

    if chained:
        keep, give, low_same, low_other = run(0, heads[0][0])
        keep_ref[:cut, :] = keep
        keep_ref[cut:, :] = before[0][...] + low_same
        give = jnp.concatenate([give, before[1][...] + low_other], axis=0)
        size = give.shape[0] // GIVES
        for n, ref in enumerate(give_refs):
            ref[...] = give[n * size : (n + 1) * size].astype(ref.dtype)
        return
    for n, (table, counts) in enumerate(heads):
        here = slice(n * cut, (n + 1) * cut)

        def body():
            keep, give, low_same, low_other = run(n, table)
            keep_ref[here, :] = keep
            give_refs[0][here, :] = give.astype(BF16)
            if n == 0:
                low_refs[0][...] = low_same
                low_refs[1][...] = low_other
            else:
                low_refs[0][...] += low_same
                low_refs[1][...] += low_other

        if min(counts) > 0:
            body()
        else:
            live = lookup(counts, me) > 0
            pl.when(live)(body)

            @pl.when(jnp.logical_not(live))
            def _():
                keep_ref[here, :] = jnp.zeros((cut, DH), F32)
                give_refs[0][here, :] = jnp.zeros((cut, DH), BF16)


def head_group(heads, bands, sides, adapters, before=(), after=()):
    frames = len(sides[0][0])
    arrays, places = [], []
    for side in sides:
        found = []
        for pairs_of in side:
            found.append([])
            for array, start in pairs_of:
                known = [n for n, a in enumerate(arrays) if a is array]
                if not known:
                    arrays.append(array)
                found[-1].append((known[0] if known else len(arrays) - 1, start))
        places.append(found)
    rows, rank = arrays[0].shape[0], adapters[0].shape[0]
    flat = frames * rows
    size = len(heads) * 3 * rank // 2
    chained = len(before) > 0
    args = [bands, *arrays, *adapters, *before, *after]
    specs = [pl.BlockSpec(memory_space=pltpu.SMEM)] + vmem(len(arrays) + 3 + len(before))
    specs += [pl.BlockSpec(memory_space=pl.ANY)] * len(after)
    low = jax.ShapeDtypeStruct((flat, rank), F32)
    if chained:
        part = jax.ShapeDtypeStruct(((size + flat) // GIVES, rank), BF16)
        shapes = [jax.ShapeDtypeStruct((size + flat, rank), F32)] + [part] * GIVES
    else:
        edge = jax.ShapeDtypeStruct((size, rank), F32)
        shapes = [edge, jax.ShapeDtypeStruct((size, rank), BF16), low, low]
    return pl.pallas_call(
        functools.partial(
            group_kernel, heads, frames, chained, len(after), places, len(arrays)
        ),
        in_specs=specs,
        out_specs=vmem(len(shapes)),
        out_shape=shapes,
        scratch_shapes=[pltpu.VMEM((flat, DH), BF16)] * 2
        + [pltpu.VMEM((2 * flat, DH), BF16)] * 2
        + [pltpu.VMEM((2 * flat, rank), BF16)],
        compiler_params=pltpu.CompilerParams(vmem_limit_bytes=40 * 1024 * 1024),
    )(*args)


def hand_out_kernel(frames, size, parts, keep_ref, *refs):
    gots, (piece, facing), (own_ref, *sends, total) = refs[:parts], refs[parts : parts + 2], refs[parts + 2 :]
    lows, grads = sends[: frames - 1], sends[frames - 1 :]
    me = lax.axis_index("tm")
    rows = own_ref.shape[0]
    total[...] = keep_ref[...] + jnp.concatenate([got[...].astype(F32) for got in gots], axis=0)
    for m in range(frames):
        low = total[pl.ds(pl.multiple_of(size + (me ^ m) * rows, 8), rows), :]
        if m == 0:
            own_ref[...] = low
        else:
            lows[m - 1][...] = low.astype(BF16)
            grads[m - 1][:size, :] = total[:size, :].astype(BF16)
    grads[0][size : 3 * size, :] = piece[...]
    grads[0][3 * size :, :] = facing[size:, :]
    grads[1][size:, :] = piece[:size, :]


def hand_out(frames, rows, keep, gots, piece, facing):
    size, rank = keep.shape[0] - frames * rows, keep.shape[1]
    low = jax.ShapeDtypeStruct((rows, rank), BF16)
    outs = pl.pallas_call(
        functools.partial(hand_out_kernel, frames, size, len(gots)),
        in_specs=vmem(3 + len(gots)),
        out_specs=vmem(2 * frames - 1),
        out_shape=[jax.ShapeDtypeStruct((rows, rank), F32)]
        + [low] * (frames - 1)
        + [jax.ShapeDtypeStruct((size * n, rank), BF16) for n in (4, 2, 1)],
        scratch_shapes=[pltpu.VMEM(keep.shape, F32)],
        compiler_params=SMALL,
    )(keep, *gots, piece, facing)
    return outs[0], outs[1:frames], outs[frames:]


def sum_low_kernel(own_ref, *refs):
    low = own_ref[...]
    for got in refs[:-1]:
        low = low + got[...].astype(F32)
    refs[-1][...] = low.astype(BF16)


def sum_low(own, gots):
    return pl.pallas_call(
        sum_low_kernel,
        in_specs=vmem(1 + len(gots)),
        out_specs=pl.BlockSpec(memory_space=pltpu.VMEM),
        out_shape=jax.ShapeDtypeStruct(own.shape, BF16),
        compiler_params=SMALL,
    )(own, *gots)


def collect_kernel(wide, low_ref, low_head, own, near, third, last, piece, facing, out_ref):
    rows, size = low_ref.shape[0], own.shape[0]
    out_ref[:rows, :] = (low_ref[...].astype(F32) + low_head[...].astype(F32)).astype(BF16)
    middle = lookup(wide, lax.axis_index("tm")) > 0

    def part(ref, n):
        return ref[n * size : (n + 1) * size, :]

    blocks = [part(ref, 0) for ref in (own, near, third, last)]
    blocks += [part(piece, 0), part(near, 1), part(third, 1), part(facing, 0)]
    blocks.append(jnp.where(middle, part(piece, 1), part(near, 2)))
    blocks.append(jnp.where(middle, part(facing, 1), part(near, 3)))
    for n, block in enumerate(blocks):
        out_ref[rows + n * size : rows + (n + 1) * size, :] = block


def collect(wide, low, low_head, own, gots, piece, facing):
    (rows, rank), size = low.shape, own.shape[0]
    return pl.pallas_call(
        functools.partial(collect_kernel, wide),
        in_specs=vmem(5 + len(gots)),
        out_specs=pl.BlockSpec(memory_space=pltpu.VMEM),
        out_shape=jax.ShapeDtypeStruct((rows + 10 * size, rank), BF16),
        compiler_params=SMALL,
    )(low, low_head, own, *gots, piece, facing)


def place_kernel(frames, lead, late, rest, tail, tail2, *outs):
    me, half = lax.axis_index("tm"), lax.axis_index("rep")
    first = half == 0
    rank = outs[0].shape[0]
    cut = 3 * rank // 2
    rows = outs[3].shape[0] // 2

    def both(here):
        a, b = tail[here, :].astype(F32), tail2[here, :].astype(F32)
        return jnp.concatenate([jnp.where(first, a, b), jnp.where(first, b, a)], axis=0)

    outs[3][...] = both(slice(0, rows))
    side = me // 2
    places = [lookup(late, me ^ m) for m in range(frames)] + [lookup(lead, me ^ m) for m in range(frames)]
    places += [lookup(rest, 1 + side), lookup(rest, 2 - side)]
    for n, head in enumerate(places):
        whole = both(slice(rows + n * cut, rows + (n + 1) * cut))
        for o in range(3):
            outs[o][:, column(head)] = whole[o * rank : (o + 1) * rank]


def place(frames, lead, late, rest, tail, tail2, rows, rank, width):
    return pl.pallas_call(
        functools.partial(place_kernel, frames, lead, late, rest),
        in_specs=vmem(2),
        out_specs=vmem(4),
        out_shape=[jax.ShapeDtypeStruct((rank, width), F32)] * 3
        + [jax.ShapeDtypeStruct((2 * rows, rank), F32)],
        compiler_params=SMALL,
    )(tail, tail2)


def exchange_plan(
    frozen_query,
    frozen_key,
    frozen_value,
    token_adapter_input,
    query_adapter_out,
    key_adapter_out,
    value_adapter_out,
    out_grad,
    band_width,
):
    rows, width = frozen_query.shape
    rank = token_adapter_input.shape[1]
    frames = band_width.shape[0]
    heads = width // DH
    starts, counts = head_table(heads, frames)
    most = max(counts)
    columns = [[min(starts[j] + s, heads - 1) for j in range(frames)] for s in range(most)]
    numbers = [[int(s < counts[j]) for j in range(frames)] for s in range(most)]
    slots = list(zip(columns, numbers))
    lead, late, rest = slots[0], slots[1], slots[2]
    wide = [j for j in range(frames) if counts[j] == most]
    adapters = [query_adapter_out, key_adapter_out, value_adapter_out]
    arrays = (frozen_query, out_grad, frozen_key, frozen_value, token_adapter_input)

    def meet(name, block, m, targets=range(frames)):
        with jax.named_scope(f"{name}_over_tm"):
            return lax.ppermute(block, "tm", [(j ^ m, j) for j in targets])

    def swap_in_chip(name, block):
        with jax.named_scope(f"{name}_in_chip"):
            return swap(block, "rep")

    def mine(slot, m):
        return (slot[0], m, "mine")

    sent, kept, sent_late = [], [], []
    for m in range(1, frames):
        first = [mine(lead, m), (None, m, "t")]
        if m == 1:
            sent.append(first + [mine(rest, m), mine(late, m)])
        else:
            sent += [first, [mine(rest, m)]]
            sent_late.append([mine(late, m)])
    for slot in (lead, rest, late):
        kept += [[mine(slot, 0)], [(slot[0], 0, "other")]]
    kept += [[(None, 0, "t")], [(None, 0, "other t")]]
    packed = pack(frames, sent, 56, *arrays)
    packed_late = pack(frames, sent_late + kept, 16, *arrays)
    kept = packed_late[len(sent_late) :]
    block = meet("nearest", packed[0], 1)
    lead_got, rest_got, late_got = [(block, 0)], [(block, 4 * DH + rank)], [(block, 8 * DH + rank)]
    for m in range(2, frames):
        lead_got.append((meet("lead", packed[2 * m - 3], m), 0))
        rest_got.append((meet("rest", packed[2 * m - 2], m, wide), 0))
        late_got.append((meet("late", packed_late[m - 2], m), 0))

    def sides(name, n, got, wide_t, apart, skip, after=()):
        size = 4 * DH - skip + (rank if wide_t else 0)
        picked = pick([(a, start + skip) for a, start in got], size, apart, after)
        cross = [swap_in_chip(name, block) for block in picked]
        where = 2 * DH - skip
        cross = [(cross[m], where) if apart else (cross[0], m * size + where) for m in range(frames - 1)]
        rows_here = [(kept[2 * n], 0)] + got
        rows_there = [(kept[2 * n + 1], 0)] + cross
        return rows_here, rows_there, cross

    *lead_side, cross = sides("lead", 0, lead_got, True, False, 2 * DH, kept[:1])
    t_side = (
        [(kept[6], 0)] + [(a, start + 4 * DH) for a, start in lead_got],
        [(kept[7], 0)] + [(block, start + 2 * DH) for block, start in cross],
    )
    *rest_side, _ = sides("rest", 1, rest_got, False, False, 2 * DH)
    early = [lead, rest]
    keep, give, *low = head_group(early, band_width, [t_side, lead_side, rest_side], adapters)
    got = swap_in_chip("early_gradients", give)
    piece = (keep + got.astype(F32)).astype(BF16)
    *late_side, _ = sides("late", 2, late_got, False, False, 0, [got])
    facing = meet("early_gradients", piece, 3)
    keep, *gives = head_group([late], band_width, [t_side, late_side], adapters, low, [piece])
    gives = [swap_in_chip("late_sums", g) for g in gives]
    own_low, lows, grads = hand_out(frames, rows, keep, gives, piece, facing)
    low = sum_low(own_low, [meet("low", block, m) for m, block in enumerate(lows, 1)])
    gots = [meet("late_gradients", block, m) for m, block in enumerate(grads, 1)]
    with jax.named_scope("low_over_head"):
        low_head = swap(low, "head")
    tail = collect(rest[1], low, low_head, grads[2], gots, piece, facing)
    outs = place(
        frames, lead[0], late[0], rest[0], tail, swap_in_chip("tail", tail), rows, rank, width
    )
    return tuple(outs)


def on_device(frozen_query, *rest):
    frames = rest[-1].shape[0]
    heads = frozen_query.shape[1] // DH
    whole_reach = frames == 4 and heads == 2 * frames + 2
    return (exchange_plan if whole_reach else window_plan)(frozen_query, *rest)


def solution(mesh):
    in_specs = (
        P(("groups", "tm", "rep"), "head"),
        P(("groups", "tm"), "head"),
        P(("groups", "tm"), "head"),
        P(("groups", "tm"), None),
        P(None, "head"),
        P(None, "head"),
        P(None, "head"),
        P(("groups", "tm", "rep"), "head"),
        P(),
    )
    out_specs = (
        P("groups", "head"),
        P("groups", "head"),
        P("groups", "head"),
        P(("groups", "tm"), None),
    )
    return jax.shard_map(
        on_device, mesh=mesh, in_specs=in_specs, out_specs=out_specs, check_vma=False
    )
```

```python
import functools

import jax
import jax.numpy as jnp
from jax import lax
from jax.experimental import pallas as pl
from jax.experimental.pallas import tpu as pltpu
from jax.sharding import PartitionSpec as P

DH = 128
NEAR = 1
REACH = 4
SCALE = DH ** (-0.5)
F32 = jnp.float32
BF16 = jnp.bfloat16
GIVES = 2
SMALL = pltpu.CompilerParams(vmem_limit_bytes=16 * 1024 * 1024)


def dot_nn(left, right):
    return lax.dot_general(left, right, (((1,), (0,)), ((), ())), preferred_element_type=F32)


def dot_nt(left, right):
    return lax.dot_general(left, right, (((1,), (1,)), ((), ())), preferred_element_type=F32)


def dot_tn(left, right):
    return lax.dot_general(left, right, (((0,), (0,)), ((), ())), preferred_element_type=F32)


def routes(count):
    found = []
    for d in range(1, min(REACH, count - 1) + 1):
        if 2 * d >= count:
            found.append((d, (-d, d)))
        else:
            found.append((d, (-d,)))
            found.append((d, (d,)))
    return found


def pairs(count, offsets):
    return [(i + o, i) for o in offsets for i in range(count) if 0 <= i + o < count]


def swap(block, axis):
    return lax.ppermute(block, axis, [(0, 1), (1, 0)])


def attention_kernel(
    blocks, bias_ref, fq_ref, do_ref, fk_ref, fv_ref, t_ref, tr_ref, tt_ref, aq_ref, ak_ref, av_ref, *refs
):
    k_refs = refs[:blocks]
    v_refs = refs[blocks : 2 * blocks]
    gq_ref, gk_ref, gv_ref, lowq_ref, low_ref = refs[2 * blocks :]
    rows = fq_ref.shape[0]

    @pl.when(pl.program_id(0) == 0)
    def _():
        lowq_ref[...] = jnp.zeros_like(lowq_ref)
        low_ref[...] = jnp.zeros_like(low_ref)

    aq, ak, av = aq_ref[...], ak_ref[...], av_ref[...]
    query = (fq_ref[...].astype(F32) + dot_nn(tr_ref[...], aq)).astype(BF16)
    do = do_ref[...]
    own_k = (fk_ref[...].astype(F32) + dot_nn(t_ref[...], ak)).astype(BF16)
    own_v = (fv_ref[...].astype(F32) + dot_nn(t_ref[...], av)).astype(BF16)
    keys = [own_k[:rows], own_k[rows:]] + [ref[...] for ref in k_refs]
    values = [own_v[:rows], own_v[rows:]] + [ref[...] for ref in v_refs]
    count = len(keys)
    scores = [dot_nt(keys[b], query) * SCALE + bias_ref[b] for b in range(count)]
    top = functools.reduce(jnp.maximum, scores)
    top = jnp.max(top, axis=0, keepdims=True)
    shifted = [jnp.exp(s - top) for s in scores]
    total = jnp.sum(functools.reduce(jnp.add, shifted), axis=0, keepdims=True)
    inverse = 1.0 / total
    probs = [s * inverse for s in shifted]
    lows = [p.astype(BF16) for p in probs]
    attended = functools.reduce(jnp.add, [dot_tn(lows[b], values[b]) for b in range(count)])
    attended = attended.astype(BF16).astype(F32)
    delta = jnp.sum((do.astype(F32) * attended).T, axis=0, keepdims=True)
    grads = [
        (probs[b] * (dot_nt(values[b], do) - delta)).astype(BF16) for b in range(count)
    ]
    dq = functools.reduce(jnp.add, [dot_tn(grads[b], keys[b]) for b in range(count)])
    dq = (dq * SCALE).astype(BF16)
    gq_ref[...] = dot_tn(tr_ref[...], dq)
    lowq_ref[...] += dot_nt(dq, aq)
    both = jnp.concatenate([ak, av], axis=1)
    for b in range(count):
        dk = (dot_nn(grads[b], query) * SCALE).astype(BF16)
        dv = dot_nn(lows[b], do).astype(BF16)
        part = jnp.concatenate([dk, dv], axis=1)
        low_ref[b * rows : (b + 1) * rows, :] += dot_nt(part, both)
        out = dot_nn(tt_ref[:, b * rows : (b + 1) * rows], part)
        if b == 0:
            total_part = out
        else:
            total_part += out
    gk_ref[...] = total_part[:, :DH]
    gv_ref[...] = total_part[:, DH:]


def attention(bias, fq, do, fk, fv, t, tr, tt, aq, ak, av, payloads):
    rows, width = fq.shape
    heads = width // DH
    rank = t.shape[1]
    blocks = len(payloads)
    count = blocks + 2

    def col(r):
        return pl.BlockSpec((r, DH), lambda h: (0, h))

    def whole(shape):
        return pl.BlockSpec(shape, lambda h: (0, 0))

    return pl.pallas_call(
        functools.partial(attention_kernel, blocks),
        grid=(heads,),
        out_shape=[
            jax.ShapeDtypeStruct((rank, width), F32),
            jax.ShapeDtypeStruct((rank, width), F32),
            jax.ShapeDtypeStruct((rank, width), F32),
            jax.ShapeDtypeStruct((rows, rank), F32),
            jax.ShapeDtypeStruct((count * rows, rank), F32),
        ],
        in_specs=[pl.BlockSpec(memory_space=pltpu.SMEM)]
        + [col(rows), col(rows), col(2 * rows), col(2 * rows)]
        + [whole(t.shape), whole(tr.shape), whole(tt.shape)]
        + [col(rank)] * 3
        + [col(rows)] * blocks
        + [pl.BlockSpec((rows, DH), lambda h: (0, heads + h))] * blocks,
        out_specs=[col(rank)] * 3 + [whole((rows, rank)), whole((count * rows, rank))],
        compiler_params=pltpu.CompilerParams(vmem_limit_bytes=32 * 1024 * 1024),
    )(bias, fq, do, fk, fv, t, tr, tt, aq, ak, av, *payloads, *payloads)


def sum_rows(part, frame_idx, half_idx, frames):
    rows, width = part.shape
    half = width // 2
    keep = lax.dynamic_slice_in_dim(part, half_idx * half, half, 1)
    give = lax.dynamic_slice_in_dim(part, (1 - half_idx) * half, half, 1)
    mine = keep + swap(give, "rep")
    if frames & (frames - 1) or rows % frames or frames > REACH + 1:
        total = lax.psum(mine, "tm").astype(BF16)
    else:
        chunk = rows // frames
        low = mine.astype(BF16)
        acc = lax.dynamic_slice_in_dim(mine, frame_idx * chunk, chunk, 0)
        for m in range(1, frames):
            give = lax.dynamic_slice_in_dim(low, (frame_idx ^ m) * chunk, chunk, 0)
            acc = acc + lax.ppermute(give, "tm", [(i, i ^ m) for i in range(frames)]).astype(F32)
        acc = acc.astype(BF16)
        total = jnp.zeros((rows, half), BF16)
        total = lax.dynamic_update_slice_in_dim(total, acc, frame_idx * chunk, 0)
        for m in range(1, frames):
            got = lax.ppermute(acc, "tm", [(i, i ^ m) for i in range(frames)])
            total = lax.dynamic_update_slice_in_dim(total, got, (frame_idx ^ m) * chunk, 0)
    other = swap(total, "rep")
    first = jnp.where(half_idx == 0, total, other)
    second = jnp.where(half_idx == 0, other, total)
    return jnp.concatenate([first, second], axis=1).astype(F32)


def window_plan(
    frozen_query,
    frozen_key,
    frozen_value,
    token_adapter_input,
    query_adapter_out,
    key_adapter_out,
    value_adapter_out,
    out_grad,
    band_width,
):
    rows, width = frozen_query.shape
    rank = token_adapter_input.shape[1]
    frames = band_width.shape[0]
    frame_idx = lax.axis_index("tm")
    half_idx = lax.axis_index("rep")
    t = token_adapter_input
    tr = lax.dynamic_slice_in_dim(t, half_idx * rows, rows, 0)

    def tile_rows_of(frozen, adapter):
        own = lax.dynamic_slice_in_dim(frozen, half_idx * rows, rows, 0)
        return (own.astype(F32) + dot_nn(tr, adapter)).astype(BF16)

    payload = jnp.concatenate(
        [tile_rows_of(frozen_key, key_adapter_out), tile_rows_of(frozen_value, value_adapter_out), tr],
        axis=1,
    )

    frame_ids = jnp.arange(frames)
    band_row = jnp.sum(jnp.where((frame_ids == frame_idx)[:, None], band_width, 0), axis=0)

    def band_at(offsets):
        seen = functools.reduce(jnp.logical_or, [frame_ids == frame_idx + o for o in offsets])
        return jnp.sum(jnp.where(seen, band_row, 0))

    own_band = band_at((0,))
    allowed = [jnp.abs(half_idx - tile) < own_band for tile in range(2)]
    payloads = []
    plan = routes(frames)
    for d, offsets in plan:
        got = lax.ppermute(payload, "tm", pairs(frames, offsets))
        band = band_at(offsets)
        payloads.append(got)
        allowed.append(band > 0)
        if d <= NEAR:
            payloads.append(swap(got, "rep"))
            allowed.append(band > 1)
    bias = jnp.where(jnp.stack(allowed), 0.0, -jnp.inf).astype(F32)
    tt = jnp.concatenate([t] + [p[:, 2 * width :] for p in payloads], axis=0).T

    gq, gk, gv, low_q, low_b = attention(
        bias, frozen_query, out_grad, frozen_key, frozen_value, t, tr, tt,
        query_adapter_out, key_adapter_out, value_adapter_out, payloads,
    )

    own = low_b[: 2 * rows]
    same = lax.dynamic_slice_in_dim(own, half_idx * rows, rows, 0) + low_q
    other = lax.dynamic_slice_in_dim(own, (1 - half_idx) * rows, rows, 0)
    start = 2 * rows
    for d, offsets in plan:
        size = 2 * rows if d <= NEAR else rows
        back = [(target, source) for source, target in pairs(frames, offsets)]
        got = lax.ppermute(low_b[start : start + size], "tm", back)
        start += size
        same = same + got[:rows]
        if d <= NEAR:
            other = other + got[rows:]
    low = jnp.where(
        half_idx == 0,
        jnp.concatenate([same, other], axis=0),
        jnp.concatenate([other, same], axis=0),
    )
    low = low + swap(low, "rep")
    low = low + swap(low, "head")

    grads = sum_rows(jnp.concatenate([gq, gk, gv], axis=0), frame_idx, half_idx, frames)
    return grads[:rank], grads[rank : 2 * rank], grads[2 * rank :], low


def head_table(heads, frames):
    base, extra = divmod(heads, frames)
    lead = (frames - extra) // 2
    counts = [base + (1 if lead <= j < lead + extra else 0) for j in range(frames)]
    return [sum(counts[:j]) for j in range(frames)], counts


def lookup(table, index):
    value = jnp.int32(table[0])
    for j in range(1, len(table)):
        value = jnp.where(index == j, jnp.int32(table[j]), value)
    return value


def column(head):
    return pl.ds(pl.multiple_of(head * DH, DH), DH)


def vmem(count):
    return [pl.BlockSpec(memory_space=pltpu.VMEM)] * count


def pack_kernel(frames, outputs, fq_ref, do_ref, fk_ref, fv_ref, t_ref, *refs):
    outs, (q_in, do_in, k_in, v_in, k2_in, v2_in, t_in, sems) = refs[:-8], refs[-8:]
    wanted = {what for parts in outputs for _, _, what in parts}
    me, half = lax.axis_index("tm"), lax.axis_index("rep")
    rows = fq_ref.shape[0]
    mine = pl.ds(pl.multiple_of(half * rows, rows), rows)
    rest = pl.ds(pl.multiple_of((1 - half) * rows, rows), rows)
    moves = [
        (fq_ref, q_in), (do_ref, do_in), (fk_ref.at[mine, :], k_in), (fv_ref.at[mine, :], v_in), (t_ref, t_in)
    ]
    if "other" in wanted:
        moves += [(fk_ref.at[rest, :], k2_in), (fv_ref.at[rest, :], v2_in)]
    copies = [pltpu.make_async_copy(a, b, sems.at[n]) for n, (a, b) in enumerate(moves)]
    for copy in copies:
        copy.start()
    for copy in copies:
        copy.wait()
    for out, parts in zip(outs, outputs):
        at = 0
        for table, m, what in parts:
            if what in ("t", "other t"):
                blocks = [t_in[mine if what == "t" else rest, :]]
            else:
                cols = column(lookup(table, me ^ m))
                sources = (q_in, do_in, k_in, v_in) if what == "mine" else (k2_in, v2_in)
                blocks = [ref[:, cols] for ref in sources]
            for block in blocks:
                out[:, at : at + block.shape[1]] = block
                at += block.shape[1]


def pack(frames, outputs, limit, fq, do, fk, fv, t):
    rows, width = fq.shape
    size = {"mine": 4 * DH, "other": 2 * DH, "t": t.shape[1], "other t": t.shape[1]}
    return pl.pallas_call(
        functools.partial(pack_kernel, frames, outputs),
        in_specs=[pl.BlockSpec(memory_space=pltpu.HBM)] * 5,
        out_specs=vmem(len(outputs)),
        out_shape=[
            jax.ShapeDtypeStruct((rows, sum(size[what] for _, _, what in parts)), BF16)
            for parts in outputs
        ],
        scratch_shapes=[pltpu.VMEM((rows, width), BF16)] * 6
        + [pltpu.VMEM(t.shape, BF16), pltpu.SemaphoreType.DMA((7,))],
        compiler_params=pltpu.CompilerParams(vmem_limit_bytes=limit * 1024 * 1024),
    )(fq, do, fk, fv, t)


def pick_kernel(spans, groups, *refs):
    n = 0
    for out, count in zip(refs[-len(groups) :], groups):
        for at in range(count):
            start, size = spans[n]
            out[:, at * size : (at + 1) * size] = refs[n][:, start : start + size]
            n += 1


def pick(parts, size, groups, after=()):
    arrays = [array for array, _ in parts]
    rows, dtype = arrays[0].shape[0], arrays[0].dtype
    return pl.pallas_call(
        functools.partial(pick_kernel, [(start, size) for _, start in parts], groups),
        in_specs=vmem(len(arrays)) + [pl.BlockSpec(memory_space=pl.ANY)] * len(after),
        out_specs=vmem(len(groups)),
        out_shape=[jax.ShapeDtypeStruct((rows, size * count), dtype) for count in groups],
        compiler_params=SMALL,
    )(*arrays, *after)


def one_head(frames, bands, q, do, frozen_k, frozen_v, tokens, aq, ak, av):
    flat = q.shape[0]
    rows = flat // frames
    t_same = tokens[:flat]

    def adapted(frozen, rows_of, adapter):
        return (frozen.astype(F32) + dot_nn(rows_of, adapter)).astype(BF16)

    query = adapted(q, t_same, aq)
    keys, values = adapted(frozen_k, tokens, ak), adapted(frozen_v, tokens, av)
    do_t, keys_t, values_t = do.T, keys.T, values.T

    def bias(i, b):
        j, need = (b, 0) if b < frames else (b - frames, 1)
        value = jnp.where(bands[i, j] > need, 0.0, -jnp.inf).astype(F32)
        return jnp.full((1, rows), value, F32)

    span = 2 if frames % 2 == 0 else 1
    wide = span * rows
    groups = [range(first, first + span) for first in range(0, frames, span)]
    seen = [
        list(range(frames))
        + [frames + j for j in range(frames) if any(abs(i - j) <= NEAR for i in mine)]
        for mine in groups
    ]
    here = [slice(mine[0] * rows, mine[0] * rows + wide) for mine in groups]
    pairs_of = range(len(groups))

    def gather(whole, g, axis):
        parts = [
            whole[b * rows : (b + 1) * rows] if axis == 0 else whole[:, b * rows : (b + 1) * rows]
            for b in seen[g]
        ]
        return jnp.concatenate(parts, axis=axis)

    def block(whole, n):
        return whole[n * rows : (n + 1) * rows]

    def softmax(g, raw):
        scores = [
            block(raw, n) * SCALE + jnp.concatenate([bias(i, b) for i in groups[g]], axis=1)
            for n, b in enumerate(seen[g])
        ]
        top = jnp.max(functools.reduce(jnp.maximum, scores), axis=0, keepdims=True)
        shifted = [jnp.exp(s - top) for s in scores]
        inverse = 1.0 / jnp.sum(functools.reduce(jnp.add, shifted), axis=0, keepdims=True)
        return [s * inverse for s in shifted]

    raws = [dot_nt(gather(keys, g, 0), query[here[g]]) for g in pairs_of]
    prob_grads = [dot_nt(gather(values, g, 0), do[here[g]]) for g in pairs_of]
    probs = [softmax(g, raws[g]) for g in pairs_of]
    lows = [jnp.concatenate([p.astype(BF16) for p in probs[g]], axis=0) for g in pairs_of]
    grads = []
    for g in pairs_of:
        attended = dot_nn(gather(values_t, g, 1), lows[g]).astype(BF16).astype(F32)
        delta = jnp.sum(do_t[:, here[g]].astype(F32) * attended, axis=0, keepdims=True)
        parts = [
            (probs[g][n] * (block(prob_grads[g], n) - delta)).astype(BF16) for n in range(len(seen[g]))
        ]
        grads.append(jnp.concatenate(parts, axis=0))
    dvs, dks = [None] * (2 * frames), [None] * (2 * frames)

    def add(sums, g, whole):
        for n, b in enumerate(seen[g]):
            sums[b] = block(whole, n) if sums[b] is None else sums[b] + block(whole, n)

    for g in pairs_of:
        add(dvs, g, dot_nn(lows[g], do[here[g]]))
    for g in pairs_of:
        add(dks, g, dot_nn(grads[g], query[here[g]]))
    dqs = [(dot_nn(gather(keys_t, g, 1), grads[g]) * SCALE).astype(BF16).T for g in pairs_of]
    dq = jnp.concatenate(dqs, axis=0)
    dk = (jnp.concatenate(dks, axis=0) * SCALE).astype(BF16)
    dv = jnp.concatenate(dvs, axis=0).astype(BF16)
    both = jnp.concatenate([dk, dv], axis=1)
    sums = dot_tn(tokens, both)
    grads = jnp.concatenate([dot_tn(t_same, dq), sums[:, :DH], sums[:, DH:]], axis=0)
    lows = dot_nt(both, jnp.concatenate([ak, av], axis=1))
    return grads, lows[:flat] + dot_nt(dq, aq), lows[flat:]


def group_kernel(heads, frames, chained, waits, sides, count, *refs):
    refs = list(refs)

    def take(count):
        taken = refs[:count]
        del refs[:count]
        return taken

    (bands,) = take(1)
    arrays, adapters = take(count), take(3)
    before = take(2) if chained else None
    take(waits)
    keep_ref, *give_refs = take(1 + GIVES if chained else 2)
    low_refs = [] if chained else take(2)
    q, do, k, v, tokens = refs
    me, half = lax.axis_index("tm"), lax.axis_index("rep")
    rows = arrays[0].shape[0]
    flat = frames * rows
    cut = 3 * tokens.shape[1] // 2
    first = half == 0
    same_at = [pl.ds(pl.multiple_of((me ^ m) * rows, rows), rows) for m in range(frames)]
    other_at = [pl.ds(pl.multiple_of(flat + (me ^ m) * rows, rows), rows) for m in range(frames)]

    def put(targets, places, rows_at):
        for m, (n, start) in enumerate(places):
            for c, target in enumerate(targets):
                target[rows_at[m], :] = arrays[n][:, start + c * DH : start + (c + 1) * DH]

    put([tokens], sides[0][0], same_at)
    put([tokens], sides[0][1], other_at)

    def run(n, table):
        put([q, do, k, v], sides[1 + n][0], same_at)
        put([k, v], sides[1 + n][1], other_at)
        cols = column(lookup(table, me))
        grads, low_same, low_other = one_head(
            frames, bands, q[...], do[...], k[...], v[...], tokens[...], *[a[:, cols] for a in adapters]
        )
        keep = jnp.where(first, grads[:cut], grads[cut:])
        give = jnp.where(first, grads[cut:], grads[:cut])
        return keep, give, low_same, low_other

    if chained:
        keep, give, low_same, low_other = run(0, heads[0][0])
        keep_ref[:cut, :] = keep
        keep_ref[cut:, :] = before[0][...] + low_same
        give = jnp.concatenate([give, before[1][...] + low_other], axis=0)
        size = give.shape[0] // GIVES
        for n, ref in enumerate(give_refs):
            ref[...] = give[n * size : (n + 1) * size].astype(ref.dtype)
        return
    for n, (table, counts) in enumerate(heads):
        here = slice(n * cut, (n + 1) * cut)

        def body():
            keep, give, low_same, low_other = run(n, table)
            keep_ref[here, :] = keep
            give_refs[0][here, :] = give.astype(BF16)
            if n == 0:
                low_refs[0][...] = low_same
                low_refs[1][...] = low_other
            else:
                low_refs[0][...] += low_same
                low_refs[1][...] += low_other

        if min(counts) > 0:
            body()
        else:
            live = lookup(counts, me) > 0
            pl.when(live)(body)

            @pl.when(jnp.logical_not(live))
            def _():
                keep_ref[here, :] = jnp.zeros((cut, DH), F32)
                give_refs[0][here, :] = jnp.zeros((cut, DH), BF16)


def head_group(heads, bands, sides, adapters, before=(), after=()):
    frames = len(sides[0][0])
    arrays, places = [], []
    for side in sides:
        found = []
        for pairs_of in side:
            found.append([])
            for array, start in pairs_of:
                known = [n for n, a in enumerate(arrays) if a is array]
                if not known:
                    arrays.append(array)
                found[-1].append((known[0] if known else len(arrays) - 1, start))
        places.append(found)
    rows, rank = arrays[0].shape[0], adapters[0].shape[0]
    flat = frames * rows
    size = len(heads) * 3 * rank // 2
    chained = len(before) > 0
    args = [bands, *arrays, *adapters, *before, *after]
    specs = [pl.BlockSpec(memory_space=pltpu.SMEM)] + vmem(len(arrays) + 3 + len(before))
    specs += [pl.BlockSpec(memory_space=pl.ANY)] * len(after)
    low = jax.ShapeDtypeStruct((flat, rank), F32)
    if chained:
        part = jax.ShapeDtypeStruct(((size + flat) // GIVES, rank), BF16)
        shapes = [jax.ShapeDtypeStruct((size + flat, rank), F32)] + [part] * GIVES
    else:
        edge = jax.ShapeDtypeStruct((size, rank), F32)
        shapes = [edge, jax.ShapeDtypeStruct((size, rank), BF16), low, low]
    return pl.pallas_call(
        functools.partial(
            group_kernel, heads, frames, chained, len(after), places, len(arrays)
        ),
        in_specs=specs,
        out_specs=vmem(len(shapes)),
        out_shape=shapes,
        scratch_shapes=[pltpu.VMEM((flat, DH), BF16)] * 2
        + [pltpu.VMEM((2 * flat, DH), BF16)] * 2
        + [pltpu.VMEM((2 * flat, rank), BF16)],
        compiler_params=pltpu.CompilerParams(vmem_limit_bytes=40 * 1024 * 1024),
    )(*args)


def hand_out_kernel(frames, size, parts, keep_ref, *refs):
    gots, (piece, facing), (own_ref, *sends, total) = refs[:parts], refs[parts : parts + 2], refs[parts + 2 :]
    me = lax.axis_index("tm")
    rows = own_ref.shape[0]
    total[...] = keep_ref[...] + jnp.concatenate([got[...].astype(F32) for got in gots], axis=0)
    for m in range(frames):
        low = total[pl.ds(pl.multiple_of(size + (me ^ m) * rows, 8), rows), :]
        if m == 0:
            own_ref[...] = low
        else:
            sends[m - 1][:rows, :] = low.astype(BF16)
            sends[m - 1][rows : rows + size, :] = total[:size, :].astype(BF16)
    sends[0][rows + size : rows + 3 * size, :] = piece[...]
    sends[0][rows + 3 * size :, :] = facing[size:, :]
    sends[1][rows + size :, :] = piece[:size, :]


def hand_out(frames, rows, keep, gots, piece, facing):
    size, rank = keep.shape[0] - frames * rows, keep.shape[1]
    own, *sends = pl.pallas_call(
        functools.partial(hand_out_kernel, frames, size, len(gots)),
        in_specs=vmem(3 + len(gots)),
        out_specs=vmem(frames),
        out_shape=[jax.ShapeDtypeStruct((rows, rank), F32)]
        + [jax.ShapeDtypeStruct((rows + size * n, rank), BF16) for n in (4, 2, 1)],
        scratch_shapes=[pltpu.VMEM(keep.shape, F32)],
        compiler_params=SMALL,
    )(keep, *gots, piece, facing)
    return own, sends


def collect_kernel(wide, own_low, own, near, third, last, piece, facing, out_ref, low_ref):
    rows = own_low.shape[0]
    size = own.shape[0] - rows
    low = own_low[...]
    for got in (near, third, last):
        low = low + got[:rows, :].astype(F32)
    out_ref[:rows, :] = low.astype(BF16)
    low_ref[...] = low.astype(BF16)
    middle = lookup(wide, lax.axis_index("tm")) > 0

    def part(ref, n):
        return ref[rows + n * size : rows + (n + 1) * size, :]

    blocks = [part(ref, 0) for ref in (own, near, third, last)]
    blocks += [piece[:size, :], part(near, 1), part(third, 1), facing[:size, :]]
    blocks.append(jnp.where(middle, piece[size:, :], part(near, 2)))
    blocks.append(jnp.where(middle, facing[size:, :], part(near, 3)))
    for n, block in enumerate(blocks):
        out_ref[rows + n * size : rows + (n + 1) * size, :] = block


def collect(wide, own_low, own, gots, piece, facing):
    (rows, rank), size = own_low.shape, piece.shape[0] // 2
    return pl.pallas_call(
        functools.partial(collect_kernel, wide),
        in_specs=vmem(4 + len(gots)),
        out_specs=vmem(2),
        out_shape=[
            jax.ShapeDtypeStruct((rows + 10 * size, rank), BF16),
            jax.ShapeDtypeStruct((rows, rank), BF16),
        ],
        compiler_params=SMALL,
    )(own_low, own, *gots, piece, facing)


def place_kernel(frames, lead, late, rest, tail, tail2, low_head, low_diag, *outs):
    me, half = lax.axis_index("tm"), lax.axis_index("rep")
    first = half == 0
    rank = outs[0].shape[0]
    cut = 3 * rank // 2
    rows = low_head.shape[0]
    same = tail[:rows, :].astype(F32) + low_head[...].astype(F32)
    other = tail2[:rows, :].astype(F32) + low_diag[...].astype(F32)
    outs[3][:rows, :] = jnp.where(first, same, other)
    outs[3][rows:, :] = jnp.where(first, other, same)
    side = me // 2
    places = [lookup(late, me ^ m) for m in range(frames)] + [lookup(lead, me ^ m) for m in range(frames)]
    places += [lookup(rest, 1 + side), lookup(rest, 2 - side)]
    for n, head in enumerate(places):
        here = slice(rows + n * cut, rows + (n + 1) * cut)
        a, b = tail[here, :].astype(F32), tail2[here, :].astype(F32)
        both = jnp.concatenate([jnp.where(first, a, b), jnp.where(first, b, a)], axis=0)
        for o in range(3):
            outs[o][:, column(head)] = both[o * rank : (o + 1) * rank]


def place(frames, lead, late, rest, tail, tail2, low_head, low_diag, rank, width):
    rows = low_head.shape[0]
    return pl.pallas_call(
        functools.partial(place_kernel, frames, lead, late, rest),
        in_specs=vmem(4),
        out_specs=vmem(4),
        out_shape=[jax.ShapeDtypeStruct((rank, width), F32)] * 3
        + [jax.ShapeDtypeStruct((2 * rows, rank), F32)],
        compiler_params=SMALL,
    )(tail, tail2, low_head, low_diag)


def exchange_plan(
    frozen_query,
    frozen_key,
    frozen_value,
    token_adapter_input,
    query_adapter_out,
    key_adapter_out,
    value_adapter_out,
    out_grad,
    band_width,
):
    rows, width = frozen_query.shape
    rank = token_adapter_input.shape[1]
    frames = band_width.shape[0]
    heads = width // DH
    starts, counts = head_table(heads, frames)
    most = max(counts)
    columns = [[min(starts[j] + s, heads - 1) for j in range(frames)] for s in range(most)]
    numbers = [[int(s < counts[j]) for j in range(frames)] for s in range(most)]
    slots = list(zip(columns, numbers))
    lead, late, rest = slots[0], slots[1], slots[2]
    wide = [j for j in range(frames) if counts[j] == most]
    adapters = [query_adapter_out, key_adapter_out, value_adapter_out]
    arrays = (frozen_query, out_grad, frozen_key, frozen_value, token_adapter_input)

    def meet(name, block, m, targets=range(frames)):
        with jax.named_scope(f"{name}_over_tm"):
            return lax.ppermute(block, "tm", [(j ^ m, j) for j in targets])

    def swap_in_chip(name, block):
        with jax.named_scope(f"{name}_in_chip"):
            return swap(block, "rep")

    def mine(slot, m):
        return (slot[0], m, "mine")

    sent, kept, sent_late = [], [], []
    for m in range(1, frames):
        first = [mine(lead, m), (None, m, "t")]
        if m == 1:
            sent.append(first + [mine(rest, m), mine(late, m)])
        else:
            sent += [first, [mine(rest, m)]]
            sent_late.append([mine(late, m)])
    for slot in (lead, rest, late):
        kept += [[mine(slot, 0)], [(slot[0], 0, "other")]]
    kept += [[(None, 0, "t")], [(None, 0, "other t")]]
    packed = pack(frames, sent, 56, *arrays)
    packed_late = pack(frames, sent_late + kept, 16, *arrays)
    kept = packed_late[len(sent_late) :]
    block = meet("nearest", packed[0], 1)
    lead_got, rest_got, late_got = [(block, 0)], [(block, 4 * DH + rank)], [(block, 8 * DH + rank)]
    for m in range(2, frames):
        lead_got.append((meet("lead", packed[2 * m - 3], m), 0))
        rest_got.append((meet("rest", packed[2 * m - 2], m, wide), 0))
        late_got.append((meet("late", packed_late[m - 2], m), 0))

    def sides(name, n, got, wide_t, groups, skip, after=()):
        size = 4 * DH - skip + (rank if wide_t else 0)
        picked = pick([(a, start + skip) for a, start in got], size, groups, after)
        cross = [swap_in_chip(name, block) for block in picked]
        where = 2 * DH - skip
        cross = [(block, at * size + where) for block, count in zip(cross, groups) for at in range(count)]
        rows_here = [(kept[2 * n], 0)] + got
        rows_there = [(kept[2 * n + 1], 0)] + cross
        return rows_here, rows_there, cross

    *lead_side, cross = sides("lead", 0, lead_got, True, (3,), 2 * DH, kept[:1])
    t_side = (
        [(kept[6], 0)] + [(a, start + 4 * DH) for a, start in lead_got],
        [(kept[7], 0)] + [(block, start + 2 * DH) for block, start in cross],
    )
    *rest_side, _ = sides("rest", 1, rest_got, False, (3,), 2 * DH)
    early = [lead, rest]
    keep, give, *low = head_group(early, band_width, [t_side, lead_side, rest_side], adapters)
    got = swap_in_chip("early_gradients", give)
    piece = (keep + got.astype(F32)).astype(BF16)
    *late_side, _ = sides("late", 2, late_got, False, (3,), 0, [got])
    facing = meet("early_gradients", piece, 3)
    keep, *gives = head_group([late], band_width, [t_side, late_side], adapters, low, [piece])
    gives = [swap_in_chip("late_sums", g) for g in gives]
    own_low, sends = hand_out(frames, rows, keep, gives, piece, facing)
    gots = [meet("late_sums", block, m) for m, block in enumerate(sends, 1)]
    tail, low = collect(rest[1], own_low, sends[2], gots, piece, facing)
    diag = [(0, 3), (1, 2), (2, 1), (3, 0)]
    with jax.named_scope("low_over_head"):
        low_head, low_diag = swap(low, "head"), lax.ppermute(low, ("head", "rep"), diag)
    outs = place(
        frames, lead[0], late[0], rest[0], tail, swap_in_chip("tail", tail), low_head, low_diag, rank, width
    )
    return tuple(outs)


def on_device(frozen_query, *rest):
    frames = rest[-1].shape[0]
    heads = frozen_query.shape[1] // DH
    whole_reach = frames == 4 and heads == 2 * frames + 2
    return (exchange_plan if whole_reach else window_plan)(frozen_query, *rest)


def solution(mesh):
    in_specs = (
        P(("groups", "tm", "rep"), "head"),
        P(("groups", "tm"), "head"),
        P(("groups", "tm"), "head"),
        P(("groups", "tm"), None),
        P(None, "head"),
        P(None, "head"),
        P(None, "head"),
        P(("groups", "tm", "rep"), "head"),
        P(),
    )
    out_specs = (
        P("groups", "head"),
        P("groups", "head"),
        P("groups", "head"),
        P(("groups", "tm"), None),
    )
    return jax.shard_map(
        on_device, mesh=mesh, in_specs=in_specs, out_specs=out_specs, check_vma=False
    )
```

```python
import functools

import jax
import jax.numpy as jnp
from jax import lax
from jax.experimental import pallas as pl
from jax.experimental.pallas import tpu as pltpu
from jax.sharding import PartitionSpec as P

DH = 128
NEAR = 1
REACH = 4
SCALE = DH ** (-0.5)
F32 = jnp.float32
BF16 = jnp.bfloat16
GIVES = 2
SMALL = pltpu.CompilerParams(vmem_limit_bytes=16 * 1024 * 1024)


def dot_nn(left, right):
    return lax.dot_general(left, right, (((1,), (0,)), ((), ())), preferred_element_type=F32)


def dot_nt(left, right):
    return lax.dot_general(left, right, (((1,), (1,)), ((), ())), preferred_element_type=F32)


def dot_tn(left, right):
    return lax.dot_general(left, right, (((0,), (0,)), ((), ())), preferred_element_type=F32)


def routes(count):
    found = []
    for d in range(1, min(REACH, count - 1) + 1):
        if 2 * d >= count:
            found.append((d, (-d, d)))
        else:
            found.append((d, (-d,)))
            found.append((d, (d,)))
    return found


def pairs(count, offsets):
    return [(i + o, i) for o in offsets for i in range(count) if 0 <= i + o < count]


def swap(block, axis):
    return lax.ppermute(block, axis, [(0, 1), (1, 0)])


def attention_kernel(
    blocks, bias_ref, fq_ref, do_ref, fk_ref, fv_ref, t_ref, tr_ref, tt_ref, aq_ref, ak_ref, av_ref, *refs
):
    k_refs = refs[:blocks]
    v_refs = refs[blocks : 2 * blocks]
    gq_ref, gk_ref, gv_ref, lowq_ref, low_ref = refs[2 * blocks :]
    rows = fq_ref.shape[0]

    @pl.when(pl.program_id(0) == 0)
    def _():
        lowq_ref[...] = jnp.zeros_like(lowq_ref)
        low_ref[...] = jnp.zeros_like(low_ref)

    aq, ak, av = aq_ref[...], ak_ref[...], av_ref[...]
    query = (fq_ref[...].astype(F32) + dot_nn(tr_ref[...], aq)).astype(BF16)
    do = do_ref[...]
    own_k = (fk_ref[...].astype(F32) + dot_nn(t_ref[...], ak)).astype(BF16)
    own_v = (fv_ref[...].astype(F32) + dot_nn(t_ref[...], av)).astype(BF16)
    keys = [own_k[:rows], own_k[rows:]] + [ref[...] for ref in k_refs]
    values = [own_v[:rows], own_v[rows:]] + [ref[...] for ref in v_refs]
    count = len(keys)
    scores = [dot_nt(keys[b], query) * SCALE + bias_ref[b] for b in range(count)]
    top = functools.reduce(jnp.maximum, scores)
    top = jnp.max(top, axis=0, keepdims=True)
    shifted = [jnp.exp(s - top) for s in scores]
    total = jnp.sum(functools.reduce(jnp.add, shifted), axis=0, keepdims=True)
    inverse = 1.0 / total
    probs = [s * inverse for s in shifted]
    lows = [p.astype(BF16) for p in probs]
    attended = functools.reduce(jnp.add, [dot_tn(lows[b], values[b]) for b in range(count)])
    attended = attended.astype(BF16).astype(F32)
    delta = jnp.sum((do.astype(F32) * attended).T, axis=0, keepdims=True)
    grads = [
        (probs[b] * (dot_nt(values[b], do) - delta)).astype(BF16) for b in range(count)
    ]
    dq = functools.reduce(jnp.add, [dot_tn(grads[b], keys[b]) for b in range(count)])
    dq = (dq * SCALE).astype(BF16)
    gq_ref[...] = dot_tn(tr_ref[...], dq)
    lowq_ref[...] += dot_nt(dq, aq)
    both = jnp.concatenate([ak, av], axis=1)
    for b in range(count):
        dk = (dot_nn(grads[b], query) * SCALE).astype(BF16)
        dv = dot_nn(lows[b], do).astype(BF16)
        part = jnp.concatenate([dk, dv], axis=1)
        low_ref[b * rows : (b + 1) * rows, :] += dot_nt(part, both)
        out = dot_nn(tt_ref[:, b * rows : (b + 1) * rows], part)
        if b == 0:
            total_part = out
        else:
            total_part += out
    gk_ref[...] = total_part[:, :DH]
    gv_ref[...] = total_part[:, DH:]


def attention(bias, fq, do, fk, fv, t, tr, tt, aq, ak, av, payloads):
    rows, width = fq.shape
    heads = width // DH
    rank = t.shape[1]
    blocks = len(payloads)
    count = blocks + 2

    def col(r):
        return pl.BlockSpec((r, DH), lambda h: (0, h))

    def whole(shape):
        return pl.BlockSpec(shape, lambda h: (0, 0))

    return pl.pallas_call(
        functools.partial(attention_kernel, blocks),
        grid=(heads,),
        out_shape=[
            jax.ShapeDtypeStruct((rank, width), F32),
            jax.ShapeDtypeStruct((rank, width), F32),
            jax.ShapeDtypeStruct((rank, width), F32),
            jax.ShapeDtypeStruct((rows, rank), F32),
            jax.ShapeDtypeStruct((count * rows, rank), F32),
        ],
        in_specs=[pl.BlockSpec(memory_space=pltpu.SMEM)]
        + [col(rows), col(rows), col(2 * rows), col(2 * rows)]
        + [whole(t.shape), whole(tr.shape), whole(tt.shape)]
        + [col(rank)] * 3
        + [col(rows)] * blocks
        + [pl.BlockSpec((rows, DH), lambda h: (0, heads + h))] * blocks,
        out_specs=[col(rank)] * 3 + [whole((rows, rank)), whole((count * rows, rank))],
        compiler_params=pltpu.CompilerParams(vmem_limit_bytes=32 * 1024 * 1024),
    )(bias, fq, do, fk, fv, t, tr, tt, aq, ak, av, *payloads, *payloads)


def sum_rows(part, frame_idx, half_idx, frames):
    rows, width = part.shape
    half = width // 2
    keep = lax.dynamic_slice_in_dim(part, half_idx * half, half, 1)
    give = lax.dynamic_slice_in_dim(part, (1 - half_idx) * half, half, 1)
    mine = keep + swap(give, "rep")
    if frames & (frames - 1) or rows % frames or frames > REACH + 1:
        total = lax.psum(mine, "tm").astype(BF16)
    else:
        chunk = rows // frames
        low = mine.astype(BF16)
        acc = lax.dynamic_slice_in_dim(mine, frame_idx * chunk, chunk, 0)
        for m in range(1, frames):
            give = lax.dynamic_slice_in_dim(low, (frame_idx ^ m) * chunk, chunk, 0)
            acc = acc + lax.ppermute(give, "tm", [(i, i ^ m) for i in range(frames)]).astype(F32)
        acc = acc.astype(BF16)
        total = jnp.zeros((rows, half), BF16)
        total = lax.dynamic_update_slice_in_dim(total, acc, frame_idx * chunk, 0)
        for m in range(1, frames):
            got = lax.ppermute(acc, "tm", [(i, i ^ m) for i in range(frames)])
            total = lax.dynamic_update_slice_in_dim(total, got, (frame_idx ^ m) * chunk, 0)
    other = swap(total, "rep")
    first = jnp.where(half_idx == 0, total, other)
    second = jnp.where(half_idx == 0, other, total)
    return jnp.concatenate([first, second], axis=1).astype(F32)


def window_plan(
    frozen_query,
    frozen_key,
    frozen_value,
    token_adapter_input,
    query_adapter_out,
    key_adapter_out,
    value_adapter_out,
    out_grad,
    band_width,
):
    rows, width = frozen_query.shape
    rank = token_adapter_input.shape[1]
    frames = band_width.shape[0]
    frame_idx = lax.axis_index("tm")
    half_idx = lax.axis_index("rep")
    t = token_adapter_input
    tr = lax.dynamic_slice_in_dim(t, half_idx * rows, rows, 0)

    def tile_rows_of(frozen, adapter):
        own = lax.dynamic_slice_in_dim(frozen, half_idx * rows, rows, 0)
        return (own.astype(F32) + dot_nn(tr, adapter)).astype(BF16)

    payload = jnp.concatenate(
        [tile_rows_of(frozen_key, key_adapter_out), tile_rows_of(frozen_value, value_adapter_out), tr],
        axis=1,
    )

    frame_ids = jnp.arange(frames)
    band_row = jnp.sum(jnp.where((frame_ids == frame_idx)[:, None], band_width, 0), axis=0)

    def band_at(offsets):
        seen = functools.reduce(jnp.logical_or, [frame_ids == frame_idx + o for o in offsets])
        return jnp.sum(jnp.where(seen, band_row, 0))

    own_band = band_at((0,))
    allowed = [jnp.abs(half_idx - tile) < own_band for tile in range(2)]
    payloads = []
    plan = routes(frames)
    for d, offsets in plan:
        got = lax.ppermute(payload, "tm", pairs(frames, offsets))
        band = band_at(offsets)
        payloads.append(got)
        allowed.append(band > 0)
        if d <= NEAR:
            payloads.append(swap(got, "rep"))
            allowed.append(band > 1)
    bias = jnp.where(jnp.stack(allowed), 0.0, -jnp.inf).astype(F32)
    tt = jnp.concatenate([t] + [p[:, 2 * width :] for p in payloads], axis=0).T

    gq, gk, gv, low_q, low_b = attention(
        bias, frozen_query, out_grad, frozen_key, frozen_value, t, tr, tt,
        query_adapter_out, key_adapter_out, value_adapter_out, payloads,
    )

    own = low_b[: 2 * rows]
    same = lax.dynamic_slice_in_dim(own, half_idx * rows, rows, 0) + low_q
    other = lax.dynamic_slice_in_dim(own, (1 - half_idx) * rows, rows, 0)
    start = 2 * rows
    for d, offsets in plan:
        size = 2 * rows if d <= NEAR else rows
        back = [(target, source) for source, target in pairs(frames, offsets)]
        got = lax.ppermute(low_b[start : start + size], "tm", back)
        start += size
        same = same + got[:rows]
        if d <= NEAR:
            other = other + got[rows:]
    low = jnp.where(
        half_idx == 0,
        jnp.concatenate([same, other], axis=0),
        jnp.concatenate([other, same], axis=0),
    )
    low = low + swap(low, "rep")
    low = low + swap(low, "head")

    grads = sum_rows(jnp.concatenate([gq, gk, gv], axis=0), frame_idx, half_idx, frames)
    return grads[:rank], grads[rank : 2 * rank], grads[2 * rank :], low


def head_table(heads, frames):
    base, extra = divmod(heads, frames)
    lead = (frames - extra) // 2
    counts = [base + (1 if lead <= j < lead + extra else 0) for j in range(frames)]
    return [sum(counts[:j]) for j in range(frames)], counts


def lookup(table, index):
    value = jnp.int32(table[0])
    for j in range(1, len(table)):
        value = jnp.where(index == j, jnp.int32(table[j]), value)
    return value


def column(head):
    return pl.ds(pl.multiple_of(head * DH, DH), DH)


def vmem(count):
    return [pl.BlockSpec(memory_space=pltpu.VMEM)] * count


def pack_kernel(frames, outputs, fq_ref, do_ref, fk_ref, fv_ref, t_ref, *refs):
    outs, (q_in, do_in, k_in, v_in, k2_in, v2_in, t_in, sems) = refs[:-8], refs[-8:]
    wanted = {what for parts in outputs for _, _, what in parts}
    me, half = lax.axis_index("tm"), lax.axis_index("rep")
    rows = fq_ref.shape[0]
    mine = pl.ds(pl.multiple_of(half * rows, rows), rows)
    rest = pl.ds(pl.multiple_of((1 - half) * rows, rows), rows)
    moves = [
        (fq_ref, q_in), (do_ref, do_in), (fk_ref.at[mine, :], k_in), (fv_ref.at[mine, :], v_in), (t_ref, t_in)
    ]
    if "other" in wanted:
        moves += [(fk_ref.at[rest, :], k2_in), (fv_ref.at[rest, :], v2_in)]
    copies = [pltpu.make_async_copy(a, b, sems.at[n]) for n, (a, b) in enumerate(moves)]
    for copy in copies:
        copy.start()
    for copy in copies:
        copy.wait()
    for out, parts in zip(outs, outputs):
        at = 0
        for table, m, what in parts:
            if what in ("t", "other t"):
                blocks = [t_in[mine if what == "t" else rest, :]]
            else:
                cols = column(lookup(table, me ^ m))
                sources = (q_in, do_in, k_in, v_in) if what == "mine" else (k2_in, v2_in)
                blocks = [ref[:, cols] for ref in sources]
            for block in blocks:
                out[:, at : at + block.shape[1]] = block
                at += block.shape[1]


def pack(frames, outputs, limit, fq, do, fk, fv, t):
    rows, width = fq.shape
    size = {"mine": 4 * DH, "other": 2 * DH, "t": t.shape[1], "other t": t.shape[1]}
    return pl.pallas_call(
        functools.partial(pack_kernel, frames, outputs),
        in_specs=[pl.BlockSpec(memory_space=pltpu.HBM)] * 5,
        out_specs=vmem(len(outputs)),
        out_shape=[
            jax.ShapeDtypeStruct((rows, sum(size[what] for _, _, what in parts)), BF16)
            for parts in outputs
        ],
        scratch_shapes=[pltpu.VMEM((rows, width), BF16)] * 6
        + [pltpu.VMEM(t.shape, BF16), pltpu.SemaphoreType.DMA((7,))],
        compiler_params=pltpu.CompilerParams(vmem_limit_bytes=limit * 1024 * 1024),
    )(fq, do, fk, fv, t)


def pick_kernel(spans, groups, *refs):
    n = 0
    for out, count in zip(refs[-len(groups) :], groups):
        for at in range(count):
            start, size = spans[n]
            out[:, at * size : (at + 1) * size] = refs[n][:, start : start + size]
            n += 1


def pick(parts, size, groups, after=()):
    arrays = [array for array, _ in parts]
    rows, dtype = arrays[0].shape[0], arrays[0].dtype
    return pl.pallas_call(
        functools.partial(pick_kernel, [(start, size) for _, start in parts], groups),
        in_specs=vmem(len(arrays)) + [pl.BlockSpec(memory_space=pl.ANY)] * len(after),
        out_specs=vmem(len(groups)),
        out_shape=[jax.ShapeDtypeStruct((rows, size * count), dtype) for count in groups],
        compiler_params=SMALL,
    )(*arrays, *after)


def one_head(frames, bands, q, do, frozen_k, frozen_v, tokens, aq, ak, av):
    flat = q.shape[0]
    rows = flat // frames
    t_same = tokens[:flat]

    def adapted(frozen, rows_of, adapter):
        return (frozen.astype(F32) + dot_nn(rows_of, adapter)).astype(BF16)

    query = adapted(q, t_same, aq)
    keys, values = adapted(frozen_k, tokens, ak), adapted(frozen_v, tokens, av)
    do_t, keys_t, values_t = do.T, keys.T, values.T

    def bias(i, b):
        j, need = (b, 0) if b < frames else (b - frames, 1)
        value = jnp.where(bands[i, j] > need, 0.0, -jnp.inf).astype(F32)
        return jnp.full((1, rows), value, F32)

    span = 2 if frames % 2 == 0 else 1
    wide = span * rows
    groups = [range(first, first + span) for first in range(0, frames, span)]
    seen = [
        list(range(frames))
        + [frames + j for j in range(frames) if any(abs(i - j) <= NEAR for i in mine)]
        for mine in groups
    ]
    here = [slice(mine[0] * rows, mine[0] * rows + wide) for mine in groups]
    pairs_of = range(len(groups))

    def gather(whole, g, axis):
        parts = [
            whole[b * rows : (b + 1) * rows] if axis == 0 else whole[:, b * rows : (b + 1) * rows]
            for b in seen[g]
        ]
        return jnp.concatenate(parts, axis=axis)

    def block(whole, n):
        return whole[n * rows : (n + 1) * rows]

    def softmax(g, raw):
        scores = [
            block(raw, n) * SCALE + jnp.concatenate([bias(i, b) for i in groups[g]], axis=1)
            for n, b in enumerate(seen[g])
        ]
        top = jnp.max(functools.reduce(jnp.maximum, scores), axis=0, keepdims=True)
        shifted = [jnp.exp(s - top) for s in scores]
        inverse = 1.0 / jnp.sum(functools.reduce(jnp.add, shifted), axis=0, keepdims=True)
        return [s * inverse for s in shifted]

    raws = [dot_nt(gather(keys, g, 0), query[here[g]]) for g in pairs_of]
    prob_grads = [dot_nt(gather(values, g, 0), do[here[g]]) for g in pairs_of]
    probs = [softmax(g, raws[g]) for g in pairs_of]
    lows = [jnp.concatenate([p.astype(BF16) for p in probs[g]], axis=0) for g in pairs_of]
    grads = []
    for g in pairs_of:
        attended = dot_nn(gather(values_t, g, 1), lows[g]).astype(BF16).astype(F32)
        delta = jnp.sum(do_t[:, here[g]].astype(F32) * attended, axis=0, keepdims=True)
        parts = [
            (probs[g][n] * (block(prob_grads[g], n) - delta)).astype(BF16) for n in range(len(seen[g]))
        ]
        grads.append(jnp.concatenate(parts, axis=0))
    dvs, dks = [None] * (2 * frames), [None] * (2 * frames)

    def add(sums, g, whole):
        for n, b in enumerate(seen[g]):
            sums[b] = block(whole, n) if sums[b] is None else sums[b] + block(whole, n)

    for g in pairs_of:
        add(dvs, g, dot_nn(lows[g], do[here[g]]))
    for g in pairs_of:
        add(dks, g, dot_nn(grads[g], query[here[g]]))
    dqs = [(dot_nn(gather(keys_t, g, 1), grads[g]) * SCALE).astype(BF16).T for g in pairs_of]
    dq = jnp.concatenate(dqs, axis=0)
    dk = (jnp.concatenate(dks, axis=0) * SCALE).astype(BF16)
    dv = jnp.concatenate(dvs, axis=0).astype(BF16)
    both = jnp.concatenate([dk, dv], axis=1)
    sums = dot_tn(tokens, both)
    grads = jnp.concatenate([dot_tn(t_same, dq), sums[:, :DH], sums[:, DH:]], axis=0)
    lows = dot_nt(both, jnp.concatenate([ak, av], axis=1))
    return grads, lows[:flat] + dot_nt(dq, aq), lows[flat:]


def group_kernel(heads, frames, chained, waits, sides, count, *refs):
    refs = list(refs)

    def take(count):
        taken = refs[:count]
        del refs[:count]
        return taken

    (bands,) = take(1)
    arrays, adapters = take(count), take(3)
    before = take(2) if chained else None
    take(waits)
    keep_ref, *give_refs = take(1 + GIVES if chained else 2)
    low_refs = [] if chained else take(2)
    q, do, k, v, tokens = refs
    me, half = lax.axis_index("tm"), lax.axis_index("rep")
    rows = arrays[0].shape[0]
    flat = frames * rows
    cut = 3 * tokens.shape[1] // 2
    first = half == 0
    same_at = [pl.ds(pl.multiple_of((me ^ m) * rows, rows), rows) for m in range(frames)]
    other_at = [pl.ds(pl.multiple_of(flat + (me ^ m) * rows, rows), rows) for m in range(frames)]

    def put(targets, places, rows_at):
        for m, (n, start) in enumerate(places):
            for c, target in enumerate(targets):
                target[rows_at[m], :] = arrays[n][:, start + c * DH : start + (c + 1) * DH]

    put([tokens], sides[0][0], same_at)
    put([tokens], sides[0][1], other_at)

    def run(n, table):
        put([q, do, k, v], sides[1 + n][0], same_at)
        put([k, v], sides[1 + n][1], other_at)
        cols = column(lookup(table, me))
        grads, low_same, low_other = one_head(
            frames, bands, q[...], do[...], k[...], v[...], tokens[...], *[a[:, cols] for a in adapters]
        )
        keep = jnp.where(first, grads[:cut], grads[cut:])
        give = jnp.where(first, grads[cut:], grads[:cut])
        return keep, give, low_same, low_other

    if chained:
        keep, give, low_same, low_other = run(0, heads[0][0])
        keep_ref[:cut, :] = keep
        keep_ref[cut:, :] = before[0][...] + low_same
        give = jnp.concatenate([give, before[1][...] + low_other], axis=0)
        size = give.shape[0] // GIVES
        for n, ref in enumerate(give_refs):
            ref[...] = give[n * size : (n + 1) * size].astype(ref.dtype)
        return
    for n, (table, counts) in enumerate(heads):
        here = slice(n * cut, (n + 1) * cut)

        def body():
            keep, give, low_same, low_other = run(n, table)
            keep_ref[here, :] = keep
            give_refs[0][here, :] = give.astype(BF16)
            if n == 0:
                low_refs[0][...] = low_same
                low_refs[1][...] = low_other
            else:
                low_refs[0][...] += low_same
                low_refs[1][...] += low_other

        if min(counts) > 0:
            body()
        else:
            live = lookup(counts, me) > 0
            pl.when(live)(body)

            @pl.when(jnp.logical_not(live))
            def _():
                keep_ref[here, :] = jnp.zeros((cut, DH), F32)
                give_refs[0][here, :] = jnp.zeros((cut, DH), BF16)


def head_group(heads, bands, sides, adapters, before=(), after=()):
    frames = len(sides[0][0])
    arrays, places = [], []
    for side in sides:
        found = []
        for pairs_of in side:
            found.append([])
            for array, start in pairs_of:
                known = [n for n, a in enumerate(arrays) if a is array]
                if not known:
                    arrays.append(array)
                found[-1].append((known[0] if known else len(arrays) - 1, start))
        places.append(found)
    rows, rank = arrays[0].shape[0], adapters[0].shape[0]
    flat = frames * rows
    size = len(heads) * 3 * rank // 2
    chained = len(before) > 0
    args = [bands, *arrays, *adapters, *before, *after]
    specs = [pl.BlockSpec(memory_space=pltpu.SMEM)] + vmem(len(arrays) + 3 + len(before))
    specs += [pl.BlockSpec(memory_space=pl.ANY)] * len(after)
    low = jax.ShapeDtypeStruct((flat, rank), F32)
    if chained:
        part = jax.ShapeDtypeStruct(((size + flat) // GIVES, rank), BF16)
        shapes = [jax.ShapeDtypeStruct((size + flat, rank), F32)] + [part] * GIVES
    else:
        edge = jax.ShapeDtypeStruct((size, rank), F32)
        shapes = [edge, jax.ShapeDtypeStruct((size, rank), BF16), low, low]
    return pl.pallas_call(
        functools.partial(
            group_kernel, heads, frames, chained, len(after), places, len(arrays)
        ),
        in_specs=specs,
        out_specs=vmem(len(shapes)),
        out_shape=shapes,
        scratch_shapes=[pltpu.VMEM((flat, DH), BF16)] * 2
        + [pltpu.VMEM((2 * flat, DH), BF16)] * 2
        + [pltpu.VMEM((2 * flat, rank), BF16)],
        compiler_params=pltpu.CompilerParams(vmem_limit_bytes=40 * 1024 * 1024),
    )(*args)


def stack_kernel(first, second, out):
    at = first.shape[0]
    out[:at, :] = first[...]
    out[at:, :] = second[: out.shape[0] - at, :]


def stack(first, second, rows):
    return pl.pallas_call(
        stack_kernel,
        in_specs=vmem(2),
        out_specs=pl.BlockSpec(memory_space=pltpu.VMEM),
        out_shape=jax.ShapeDtypeStruct((rows, first.shape[1]), first.dtype),
        compiler_params=SMALL,
    )(first, second)


def hand_out_kernel(frames, size, parts, keep_ref, *refs):
    gots, (own_ref, *sends, total) = refs[:parts], refs[-frames - 1 :]
    me = lax.axis_index("tm")
    rows = own_ref.shape[0]
    total[...] = keep_ref[...] + jnp.concatenate([got[...].astype(F32) for got in gots], axis=0)
    for m in range(frames):
        low = total[pl.ds(pl.multiple_of(size + (me ^ m) * rows, 8), rows), :]
        if m == 0:
            own_ref[...] = low
        else:
            sends[m - 1][:rows, :] = low.astype(BF16)
            sends[m - 1][rows:, :] = total[:size, :].astype(BF16)


def hand_out(frames, rows, keep, gots, after):
    size, rank = keep.shape[0] - frames * rows, keep.shape[1]
    own, *sends = pl.pallas_call(
        functools.partial(hand_out_kernel, frames, size, len(gots)),
        in_specs=vmem(1 + len(gots)) + [pl.BlockSpec(memory_space=pl.ANY)] * len(after),
        out_specs=vmem(frames),
        out_shape=[jax.ShapeDtypeStruct((rows, rank), F32)]
        + [jax.ShapeDtypeStruct((rows + size, rank), BF16)] * (frames - 1),
        scratch_shapes=[pltpu.VMEM(keep.shape, F32)],
        compiler_params=SMALL,
    )(keep, *gots, *after)
    return own, sends


def collect_kernel(wide, own_low, own, near, third, last, piece, pair, facing, passed, *outs):
    out_ref, low_ref = outs
    rows, size = own_low.shape[0], piece.shape[0] // 2
    low = own_low[...]
    for got in (near, third, last):
        low = low + got[:rows, :].astype(F32)
    out_ref[:rows, :] = low.astype(BF16)
    low_ref[...] = low.astype(BF16)
    middle = lookup(wide, lax.axis_index("tm")) > 0
    far = [jnp.where(middle, facing[part, :], passed[part, :]) for part in (slice(n * size, (n + 1) * size) for n in range(3))]
    blocks = [ref[rows:, :] for ref in (own, near, third, last)]
    blocks += [piece[:size, :], pair[:size, :], far[0], far[2]]
    blocks += [jnp.where(middle, piece[size:, :], pair[size:, :]), far[1]]
    for n, block in enumerate(blocks):
        out_ref[rows + n * size : rows + (n + 1) * size, :] = block


def collect(wide, own_low, own, gots, *pieces):
    (rows, rank), size = own_low.shape, pieces[0].shape[0] // 2
    return pl.pallas_call(
        functools.partial(collect_kernel, wide),
        in_specs=vmem(2 + len(gots) + len(pieces)),
        out_specs=vmem(2),
        out_shape=[
            jax.ShapeDtypeStruct((rows + 10 * size, rank), BF16),
            jax.ShapeDtypeStruct((rows, rank), BF16),
        ],
        compiler_params=SMALL,
    )(own_low, own, *gots, *pieces)


def place_kernel(frames, lead, late, rest, tail, tail2, low_head, low_diag, *outs):
    me, half = lax.axis_index("tm"), lax.axis_index("rep")
    first = half == 0
    rank = outs[0].shape[0]
    cut = 3 * rank // 2
    rows = low_head.shape[0]
    same = tail[:rows, :].astype(F32) + low_head[...].astype(F32)
    other = tail2[:rows, :].astype(F32) + low_diag[...].astype(F32)
    outs[3][:rows, :] = jnp.where(first, same, other)
    outs[3][rows:, :] = jnp.where(first, other, same)
    side = me // 2
    facing = 2 - side
    places = [lookup(late, me ^ m) for m in range(frames)]
    places += [lookup(lead, chip) for chip in (me, me ^ 1, facing, facing ^ 1)]
    places += [lookup(rest, 1 + side), lookup(rest, facing)]
    for n, head in enumerate(places):
        here = slice(rows + n * cut, rows + (n + 1) * cut)
        a, b = tail[here, :].astype(F32), tail2[here, :].astype(F32)
        both = jnp.concatenate([jnp.where(first, a, b), jnp.where(first, b, a)], axis=0)
        for o in range(3):
            outs[o][:, column(head)] = both[o * rank : (o + 1) * rank]


def place(frames, lead, late, rest, tail, tail2, low_head, low_diag, rank, width):
    rows = low_head.shape[0]
    return pl.pallas_call(
        functools.partial(place_kernel, frames, lead, late, rest),
        in_specs=vmem(4),
        out_specs=vmem(4),
        out_shape=[jax.ShapeDtypeStruct((rank, width), F32)] * 3
        + [jax.ShapeDtypeStruct((2 * rows, rank), F32)],
        compiler_params=SMALL,
    )(tail, tail2, low_head, low_diag)


def exchange_plan(
    frozen_query,
    frozen_key,
    frozen_value,
    token_adapter_input,
    query_adapter_out,
    key_adapter_out,
    value_adapter_out,
    out_grad,
    band_width,
):
    rows, width = frozen_query.shape
    rank = token_adapter_input.shape[1]
    frames = band_width.shape[0]
    heads = width // DH
    starts, counts = head_table(heads, frames)
    most = max(counts)
    columns = [[min(starts[j] + s, heads - 1) for j in range(frames)] for s in range(most)]
    numbers = [[int(s < counts[j]) for j in range(frames)] for s in range(most)]
    slots = list(zip(columns, numbers))
    lead, late, rest = slots[0], slots[1], slots[2]
    wide = [j for j in range(frames) if counts[j] == most]
    adapters = [query_adapter_out, key_adapter_out, value_adapter_out]
    arrays = (frozen_query, out_grad, frozen_key, frozen_value, token_adapter_input)

    def meet(name, block, m, targets=range(frames)):
        with jax.named_scope(f"{name}_over_tm"):
            return lax.ppermute(block, "tm", [(j ^ m, j) for j in targets])

    def swap_in_chip(name, block):
        with jax.named_scope(f"{name}_in_chip"):
            return swap(block, "rep")

    def mine(slot, m):
        return (slot[0], m, "mine")

    sent, kept, sent_late = [], [], []
    for m in range(1, frames):
        first = [mine(lead, m), (None, m, "t")]
        if m == 1:
            sent.append(first + [mine(rest, m), mine(late, m)])
        else:
            sent += [first, [mine(rest, m)]]
            sent_late.append([mine(late, m)])
    for slot in (lead, rest, late):
        kept += [[mine(slot, 0)], [(slot[0], 0, "other")]]
    kept += [[(None, 0, "t")], [(None, 0, "other t")]]
    packed = pack(frames, sent, 56, *arrays)
    packed_late = pack(frames, sent_late + kept, 16, *arrays)
    kept = packed_late[len(sent_late) :]
    block = meet("nearest", packed[0], 1)
    lead_got, rest_got, late_got = [(block, 0)], [(block, 4 * DH + rank)], [(block, 8 * DH + rank)]
    for m in range(2, frames):
        lead_got.append((meet("lead", packed[2 * m - 3], m), 0))
        rest_got.append((meet("rest", packed[2 * m - 2], m, wide), 0))
        late_got.append((meet("late", packed_late[m - 2], m), 0))

    def sides(name, n, got, wide_t, groups, skip, after=()):
        size = 4 * DH - skip + (rank if wide_t else 0)
        picked = pick([(a, start + skip) for a, start in got], size, groups, after)
        cross = [swap_in_chip(name, block) for block in picked]
        where = 2 * DH - skip
        cross = [(block, at * size + where) for block, count in zip(cross, groups) for at in range(count)]
        rows_here = [(kept[2 * n], 0)] + got
        rows_there = [(kept[2 * n + 1], 0)] + cross
        return rows_here, rows_there, cross

    *lead_side, cross = sides("lead", 0, lead_got, True, (3,), 2 * DH, kept[:1])
    t_side = (
        [(kept[6], 0)] + [(a, start + 4 * DH) for a, start in lead_got],
        [(kept[7], 0)] + [(block, start + 2 * DH) for block, start in cross],
    )
    *rest_side, _ = sides("rest", 1, rest_got, False, (3,), 2 * DH)
    early = [lead, rest]
    keep, give, *low = head_group(early, band_width, [t_side, lead_side, rest_side], adapters)
    cut = 3 * rank // 2

    def hand_on(name, block, targets):
        with jax.named_scope(f"{name}_over_tm"):
            return lax.ppermute(block, "tm", targets)

    inner, outer = [(1, 2), (2, 1)], [(1, 0), (2, 3)]
    got = swap_in_chip("early_gradients", give)
    piece = (keep + got.astype(F32)).astype(BF16)
    pair = meet("early_gradients", piece, 1)
    *late_side, _ = sides("late", 2, late_got, False, (3,), 0, [got])
    facing = hand_on("early_pairs", stack(piece, pair, 3 * cut), inner)
    passed = hand_on("early_passed", facing, outer)
    keep, *gives = head_group([late], band_width, [t_side, late_side], adapters, low, [])
    gives = [swap_in_chip("late_sums", g) for g in gives]
    own_low, sends = hand_out(frames, rows, keep, gives, [])
    gots = [meet("late_sums", block, m) for m, block in enumerate(sends, 1)]
    tail, low = collect(
        rest[1], own_low, sends[0], gots, piece, pair, facing, passed
    )
    diag = [(0, 3), (1, 2), (2, 1), (3, 0)]
    with jax.named_scope("low_over_head"):
        low_head, low_diag = swap(low, "head"), lax.ppermute(low, ("head", "rep"), diag)
    outs = place(
        frames, lead[0], late[0], rest[0], tail, swap_in_chip("tail", tail), low_head, low_diag, rank, width
    )
    return tuple(outs)


def on_device(frozen_query, *rest):
    frames = rest[-1].shape[0]
    heads = frozen_query.shape[1] // DH
    whole_reach = frames == 4 and heads == 2 * frames + 2
    return (exchange_plan if whole_reach else window_plan)(frozen_query, *rest)


def solution(mesh):
    in_specs = (
        P(("groups", "tm", "rep"), "head"),
        P(("groups", "tm"), "head"),
        P(("groups", "tm"), "head"),
        P(("groups", "tm"), None),
        P(None, "head"),
        P(None, "head"),
        P(None, "head"),
        P(("groups", "tm", "rep"), "head"),
        P(),
    )
    out_specs = (
        P("groups", "head"),
        P("groups", "head"),
        P("groups", "head"),
        P(("groups", "tm"), None),
    )
    return jax.shard_map(
        on_device, mesh=mesh, in_specs=in_specs, out_specs=out_specs, check_vma=False
    )
```

```python
import functools

import jax
import jax.numpy as jnp
from jax import lax
from jax.experimental import pallas as pl
from jax.experimental.pallas import tpu as pltpu
from jax.sharding import PartitionSpec as P

DH = 128
NEAR = 1
REACH = 4
SCALE = DH ** (-0.5)
F32 = jnp.float32
BF16 = jnp.bfloat16
GIVES = 2
SMALL = pltpu.CompilerParams(vmem_limit_bytes=16 * 1024 * 1024)


def dot_nn(left, right):
    return lax.dot_general(left, right, (((1,), (0,)), ((), ())), preferred_element_type=F32)


def dot_nt(left, right):
    return lax.dot_general(left, right, (((1,), (1,)), ((), ())), preferred_element_type=F32)


def dot_tn(left, right):
    return lax.dot_general(left, right, (((0,), (0,)), ((), ())), preferred_element_type=F32)


def routes(count):
    found = []
    for d in range(1, min(REACH, count - 1) + 1):
        if 2 * d >= count:
            found.append((d, (-d, d)))
        else:
            found.append((d, (-d,)))
            found.append((d, (d,)))
    return found


def pairs(count, offsets):
    return [(i + o, i) for o in offsets for i in range(count) if 0 <= i + o < count]


def swap(block, axis):
    return lax.ppermute(block, axis, [(0, 1), (1, 0)])


def attention_kernel(
    blocks, bias_ref, fq_ref, do_ref, fk_ref, fv_ref, t_ref, tr_ref, tt_ref, aq_ref, ak_ref, av_ref, *refs
):
    k_refs = refs[:blocks]
    v_refs = refs[blocks : 2 * blocks]
    gq_ref, gk_ref, gv_ref, lowq_ref, low_ref = refs[2 * blocks :]
    rows = fq_ref.shape[0]

    @pl.when(pl.program_id(0) == 0)
    def _():
        lowq_ref[...] = jnp.zeros_like(lowq_ref)
        low_ref[...] = jnp.zeros_like(low_ref)

    aq, ak, av = aq_ref[...], ak_ref[...], av_ref[...]
    query = (fq_ref[...].astype(F32) + dot_nn(tr_ref[...], aq)).astype(BF16)
    do = do_ref[...]
    own_k = (fk_ref[...].astype(F32) + dot_nn(t_ref[...], ak)).astype(BF16)
    own_v = (fv_ref[...].astype(F32) + dot_nn(t_ref[...], av)).astype(BF16)
    keys = [own_k[:rows], own_k[rows:]] + [ref[...] for ref in k_refs]
    values = [own_v[:rows], own_v[rows:]] + [ref[...] for ref in v_refs]
    count = len(keys)
    scores = [dot_nt(keys[b], query) * SCALE + bias_ref[b] for b in range(count)]
    top = functools.reduce(jnp.maximum, scores)
    top = jnp.max(top, axis=0, keepdims=True)
    shifted = [jnp.exp(s - top) for s in scores]
    total = jnp.sum(functools.reduce(jnp.add, shifted), axis=0, keepdims=True)
    inverse = 1.0 / total
    probs = [s * inverse for s in shifted]
    lows = [p.astype(BF16) for p in probs]
    attended = functools.reduce(jnp.add, [dot_tn(lows[b], values[b]) for b in range(count)])
    attended = attended.astype(BF16).astype(F32)
    delta = jnp.sum((do.astype(F32) * attended).T, axis=0, keepdims=True)
    grads = [
        (probs[b] * (dot_nt(values[b], do) - delta)).astype(BF16) for b in range(count)
    ]
    dq = functools.reduce(jnp.add, [dot_tn(grads[b], keys[b]) for b in range(count)])
    dq = (dq * SCALE).astype(BF16)
    gq_ref[...] = dot_tn(tr_ref[...], dq)
    lowq_ref[...] += dot_nt(dq, aq)
    both = jnp.concatenate([ak, av], axis=1)
    for b in range(count):
        dk = (dot_nn(grads[b], query) * SCALE).astype(BF16)
        dv = dot_nn(lows[b], do).astype(BF16)
        part = jnp.concatenate([dk, dv], axis=1)
        low_ref[b * rows : (b + 1) * rows, :] += dot_nt(part, both)
        out = dot_nn(tt_ref[:, b * rows : (b + 1) * rows], part)
        if b == 0:
            total_part = out
        else:
            total_part += out
    gk_ref[...] = total_part[:, :DH]
    gv_ref[...] = total_part[:, DH:]


def attention(bias, fq, do, fk, fv, t, tr, tt, aq, ak, av, payloads):
    rows, width = fq.shape
    heads = width // DH
    rank = t.shape[1]
    blocks = len(payloads)
    count = blocks + 2

    def col(r):
        return pl.BlockSpec((r, DH), lambda h: (0, h))

    def whole(shape):
        return pl.BlockSpec(shape, lambda h: (0, 0))

    return pl.pallas_call(
        functools.partial(attention_kernel, blocks),
        grid=(heads,),
        out_shape=[
            jax.ShapeDtypeStruct((rank, width), F32),
            jax.ShapeDtypeStruct((rank, width), F32),
            jax.ShapeDtypeStruct((rank, width), F32),
            jax.ShapeDtypeStruct((rows, rank), F32),
            jax.ShapeDtypeStruct((count * rows, rank), F32),
        ],
        in_specs=[pl.BlockSpec(memory_space=pltpu.SMEM)]
        + [col(rows), col(rows), col(2 * rows), col(2 * rows)]
        + [whole(t.shape), whole(tr.shape), whole(tt.shape)]
        + [col(rank)] * 3
        + [col(rows)] * blocks
        + [pl.BlockSpec((rows, DH), lambda h: (0, heads + h))] * blocks,
        out_specs=[col(rank)] * 3 + [whole((rows, rank)), whole((count * rows, rank))],
        compiler_params=pltpu.CompilerParams(vmem_limit_bytes=32 * 1024 * 1024),
    )(bias, fq, do, fk, fv, t, tr, tt, aq, ak, av, *payloads, *payloads)


def sum_rows(part, frame_idx, half_idx, frames):
    rows, width = part.shape
    half = width // 2
    keep = lax.dynamic_slice_in_dim(part, half_idx * half, half, 1)
    give = lax.dynamic_slice_in_dim(part, (1 - half_idx) * half, half, 1)
    mine = keep + swap(give, "rep")
    if frames & (frames - 1) or rows % frames or frames > REACH + 1:
        total = lax.psum(mine, "tm").astype(BF16)
    else:
        chunk = rows // frames
        low = mine.astype(BF16)
        acc = lax.dynamic_slice_in_dim(mine, frame_idx * chunk, chunk, 0)
        for m in range(1, frames):
            give = lax.dynamic_slice_in_dim(low, (frame_idx ^ m) * chunk, chunk, 0)
            acc = acc + lax.ppermute(give, "tm", [(i, i ^ m) for i in range(frames)]).astype(F32)
        acc = acc.astype(BF16)
        total = jnp.zeros((rows, half), BF16)
        total = lax.dynamic_update_slice_in_dim(total, acc, frame_idx * chunk, 0)
        for m in range(1, frames):
            got = lax.ppermute(acc, "tm", [(i, i ^ m) for i in range(frames)])
            total = lax.dynamic_update_slice_in_dim(total, got, (frame_idx ^ m) * chunk, 0)
    other = swap(total, "rep")
    first = jnp.where(half_idx == 0, total, other)
    second = jnp.where(half_idx == 0, other, total)
    return jnp.concatenate([first, second], axis=1).astype(F32)


def window_plan(
    frozen_query,
    frozen_key,
    frozen_value,
    token_adapter_input,
    query_adapter_out,
    key_adapter_out,
    value_adapter_out,
    out_grad,
    band_width,
):
    rows, width = frozen_query.shape
    rank = token_adapter_input.shape[1]
    frames = band_width.shape[0]
    frame_idx = lax.axis_index("tm")
    half_idx = lax.axis_index("rep")
    t = token_adapter_input
    tr = lax.dynamic_slice_in_dim(t, half_idx * rows, rows, 0)

    def tile_rows_of(frozen, adapter):
        own = lax.dynamic_slice_in_dim(frozen, half_idx * rows, rows, 0)
        return (own.astype(F32) + dot_nn(tr, adapter)).astype(BF16)

    payload = jnp.concatenate(
        [tile_rows_of(frozen_key, key_adapter_out), tile_rows_of(frozen_value, value_adapter_out), tr],
        axis=1,
    )

    frame_ids = jnp.arange(frames)
    band_row = jnp.sum(jnp.where((frame_ids == frame_idx)[:, None], band_width, 0), axis=0)

    def band_at(offsets):
        seen = functools.reduce(jnp.logical_or, [frame_ids == frame_idx + o for o in offsets])
        return jnp.sum(jnp.where(seen, band_row, 0))

    own_band = band_at((0,))
    allowed = [jnp.abs(half_idx - tile) < own_band for tile in range(2)]
    payloads = []
    plan = routes(frames)
    for d, offsets in plan:
        got = lax.ppermute(payload, "tm", pairs(frames, offsets))
        band = band_at(offsets)
        payloads.append(got)
        allowed.append(band > 0)
        if d <= NEAR:
            payloads.append(swap(got, "rep"))
            allowed.append(band > 1)
    bias = jnp.where(jnp.stack(allowed), 0.0, -jnp.inf).astype(F32)
    tt = jnp.concatenate([t] + [p[:, 2 * width :] for p in payloads], axis=0).T

    gq, gk, gv, low_q, low_b = attention(
        bias, frozen_query, out_grad, frozen_key, frozen_value, t, tr, tt,
        query_adapter_out, key_adapter_out, value_adapter_out, payloads,
    )

    own = low_b[: 2 * rows]
    same = lax.dynamic_slice_in_dim(own, half_idx * rows, rows, 0) + low_q
    other = lax.dynamic_slice_in_dim(own, (1 - half_idx) * rows, rows, 0)
    start = 2 * rows
    for d, offsets in plan:
        size = 2 * rows if d <= NEAR else rows
        back = [(target, source) for source, target in pairs(frames, offsets)]
        got = lax.ppermute(low_b[start : start + size], "tm", back)
        start += size
        same = same + got[:rows]
        if d <= NEAR:
            other = other + got[rows:]
    low = jnp.where(
        half_idx == 0,
        jnp.concatenate([same, other], axis=0),
        jnp.concatenate([other, same], axis=0),
    )
    low = low + swap(low, "rep")
    low = low + swap(low, "head")

    grads = sum_rows(jnp.concatenate([gq, gk, gv], axis=0), frame_idx, half_idx, frames)
    return grads[:rank], grads[rank : 2 * rank], grads[2 * rank :], low


def head_table(heads, frames):
    base, extra = divmod(heads, frames)
    lead = (frames - extra) // 2
    counts = [base + (1 if lead <= j < lead + extra else 0) for j in range(frames)]
    return [sum(counts[:j]) for j in range(frames)], counts


def lookup(table, index):
    value = jnp.int32(table[0])
    for j in range(1, len(table)):
        value = jnp.where(index == j, jnp.int32(table[j]), value)
    return value


def column(head):
    return pl.ds(pl.multiple_of(head * DH, DH), DH)


def vmem(count):
    return [pl.BlockSpec(memory_space=pltpu.VMEM)] * count


def pack_kernel(frames, outputs, fq_ref, do_ref, fk_ref, fv_ref, t_ref, *refs):
    outs, (q_in, do_in, k_in, v_in, k2_in, v2_in, t_in, sems) = refs[:-8], refs[-8:]
    wanted = {what for parts in outputs for _, _, what in parts}
    me, half = lax.axis_index("tm"), lax.axis_index("rep")
    rows = fq_ref.shape[0]
    mine = pl.ds(pl.multiple_of(half * rows, rows), rows)
    rest = pl.ds(pl.multiple_of((1 - half) * rows, rows), rows)
    moves = [
        (fq_ref, q_in), (do_ref, do_in), (fk_ref.at[mine, :], k_in), (fv_ref.at[mine, :], v_in), (t_ref, t_in)
    ]
    if "other" in wanted:
        moves += [(fk_ref.at[rest, :], k2_in), (fv_ref.at[rest, :], v2_in)]
    copies = [pltpu.make_async_copy(a, b, sems.at[n]) for n, (a, b) in enumerate(moves)]
    for copy in copies:
        copy.start()
    for copy in copies:
        copy.wait()
    for out, parts in zip(outs, outputs):
        at = 0
        for table, m, what in parts:
            if what in ("t", "other t"):
                blocks = [t_in[mine if what == "t" else rest, :]]
            else:
                cols = column(lookup(table, me ^ m))
                sources = (q_in, do_in, k_in, v_in) if what == "mine" else (k2_in, v2_in)
                blocks = [ref[:, cols] for ref in sources]
            for block in blocks:
                out[:, at : at + block.shape[1]] = block
                at += block.shape[1]


def pack(frames, outputs, limit, fq, do, fk, fv, t):
    rows, width = fq.shape
    size = {"mine": 4 * DH, "other": 2 * DH, "t": t.shape[1], "other t": t.shape[1]}
    return pl.pallas_call(
        functools.partial(pack_kernel, frames, outputs),
        in_specs=[pl.BlockSpec(memory_space=pltpu.HBM)] * 5,
        out_specs=vmem(len(outputs)),
        out_shape=[
            jax.ShapeDtypeStruct((rows, sum(size[what] for _, _, what in parts)), BF16)
            for parts in outputs
        ],
        scratch_shapes=[pltpu.VMEM((rows, width), BF16)] * 6
        + [pltpu.VMEM(t.shape, BF16), pltpu.SemaphoreType.DMA((7,))],
        compiler_params=pltpu.CompilerParams(vmem_limit_bytes=limit * 1024 * 1024),
    )(fq, do, fk, fv, t)


def pick_kernel(spans, groups, *refs):
    n = 0
    for out, count in zip(refs[-len(groups) :], groups):
        for at in range(count):
            start, size = spans[n]
            out[:, at * size : (at + 1) * size] = refs[n][:, start : start + size]
            n += 1


def pick(parts, size, groups, after=()):
    arrays = [array for array, _ in parts]
    rows, dtype = arrays[0].shape[0], arrays[0].dtype
    return pl.pallas_call(
        functools.partial(pick_kernel, [(start, size) for _, start in parts], groups),
        in_specs=vmem(len(arrays)) + [pl.BlockSpec(memory_space=pl.ANY)] * len(after),
        out_specs=vmem(len(groups)),
        out_shape=[jax.ShapeDtypeStruct((rows, size * count), dtype) for count in groups],
        compiler_params=SMALL,
    )(*arrays, *after)


def one_head(frames, bands, q, do, frozen_k, frozen_v, tokens, aq, ak, av):
    flat = q.shape[0]
    rows = flat // frames
    t_same = tokens[:flat]

    def adapted(frozen, rows_of, adapter):
        return (frozen.astype(F32) + dot_nn(rows_of, adapter)).astype(BF16)

    query = adapted(q, t_same, aq)
    keys, values = adapted(frozen_k, tokens, ak), adapted(frozen_v, tokens, av)
    do_t, keys_t, values_t = do.T, keys.T, values.T

    def bias(i, b):
        j, need = (b, 0) if b < frames else (b - frames, 1)
        value = jnp.where(bands[i, j] > need, 0.0, -jnp.inf).astype(F32)
        return jnp.full((1, rows), value, F32)

    span = 2 if frames % 2 == 0 else 1
    wide = span * rows
    groups = [range(first, first + span) for first in range(0, frames, span)]
    seen = [
        list(range(frames))
        + [frames + j for j in range(frames) if any(abs(i - j) <= NEAR for i in mine)]
        for mine in groups
    ]
    here = [slice(mine[0] * rows, mine[0] * rows + wide) for mine in groups]
    pairs_of = range(len(groups))

    def gather(whole, g, axis):
        parts = [
            whole[b * rows : (b + 1) * rows] if axis == 0 else whole[:, b * rows : (b + 1) * rows]
            for b in seen[g]
        ]
        return jnp.concatenate(parts, axis=axis)

    def block(whole, n):
        return whole[n * rows : (n + 1) * rows]

    def softmax(g, raw):
        scores = [
            block(raw, n) * SCALE + jnp.concatenate([bias(i, b) for i in groups[g]], axis=1)
            for n, b in enumerate(seen[g])
        ]
        top = jnp.max(functools.reduce(jnp.maximum, scores), axis=0, keepdims=True)
        shifted = [jnp.exp(s - top) for s in scores]
        inverse = 1.0 / jnp.sum(functools.reduce(jnp.add, shifted), axis=0, keepdims=True)
        return [s * inverse for s in shifted]

    raws = [dot_nt(gather(keys, g, 0), query[here[g]]) for g in pairs_of]
    prob_grads = [dot_nt(gather(values, g, 0), do[here[g]]) for g in pairs_of]
    probs = [softmax(g, raws[g]) for g in pairs_of]
    lows = [jnp.concatenate([p.astype(BF16) for p in probs[g]], axis=0) for g in pairs_of]
    grads = []
    for g in pairs_of:
        attended = dot_nn(gather(values_t, g, 1), lows[g]).astype(BF16).astype(F32)
        delta = jnp.sum(do_t[:, here[g]].astype(F32) * attended, axis=0, keepdims=True)
        parts = [
            (probs[g][n] * (block(prob_grads[g], n) - delta)).astype(BF16) for n in range(len(seen[g]))
        ]
        grads.append(jnp.concatenate(parts, axis=0))
    dvs, dks = [None] * (2 * frames), [None] * (2 * frames)

    def add(sums, g, whole):
        for n, b in enumerate(seen[g]):
            sums[b] = block(whole, n) if sums[b] is None else sums[b] + block(whole, n)

    for g in pairs_of:
        add(dvs, g, dot_nn(lows[g], do[here[g]]))
    for g in pairs_of:
        add(dks, g, dot_nn(grads[g], query[here[g]]))
    dqs = [(dot_nn(gather(keys_t, g, 1), grads[g]) * SCALE).astype(BF16).T for g in pairs_of]
    dq = jnp.concatenate(dqs, axis=0)
    dk = (jnp.concatenate(dks, axis=0) * SCALE).astype(BF16)
    dv = jnp.concatenate(dvs, axis=0).astype(BF16)
    both = jnp.concatenate([dk, dv], axis=1)
    sums = dot_tn(tokens, both)
    grads = jnp.concatenate([dot_tn(t_same, dq), sums[:, :DH], sums[:, DH:]], axis=0)
    lows = dot_nt(both, jnp.concatenate([ak, av], axis=1))
    return grads, lows[:flat] + dot_nt(dq, aq), lows[flat:]


def group_kernel(heads, frames, chained, waits, sides, count, *refs):
    refs = list(refs)

    def take(count):
        taken = refs[:count]
        del refs[:count]
        return taken

    (bands,) = take(1)
    arrays, adapters = take(count), take(3)
    before = take(2) if chained else None
    take(waits)
    keep_ref, *give_refs = take(1 + GIVES if chained else 2)
    low_refs = [] if chained else take(2)
    q, do, k, v, tokens = refs
    me, half = lax.axis_index("tm"), lax.axis_index("rep")
    rows = arrays[0].shape[0]
    flat = frames * rows
    cut = 3 * tokens.shape[1] // 2
    first = half == 0
    same_at = [pl.ds(pl.multiple_of((me ^ m) * rows, rows), rows) for m in range(frames)]
    other_at = [pl.ds(pl.multiple_of(flat + (me ^ m) * rows, rows), rows) for m in range(frames)]

    def put(targets, places, rows_at):
        for m, (n, start) in enumerate(places):
            for c, target in enumerate(targets):
                target[rows_at[m], :] = arrays[n][:, start + c * DH : start + (c + 1) * DH]

    put([tokens], sides[0][0], same_at)
    put([tokens], sides[0][1], other_at)

    def run(n, table):
        put([q, do, k, v], sides[1 + n][0], same_at)
        put([k, v], sides[1 + n][1], other_at)
        cols = column(lookup(table, me))
        grads, low_same, low_other = one_head(
            frames, bands, q[...], do[...], k[...], v[...], tokens[...], *[a[:, cols] for a in adapters]
        )
        keep = jnp.where(first, grads[:cut], grads[cut:])
        give = jnp.where(first, grads[cut:], grads[:cut])
        return keep, give, low_same, low_other

    if chained:
        keep, give, low_same, low_other = run(0, heads[0][0])
        keep_ref[:cut, :] = keep
        keep_ref[cut:, :] = before[0][...] + low_same
        give = jnp.concatenate([give, before[1][...] + low_other], axis=0)
        size = give.shape[0] // GIVES
        for n, ref in enumerate(give_refs):
            ref[...] = give[n * size : (n + 1) * size].astype(ref.dtype)
        return
    for n, (table, counts) in enumerate(heads):
        here = slice(n * cut, (n + 1) * cut)

        def body():
            keep, give, low_same, low_other = run(n, table)
            keep_ref[here, :] = keep
            give_refs[0][here, :] = give.astype(BF16)
            if n == 0:
                low_refs[0][...] = low_same
                low_refs[1][...] = low_other
            else:
                low_refs[0][...] += low_same
                low_refs[1][...] += low_other

        if min(counts) > 0:
            body()
        else:
            live = lookup(counts, me) > 0
            pl.when(live)(body)

            @pl.when(jnp.logical_not(live))
            def _():
                keep_ref[here, :] = jnp.zeros((cut, DH), F32)
                give_refs[0][here, :] = jnp.zeros((cut, DH), BF16)


def head_group(heads, bands, sides, adapters, before=(), after=()):
    frames = len(sides[0][0])
    arrays, places = [], []
    for side in sides:
        found = []
        for pairs_of in side:
            found.append([])
            for array, start in pairs_of:
                known = [n for n, a in enumerate(arrays) if a is array]
                if not known:
                    arrays.append(array)
                found[-1].append((known[0] if known else len(arrays) - 1, start))
        places.append(found)
    rows, rank = arrays[0].shape[0], adapters[0].shape[0]
    flat = frames * rows
    size = len(heads) * 3 * rank // 2
    chained = len(before) > 0
    args = [bands, *arrays, *adapters, *before, *after]
    specs = [pl.BlockSpec(memory_space=pltpu.SMEM)] + vmem(len(arrays) + 3 + len(before))
    specs += [pl.BlockSpec(memory_space=pl.ANY)] * len(after)
    low = jax.ShapeDtypeStruct((flat, rank), F32)
    if chained:
        part = jax.ShapeDtypeStruct(((size + flat) // GIVES, rank), BF16)
        shapes = [jax.ShapeDtypeStruct((size + flat, rank), F32)] + [part] * GIVES
    else:
        edge = jax.ShapeDtypeStruct((size, rank), F32)
        shapes = [edge, jax.ShapeDtypeStruct((size, rank), BF16), low, low]
    return pl.pallas_call(
        functools.partial(
            group_kernel, heads, frames, chained, len(after), places, len(arrays)
        ),
        in_specs=specs,
        out_specs=vmem(len(shapes)),
        out_shape=shapes,
        scratch_shapes=[pltpu.VMEM((flat, DH), BF16)] * 2
        + [pltpu.VMEM((2 * flat, DH), BF16)] * 2
        + [pltpu.VMEM((2 * flat, rank), BF16)],
        compiler_params=pltpu.CompilerParams(vmem_limit_bytes=40 * 1024 * 1024),
    )(*args)


def hand_out_kernel(frames, size, parts, keep_ref, *refs):
    gots, (piece, facing) = refs[:parts], refs[parts : parts + 2]
    own_low, own_late, near, last, low_third, third, total = refs[-7:]
    me = lax.axis_index("tm")
    rows = own_low.shape[0]
    total[...] = keep_ref[...] + jnp.concatenate([got[...].astype(F32) for got in gots], axis=0)

    def low(m):
        return total[pl.ds(pl.multiple_of(size + (me ^ m) * rows, 8), rows), :]

    late = total[:size, :].astype(BF16)
    own_low[...] = low(0)
    own_late[...] = late
    near[:rows, :] = low(1).astype(BF16)
    near[rows : rows + size, :] = late
    near[rows + size :, :] = facing[size:, :]
    low_third[...] = low(2).astype(BF16)
    last[:rows, :] = low(3).astype(BF16)
    last[rows:, :] = late
    third[:size, :] = late
    third[size:, :] = piece[:size, :]


def hand_out(frames, rows, keep, gots, piece, facing, after):
    size, rank = keep.shape[0] - frames * rows, keep.shape[1]
    sizes = (size, rows + 2 * size, rows + size, rows, 2 * size)
    return pl.pallas_call(
        functools.partial(hand_out_kernel, frames, size, len(gots)),
        in_specs=vmem(3 + len(gots)) + [pl.BlockSpec(memory_space=pl.ANY)] * len(after),
        out_specs=vmem(1 + len(sizes)),
        out_shape=[jax.ShapeDtypeStruct((rows, rank), F32)]
        + [jax.ShapeDtypeStruct((n, rank), BF16) for n in sizes],
        scratch_shapes=[pltpu.VMEM(keep.shape, F32)],
        compiler_params=SMALL,
    )(keep, *gots, piece, facing, *after)


def sum_low_kernel(own, near, third, last, out):
    rows = own.shape[0]
    out[...] = own[...] + near[:rows, :].astype(F32) + third[...].astype(F32) + last[:rows, :].astype(F32)


def sum_low(own, near, third, last):
    return pl.pallas_call(
        sum_low_kernel,
        in_specs=vmem(4),
        out_specs=pl.BlockSpec(memory_space=pltpu.VMEM),
        out_shape=jax.ShapeDtypeStruct(own.shape, F32),
        compiler_params=SMALL,
    )(own, near, third, last)


def collect_kernel(wide, low_ref, low_head, own, near, third, last, piece, pair, facing, out_ref):
    rows, size = low_ref.shape[0], own.shape[0]
    out_ref[:rows, :] = (low_ref[...] + low_head[...]).astype(BF16)
    middle = lookup(wide, lax.axis_index("tm")) > 0
    blocks = [own[...], near[rows : rows + size, :], third[:size, :], last[rows:, :]]
    blocks += [piece[:size, :], pair[:size, :], third[size:, :], facing[:size, :]]
    blocks.append(jnp.where(middle, piece[size:, :], pair[size:, :]))
    blocks.append(jnp.where(middle, facing[size:, :], near[rows + size :, :]))
    for n, block in enumerate(blocks):
        out_ref[rows + n * size : rows + (n + 1) * size, :] = block


def collect(wide, low, low_head, *pieces):
    (rows, rank), size = low.shape, pieces[0].shape[0]
    return pl.pallas_call(
        functools.partial(collect_kernel, wide),
        in_specs=vmem(2 + len(pieces)),
        out_specs=pl.BlockSpec(memory_space=pltpu.VMEM),
        out_shape=jax.ShapeDtypeStruct((rows + 10 * size, rank), BF16),
        compiler_params=SMALL,
    )(low, low_head, *pieces)


def place_kernel(frames, lead, late, rest, tail, tail2, *outs):
    me, half = lax.axis_index("tm"), lax.axis_index("rep")
    first = half == 0
    rank = outs[0].shape[0]
    cut = 3 * rank // 2
    rows = outs[3].shape[0] // 2

    def both(here):
        a, b = tail[here, :].astype(F32), tail2[here, :].astype(F32)
        return jnp.concatenate([jnp.where(first, a, b), jnp.where(first, b, a)], axis=0)

    outs[3][...] = both(slice(0, rows))
    side = me // 2
    places = [lookup(late, me ^ m) for m in range(frames)] + [lookup(lead, me ^ m) for m in range(frames)]
    places += [lookup(rest, 1 + side), lookup(rest, 2 - side)]
    for n, head in enumerate(places):
        whole = both(slice(rows + n * cut, rows + (n + 1) * cut))
        for o in range(3):
            outs[o][:, column(head)] = whole[o * rank : (o + 1) * rank]


def place(frames, lead, late, rest, tail, tail2, rows, rank, width):
    return pl.pallas_call(
        functools.partial(place_kernel, frames, lead, late, rest),
        in_specs=vmem(2),
        out_specs=vmem(4),
        out_shape=[jax.ShapeDtypeStruct((rank, width), F32)] * 3
        + [jax.ShapeDtypeStruct((2 * rows, rank), F32)],
        compiler_params=SMALL,
    )(tail, tail2)


def exchange_plan(
    frozen_query,
    frozen_key,
    frozen_value,
    token_adapter_input,
    query_adapter_out,
    key_adapter_out,
    value_adapter_out,
    out_grad,
    band_width,
):
    rows, width = frozen_query.shape
    rank = token_adapter_input.shape[1]
    frames = band_width.shape[0]
    heads = width // DH
    starts, counts = head_table(heads, frames)
    most = max(counts)
    columns = [[min(starts[j] + s, heads - 1) for j in range(frames)] for s in range(most)]
    numbers = [[int(s < counts[j]) for j in range(frames)] for s in range(most)]
    slots = list(zip(columns, numbers))
    lead, late, rest = slots[0], slots[1], slots[2]
    wide = [j for j in range(frames) if counts[j] == most]
    adapters = [query_adapter_out, key_adapter_out, value_adapter_out]
    arrays = (frozen_query, out_grad, frozen_key, frozen_value, token_adapter_input)

    def meet(name, block, m, targets=range(frames)):
        with jax.named_scope(f"{name}_over_tm"):
            return lax.ppermute(block, "tm", [(j ^ m, j) for j in targets])

    def swap_in_chip(name, block):
        with jax.named_scope(f"{name}_in_chip"):
            return swap(block, "rep")

    def mine(slot, m):
        return (slot[0], m, "mine")

    sent, kept, sent_late = [], [], []
    for m in range(1, frames):
        first = [mine(lead, m), (None, m, "t")]
        if m == 1:
            sent.append(first + [mine(rest, m), mine(late, m)])
        else:
            sent += [first, [mine(rest, m)]]
            sent_late.append([mine(late, m)])
    for slot in (lead, rest, late):
        kept += [[mine(slot, 0)], [(slot[0], 0, "other")]]
    kept += [[(None, 0, "t")], [(None, 0, "other t")]]
    packed = pack(frames, sent, 56, *arrays)
    packed_late = pack(frames, sent_late + kept, 16, *arrays)
    kept = packed_late[len(sent_late) :]
    block = meet("nearest", packed[0], 1)
    lead_got, rest_got, late_got = [(block, 0)], [(block, 4 * DH + rank)], [(block, 8 * DH + rank)]
    for m in range(2, frames):
        lead_got.append((meet("lead", packed[2 * m - 3], m), 0))
        rest_got.append((meet("rest", packed[2 * m - 2], m, wide), 0))
        late_got.append((meet("late", packed_late[m - 2], m), 0))

    def sides(name, n, got, wide_t, groups, skip, after=()):
        size = 4 * DH - skip + (rank if wide_t else 0)
        picked = pick([(a, start + skip) for a, start in got], size, groups, after)
        cross = [swap_in_chip(name, block) for block in picked]
        where = 2 * DH - skip
        cross = [(block, at * size + where) for block, count in zip(cross, groups) for at in range(count)]
        rows_here = [(kept[2 * n], 0)] + got
        rows_there = [(kept[2 * n + 1], 0)] + cross
        return rows_here, rows_there, cross

    *lead_side, cross = sides("lead", 0, lead_got, True, (3,), 2 * DH, kept[:1])
    t_side = (
        [(kept[6], 0)] + [(a, start + 4 * DH) for a, start in lead_got],
        [(kept[7], 0)] + [(block, start + 2 * DH) for block, start in cross],
    )
    *rest_side, _ = sides("rest", 1, rest_got, False, (3,), 2 * DH)
    early = [lead, rest]
    keep, give, *low = head_group(early, band_width, [t_side, lead_side, rest_side], adapters)
    got = swap_in_chip("early_gradients", give)
    piece = (keep + got.astype(F32)).astype(BF16)
    *late_side, _ = sides("late", 2, late_got, False, (3,), 0, [got])
    pair = meet("early_gradients", piece, 1)
    facing = meet("early_gradients", piece, 3)
    keep, *gives = head_group([late], band_width, [t_side, late_side], adapters, low, [])
    gives = [swap_in_chip("late_sums", g) for g in gives]
    own_low, own, near, last, low_third, third = hand_out(
        frames, rows, keep, gives, piece, facing, [pair]
    )
    near, last = meet("late_sums", near, 1), meet("late_sums", last, 3)
    low = sum_low(own_low, near, meet("low", low_third, 2), last)
    third = meet("late_gradients", third, 2)
    with jax.named_scope("low_over_head"):
        low_head = swap(low, "head")
    tail = collect(rest[1], low, low_head, own, near, third, last, piece, pair, facing)
    outs = place(
        frames, lead[0], late[0], rest[0], tail, swap_in_chip("tail", tail), rows, rank, width
    )
    return tuple(outs)


def on_device(frozen_query, *rest):
    frames = rest[-1].shape[0]
    heads = frozen_query.shape[1] // DH
    whole_reach = frames == 4 and heads == 2 * frames + 2
    return (exchange_plan if whole_reach else window_plan)(frozen_query, *rest)


def solution(mesh):
    in_specs = (
        P(("groups", "tm", "rep"), "head"),
        P(("groups", "tm"), "head"),
        P(("groups", "tm"), "head"),
        P(("groups", "tm"), None),
        P(None, "head"),
        P(None, "head"),
        P(None, "head"),
        P(("groups", "tm", "rep"), "head"),
        P(),
    )
    out_specs = (
        P("groups", "head"),
        P("groups", "head"),
        P("groups", "head"),
        P(("groups", "tm"), None),
    )
    return jax.shard_map(
        on_device, mesh=mesh, in_specs=in_specs, out_specs=out_specs, check_vma=False
    )
```

```python
import functools

import jax
import jax.numpy as jnp
from jax import lax
from jax.experimental import pallas as pl
from jax.experimental.pallas import tpu as pltpu
from jax.sharding import PartitionSpec as P

DH = 128
NEAR = 1
REACH = 4
SCALE = DH ** (-0.5)
F32 = jnp.float32
BF16 = jnp.bfloat16
GIVES = 2
SMALL = pltpu.CompilerParams(vmem_limit_bytes=16 * 1024 * 1024)


def dot_nn(left, right):
    return lax.dot_general(left, right, (((1,), (0,)), ((), ())), preferred_element_type=F32)


def dot_nt(left, right):
    return lax.dot_general(left, right, (((1,), (1,)), ((), ())), preferred_element_type=F32)


def dot_tn(left, right):
    return lax.dot_general(left, right, (((0,), (0,)), ((), ())), preferred_element_type=F32)


def routes(count):
    found = []
    for d in range(1, min(REACH, count - 1) + 1):
        if 2 * d >= count:
            found.append((d, (-d, d)))
        else:
            found.append((d, (-d,)))
            found.append((d, (d,)))
    return found


def pairs(count, offsets):
    return [(i + o, i) for o in offsets for i in range(count) if 0 <= i + o < count]


def swap(block, axis):
    return lax.ppermute(block, axis, [(0, 1), (1, 0)])


def attention_kernel(
    blocks, bias_ref, fq_ref, do_ref, fk_ref, fv_ref, t_ref, tr_ref, tt_ref, aq_ref, ak_ref, av_ref, *refs
):
    k_refs = refs[:blocks]
    v_refs = refs[blocks : 2 * blocks]
    gq_ref, gk_ref, gv_ref, lowq_ref, low_ref = refs[2 * blocks :]
    rows = fq_ref.shape[0]

    @pl.when(pl.program_id(0) == 0)
    def _():
        lowq_ref[...] = jnp.zeros_like(lowq_ref)
        low_ref[...] = jnp.zeros_like(low_ref)

    aq, ak, av = aq_ref[...], ak_ref[...], av_ref[...]
    query = (fq_ref[...].astype(F32) + dot_nn(tr_ref[...], aq)).astype(BF16)
    do = do_ref[...]
    own_k = (fk_ref[...].astype(F32) + dot_nn(t_ref[...], ak)).astype(BF16)
    own_v = (fv_ref[...].astype(F32) + dot_nn(t_ref[...], av)).astype(BF16)
    keys = [own_k[:rows], own_k[rows:]] + [ref[...] for ref in k_refs]
    values = [own_v[:rows], own_v[rows:]] + [ref[...] for ref in v_refs]
    count = len(keys)
    scores = [dot_nt(keys[b], query) * SCALE + bias_ref[b] for b in range(count)]
    top = functools.reduce(jnp.maximum, scores)
    top = jnp.max(top, axis=0, keepdims=True)
    shifted = [jnp.exp(s - top) for s in scores]
    total = jnp.sum(functools.reduce(jnp.add, shifted), axis=0, keepdims=True)
    inverse = 1.0 / total
    probs = [s * inverse for s in shifted]
    lows = [p.astype(BF16) for p in probs]
    attended = functools.reduce(jnp.add, [dot_tn(lows[b], values[b]) for b in range(count)])
    attended = attended.astype(BF16).astype(F32)
    delta = jnp.sum((do.astype(F32) * attended).T, axis=0, keepdims=True)
    grads = [
        (probs[b] * (dot_nt(values[b], do) - delta)).astype(BF16) for b in range(count)
    ]
    dq = functools.reduce(jnp.add, [dot_tn(grads[b], keys[b]) for b in range(count)])
    dq = (dq * SCALE).astype(BF16)
    gq_ref[...] = dot_tn(tr_ref[...], dq)
    lowq_ref[...] += dot_nt(dq, aq)
    both = jnp.concatenate([ak, av], axis=1)
    for b in range(count):
        dk = (dot_nn(grads[b], query) * SCALE).astype(BF16)
        dv = dot_nn(lows[b], do).astype(BF16)
        part = jnp.concatenate([dk, dv], axis=1)
        low_ref[b * rows : (b + 1) * rows, :] += dot_nt(part, both)
        out = dot_nn(tt_ref[:, b * rows : (b + 1) * rows], part)
        if b == 0:
            total_part = out
        else:
            total_part += out
    gk_ref[...] = total_part[:, :DH]
    gv_ref[...] = total_part[:, DH:]


def attention(bias, fq, do, fk, fv, t, tr, tt, aq, ak, av, payloads):
    rows, width = fq.shape
    heads = width // DH
    rank = t.shape[1]
    blocks = len(payloads)
    count = blocks + 2

    def col(r):
        return pl.BlockSpec((r, DH), lambda h: (0, h))

    def whole(shape):
        return pl.BlockSpec(shape, lambda h: (0, 0))

    return pl.pallas_call(
        functools.partial(attention_kernel, blocks),
        grid=(heads,),
        out_shape=[
            jax.ShapeDtypeStruct((rank, width), F32),
            jax.ShapeDtypeStruct((rank, width), F32),
            jax.ShapeDtypeStruct((rank, width), F32),
            jax.ShapeDtypeStruct((rows, rank), F32),
            jax.ShapeDtypeStruct((count * rows, rank), F32),
        ],
        in_specs=[pl.BlockSpec(memory_space=pltpu.SMEM)]
        + [col(rows), col(rows), col(2 * rows), col(2 * rows)]
        + [whole(t.shape), whole(tr.shape), whole(tt.shape)]
        + [col(rank)] * 3
        + [col(rows)] * blocks
        + [pl.BlockSpec((rows, DH), lambda h: (0, heads + h))] * blocks,
        out_specs=[col(rank)] * 3 + [whole((rows, rank)), whole((count * rows, rank))],
        compiler_params=pltpu.CompilerParams(vmem_limit_bytes=32 * 1024 * 1024),
    )(bias, fq, do, fk, fv, t, tr, tt, aq, ak, av, *payloads, *payloads)


def sum_rows(part, frame_idx, half_idx, frames):
    rows, width = part.shape
    half = width // 2
    keep = lax.dynamic_slice_in_dim(part, half_idx * half, half, 1)
    give = lax.dynamic_slice_in_dim(part, (1 - half_idx) * half, half, 1)
    mine = keep + swap(give, "rep")
    if frames & (frames - 1) or rows % frames or frames > REACH + 1:
        total = lax.psum(mine, "tm").astype(BF16)
    else:
        chunk = rows // frames
        low = mine.astype(BF16)
        acc = lax.dynamic_slice_in_dim(mine, frame_idx * chunk, chunk, 0)
        for m in range(1, frames):
            give = lax.dynamic_slice_in_dim(low, (frame_idx ^ m) * chunk, chunk, 0)
            acc = acc + lax.ppermute(give, "tm", [(i, i ^ m) for i in range(frames)]).astype(F32)
        acc = acc.astype(BF16)
        total = jnp.zeros((rows, half), BF16)
        total = lax.dynamic_update_slice_in_dim(total, acc, frame_idx * chunk, 0)
        for m in range(1, frames):
            got = lax.ppermute(acc, "tm", [(i, i ^ m) for i in range(frames)])
            total = lax.dynamic_update_slice_in_dim(total, got, (frame_idx ^ m) * chunk, 0)
    other = swap(total, "rep")
    first = jnp.where(half_idx == 0, total, other)
    second = jnp.where(half_idx == 0, other, total)
    return jnp.concatenate([first, second], axis=1).astype(F32)


def window_plan(
    frozen_query,
    frozen_key,
    frozen_value,
    token_adapter_input,
    query_adapter_out,
    key_adapter_out,
    value_adapter_out,
    out_grad,
    band_width,
):
    rows, width = frozen_query.shape
    rank = token_adapter_input.shape[1]
    frames = band_width.shape[0]
    frame_idx = lax.axis_index("tm")
    half_idx = lax.axis_index("rep")
    t = token_adapter_input
    tr = lax.dynamic_slice_in_dim(t, half_idx * rows, rows, 0)

    def tile_rows_of(frozen, adapter):
        own = lax.dynamic_slice_in_dim(frozen, half_idx * rows, rows, 0)
        return (own.astype(F32) + dot_nn(tr, adapter)).astype(BF16)

    payload = jnp.concatenate(
        [tile_rows_of(frozen_key, key_adapter_out), tile_rows_of(frozen_value, value_adapter_out), tr],
        axis=1,
    )

    frame_ids = jnp.arange(frames)
    band_row = jnp.sum(jnp.where((frame_ids == frame_idx)[:, None], band_width, 0), axis=0)

    def band_at(offsets):
        seen = functools.reduce(jnp.logical_or, [frame_ids == frame_idx + o for o in offsets])
        return jnp.sum(jnp.where(seen, band_row, 0))

    own_band = band_at((0,))
    allowed = [jnp.abs(half_idx - tile) < own_band for tile in range(2)]
    payloads = []
    plan = routes(frames)
    for d, offsets in plan:
        got = lax.ppermute(payload, "tm", pairs(frames, offsets))
        band = band_at(offsets)
        payloads.append(got)
        allowed.append(band > 0)
        if d <= NEAR:
            payloads.append(swap(got, "rep"))
            allowed.append(band > 1)
    bias = jnp.where(jnp.stack(allowed), 0.0, -jnp.inf).astype(F32)
    tt = jnp.concatenate([t] + [p[:, 2 * width :] for p in payloads], axis=0).T

    gq, gk, gv, low_q, low_b = attention(
        bias, frozen_query, out_grad, frozen_key, frozen_value, t, tr, tt,
        query_adapter_out, key_adapter_out, value_adapter_out, payloads,
    )

    own = low_b[: 2 * rows]
    same = lax.dynamic_slice_in_dim(own, half_idx * rows, rows, 0) + low_q
    other = lax.dynamic_slice_in_dim(own, (1 - half_idx) * rows, rows, 0)
    start = 2 * rows
    for d, offsets in plan:
        size = 2 * rows if d <= NEAR else rows
        back = [(target, source) for source, target in pairs(frames, offsets)]
        got = lax.ppermute(low_b[start : start + size], "tm", back)
        start += size
        same = same + got[:rows]
        if d <= NEAR:
            other = other + got[rows:]
    low = jnp.where(
        half_idx == 0,
        jnp.concatenate([same, other], axis=0),
        jnp.concatenate([other, same], axis=0),
    )
    low = low + swap(low, "rep")
    low = low + swap(low, "head")

    grads = sum_rows(jnp.concatenate([gq, gk, gv], axis=0), frame_idx, half_idx, frames)
    return grads[:rank], grads[rank : 2 * rank], grads[2 * rank :], low


def head_table(heads, frames):
    base, extra = divmod(heads, frames)
    lead = (frames - extra) // 2
    counts = [base + (1 if lead <= j < lead + extra else 0) for j in range(frames)]
    return [sum(counts[:j]) for j in range(frames)], counts


def lookup(table, index):
    value = jnp.int32(table[0])
    for j in range(1, len(table)):
        value = jnp.where(index == j, jnp.int32(table[j]), value)
    return value


def column(head):
    return pl.ds(pl.multiple_of(head * DH, DH), DH)


def vmem(count):
    return [pl.BlockSpec(memory_space=pltpu.VMEM)] * count


def pack_kernel(frames, outputs, fq_ref, do_ref, fk_ref, fv_ref, t_ref, *refs):
    outs, (q_in, do_in, k_in, v_in, k2_in, v2_in, t_in, sems) = refs[:-8], refs[-8:]
    wanted = {what for parts in outputs for _, _, what in parts}
    me, half = lax.axis_index("tm"), lax.axis_index("rep")
    rows = fq_ref.shape[0]
    mine = pl.ds(pl.multiple_of(half * rows, rows), rows)
    rest = pl.ds(pl.multiple_of((1 - half) * rows, rows), rows)
    moves = [
        (fq_ref, q_in), (do_ref, do_in), (fk_ref.at[mine, :], k_in), (fv_ref.at[mine, :], v_in), (t_ref, t_in)
    ]
    if "other" in wanted:
        moves += [(fk_ref.at[rest, :], k2_in), (fv_ref.at[rest, :], v2_in)]
    copies = [pltpu.make_async_copy(a, b, sems.at[n]) for n, (a, b) in enumerate(moves)]
    for copy in copies:
        copy.start()
    for copy in copies:
        copy.wait()
    for out, parts in zip(outs, outputs):
        at = 0
        for table, m, what in parts:
            if what in ("t", "other t"):
                blocks = [t_in[mine if what == "t" else rest, :]]
            else:
                cols = column(lookup(table, me ^ m))
                sources = (q_in, do_in, k_in, v_in) if what == "mine" else (k2_in, v2_in)
                blocks = [ref[:, cols] for ref in sources]
            for block in blocks:
                out[:, at : at + block.shape[1]] = block
                at += block.shape[1]


def pack(frames, outputs, limit, fq, do, fk, fv, t):
    rows, width = fq.shape
    size = {"mine": 4 * DH, "other": 2 * DH, "t": t.shape[1], "other t": t.shape[1]}
    return pl.pallas_call(
        functools.partial(pack_kernel, frames, outputs),
        in_specs=[pl.BlockSpec(memory_space=pltpu.HBM)] * 5,
        out_specs=vmem(len(outputs)),
        out_shape=[
            jax.ShapeDtypeStruct((rows, sum(size[what] for _, _, what in parts)), BF16)
            for parts in outputs
        ],
        scratch_shapes=[pltpu.VMEM((rows, width), BF16)] * 6
        + [pltpu.VMEM(t.shape, BF16), pltpu.SemaphoreType.DMA((7,))],
        compiler_params=pltpu.CompilerParams(vmem_limit_bytes=limit * 1024 * 1024),
    )(fq, do, fk, fv, t)


def pick_kernel(spans, groups, *refs):
    n = 0
    for out, count in zip(refs[-len(groups) :], groups):
        for at in range(count):
            start, size = spans[n]
            out[:, at * size : (at + 1) * size] = refs[n][:, start : start + size]
            n += 1


def pick(parts, size, groups, after=()):
    arrays = [array for array, _ in parts]
    rows, dtype = arrays[0].shape[0], arrays[0].dtype
    return pl.pallas_call(
        functools.partial(pick_kernel, [(start, size) for _, start in parts], groups),
        in_specs=vmem(len(arrays)) + [pl.BlockSpec(memory_space=pl.ANY)] * len(after),
        out_specs=vmem(len(groups)),
        out_shape=[jax.ShapeDtypeStruct((rows, size * count), dtype) for count in groups],
        compiler_params=SMALL,
    )(*arrays, *after)


def one_head(frames, bands, q, do, frozen_k, frozen_v, tokens, aq, ak, av):
    flat = q.shape[0]
    rows = flat // frames
    t_same = tokens[:flat]

    def adapted(frozen, rows_of, adapter):
        return (frozen.astype(F32) + dot_nn(rows_of, adapter)).astype(BF16)

    query = adapted(q, t_same, aq)
    keys, values = adapted(frozen_k, tokens, ak), adapted(frozen_v, tokens, av)
    do_t, keys_t, values_t = do.T, keys.T, values.T

    def bias(i, b):
        j, need = (b, 0) if b < frames else (b - frames, 1)
        value = jnp.where(bands[i, j] > need, 0.0, -jnp.inf).astype(F32)
        return jnp.full((1, rows), value, F32)

    span = 2 if frames % 2 == 0 else 1
    wide = span * rows
    groups = [range(first, first + span) for first in range(0, frames, span)]
    seen = [
        list(range(frames))
        + [frames + j for j in range(frames) if any(abs(i - j) <= NEAR for i in mine)]
        for mine in groups
    ]
    here = [slice(mine[0] * rows, mine[0] * rows + wide) for mine in groups]
    pairs_of = range(len(groups))

    def gather(whole, g, axis):
        parts = [
            whole[b * rows : (b + 1) * rows] if axis == 0 else whole[:, b * rows : (b + 1) * rows]
            for b in seen[g]
        ]
        return jnp.concatenate(parts, axis=axis)

    def block(whole, n):
        return whole[n * rows : (n + 1) * rows]

    def softmax(g, raw):
        scores = [
            block(raw, n) * SCALE + jnp.concatenate([bias(i, b) for i in groups[g]], axis=1)
            for n, b in enumerate(seen[g])
        ]
        top = jnp.max(functools.reduce(jnp.maximum, scores), axis=0, keepdims=True)
        shifted = [jnp.exp(s - top) for s in scores]
        inverse = 1.0 / jnp.sum(functools.reduce(jnp.add, shifted), axis=0, keepdims=True)
        return [s * inverse for s in shifted]

    raws = [dot_nt(gather(keys, g, 0), query[here[g]]) for g in pairs_of]
    prob_grads = [dot_nt(gather(values, g, 0), do[here[g]]) for g in pairs_of]
    probs = [softmax(g, raws[g]) for g in pairs_of]
    lows = [jnp.concatenate([p.astype(BF16) for p in probs[g]], axis=0) for g in pairs_of]
    grads = []
    for g in pairs_of:
        attended = dot_nn(gather(values_t, g, 1), lows[g]).astype(BF16).astype(F32)
        delta = jnp.sum(do_t[:, here[g]].astype(F32) * attended, axis=0, keepdims=True)
        parts = [
            (probs[g][n] * (block(prob_grads[g], n) - delta)).astype(BF16) for n in range(len(seen[g]))
        ]
        grads.append(jnp.concatenate(parts, axis=0))
    dvs, dks = [None] * (2 * frames), [None] * (2 * frames)

    def add(sums, g, whole):
        for n, b in enumerate(seen[g]):
            sums[b] = block(whole, n) if sums[b] is None else sums[b] + block(whole, n)

    for g in pairs_of:
        add(dvs, g, dot_nn(lows[g], do[here[g]]))
    for g in pairs_of:
        add(dks, g, dot_nn(grads[g], query[here[g]]))
    dqs = [(dot_nn(gather(keys_t, g, 1), grads[g]) * SCALE).astype(BF16).T for g in pairs_of]
    dq = jnp.concatenate(dqs, axis=0)
    dk = (jnp.concatenate(dks, axis=0) * SCALE).astype(BF16)
    dv = jnp.concatenate(dvs, axis=0).astype(BF16)
    both = jnp.concatenate([dk, dv], axis=1)
    sums = dot_tn(tokens, both)
    grads = jnp.concatenate([dot_tn(t_same, dq), sums[:, :DH], sums[:, DH:]], axis=0)
    lows = dot_nt(both, jnp.concatenate([ak, av], axis=1))
    return grads, lows[:flat] + dot_nt(dq, aq), lows[flat:]


def group_kernel(heads, frames, chained, waits, sides, count, *refs):
    refs = list(refs)

    def take(count):
        taken = refs[:count]
        del refs[:count]
        return taken

    (bands,) = take(1)
    arrays, adapters = take(count), take(3)
    before = take(2) if chained else None
    take(waits)
    keep_ref, *give_refs = take(1 + GIVES if chained else 2)
    low_refs = [] if chained else take(2)
    q, do, k, v, tokens = refs
    me, half = lax.axis_index("tm"), lax.axis_index("rep")
    rows = arrays[0].shape[0]
    flat = frames * rows
    cut = 3 * tokens.shape[1] // 2
    first = half == 0
    same_at = [pl.ds(pl.multiple_of((me ^ m) * rows, rows), rows) for m in range(frames)]
    other_at = [pl.ds(pl.multiple_of(flat + (me ^ m) * rows, rows), rows) for m in range(frames)]

    def put(targets, places, rows_at):
        for m, (n, start) in enumerate(places):
            for c, target in enumerate(targets):
                target[rows_at[m], :] = arrays[n][:, start + c * DH : start + (c + 1) * DH]

    put([tokens], sides[0][0], same_at)
    put([tokens], sides[0][1], other_at)

    def run(n, table):
        put([q, do, k, v], sides[1 + n][0], same_at)
        put([k, v], sides[1 + n][1], other_at)
        cols = column(lookup(table, me))
        grads, low_same, low_other = one_head(
            frames, bands, q[...], do[...], k[...], v[...], tokens[...], *[a[:, cols] for a in adapters]
        )
        keep = jnp.where(first, grads[:cut], grads[cut:])
        give = jnp.where(first, grads[cut:], grads[:cut])
        return keep, give, low_same, low_other

    if chained:
        keep, give, low_same, low_other = run(0, heads[0][0])
        keep_ref[:cut, :] = keep
        keep_ref[cut:, :] = before[0][...] + low_same
        give = jnp.concatenate([give, before[1][...] + low_other], axis=0)
        size = give.shape[0] // GIVES
        for n, ref in enumerate(give_refs):
            ref[...] = give[n * size : (n + 1) * size].astype(ref.dtype)
        return
    for n, (table, counts) in enumerate(heads):
        here = slice(n * cut, (n + 1) * cut)

        def body():
            keep, give, low_same, low_other = run(n, table)
            keep_ref[here, :] = keep
            give_refs[0][here, :] = give.astype(BF16)
            if n == 0:
                low_refs[0][...] = low_same
                low_refs[1][...] = low_other
            else:
                low_refs[0][...] += low_same
                low_refs[1][...] += low_other

        if min(counts) > 0:
            body()
        else:
            live = lookup(counts, me) > 0
            pl.when(live)(body)

            @pl.when(jnp.logical_not(live))
            def _():
                keep_ref[here, :] = jnp.zeros((cut, DH), F32)
                give_refs[0][here, :] = jnp.zeros((cut, DH), BF16)


def head_group(heads, bands, sides, adapters, before=(), after=()):
    frames = len(sides[0][0])
    arrays, places = [], []
    for side in sides:
        found = []
        for pairs_of in side:
            found.append([])
            for array, start in pairs_of:
                known = [n for n, a in enumerate(arrays) if a is array]
                if not known:
                    arrays.append(array)
                found[-1].append((known[0] if known else len(arrays) - 1, start))
        places.append(found)
    rows, rank = arrays[0].shape[0], adapters[0].shape[0]
    flat = frames * rows
    size = len(heads) * 3 * rank // 2
    chained = len(before) > 0
    args = [bands, *arrays, *adapters, *before, *after]
    specs = [pl.BlockSpec(memory_space=pltpu.SMEM)] + vmem(len(arrays) + 3 + len(before))
    specs += [pl.BlockSpec(memory_space=pl.ANY)] * len(after)
    low = jax.ShapeDtypeStruct((flat, rank), F32)
    if chained:
        part = jax.ShapeDtypeStruct(((size + flat) // GIVES, rank), BF16)
        shapes = [jax.ShapeDtypeStruct((size + flat, rank), F32)] + [part] * GIVES
    else:
        edge = jax.ShapeDtypeStruct((size, rank), F32)
        shapes = [edge, jax.ShapeDtypeStruct((size, rank), BF16), low, low]
    return pl.pallas_call(
        functools.partial(
            group_kernel, heads, frames, chained, len(after), places, len(arrays)
        ),
        in_specs=specs,
        out_specs=vmem(len(shapes)),
        out_shape=shapes,
        scratch_shapes=[pltpu.VMEM((flat, DH), BF16)] * 2
        + [pltpu.VMEM((2 * flat, DH), BF16)] * 2
        + [pltpu.VMEM((2 * flat, rank), BF16)],
        compiler_params=pltpu.CompilerParams(vmem_limit_bytes=40 * 1024 * 1024),
    )(*args)


def hand_out_kernel(frames, size, parts, keep_ref, *refs):
    gots, facing, (own_ref, *sends, total) = refs[:parts], refs[parts], refs[-frames - 1 :]
    me = lax.axis_index("tm")
    rows = own_ref.shape[0]
    total[...] = keep_ref[...] + jnp.concatenate([got[...].astype(F32) for got in gots], axis=0)
    for m in range(frames):
        low = total[pl.ds(pl.multiple_of(size + (me ^ m) * rows, 8), rows), :]
        if m == 0:
            own_ref[...] = low
        else:
            sends[m - 1][:rows, :] = low.astype(BF16)
            sends[m - 1][rows : rows + size, :] = total[:size, :].astype(BF16)
    sends[0][rows + size :, :] = facing[...]


def hand_out(frames, rows, keep, gots, facing, after):
    size, rank = keep.shape[0] - frames * rows, keep.shape[1]
    own, *sends = pl.pallas_call(
        functools.partial(hand_out_kernel, frames, size, len(gots)),
        in_specs=vmem(2 + len(gots)) + [pl.BlockSpec(memory_space=pl.ANY)] * len(after),
        out_specs=vmem(frames),
        out_shape=[jax.ShapeDtypeStruct((rows, rank), F32)]
        + [jax.ShapeDtypeStruct((rows + size * n, rank), BF16) for n in (3, 1, 1)],
        scratch_shapes=[pltpu.VMEM(keep.shape, F32)],
        compiler_params=SMALL,
    )(keep, *gots, facing, *after)
    return own, sends


def collect_kernel(wide, own_low, own, near, third, last, piece, pair, far, facing, out_ref, low_ref):
    rows = own_low.shape[0]
    size = own.shape[0] - rows
    low = own_low[...]
    for got in (near, third, last):
        low = low + got[:rows, :].astype(F32)
    out_ref[:rows, :] = low.astype(BF16)
    low_ref[...] = low.astype(BF16)
    middle = lookup(wide, lax.axis_index("tm")) > 0

    def part(ref, n):
        return ref[rows + n * size : rows + (n + 1) * size, :]

    blocks = [part(ref, 0) for ref in (own, near, third, last)]
    blocks += [piece[:size, :], pair[:size, :]]
    blocks += [jnp.where(middle, far[...], part(near, 1)), facing[:size, :]]
    blocks.append(jnp.where(middle, piece[size:, :], pair[size:, :]))
    blocks.append(jnp.where(middle, facing[size:, :], part(near, 2)))
    for n, block in enumerate(blocks):
        out_ref[rows + n * size : rows + (n + 1) * size, :] = block


def collect(wide, own_low, own, gots, *pieces):
    (rows, rank), size = own_low.shape, pieces[0].shape[0] // 2
    return pl.pallas_call(
        functools.partial(collect_kernel, wide),
        in_specs=vmem(2 + len(gots) + len(pieces)),
        out_specs=vmem(2),
        out_shape=[
            jax.ShapeDtypeStruct((rows + 10 * size, rank), BF16),
            jax.ShapeDtypeStruct((rows, rank), BF16),
        ],
        compiler_params=SMALL,
    )(own_low, own, *gots, *pieces)


def place_kernel(frames, lead, late, rest, tail, tail2, low_head, low_diag, *outs):
    me, half = lax.axis_index("tm"), lax.axis_index("rep")
    first = half == 0
    rank = outs[0].shape[0]
    cut = 3 * rank // 2
    rows = low_head.shape[0]
    same = tail[:rows, :].astype(F32) + low_head[...].astype(F32)
    other = tail2[:rows, :].astype(F32) + low_diag[...].astype(F32)
    outs[3][:rows, :] = jnp.where(first, same, other)
    outs[3][rows:, :] = jnp.where(first, other, same)
    side = me // 2
    places = [lookup(late, me ^ m) for m in range(frames)] + [lookup(lead, me ^ m) for m in range(frames)]
    places += [lookup(rest, 1 + side), lookup(rest, 2 - side)]
    for n, head in enumerate(places):
        here = slice(rows + n * cut, rows + (n + 1) * cut)
        a, b = tail[here, :].astype(F32), tail2[here, :].astype(F32)
        both = jnp.concatenate([jnp.where(first, a, b), jnp.where(first, b, a)], axis=0)
        for o in range(3):
            outs[o][:, column(head)] = both[o * rank : (o + 1) * rank]


def place(frames, lead, late, rest, tail, tail2, low_head, low_diag, rank, width):
    rows = low_head.shape[0]
    return pl.pallas_call(
        functools.partial(place_kernel, frames, lead, late, rest),
        in_specs=vmem(4),
        out_specs=vmem(4),
        out_shape=[jax.ShapeDtypeStruct((rank, width), F32)] * 3
        + [jax.ShapeDtypeStruct((2 * rows, rank), F32)],
        compiler_params=SMALL,
    )(tail, tail2, low_head, low_diag)


def exchange_plan(
    frozen_query,
    frozen_key,
    frozen_value,
    token_adapter_input,
    query_adapter_out,
    key_adapter_out,
    value_adapter_out,
    out_grad,
    band_width,
):
    rows, width = frozen_query.shape
    rank = token_adapter_input.shape[1]
    frames = band_width.shape[0]
    heads = width // DH
    starts, counts = head_table(heads, frames)
    most = max(counts)
    columns = [[min(starts[j] + s, heads - 1) for j in range(frames)] for s in range(most)]
    numbers = [[int(s < counts[j]) for j in range(frames)] for s in range(most)]
    slots = list(zip(columns, numbers))
    lead, late, rest = slots[0], slots[1], slots[2]
    wide = [j for j in range(frames) if counts[j] == most]
    adapters = [query_adapter_out, key_adapter_out, value_adapter_out]
    arrays = (frozen_query, out_grad, frozen_key, frozen_value, token_adapter_input)

    def meet(name, block, m, targets=range(frames)):
        with jax.named_scope(f"{name}_over_tm"):
            return lax.ppermute(block, "tm", [(j ^ m, j) for j in targets])

    def swap_in_chip(name, block):
        with jax.named_scope(f"{name}_in_chip"):
            return swap(block, "rep")

    def mine(slot, m):
        return (slot[0], m, "mine")

    sent, kept, sent_late = [], [], []
    for m in range(1, frames):
        first = [mine(lead, m), (None, m, "t")]
        if m == 1:
            sent.append(first + [mine(rest, m), mine(late, m)])
        else:
            sent += [first, [mine(rest, m)]]
            sent_late.append([mine(late, m)])
    for slot in (lead, rest, late):
        kept += [[mine(slot, 0)], [(slot[0], 0, "other")]]
    kept += [[(None, 0, "t")], [(None, 0, "other t")]]
    packed = pack(frames, sent, 56, *arrays)
    packed_late = pack(frames, sent_late + kept, 16, *arrays)
    kept = packed_late[len(sent_late) :]
    block = meet("nearest", packed[0], 1)
    lead_got, rest_got, late_got = [(block, 0)], [(block, 4 * DH + rank)], [(block, 8 * DH + rank)]
    for m in range(2, frames):
        lead_got.append((meet("lead", packed[2 * m - 3], m), 0))
        rest_got.append((meet("rest", packed[2 * m - 2], m, wide), 0))
        late_got.append((meet("late", packed_late[m - 2], m), 0))

    def sides(name, n, got, wide_t, groups, skip, after=()):
        size = 4 * DH - skip + (rank if wide_t else 0)
        picked = pick([(a, start + skip) for a, start in got], size, groups, after)
        cross = [swap_in_chip(name, block) for block in picked]
        where = 2 * DH - skip
        cross = [(block, at * size + where) for block, count in zip(cross, groups) for at in range(count)]
        rows_here = [(kept[2 * n], 0)] + got
        rows_there = [(kept[2 * n + 1], 0)] + cross
        return rows_here, rows_there, cross

    *lead_side, cross = sides("lead", 0, lead_got, True, (3,), 2 * DH, kept[:1])
    t_side = (
        [(kept[6], 0)] + [(a, start + 4 * DH) for a, start in lead_got],
        [(kept[7], 0)] + [(block, start + 2 * DH) for block, start in cross],
    )
    *rest_side, _ = sides("rest", 1, rest_got, False, (3,), 2 * DH)
    early = [lead, rest]
    keep, give, *low = head_group(early, band_width, [t_side, lead_side, rest_side], adapters)
    got = swap_in_chip("early_gradients", give)
    piece = (keep + got.astype(F32)).astype(BF16)
    *late_side, _ = sides("late", 2, late_got, False, (3,), 0, [got])
    cut = 3 * rank // 2
    pair = meet("early_gradients", piece, 1)
    facing = meet("early_gradients", piece, 3)
    with jax.named_scope("early_lead_over_tm"):
        far = lax.ppermute(piece[:cut], "tm", [(0, 2), (3, 1)])
    keep, *gives = head_group([late], band_width, [t_side, late_side], adapters, low, [piece])
    gives = [swap_in_chip("late_sums", g) for g in gives]
    own_low, sends = hand_out(frames, rows, keep, gives, facing, [pair])
    gots = [meet("late_sums", block, m) for m, block in enumerate(sends, 1)]
    tail, low = collect(rest[1], own_low, sends[2], gots, piece, pair, far, facing)
    diag = [(0, 3), (1, 2), (2, 1), (3, 0)]
    with jax.named_scope("low_over_head"):
        low_head, low_diag = swap(low, "head"), lax.ppermute(low, ("head", "rep"), diag)
    outs = place(
        frames, lead[0], late[0], rest[0], tail, swap_in_chip("tail", tail), low_head, low_diag, rank, width
    )
    return tuple(outs)


def on_device(frozen_query, *rest):
    frames = rest[-1].shape[0]
    heads = frozen_query.shape[1] // DH
    whole_reach = frames == 4 and heads == 2 * frames + 2
    return (exchange_plan if whole_reach else window_plan)(frozen_query, *rest)


def solution(mesh):
    in_specs = (
        P(("groups", "tm", "rep"), "head"),
        P(("groups", "tm"), "head"),
        P(("groups", "tm"), "head"),
        P(("groups", "tm"), None),
        P(None, "head"),
        P(None, "head"),
        P(None, "head"),
        P(("groups", "tm", "rep"), "head"),
        P(),
    )
    out_specs = (
        P("groups", "head"),
        P("groups", "head"),
        P("groups", "head"),
        P(("groups", "tm"), None),
    )
    return jax.shard_map(
        on_device, mesh=mesh, in_specs=in_specs, out_specs=out_specs, check_vma=False
    )
```

```python
import functools
import math

import jax
import jax.numpy as jnp
from jax import lax
from jax.experimental import pallas as pl
from jax.experimental.pallas import tpu as pltpu
from jax.sharding import PartitionSpec as P

DH = 128
NEAR = 1
REACH = 4
SCALE = DH ** (-0.5)
SCALE_2 = SCALE * math.log2(math.e)
F32 = jnp.float32
BF16 = jnp.bfloat16
GIVES = 2
SMALL = pltpu.CompilerParams(vmem_limit_bytes=16 * 1024 * 1024)


def dot_nn(left, right):
    return lax.dot_general(left, right, (((1,), (0,)), ((), ())), preferred_element_type=F32)


def dot_nt(left, right):
    return lax.dot_general(left, right, (((1,), (1,)), ((), ())), preferred_element_type=F32)


def dot_tn(left, right):
    return lax.dot_general(left, right, (((0,), (0,)), ((), ())), preferred_element_type=F32)


def routes(count):
    found = []
    for d in range(1, min(REACH, count - 1) + 1):
        if 2 * d >= count:
            found.append((d, (-d, d)))
        else:
            found.append((d, (-d,)))
            found.append((d, (d,)))
    return found


def pairs(count, offsets):
    return [(i + o, i) for o in offsets for i in range(count) if 0 <= i + o < count]


def swap(block, axis):
    return lax.ppermute(block, axis, [(0, 1), (1, 0)])


def attention_kernel(
    blocks, bias_ref, fq_ref, do_ref, fk_ref, fv_ref, t_ref, tr_ref, tt_ref, aq_ref, ak_ref, av_ref, *refs
):
    k_refs = refs[:blocks]
    v_refs = refs[blocks : 2 * blocks]
    gq_ref, gk_ref, gv_ref, lowq_ref, low_ref = refs[2 * blocks :]
    rows = fq_ref.shape[0]

    @pl.when(pl.program_id(0) == 0)
    def _():
        lowq_ref[...] = jnp.zeros_like(lowq_ref)
        low_ref[...] = jnp.zeros_like(low_ref)

    aq, ak, av = aq_ref[...], ak_ref[...], av_ref[...]
    query = (fq_ref[...].astype(F32) + dot_nn(tr_ref[...], aq)).astype(BF16)
    do = do_ref[...]
    own_k = (fk_ref[...].astype(F32) + dot_nn(t_ref[...], ak)).astype(BF16)
    own_v = (fv_ref[...].astype(F32) + dot_nn(t_ref[...], av)).astype(BF16)
    keys = [own_k[:rows], own_k[rows:]] + [ref[...] for ref in k_refs]
    values = [own_v[:rows], own_v[rows:]] + [ref[...] for ref in v_refs]
    count = len(keys)
    scores = [dot_nt(keys[b], query) * SCALE + bias_ref[b] for b in range(count)]
    top = functools.reduce(jnp.maximum, scores)
    top = jnp.max(top, axis=0, keepdims=True)
    shifted = [jnp.exp(s - top) for s in scores]
    total = jnp.sum(functools.reduce(jnp.add, shifted), axis=0, keepdims=True)
    inverse = 1.0 / total
    probs = [s * inverse for s in shifted]
    lows = [p.astype(BF16) for p in probs]
    attended = functools.reduce(jnp.add, [dot_tn(lows[b], values[b]) for b in range(count)])
    attended = attended.astype(BF16).astype(F32)
    delta = jnp.sum((do.astype(F32) * attended).T, axis=0, keepdims=True)
    grads = [
        (probs[b] * (dot_nt(values[b], do) - delta)).astype(BF16) for b in range(count)
    ]
    dq = functools.reduce(jnp.add, [dot_tn(grads[b], keys[b]) for b in range(count)])
    dq = (dq * SCALE).astype(BF16)
    gq_ref[...] = dot_tn(tr_ref[...], dq)
    lowq_ref[...] += dot_nt(dq, aq)
    both = jnp.concatenate([ak, av], axis=1)
    for b in range(count):
        dk = (dot_nn(grads[b], query) * SCALE).astype(BF16)
        dv = dot_nn(lows[b], do).astype(BF16)
        part = jnp.concatenate([dk, dv], axis=1)
        low_ref[b * rows : (b + 1) * rows, :] += dot_nt(part, both)
        out = dot_nn(tt_ref[:, b * rows : (b + 1) * rows], part)
        if b == 0:
            total_part = out
        else:
            total_part += out
    gk_ref[...] = total_part[:, :DH]
    gv_ref[...] = total_part[:, DH:]


def attention(bias, fq, do, fk, fv, t, tr, tt, aq, ak, av, payloads):
    rows, width = fq.shape
    heads = width // DH
    rank = t.shape[1]
    blocks = len(payloads)
    count = blocks + 2

    def col(r):
        return pl.BlockSpec((r, DH), lambda h: (0, h))

    def whole(shape):
        return pl.BlockSpec(shape, lambda h: (0, 0))

    return pl.pallas_call(
        functools.partial(attention_kernel, blocks),
        grid=(heads,),
        out_shape=[
            jax.ShapeDtypeStruct((rank, width), F32),
            jax.ShapeDtypeStruct((rank, width), F32),
            jax.ShapeDtypeStruct((rank, width), F32),
            jax.ShapeDtypeStruct((rows, rank), F32),
            jax.ShapeDtypeStruct((count * rows, rank), F32),
        ],
        in_specs=[pl.BlockSpec(memory_space=pltpu.SMEM)]
        + [col(rows), col(rows), col(2 * rows), col(2 * rows)]
        + [whole(t.shape), whole(tr.shape), whole(tt.shape)]
        + [col(rank)] * 3
        + [col(rows)] * blocks
        + [pl.BlockSpec((rows, DH), lambda h: (0, heads + h))] * blocks,
        out_specs=[col(rank)] * 3 + [whole((rows, rank)), whole((count * rows, rank))],
        compiler_params=pltpu.CompilerParams(vmem_limit_bytes=32 * 1024 * 1024),
    )(bias, fq, do, fk, fv, t, tr, tt, aq, ak, av, *payloads, *payloads)


def sum_rows(part, frame_idx, half_idx, frames):
    rows, width = part.shape
    half = width // 2
    keep = lax.dynamic_slice_in_dim(part, half_idx * half, half, 1)
    give = lax.dynamic_slice_in_dim(part, (1 - half_idx) * half, half, 1)
    mine = keep + swap(give, "rep")
    if frames & (frames - 1) or rows % frames or frames > REACH + 1:
        total = lax.psum(mine, "tm").astype(BF16)
    else:
        chunk = rows // frames
        low = mine.astype(BF16)
        acc = lax.dynamic_slice_in_dim(mine, frame_idx * chunk, chunk, 0)
        for m in range(1, frames):
            give = lax.dynamic_slice_in_dim(low, (frame_idx ^ m) * chunk, chunk, 0)
            acc = acc + lax.ppermute(give, "tm", [(i, i ^ m) for i in range(frames)]).astype(F32)
        acc = acc.astype(BF16)
        total = jnp.zeros((rows, half), BF16)
        total = lax.dynamic_update_slice_in_dim(total, acc, frame_idx * chunk, 0)
        for m in range(1, frames):
            got = lax.ppermute(acc, "tm", [(i, i ^ m) for i in range(frames)])
            total = lax.dynamic_update_slice_in_dim(total, got, (frame_idx ^ m) * chunk, 0)
    other = swap(total, "rep")
    first = jnp.where(half_idx == 0, total, other)
    second = jnp.where(half_idx == 0, other, total)
    return jnp.concatenate([first, second], axis=1).astype(F32)


def window_plan(
    frozen_query,
    frozen_key,
    frozen_value,
    token_adapter_input,
    query_adapter_out,
    key_adapter_out,
    value_adapter_out,
    out_grad,
    band_width,
):
    rows, width = frozen_query.shape
    rank = token_adapter_input.shape[1]
    frames = band_width.shape[0]
    frame_idx = lax.axis_index("tm")
    half_idx = lax.axis_index("rep")
    t = token_adapter_input
    tr = lax.dynamic_slice_in_dim(t, half_idx * rows, rows, 0)

    def tile_rows_of(frozen, adapter):
        own = lax.dynamic_slice_in_dim(frozen, half_idx * rows, rows, 0)
        return (own.astype(F32) + dot_nn(tr, adapter)).astype(BF16)

    payload = jnp.concatenate(
        [tile_rows_of(frozen_key, key_adapter_out), tile_rows_of(frozen_value, value_adapter_out), tr],
        axis=1,
    )

    frame_ids = jnp.arange(frames)
    band_row = jnp.sum(jnp.where((frame_ids == frame_idx)[:, None], band_width, 0), axis=0)

    def band_at(offsets):
        seen = functools.reduce(jnp.logical_or, [frame_ids == frame_idx + o for o in offsets])
        return jnp.sum(jnp.where(seen, band_row, 0))

    own_band = band_at((0,))
    allowed = [jnp.abs(half_idx - tile) < own_band for tile in range(2)]
    payloads = []
    plan = routes(frames)
    for d, offsets in plan:
        got = lax.ppermute(payload, "tm", pairs(frames, offsets))
        band = band_at(offsets)
        payloads.append(got)
        allowed.append(band > 0)
        if d <= NEAR:
            payloads.append(swap(got, "rep"))
            allowed.append(band > 1)
    bias = jnp.where(jnp.stack(allowed), 0.0, -jnp.inf).astype(F32)
    tt = jnp.concatenate([t] + [p[:, 2 * width :] for p in payloads], axis=0).T

    gq, gk, gv, low_q, low_b = attention(
        bias, frozen_query, out_grad, frozen_key, frozen_value, t, tr, tt,
        query_adapter_out, key_adapter_out, value_adapter_out, payloads,
    )

    own = low_b[: 2 * rows]
    same = lax.dynamic_slice_in_dim(own, half_idx * rows, rows, 0) + low_q
    other = lax.dynamic_slice_in_dim(own, (1 - half_idx) * rows, rows, 0)
    start = 2 * rows
    for d, offsets in plan:
        size = 2 * rows if d <= NEAR else rows
        back = [(target, source) for source, target in pairs(frames, offsets)]
        got = lax.ppermute(low_b[start : start + size], "tm", back)
        start += size
        same = same + got[:rows]
        if d <= NEAR:
            other = other + got[rows:]
    low = jnp.where(
        half_idx == 0,
        jnp.concatenate([same, other], axis=0),
        jnp.concatenate([other, same], axis=0),
    )
    low = low + swap(low, "rep")
    low = low + swap(low, "head")

    grads = sum_rows(jnp.concatenate([gq, gk, gv], axis=0), frame_idx, half_idx, frames)
    return grads[:rank], grads[rank : 2 * rank], grads[2 * rank :], low


def head_table(heads, frames):
    base, extra = divmod(heads, frames)
    lead = (frames - extra) // 2
    counts = [base + (1 if lead <= j < lead + extra else 0) for j in range(frames)]
    return [sum(counts[:j]) for j in range(frames)], counts


def lookup(table, index):
    value = jnp.int32(table[0])
    for j in range(1, len(table)):
        value = jnp.where(index == j, jnp.int32(table[j]), value)
    return value


def column(head):
    return pl.ds(pl.multiple_of(head * DH, DH), DH)


def vmem(count):
    return [pl.BlockSpec(memory_space=pltpu.VMEM)] * count


def pack_kernel(frames, outputs, fq_ref, do_ref, fk_ref, fv_ref, t_ref, *refs):
    outs, (q_in, do_in, k_in, v_in, k2_in, v2_in, t_in, sems) = refs[:-8], refs[-8:]
    wanted = {what for parts in outputs for _, _, what in parts}
    me, half = lax.axis_index("tm"), lax.axis_index("rep")
    rows = fq_ref.shape[0]
    mine = pl.ds(pl.multiple_of(half * rows, rows), rows)
    rest = pl.ds(pl.multiple_of((1 - half) * rows, rows), rows)
    moves = [
        (fq_ref, q_in), (do_ref, do_in), (fk_ref.at[mine, :], k_in), (fv_ref.at[mine, :], v_in), (t_ref, t_in)
    ]
    if "other" in wanted:
        moves += [(fk_ref.at[rest, :], k2_in), (fv_ref.at[rest, :], v2_in)]
    copies = [pltpu.make_async_copy(a, b, sems.at[n]) for n, (a, b) in enumerate(moves)]
    for copy in copies:
        copy.start()
    for copy in copies:
        copy.wait()
    for out, parts in zip(outs, outputs):
        at = 0
        for table, m, what in parts:
            if what in ("t", "other t"):
                blocks = [t_in[mine if what == "t" else rest, :]]
            else:
                cols = column(lookup(table, me ^ m))
                sources = (q_in, do_in, k_in, v_in) if what == "mine" else (k2_in, v2_in)
                blocks = [ref[:, cols] for ref in sources]
            for block in blocks:
                out[:, at : at + block.shape[1]] = block
                at += block.shape[1]


def pack(frames, outputs, limit, fq, do, fk, fv, t):
    rows, width = fq.shape
    size = {"mine": 4 * DH, "other": 2 * DH, "t": t.shape[1], "other t": t.shape[1]}
    return pl.pallas_call(
        functools.partial(pack_kernel, frames, outputs),
        in_specs=[pl.BlockSpec(memory_space=pltpu.HBM)] * 5,
        out_specs=vmem(len(outputs)),
        out_shape=[
            jax.ShapeDtypeStruct((rows, sum(size[what] for _, _, what in parts)), BF16)
            for parts in outputs
        ],
        scratch_shapes=[pltpu.VMEM((rows, width), BF16)] * 6
        + [pltpu.VMEM(t.shape, BF16), pltpu.SemaphoreType.DMA((7,))],
        compiler_params=pltpu.CompilerParams(vmem_limit_bytes=limit * 1024 * 1024),
    )(fq, do, fk, fv, t)


def pick_kernel(spans, groups, *refs):
    n = 0
    for out, count in zip(refs[-len(groups) :], groups):
        for at in range(count):
            start, size = spans[n]
            out[:, at * size : (at + 1) * size] = refs[n][:, start : start + size]
            n += 1


def pick(parts, size, groups, after=()):
    arrays = [array for array, _ in parts]
    rows, dtype = arrays[0].shape[0], arrays[0].dtype
    return pl.pallas_call(
        functools.partial(pick_kernel, [(start, size) for _, start in parts], groups),
        in_specs=vmem(len(arrays)) + [pl.BlockSpec(memory_space=pl.ANY)] * len(after),
        out_specs=vmem(len(groups)),
        out_shape=[jax.ShapeDtypeStruct((rows, size * count), dtype) for count in groups],
        compiler_params=SMALL,
    )(*arrays, *after)


def one_head(frames, bands, q, do, frozen_k, frozen_v, tokens, aq, ak, av):
    flat = q.shape[0]
    rows = flat // frames
    t_same = tokens[:flat]

    def adapted(frozen, rows_of, adapter):
        return (frozen.astype(F32) + dot_nn(rows_of, adapter)).astype(BF16)

    query = adapted(q, t_same, aq)
    keys, values = adapted(frozen_k, tokens, ak), adapted(frozen_v, tokens, av)
    do_t, keys_t, values_t = do.T, keys.T, values.T

    def bias(i, b):
        j, need = (b, 0) if b < frames else (b - frames, 1)
        value = jnp.where(bands[i, j] > need, 0.0, -jnp.inf).astype(F32)
        return jnp.full((1, rows), value, F32)

    span = 2 if frames % 2 == 0 else 1
    wide = span * rows
    groups = [range(first, first + span) for first in range(0, frames, span)]
    seen = [
        list(range(frames))
        + [frames + j for j in range(frames) if any(abs(i - j) <= NEAR for i in mine)]
        for mine in groups
    ]
    here = [slice(mine[0] * rows, mine[0] * rows + wide) for mine in groups]
    pairs_of = range(len(groups))

    def gather(whole, g, axis):
        parts = [
            whole[b * rows : (b + 1) * rows] if axis == 0 else whole[:, b * rows : (b + 1) * rows]
            for b in seen[g]
        ]
        return jnp.concatenate(parts, axis=axis)

    def block(whole, n):
        return whole[n * rows : (n + 1) * rows]

    def softmax(g, raw):
        scores = [
            block(raw, n) * SCALE_2 + jnp.concatenate([bias(i, b) for i in groups[g]], axis=1)
            for n, b in enumerate(seen[g])
        ]
        top = jnp.max(functools.reduce(jnp.maximum, scores), axis=0, keepdims=True)
        shifted = [jnp.exp2(s - top) for s in scores]
        inverse = 1.0 / jnp.sum(functools.reduce(jnp.add, shifted), axis=0, keepdims=True)
        return [s * inverse for s in shifted]

    raws = [dot_nt(gather(keys, g, 0), query[here[g]]) for g in pairs_of]
    prob_grads = [dot_nt(gather(values, g, 0), do[here[g]]) for g in pairs_of]
    probs = [softmax(g, raws[g]) for g in pairs_of]
    lows = [jnp.concatenate([p.astype(BF16) for p in probs[g]], axis=0) for g in pairs_of]
    grads = []
    for g in pairs_of:
        attended = dot_nn(gather(values_t, g, 1), lows[g]).astype(BF16).astype(F32)
        delta = jnp.sum(do_t[:, here[g]].astype(F32) * attended, axis=0, keepdims=True)
        parts = [
            (probs[g][n] * (block(prob_grads[g], n) - delta)).astype(BF16) for n in range(len(seen[g]))
        ]
        grads.append(jnp.concatenate(parts, axis=0))
    dvs, dks = [None] * (2 * frames), [None] * (2 * frames)

    def add(sums, g, whole):
        for n, b in enumerate(seen[g]):
            sums[b] = block(whole, n) if sums[b] is None else sums[b] + block(whole, n)

    for g in pairs_of:
        add(dvs, g, dot_nn(lows[g], do[here[g]]))
    for g in pairs_of:
        add(dks, g, dot_nn(grads[g], query[here[g]]))
    dqs = [(dot_nn(gather(keys_t, g, 1), grads[g]) * SCALE).astype(BF16).T for g in pairs_of]
    dq = jnp.concatenate(dqs, axis=0)
    dk = (jnp.concatenate(dks, axis=0) * SCALE).astype(BF16)
    dv = jnp.concatenate(dvs, axis=0).astype(BF16)
    both = jnp.concatenate([dk, dv], axis=1)
    sums = dot_tn(tokens, both)
    grads = jnp.concatenate([dot_tn(t_same, dq), sums[:, :DH], sums[:, DH:]], axis=0)
    lows = dot_nt(both, jnp.concatenate([ak, av], axis=1))
    return grads, lows[:flat] + dot_nt(dq, aq), lows[flat:]


def group_kernel(heads, frames, chained, waits, sides, count, *refs):
    refs = list(refs)

    def take(count):
        taken = refs[:count]
        del refs[:count]
        return taken

    (bands,) = take(1)
    arrays, adapters = take(count), take(3)
    before = take(2) if chained else None
    take(waits)
    keep_ref, *give_refs = take(1 + GIVES if chained else 2)
    low_refs = [] if chained else take(2)
    q, do, k, v, tokens = refs
    me, half = lax.axis_index("tm"), lax.axis_index("rep")
    rows = arrays[0].shape[0]
    flat = frames * rows
    cut = 3 * tokens.shape[1] // 2
    first = half == 0
    same_at = [pl.ds(pl.multiple_of((me ^ m) * rows, rows), rows) for m in range(frames)]
    other_at = [pl.ds(pl.multiple_of(flat + (me ^ m) * rows, rows), rows) for m in range(frames)]

    def put(targets, places, rows_at):
        for m, (n, start) in enumerate(places):
            for c, target in enumerate(targets):
                target[rows_at[m], :] = arrays[n][:, start + c * DH : start + (c + 1) * DH]

    put([tokens], sides[0][0], same_at)
    put([tokens], sides[0][1], other_at)

    def run(n, table):
        put([q, do, k, v], sides[1 + n][0], same_at)
        put([k, v], sides[1 + n][1], other_at)
        cols = column(lookup(table, me))
        grads, low_same, low_other = one_head(
            frames, bands, q[...], do[...], k[...], v[...], tokens[...], *[a[:, cols] for a in adapters]
        )
        keep = jnp.where(first, grads[:cut], grads[cut:])
        give = jnp.where(first, grads[cut:], grads[:cut])
        return keep, give, low_same, low_other

    if chained:
        keep, give, low_same, low_other = run(0, heads[0][0])
        keep_ref[:cut, :] = keep
        keep_ref[cut:, :] = before[0][...] + low_same
        give = jnp.concatenate([give, before[1][...] + low_other], axis=0)
        size = give.shape[0] // GIVES
        for n, ref in enumerate(give_refs):
            ref[...] = give[n * size : (n + 1) * size].astype(ref.dtype)
        return
    for n, (table, counts) in enumerate(heads):
        here = slice(n * cut, (n + 1) * cut)

        def body():
            keep, give, low_same, low_other = run(n, table)
            keep_ref[here, :] = keep
            give_refs[0][here, :] = give.astype(BF16)
            if n == 0:
                low_refs[0][...] = low_same
                low_refs[1][...] = low_other
            else:
                low_refs[0][...] += low_same
                low_refs[1][...] += low_other

        if min(counts) > 0:
            body()
        else:
            live = lookup(counts, me) > 0
            pl.when(live)(body)

            @pl.when(jnp.logical_not(live))
            def _():
                keep_ref[here, :] = jnp.zeros((cut, DH), F32)
                give_refs[0][here, :] = jnp.zeros((cut, DH), BF16)


def head_group(heads, bands, sides, adapters, before=(), after=()):
    frames = len(sides[0][0])
    arrays, places = [], []
    for side in sides:
        found = []
        for pairs_of in side:
            found.append([])
            for array, start in pairs_of:
                known = [n for n, a in enumerate(arrays) if a is array]
                if not known:
                    arrays.append(array)
                found[-1].append((known[0] if known else len(arrays) - 1, start))
        places.append(found)
    rows, rank = arrays[0].shape[0], adapters[0].shape[0]
    flat = frames * rows
    size = len(heads) * 3 * rank // 2
    chained = len(before) > 0
    args = [bands, *arrays, *adapters, *before, *after]
    specs = [pl.BlockSpec(memory_space=pltpu.SMEM)] + vmem(len(arrays) + 3 + len(before))
    specs += [pl.BlockSpec(memory_space=pl.ANY)] * len(after)
    low = jax.ShapeDtypeStruct((flat, rank), F32)
    if chained:
        part = jax.ShapeDtypeStruct(((size + flat) // GIVES, rank), BF16)
        shapes = [jax.ShapeDtypeStruct((size + flat, rank), F32)] + [part] * GIVES
    else:
        edge = jax.ShapeDtypeStruct((size, rank), F32)
        shapes = [edge, jax.ShapeDtypeStruct((size, rank), BF16), low, low]
    return pl.pallas_call(
        functools.partial(
            group_kernel, heads, frames, chained, len(after), places, len(arrays)
        ),
        in_specs=specs,
        out_specs=vmem(len(shapes)),
        out_shape=shapes,
        scratch_shapes=[pltpu.VMEM((flat, DH), BF16)] * 2
        + [pltpu.VMEM((2 * flat, DH), BF16)] * 2
        + [pltpu.VMEM((2 * flat, rank), BF16)],
        compiler_params=pltpu.CompilerParams(vmem_limit_bytes=40 * 1024 * 1024),
    )(*args)


def hand_out_kernel(frames, size, parts, keep_ref, *refs):
    gots, facing, (own_ref, *sends, total) = refs[:parts], refs[parts], refs[-frames - 1 :]
    me = lax.axis_index("tm")
    rows = own_ref.shape[0]
    total[...] = keep_ref[...] + jnp.concatenate([got[...].astype(F32) for got in gots], axis=0)
    for m in range(frames):
        low = total[pl.ds(pl.multiple_of(size + (me ^ m) * rows, 8), rows), :]
        if m == 0:
            own_ref[...] = low
        else:
            sends[m - 1][:rows, :] = low.astype(BF16)
            sends[m - 1][rows : rows + size, :] = total[:size, :].astype(BF16)
    sends[0][rows + size :, :] = facing[...]


def hand_out(frames, rows, keep, gots, facing, after):
    size, rank = keep.shape[0] - frames * rows, keep.shape[1]
    own, *sends = pl.pallas_call(
        functools.partial(hand_out_kernel, frames, size, len(gots)),
        in_specs=vmem(2 + len(gots)) + [pl.BlockSpec(memory_space=pl.ANY)] * len(after),
        out_specs=vmem(frames),
        out_shape=[jax.ShapeDtypeStruct((rows, rank), F32)]
        + [jax.ShapeDtypeStruct((rows + size * n, rank), BF16) for n in (3, 1, 1)],
        scratch_shapes=[pltpu.VMEM(keep.shape, F32)],
        compiler_params=SMALL,
    )(keep, *gots, facing, *after)
    return own, sends


def collect_kernel(wide, own_low, own, near, third, last, piece, pair, far, facing, out_ref, low_ref):
    rows = own_low.shape[0]
    size = own.shape[0] - rows
    low = own_low[...]
    for got in (near, third, last):
        low = low + got[:rows, :].astype(F32)
    out_ref[:rows, :] = low.astype(BF16)
    low_ref[...] = low.astype(BF16)
    middle = lookup(wide, lax.axis_index("tm")) > 0

    def part(ref, n):
        return ref[rows + n * size : rows + (n + 1) * size, :]

    blocks = [part(ref, 0) for ref in (own, near, third, last)]
    blocks += [piece[:size, :], pair[:size, :]]
    blocks += [jnp.where(middle, far[...], part(near, 1)), facing[:size, :]]
    blocks.append(jnp.where(middle, piece[size:, :], pair[size:, :]))
    blocks.append(jnp.where(middle, facing[size:, :], part(near, 2)))
    for n, block in enumerate(blocks):
        out_ref[rows + n * size : rows + (n + 1) * size, :] = block


def collect(wide, own_low, own, gots, *pieces):
    (rows, rank), size = own_low.shape, pieces[0].shape[0] // 2
    return pl.pallas_call(
        functools.partial(collect_kernel, wide),
        in_specs=vmem(2 + len(gots) + len(pieces)),
        out_specs=vmem(2),
        out_shape=[
            jax.ShapeDtypeStruct((rows + 10 * size, rank), BF16),
            jax.ShapeDtypeStruct((rows, rank), BF16),
        ],
        compiler_params=SMALL,
    )(own_low, own, *gots, *pieces)


def place_kernel(frames, lead, late, rest, tail, tail2, low_head, low_diag, *refs):
    outs, filled, sems = refs[:4], refs[4:8], refs[8]
    me, half = lax.axis_index("tm"), lax.axis_index("rep")
    first = half == 0
    rank = filled[0].shape[0]
    cut = 3 * rank // 2
    rows = low_head.shape[0]
    side = me // 2
    places = [lookup(late, me ^ m) for m in range(frames)] + [lookup(lead, me ^ m) for m in range(frames)]
    places += [lookup(rest, 1 + side), lookup(rest, 2 - side)]
    copies = [pltpu.make_async_copy(filled[o], outs[o], sems.at[o]) for o in range(4)]

    def rows_of(ref, n, start, stop):
        return ref[rows + n * cut + start : rows + n * cut + stop, :].astype(F32)

    for o in range(3):
        for n, head in enumerate(places):
            parts = []
            for owner, low_end, high_end in ((0, 0, cut), (1, cut, 2 * cut)):
                start, stop = max(o * rank, low_end), min((o + 1) * rank, high_end)
                if start < stop:
                    mine, its = (rows_of(ref, n, start - low_end, stop - low_end) for ref in (tail, tail2))
                    parts.append(jnp.where(first, mine, its) if owner == 0 else jnp.where(first, its, mine))
            filled[o][:, column(head)] = parts[0] if len(parts) == 1 else jnp.concatenate(parts, axis=0)
        copies[o].start()
    same = tail[:rows, :].astype(F32) + low_head[...].astype(F32)
    other = tail2[:rows, :].astype(F32) + low_diag[...].astype(F32)
    filled[3][:rows, :] = jnp.where(first, same, other)
    filled[3][rows:, :] = jnp.where(first, other, same)
    copies[3].start()
    for copy in copies:
        copy.wait()


def place(frames, lead, late, rest, tail, tail2, low_head, low_diag, rank, width):
    rows = low_head.shape[0]
    shapes = [(rank, width)] * 3 + [(2 * rows, rank)]
    return pl.pallas_call(
        functools.partial(place_kernel, frames, lead, late, rest),
        in_specs=vmem(4),
        out_specs=[pl.BlockSpec(memory_space=pl.ANY)] * 4,
        out_shape=[jax.ShapeDtypeStruct(shape, F32) for shape in shapes],
        scratch_shapes=[pltpu.VMEM(shape, F32) for shape in shapes] + [pltpu.SemaphoreType.DMA((4,))],
        compiler_params=SMALL,
    )(tail, tail2, low_head, low_diag)


def exchange_plan(
    frozen_query,
    frozen_key,
    frozen_value,
    token_adapter_input,
    query_adapter_out,
    key_adapter_out,
    value_adapter_out,
    out_grad,
    band_width,
):
    rows, width = frozen_query.shape
    rank = token_adapter_input.shape[1]
    frames = band_width.shape[0]
    heads = width // DH
    starts, counts = head_table(heads, frames)
    most = max(counts)
    columns = [[min(starts[j] + s, heads - 1) for j in range(frames)] for s in range(most)]
    numbers = [[int(s < counts[j]) for j in range(frames)] for s in range(most)]
    slots = list(zip(columns, numbers))
    lead, late, rest = slots[0], slots[1], slots[2]
    wide = [j for j in range(frames) if counts[j] == most]
    adapters = [query_adapter_out, key_adapter_out, value_adapter_out]
    arrays = (frozen_query, out_grad, frozen_key, frozen_value, token_adapter_input)

    def meet(name, block, m, targets=range(frames)):
        with jax.named_scope(f"{name}_over_tm"):
            return lax.ppermute(block, "tm", [(j ^ m, j) for j in targets])

    def swap_in_chip(name, block):
        with jax.named_scope(f"{name}_in_chip"):
            return swap(block, "rep")

    def mine(slot, m):
        return (slot[0], m, "mine")

    sent, kept, sent_late = [], [], []
    for m in range(1, frames):
        first = [mine(lead, m), (None, m, "t")]
        if m == 1:
            sent.append(first + [mine(rest, m), mine(late, m)])
        else:
            sent += [first, [mine(rest, m)]]
            sent_late.append([mine(late, m)])
    for slot in (lead, rest, late):
        kept += [[mine(slot, 0)], [(slot[0], 0, "other")]]
    kept += [[(None, 0, "t")], [(None, 0, "other t")]]
    packed = pack(frames, sent, 56, *arrays)
    packed_late = pack(frames, sent_late + kept, 16, *arrays)
    kept = packed_late[len(sent_late) :]
    block = meet("nearest", packed[0], 1)
    lead_got, rest_got, late_got = [(block, 0)], [(block, 4 * DH + rank)], [(block, 8 * DH + rank)]
    for m in range(2, frames):
        lead_got.append((meet("lead", packed[2 * m - 3], m), 0))
        rest_got.append((meet("rest", packed[2 * m - 2], m, wide), 0))
        late_got.append((meet("late", packed_late[m - 2], m), 0))

    def sides(name, n, got, wide_t, groups, skip, after=()):
        size = 4 * DH - skip + (rank if wide_t else 0)
        picked = pick([(a, start + skip) for a, start in got], size, groups, after)
        cross = [swap_in_chip(name, block) for block in picked]
        where = 2 * DH - skip
        cross = [(block, at * size + where) for block, count in zip(cross, groups) for at in range(count)]
        rows_here = [(kept[2 * n], 0)] + got
        rows_there = [(kept[2 * n + 1], 0)] + cross
        return rows_here, rows_there, cross

    *lead_side, cross = sides("lead", 0, lead_got, True, (3,), 2 * DH, kept[:1])
    t_side = (
        [(kept[6], 0)] + [(a, start + 4 * DH) for a, start in lead_got],
        [(kept[7], 0)] + [(block, start + 2 * DH) for block, start in cross],
    )
    *rest_side, _ = sides("rest", 1, rest_got, False, (3,), 2 * DH)
    early = [lead, rest]
    keep, give, *low = head_group(early, band_width, [t_side, lead_side, rest_side], adapters)
    got = swap_in_chip("early_gradients", give)
    piece = (keep + got.astype(F32)).astype(BF16)
    *late_side, _ = sides("late", 2, late_got, False, (3,), 0, [got])
    cut = 3 * rank // 2
    pair = meet("early_gradients", piece, 1)
    facing = meet("early_gradients", piece, 3)
    with jax.named_scope("early_lead_over_tm"):
        far = lax.ppermute(piece[:cut], "tm", [(0, 2), (3, 1)])
    keep, *gives = head_group([late], band_width, [t_side, late_side], adapters, low, [piece])
    gives = [swap_in_chip("late_sums", g) for g in gives]
    own_low, sends = hand_out(frames, rows, keep, gives, facing, [pair])
    gots = [meet("late_sums", block, m) for m, block in enumerate(sends, 1)]
    tail, low = collect(rest[1], own_low, sends[2], gots, piece, pair, far, facing)
    diag = [(0, 3), (1, 2), (2, 1), (3, 0)]
    with jax.named_scope("low_over_head"):
        low_head, low_diag = swap(low, "head"), lax.ppermute(low, ("head", "rep"), diag)
    outs = place(
        frames, lead[0], late[0], rest[0], tail, swap_in_chip("tail", tail), low_head, low_diag, rank, width
    )
    return tuple(outs)


def on_device(frozen_query, *rest):
    frames = rest[-1].shape[0]
    heads = frozen_query.shape[1] // DH
    whole_reach = frames == 4 and heads == 2 * frames + 2
    return (exchange_plan if whole_reach else window_plan)(frozen_query, *rest)


def solution(mesh):
    in_specs = (
        P(("groups", "tm", "rep"), "head"),
        P(("groups", "tm"), "head"),
        P(("groups", "tm"), "head"),
        P(("groups", "tm"), None),
        P(None, "head"),
        P(None, "head"),
        P(None, "head"),
        P(("groups", "tm", "rep"), "head"),
        P(),
    )
    out_specs = (
        P("groups", "head"),
        P("groups", "head"),
        P("groups", "head"),
        P(("groups", "tm"), None),
    )
    return jax.shard_map(
        on_device, mesh=mesh, in_specs=in_specs, out_specs=out_specs, check_vma=False
    )
```

```python
import functools
import math

import jax
import jax.numpy as jnp
from jax import lax
from jax.experimental import pallas as pl
from jax.experimental.pallas import tpu as pltpu
from jax.sharding import PartitionSpec as P

DH = 128
NEAR = 1
REACH = 4
SCALE = DH ** (-0.5)
SCALE_2 = SCALE * math.log2(math.e)
F32 = jnp.float32
BF16 = jnp.bfloat16
GIVES = 2
CHUNK = 32
SMALL = pltpu.CompilerParams(vmem_limit_bytes=16 * 1024 * 1024)


def dot_nn(left, right):
    return lax.dot_general(left, right, (((1,), (0,)), ((), ())), preferred_element_type=F32)


def dot_nt(left, right):
    return lax.dot_general(left, right, (((1,), (1,)), ((), ())), preferred_element_type=F32)


def dot_tn(left, right):
    return lax.dot_general(left, right, (((0,), (0,)), ((), ())), preferred_element_type=F32)


def routes(count):
    found = []
    for d in range(1, min(REACH, count - 1) + 1):
        if 2 * d >= count:
            found.append((d, (-d, d)))
        else:
            found.append((d, (-d,)))
            found.append((d, (d,)))
    return found


def pairs(count, offsets):
    return [(i + o, i) for o in offsets for i in range(count) if 0 <= i + o < count]


def swap(block, axis):
    return lax.ppermute(block, axis, [(0, 1), (1, 0)])


def attention_kernel(
    blocks, bias_ref, fq_ref, do_ref, fk_ref, fv_ref, t_ref, tr_ref, tt_ref, aq_ref, ak_ref, av_ref, *refs
):
    k_refs = refs[:blocks]
    v_refs = refs[blocks : 2 * blocks]
    gq_ref, gk_ref, gv_ref, lowq_ref, low_ref = refs[2 * blocks :]
    rows = fq_ref.shape[0]

    @pl.when(pl.program_id(0) == 0)
    def _():
        lowq_ref[...] = jnp.zeros_like(lowq_ref)
        low_ref[...] = jnp.zeros_like(low_ref)

    aq, ak, av = aq_ref[...], ak_ref[...], av_ref[...]
    query = (fq_ref[...].astype(F32) + dot_nn(tr_ref[...], aq)).astype(BF16)
    do = do_ref[...]
    own_k = (fk_ref[...].astype(F32) + dot_nn(t_ref[...], ak)).astype(BF16)
    own_v = (fv_ref[...].astype(F32) + dot_nn(t_ref[...], av)).astype(BF16)
    keys = [own_k[:rows], own_k[rows:]] + [ref[...] for ref in k_refs]
    values = [own_v[:rows], own_v[rows:]] + [ref[...] for ref in v_refs]
    count = len(keys)
    scores = [dot_nt(keys[b], query) * SCALE + bias_ref[b] for b in range(count)]
    top = functools.reduce(jnp.maximum, scores)
    top = jnp.max(top, axis=0, keepdims=True)
    shifted = [jnp.exp(s - top) for s in scores]
    total = jnp.sum(functools.reduce(jnp.add, shifted), axis=0, keepdims=True)
    inverse = 1.0 / total
    probs = [s * inverse for s in shifted]
    lows = [p.astype(BF16) for p in probs]
    attended = functools.reduce(jnp.add, [dot_tn(lows[b], values[b]) for b in range(count)])
    attended = attended.astype(BF16).astype(F32)
    delta = jnp.sum((do.astype(F32) * attended).T, axis=0, keepdims=True)
    grads = [
        (probs[b] * (dot_nt(values[b], do) - delta)).astype(BF16) for b in range(count)
    ]
    dq = functools.reduce(jnp.add, [dot_tn(grads[b], keys[b]) for b in range(count)])
    dq = (dq * SCALE).astype(BF16)
    gq_ref[...] = dot_tn(tr_ref[...], dq)
    lowq_ref[...] += dot_nt(dq, aq)
    both = jnp.concatenate([ak, av], axis=1)
    for b in range(count):
        dk = (dot_nn(grads[b], query) * SCALE).astype(BF16)
        dv = dot_nn(lows[b], do).astype(BF16)
        part = jnp.concatenate([dk, dv], axis=1)
        low_ref[b * rows : (b + 1) * rows, :] += dot_nt(part, both)
        out = dot_nn(tt_ref[:, b * rows : (b + 1) * rows], part)
        if b == 0:
            total_part = out
        else:
            total_part += out
    gk_ref[...] = total_part[:, :DH]
    gv_ref[...] = total_part[:, DH:]


def attention(bias, fq, do, fk, fv, t, tr, tt, aq, ak, av, payloads):
    rows, width = fq.shape
    heads = width // DH
    rank = t.shape[1]
    blocks = len(payloads)
    count = blocks + 2

    def col(r):
        return pl.BlockSpec((r, DH), lambda h: (0, h))

    def whole(shape):
        return pl.BlockSpec(shape, lambda h: (0, 0))

    return pl.pallas_call(
        functools.partial(attention_kernel, blocks),
        grid=(heads,),
        out_shape=[
            jax.ShapeDtypeStruct((rank, width), F32),
            jax.ShapeDtypeStruct((rank, width), F32),
            jax.ShapeDtypeStruct((rank, width), F32),
            jax.ShapeDtypeStruct((rows, rank), F32),
            jax.ShapeDtypeStruct((count * rows, rank), F32),
        ],
        in_specs=[pl.BlockSpec(memory_space=pltpu.SMEM)]
        + [col(rows), col(rows), col(2 * rows), col(2 * rows)]
        + [whole(t.shape), whole(tr.shape), whole(tt.shape)]
        + [col(rank)] * 3
        + [col(rows)] * blocks
        + [pl.BlockSpec((rows, DH), lambda h: (0, heads + h))] * blocks,
        out_specs=[col(rank)] * 3 + [whole((rows, rank)), whole((count * rows, rank))],
        compiler_params=pltpu.CompilerParams(vmem_limit_bytes=32 * 1024 * 1024),
    )(bias, fq, do, fk, fv, t, tr, tt, aq, ak, av, *payloads, *payloads)


def sum_rows(part, frame_idx, half_idx, frames):
    rows, width = part.shape
    half = width // 2
    keep = lax.dynamic_slice_in_dim(part, half_idx * half, half, 1)
    give = lax.dynamic_slice_in_dim(part, (1 - half_idx) * half, half, 1)
    mine = keep + swap(give, "rep")
    if frames & (frames - 1) or rows % frames or frames > REACH + 1:
        total = lax.psum(mine, "tm").astype(BF16)
    else:
        chunk = rows // frames
        low = mine.astype(BF16)
        acc = lax.dynamic_slice_in_dim(mine, frame_idx * chunk, chunk, 0)
        for m in range(1, frames):
            give = lax.dynamic_slice_in_dim(low, (frame_idx ^ m) * chunk, chunk, 0)
            acc = acc + lax.ppermute(give, "tm", [(i, i ^ m) for i in range(frames)]).astype(F32)
        acc = acc.astype(BF16)
        total = jnp.zeros((rows, half), BF16)
        total = lax.dynamic_update_slice_in_dim(total, acc, frame_idx * chunk, 0)
        for m in range(1, frames):
            got = lax.ppermute(acc, "tm", [(i, i ^ m) for i in range(frames)])
            total = lax.dynamic_update_slice_in_dim(total, got, (frame_idx ^ m) * chunk, 0)
    other = swap(total, "rep")
    first = jnp.where(half_idx == 0, total, other)
    second = jnp.where(half_idx == 0, other, total)
    return jnp.concatenate([first, second], axis=1).astype(F32)


def window_plan(
    frozen_query,
    frozen_key,
    frozen_value,
    token_adapter_input,
    query_adapter_out,
    key_adapter_out,
    value_adapter_out,
    out_grad,
    band_width,
):
    rows, width = frozen_query.shape
    rank = token_adapter_input.shape[1]
    frames = band_width.shape[0]
    frame_idx = lax.axis_index("tm")
    half_idx = lax.axis_index("rep")
    t = token_adapter_input
    tr = lax.dynamic_slice_in_dim(t, half_idx * rows, rows, 0)

    def tile_rows_of(frozen, adapter):
        own = lax.dynamic_slice_in_dim(frozen, half_idx * rows, rows, 0)
        return (own.astype(F32) + dot_nn(tr, adapter)).astype(BF16)

    payload = jnp.concatenate(
        [tile_rows_of(frozen_key, key_adapter_out), tile_rows_of(frozen_value, value_adapter_out), tr],
        axis=1,
    )

    frame_ids = jnp.arange(frames)
    band_row = jnp.sum(jnp.where((frame_ids == frame_idx)[:, None], band_width, 0), axis=0)

    def band_at(offsets):
        seen = functools.reduce(jnp.logical_or, [frame_ids == frame_idx + o for o in offsets])
        return jnp.sum(jnp.where(seen, band_row, 0))

    own_band = band_at((0,))
    allowed = [jnp.abs(half_idx - tile) < own_band for tile in range(2)]
    payloads = []
    plan = routes(frames)
    for d, offsets in plan:
        got = lax.ppermute(payload, "tm", pairs(frames, offsets))
        band = band_at(offsets)
        payloads.append(got)
        allowed.append(band > 0)
        if d <= NEAR:
            payloads.append(swap(got, "rep"))
            allowed.append(band > 1)
    bias = jnp.where(jnp.stack(allowed), 0.0, -jnp.inf).astype(F32)
    tt = jnp.concatenate([t] + [p[:, 2 * width :] for p in payloads], axis=0).T

    gq, gk, gv, low_q, low_b = attention(
        bias, frozen_query, out_grad, frozen_key, frozen_value, t, tr, tt,
        query_adapter_out, key_adapter_out, value_adapter_out, payloads,
    )

    own = low_b[: 2 * rows]
    same = lax.dynamic_slice_in_dim(own, half_idx * rows, rows, 0) + low_q
    other = lax.dynamic_slice_in_dim(own, (1 - half_idx) * rows, rows, 0)
    start = 2 * rows
    for d, offsets in plan:
        size = 2 * rows if d <= NEAR else rows
        back = [(target, source) for source, target in pairs(frames, offsets)]
        got = lax.ppermute(low_b[start : start + size], "tm", back)
        start += size
        same = same + got[:rows]
        if d <= NEAR:
            other = other + got[rows:]
    low = jnp.where(
        half_idx == 0,
        jnp.concatenate([same, other], axis=0),
        jnp.concatenate([other, same], axis=0),
    )
    low = low + swap(low, "rep")
    low = low + swap(low, "head")

    grads = sum_rows(jnp.concatenate([gq, gk, gv], axis=0), frame_idx, half_idx, frames)
    return grads[:rank], grads[rank : 2 * rank], grads[2 * rank :], low


def head_table(heads, frames):
    base, extra = divmod(heads, frames)
    lead = (frames - extra) // 2
    counts = [base + (1 if lead <= j < lead + extra else 0) for j in range(frames)]
    return [sum(counts[:j]) for j in range(frames)], counts


def lookup(table, index):
    value = jnp.int32(table[0])
    for j in range(1, len(table)):
        value = jnp.where(index == j, jnp.int32(table[j]), value)
    return value


def column(head):
    return pl.ds(pl.multiple_of(head * DH, DH), DH)


def vmem(count):
    return [pl.BlockSpec(memory_space=pltpu.VMEM)] * count


def chunked(source, target, sems, at, chunk):
    rows = target.shape[0]
    return [
        pltpu.make_async_copy(
            source.at[pl.ds(r * chunk, chunk), :], target.at[pl.ds(r * chunk, chunk), :], sems.at[at + r]
        )
        for r in range(rows // chunk)
    ]


def pack_kernel(frames, outputs, fq_ref, do_ref, fk_ref, fv_ref, t_ref, *refs):
    outs, (q_in, do_in, k_in, v_in, k2_in, v2_in, t_in, sems), held = refs[: len(outputs)], refs[-8:], refs[len(outputs) : -8]
    wanted = {what for parts in outputs for _, _, what in parts}
    me, half = lax.axis_index("tm"), lax.axis_index("rep")
    rows = fq_ref.shape[0]
    mine = pl.ds(pl.multiple_of(half * rows, rows), rows)
    rest = pl.ds(pl.multiple_of((1 - half) * rows, rows), rows)
    moves = [
        (fq_ref, q_in), (do_ref, do_in), (fk_ref.at[mine, :], k_in), (fv_ref.at[mine, :], v_in), (t_ref, t_in)
    ]
    if "other" in wanted:
        moves += [(fk_ref.at[rest, :], k2_in), (fv_ref.at[rest, :], v2_in)]
    copies = []
    for source, target in moves:
        copies += chunked(source, target, sems, len(copies), CHUNK)
    for copy in copies:
        copy.start()
    for copy in copies:
        copy.wait()
    leaving, used = [], len(copies)
    for n, parts in enumerate(outputs):
        out = held[n] if held else outs[n]
        at = 0
        for table, m, what in parts:
            if what in ("t", "other t"):
                blocks = [t_in[mine if what == "t" else rest, :]]
            else:
                cols = column(lookup(table, me ^ m))
                sources = (q_in, do_in, k_in, v_in) if what == "mine" else (k2_in, v2_in)
                blocks = [ref[:, cols] for ref in sources]
            for block in blocks:
                out[:, at : at + block.shape[1]] = block
                at += block.shape[1]
        if held:
            more = chunked(out, outs[n], sems, used + len(leaving), CHUNK)
            for copy in more:
                copy.start()
            leaving += more
    for copy in leaving:
        copy.wait()


def pack(frames, outputs, apart, fq, do, fk, fv, t):
    rows, width = fq.shape
    size = {"mine": 4 * DH, "other": 2 * DH, "t": t.shape[1], "other t": t.shape[1]}
    shapes = [(rows, sum(size[what] for _, _, what in parts)) for parts in outputs]
    held = [pltpu.VMEM(shape, BF16) for shape in shapes] if apart else []
    count = (8 + (len(shapes) if apart else 0)) * (rows // CHUNK)
    limit = (56 if apart else 16) * 1024 * 1024
    return pl.pallas_call(
        functools.partial(pack_kernel, frames, outputs),
        in_specs=[pl.BlockSpec(memory_space=pltpu.HBM)] * 5,
        out_specs=[pl.BlockSpec(memory_space=pl.ANY)] * len(shapes) if apart else vmem(len(shapes)),
        out_shape=[jax.ShapeDtypeStruct(shape, BF16) for shape in shapes],
        scratch_shapes=held
        + [pltpu.VMEM((rows, width), BF16)] * 6
        + [pltpu.VMEM(t.shape, BF16), pltpu.SemaphoreType.DMA((count,))],
        compiler_params=pltpu.CompilerParams(vmem_limit_bytes=limit),
    )(fq, do, fk, fv, t)


def pick_kernel(spans, groups, *refs):
    n = 0
    for out, count in zip(refs[-len(groups) :], groups):
        for at in range(count):
            start, size = spans[n]
            out[:, at * size : (at + 1) * size] = refs[n][:, start : start + size]
            n += 1


def pick(parts, size, groups, after=()):
    arrays = [array for array, _ in parts]
    rows, dtype = arrays[0].shape[0], arrays[0].dtype
    return pl.pallas_call(
        functools.partial(pick_kernel, [(start, size) for _, start in parts], groups),
        in_specs=vmem(len(arrays)) + [pl.BlockSpec(memory_space=pl.ANY)] * len(after),
        out_specs=vmem(len(groups)),
        out_shape=[jax.ShapeDtypeStruct((rows, size * count), dtype) for count in groups],
        compiler_params=SMALL,
    )(*arrays, *after)


def one_head(frames, bands, q, do, frozen_k, frozen_v, tokens, aq, ak, av):
    flat = q.shape[0]
    rows = flat // frames
    t_same = tokens[:flat]

    def adapted(frozen, rows_of, adapter):
        return (frozen.astype(F32) + dot_nn(rows_of, adapter)).astype(BF16)

    query = adapted(q, t_same, aq)
    keys, values = adapted(frozen_k, tokens, ak), adapted(frozen_v, tokens, av)
    do_t, keys_t, values_t = do.T, keys.T, values.T

    def bias(i, b):
        j, need = (b, 0) if b < frames else (b - frames, 1)
        value = jnp.where(bands[i, j] > need, 0.0, -jnp.inf).astype(F32)
        return jnp.full((1, rows), value, F32)

    span = 2 if frames % 2 == 0 else 1
    wide = span * rows
    groups = [range(first, first + span) for first in range(0, frames, span)]
    seen = [
        list(range(frames))
        + [frames + j for j in range(frames) if any(abs(i - j) <= NEAR for i in mine)]
        for mine in groups
    ]
    here = [slice(mine[0] * rows, mine[0] * rows + wide) for mine in groups]
    pairs_of = range(len(groups))

    def gather(whole, g, axis):
        parts = [
            whole[b * rows : (b + 1) * rows] if axis == 0 else whole[:, b * rows : (b + 1) * rows]
            for b in seen[g]
        ]
        return jnp.concatenate(parts, axis=axis)

    def block(whole, n):
        return whole[n * rows : (n + 1) * rows]

    def softmax(g, raw):
        scores = [
            block(raw, n) * SCALE_2 + jnp.concatenate([bias(i, b) for i in groups[g]], axis=1)
            for n, b in enumerate(seen[g])
        ]
        top = jnp.max(functools.reduce(jnp.maximum, scores), axis=0, keepdims=True)
        shifted = [jnp.exp2(s - top) for s in scores]
        inverse = 1.0 / jnp.sum(functools.reduce(jnp.add, shifted), axis=0, keepdims=True)
        return [s * inverse for s in shifted]

    raws = [dot_nt(gather(keys, g, 0), query[here[g]]) for g in pairs_of]
    prob_grads = [dot_nt(gather(values, g, 0), do[here[g]]) for g in pairs_of]
    probs = [softmax(g, raws[g]) for g in pairs_of]
    lows = [jnp.concatenate([p.astype(BF16) for p in probs[g]], axis=0) for g in pairs_of]
    grads = []
    for g in pairs_of:
        attended = dot_nn(gather(values_t, g, 1), lows[g]).astype(BF16).astype(F32)
        delta = jnp.sum(do_t[:, here[g]].astype(F32) * attended, axis=0, keepdims=True)
        parts = [
            (probs[g][n] * (block(prob_grads[g], n) - delta)).astype(BF16) for n in range(len(seen[g]))
        ]
        grads.append(jnp.concatenate(parts, axis=0))
    dvs, dks = [None] * (2 * frames), [None] * (2 * frames)

    def add(sums, g, whole):
        for n, b in enumerate(seen[g]):
            sums[b] = block(whole, n) if sums[b] is None else sums[b] + block(whole, n)

    for g in pairs_of:
        add(dvs, g, dot_nn(lows[g], do[here[g]]))
    for g in pairs_of:
        add(dks, g, dot_nn(grads[g], query[here[g]]))
    dqs = [(dot_nn(gather(keys_t, g, 1), grads[g]) * SCALE).astype(BF16).T for g in pairs_of]
    dq = jnp.concatenate(dqs, axis=0)
    dk = (jnp.concatenate(dks, axis=0) * SCALE).astype(BF16)
    dv = jnp.concatenate(dvs, axis=0).astype(BF16)
    both = jnp.concatenate([dk, dv], axis=1)
    sums = dot_tn(tokens, both)
    grads = jnp.concatenate([dot_tn(t_same, dq), sums[:, :DH], sums[:, DH:]], axis=0)
    lows = dot_nt(both, jnp.concatenate([ak, av], axis=1))
    return grads, lows[:flat] + dot_nt(dq, aq), lows[flat:]


def group_kernel(heads, frames, chained, waits, sides, count, *refs):
    refs = list(refs)

    def take(count):
        taken = refs[:count]
        del refs[:count]
        return taken

    (bands,) = take(1)
    arrays, adapters = take(count), take(3)
    before = take(2) if chained else None
    take(waits)
    keep_ref, *give_refs = take(1 + GIVES if chained else 2)
    low_refs = [] if chained else take(2)
    q, do, k, v, tokens = refs
    me, half = lax.axis_index("tm"), lax.axis_index("rep")
    rows = arrays[0].shape[0]
    flat = frames * rows
    cut = 3 * tokens.shape[1] // 2
    first = half == 0
    same_at = [pl.ds(pl.multiple_of((me ^ m) * rows, rows), rows) for m in range(frames)]
    other_at = [pl.ds(pl.multiple_of(flat + (me ^ m) * rows, rows), rows) for m in range(frames)]

    def put(targets, places, rows_at):
        for m, (n, start) in enumerate(places):
            for c, target in enumerate(targets):
                target[rows_at[m], :] = arrays[n][:, start + c * DH : start + (c + 1) * DH]

    put([tokens], sides[0][0], same_at)
    put([tokens], sides[0][1], other_at)

    def run(n, table):
        put([q, do, k, v], sides[1 + n][0], same_at)
        put([k, v], sides[1 + n][1], other_at)
        cols = column(lookup(table, me))
        grads, low_same, low_other = one_head(
            frames, bands, q[...], do[...], k[...], v[...], tokens[...], *[a[:, cols] for a in adapters]
        )
        keep = jnp.where(first, grads[:cut], grads[cut:])
        give = jnp.where(first, grads[cut:], grads[:cut])
        return keep, give, low_same, low_other

    if chained:
        keep, give, low_same, low_other = run(0, heads[0][0])
        keep_ref[:cut, :] = keep
        keep_ref[cut:, :] = before[0][...] + low_same
        give = jnp.concatenate([give, before[1][...] + low_other], axis=0)
        size = give.shape[0] // GIVES
        for n, ref in enumerate(give_refs):
            ref[...] = give[n * size : (n + 1) * size].astype(ref.dtype)
        return
    for n, (table, counts) in enumerate(heads):
        here = slice(n * cut, (n + 1) * cut)

        def body():
            keep, give, low_same, low_other = run(n, table)
            keep_ref[here, :] = keep
            give_refs[0][here, :] = give.astype(BF16)
            if n == 0:
                low_refs[0][...] = low_same
                low_refs[1][...] = low_other
            else:
                low_refs[0][...] += low_same
                low_refs[1][...] += low_other

        if min(counts) > 0:
            body()
        else:
            live = lookup(counts, me) > 0
            pl.when(live)(body)

            @pl.when(jnp.logical_not(live))
            def _():
                keep_ref[here, :] = jnp.zeros((cut, DH), F32)
                give_refs[0][here, :] = jnp.zeros((cut, DH), BF16)


def head_group(heads, bands, sides, adapters, before=(), after=()):
    frames = len(sides[0][0])
    arrays, places = [], []
    for side in sides:
        found = []
        for pairs_of in side:
            found.append([])
            for array, start in pairs_of:
                known = [n for n, a in enumerate(arrays) if a is array]
                if not known:
                    arrays.append(array)
                found[-1].append((known[0] if known else len(arrays) - 1, start))
        places.append(found)
    rows, rank = arrays[0].shape[0], adapters[0].shape[0]
    flat = frames * rows
    size = len(heads) * 3 * rank // 2
    chained = len(before) > 0
    args = [bands, *arrays, *adapters, *before, *after]
    specs = [pl.BlockSpec(memory_space=pltpu.SMEM)] + vmem(len(arrays) + 3 + len(before))
    specs += [pl.BlockSpec(memory_space=pl.ANY)] * len(after)
    low = jax.ShapeDtypeStruct((flat, rank), F32)
    if chained:
        part = jax.ShapeDtypeStruct(((size + flat) // GIVES, rank), BF16)
        shapes = [jax.ShapeDtypeStruct((size + flat, rank), F32)] + [part] * GIVES
    else:
        edge = jax.ShapeDtypeStruct((size, rank), F32)
        shapes = [edge, jax.ShapeDtypeStruct((size, rank), BF16), low, low]
    return pl.pallas_call(
        functools.partial(
            group_kernel, heads, frames, chained, len(after), places, len(arrays)
        ),
        in_specs=specs,
        out_specs=vmem(len(shapes)),
        out_shape=shapes,
        scratch_shapes=[pltpu.VMEM((flat, DH), BF16)] * 2
        + [pltpu.VMEM((2 * flat, DH), BF16)] * 2
        + [pltpu.VMEM((2 * flat, rank), BF16)],
        compiler_params=pltpu.CompilerParams(vmem_limit_bytes=40 * 1024 * 1024),
    )(*args)


def hand_out_kernel(frames, size, parts, keep_ref, *refs):
    gots, facing, (own_ref, *sends, total) = refs[:parts], refs[parts], refs[-frames - 1 :]
    me = lax.axis_index("tm")
    rows = own_ref.shape[0]
    total[...] = keep_ref[...] + jnp.concatenate([got[...].astype(F32) for got in gots], axis=0)
    for m in range(frames):
        low = total[pl.ds(pl.multiple_of(size + (me ^ m) * rows, 8), rows), :]
        if m == 0:
            own_ref[...] = low
        else:
            sends[m - 1][:rows, :] = low.astype(BF16)
            sends[m - 1][rows : rows + size, :] = total[:size, :].astype(BF16)
    sends[0][rows + size :, :] = facing[...]


def hand_out(frames, rows, keep, gots, facing, after):
    size, rank = keep.shape[0] - frames * rows, keep.shape[1]
    own, *sends = pl.pallas_call(
        functools.partial(hand_out_kernel, frames, size, len(gots)),
        in_specs=vmem(2 + len(gots)) + [pl.BlockSpec(memory_space=pl.ANY)] * len(after),
        out_specs=vmem(frames),
        out_shape=[jax.ShapeDtypeStruct((rows, rank), F32)]
        + [jax.ShapeDtypeStruct((rows + size * n, rank), BF16) for n in (3, 1, 1)],
        scratch_shapes=[pltpu.VMEM(keep.shape, F32)],
        compiler_params=SMALL,
    )(keep, *gots, facing, *after)
    return own, sends


def collect_kernel(wide, own_low, own, near, third, last, piece, pair, far, facing, out_ref, low_ref):
    rows = own_low.shape[0]
    size = own.shape[0] - rows
    low = own_low[...]
    for got in (near, third, last):
        low = low + got[:rows, :].astype(F32)
    out_ref[:rows, :] = low.astype(BF16)
    low_ref[...] = low.astype(BF16)
    middle = lookup(wide, lax.axis_index("tm")) > 0

    def part(ref, n):
        return ref[rows + n * size : rows + (n + 1) * size, :]

    blocks = [part(ref, 0) for ref in (own, near, third, last)]
    blocks += [piece[:size, :], pair[:size, :]]
    blocks += [jnp.where(middle, far[...], part(near, 1)), facing[:size, :]]
    blocks.append(jnp.where(middle, piece[size:, :], pair[size:, :]))
    blocks.append(jnp.where(middle, facing[size:, :], part(near, 2)))
    for n, block in enumerate(blocks):
        out_ref[rows + n * size : rows + (n + 1) * size, :] = block


def collect(wide, own_low, own, gots, *pieces):
    (rows, rank), size = own_low.shape, pieces[0].shape[0] // 2
    return pl.pallas_call(
        functools.partial(collect_kernel, wide),
        in_specs=vmem(2 + len(gots) + len(pieces)),
        out_specs=vmem(2),
        out_shape=[
            jax.ShapeDtypeStruct((rows + 10 * size, rank), BF16),
            jax.ShapeDtypeStruct((rows, rank), BF16),
        ],
        compiler_params=SMALL,
    )(own_low, own, *gots, *pieces)


def place_kernel(frames, lead, late, rest, tail, tail2, low_head, low_diag, *refs):
    outs, filled, sems = refs[:4], refs[4:8], refs[8]
    me, half = lax.axis_index("tm"), lax.axis_index("rep")
    first = half == 0
    rank = filled[0].shape[0]
    cut = 3 * rank // 2
    rows = low_head.shape[0]
    side = me // 2
    places = [lookup(late, me ^ m) for m in range(frames)] + [lookup(lead, me ^ m) for m in range(frames)]
    places += [lookup(rest, 1 + side), lookup(rest, 2 - side)]
    copies = []
    for o in range(4):
        copies.append(chunked(filled[o], outs[o], sems, sum(map(len, copies)), CHUNK))

    def rows_of(ref, n, start, stop):
        return ref[rows + n * cut + start : rows + n * cut + stop, :].astype(F32)

    for o in range(3):
        for n, head in enumerate(places):
            parts = []
            for owner, low_end, high_end in ((0, 0, cut), (1, cut, 2 * cut)):
                start, stop = max(o * rank, low_end), min((o + 1) * rank, high_end)
                if start < stop:
                    mine, its = (rows_of(ref, n, start - low_end, stop - low_end) for ref in (tail, tail2))
                    parts.append(jnp.where(first, mine, its) if owner == 0 else jnp.where(first, its, mine))
            filled[o][:, column(head)] = parts[0] if len(parts) == 1 else jnp.concatenate(parts, axis=0)
        for copy in copies[o]:
            copy.start()
    same = tail[:rows, :].astype(F32) + low_head[...].astype(F32)
    other = tail2[:rows, :].astype(F32) + low_diag[...].astype(F32)
    filled[3][:rows, :] = jnp.where(first, same, other)
    filled[3][rows:, :] = jnp.where(first, other, same)
    for copy in copies[3]:
        copy.start()
    for copy in sum(copies, []):
        copy.wait()


def place(frames, lead, late, rest, tail, tail2, low_head, low_diag, rank, width):
    rows = low_head.shape[0]
    shapes = [(rank, width)] * 3 + [(2 * rows, rank)]
    return pl.pallas_call(
        functools.partial(place_kernel, frames, lead, late, rest),
        in_specs=vmem(4),
        out_specs=[pl.BlockSpec(memory_space=pl.ANY)] * 4,
        out_shape=[jax.ShapeDtypeStruct(shape, F32) for shape in shapes],
        scratch_shapes=[pltpu.VMEM(shape, F32) for shape in shapes]
        + [pltpu.SemaphoreType.DMA((sum(r // CHUNK for r, _ in shapes),))],
        compiler_params=SMALL,
    )(tail, tail2, low_head, low_diag)


def exchange_plan(
    frozen_query,
    frozen_key,
    frozen_value,
    token_adapter_input,
    query_adapter_out,
    key_adapter_out,
    value_adapter_out,
    out_grad,
    band_width,
):
    rows, width = frozen_query.shape
    rank = token_adapter_input.shape[1]
    frames = band_width.shape[0]
    heads = width // DH
    starts, counts = head_table(heads, frames)
    most = max(counts)
    columns = [[min(starts[j] + s, heads - 1) for j in range(frames)] for s in range(most)]
    numbers = [[int(s < counts[j]) for j in range(frames)] for s in range(most)]
    slots = list(zip(columns, numbers))
    lead, late, rest = slots[0], slots[1], slots[2]
    wide = [j for j in range(frames) if counts[j] == most]
    adapters = [query_adapter_out, key_adapter_out, value_adapter_out]
    arrays = (frozen_query, out_grad, frozen_key, frozen_value, token_adapter_input)

    def meet(name, block, m, targets=range(frames)):
        with jax.named_scope(f"{name}_over_tm"):
            return lax.ppermute(block, "tm", [(j ^ m, j) for j in targets])

    def swap_in_chip(name, block):
        with jax.named_scope(f"{name}_in_chip"):
            return swap(block, "rep")

    def mine(slot, m):
        return (slot[0], m, "mine")

    sent, kept, sent_late = [], [], []
    for m in range(1, frames):
        first = [mine(lead, m), (None, m, "t")]
        if m == 1:
            sent.append(first + [mine(rest, m), mine(late, m)])
        else:
            sent += [first, [mine(rest, m)]]
            sent_late.append([mine(late, m)])
    for slot in (lead, rest, late):
        kept += [[mine(slot, 0)], [(slot[0], 0, "other")]]
    kept += [[(None, 0, "t")], [(None, 0, "other t")]]
    packed = pack(frames, sent, True, *arrays)
    packed_late = pack(frames, sent_late + kept, False, *arrays)
    kept = packed_late[len(sent_late) :]
    block = meet("nearest", packed[0], 1)
    lead_got, rest_got, late_got = [(block, 0)], [(block, 4 * DH + rank)], [(block, 8 * DH + rank)]
    for m in range(2, frames):
        lead_got.append((meet("lead", packed[2 * m - 3], m), 0))
        rest_got.append((meet("rest", packed[2 * m - 2], m, wide), 0))
        late_got.append((meet("late", packed_late[m - 2], m), 0))

    def sides(name, n, got, wide_t, groups, skip, after=()):
        size = 4 * DH - skip + (rank if wide_t else 0)
        picked = pick([(a, start + skip) for a, start in got], size, groups, after)
        cross = [swap_in_chip(name, block) for block in picked]
        where = 2 * DH - skip
        cross = [(block, at * size + where) for block, count in zip(cross, groups) for at in range(count)]
        rows_here = [(kept[2 * n], 0)] + got
        rows_there = [(kept[2 * n + 1], 0)] + cross
        return rows_here, rows_there, cross

    *lead_side, cross = sides("lead", 0, lead_got, True, (3,), 2 * DH, kept[:1])
    t_side = (
        [(kept[6], 0)] + [(a, start + 4 * DH) for a, start in lead_got],
        [(kept[7], 0)] + [(block, start + 2 * DH) for block, start in cross],
    )
    *rest_side, _ = sides("rest", 1, rest_got, False, (3,), 2 * DH)
    early = [lead, rest]
    keep, give, *low = head_group(early, band_width, [t_side, lead_side, rest_side], adapters)
    got = swap_in_chip("early_gradients", give)
    piece = (keep + got.astype(F32)).astype(BF16)
    *late_side, _ = sides("late", 2, late_got, False, (3,), 0, [got])
    cut = 3 * rank // 2
    pair = meet("early_gradients", piece, 1)
    facing = meet("early_gradients", piece, 3)
    with jax.named_scope("early_lead_over_tm"):
        far = lax.ppermute(piece[:cut], "tm", [(0, 2), (3, 1)])
    keep, *gives = head_group([late], band_width, [t_side, late_side], adapters, low, [piece])
    gives = [swap_in_chip("late_sums", g) for g in gives]
    own_low, sends = hand_out(frames, rows, keep, gives, facing, [pair])
    gots = [meet("late_sums", block, m) for m, block in enumerate(sends, 1)]
    tail, low = collect(rest[1], own_low, sends[2], gots, piece, pair, far, facing)
    diag = [(0, 3), (1, 2), (2, 1), (3, 0)]
    with jax.named_scope("low_over_head"):
        low_head, low_diag = swap(low, "head"), lax.ppermute(low, ("head", "rep"), diag)
    outs = place(
        frames, lead[0], late[0], rest[0], tail, swap_in_chip("tail", tail), low_head, low_diag, rank, width
    )
    return tuple(outs)


def on_device(frozen_query, *rest):
    frames = rest[-1].shape[0]
    heads = frozen_query.shape[1] // DH
    whole_reach = frames == 4 and heads == 2 * frames + 2
    return (exchange_plan if whole_reach else window_plan)(frozen_query, *rest)


def solution(mesh):
    in_specs = (
        P(("groups", "tm", "rep"), "head"),
        P(("groups", "tm"), "head"),
        P(("groups", "tm"), "head"),
        P(("groups", "tm"), None),
        P(None, "head"),
        P(None, "head"),
        P(None, "head"),
        P(("groups", "tm", "rep"), "head"),
        P(),
    )
    out_specs = (
        P("groups", "head"),
        P("groups", "head"),
        P("groups", "head"),
        P(("groups", "tm"), None),
    )
    return jax.shard_map(
        on_device, mesh=mesh, in_specs=in_specs, out_specs=out_specs, check_vma=False
    )
```

```python
import functools
import math

import jax
import jax.numpy as jnp
from jax import lax
from jax.experimental import pallas as pl
from jax.experimental.pallas import tpu as pltpu
from jax.sharding import PartitionSpec as P

DH = 128
NEAR = 1
REACH = 4
SCALE = DH ** (-0.5)
SCALE_2 = SCALE * math.log2(math.e)
F32 = jnp.float32
BF16 = jnp.bfloat16
GIVES = 4
SMALL = pltpu.CompilerParams(vmem_limit_bytes=16 * 1024 * 1024)


def dot_nn(left, right):
    return lax.dot_general(left, right, (((1,), (0,)), ((), ())), preferred_element_type=F32)


def dot_nt(left, right):
    return lax.dot_general(left, right, (((1,), (1,)), ((), ())), preferred_element_type=F32)


def dot_tn(left, right):
    return lax.dot_general(left, right, (((0,), (0,)), ((), ())), preferred_element_type=F32)


def routes(count):
    found = []
    for d in range(1, min(REACH, count - 1) + 1):
        if 2 * d >= count:
            found.append((d, (-d, d)))
        else:
            found.append((d, (-d,)))
            found.append((d, (d,)))
    return found


def pairs(count, offsets):
    return [(i + o, i) for o in offsets for i in range(count) if 0 <= i + o < count]


def swap(block, axis):
    return lax.ppermute(block, axis, [(0, 1), (1, 0)])


def attention_kernel(
    blocks, bias_ref, fq_ref, do_ref, fk_ref, fv_ref, t_ref, tr_ref, tt_ref, aq_ref, ak_ref, av_ref, *refs
):
    k_refs = refs[:blocks]
    v_refs = refs[blocks : 2 * blocks]
    gq_ref, gk_ref, gv_ref, lowq_ref, low_ref = refs[2 * blocks :]
    rows = fq_ref.shape[0]

    @pl.when(pl.program_id(0) == 0)
    def _():
        lowq_ref[...] = jnp.zeros_like(lowq_ref)
        low_ref[...] = jnp.zeros_like(low_ref)

    aq, ak, av = aq_ref[...], ak_ref[...], av_ref[...]
    query = (fq_ref[...].astype(F32) + dot_nn(tr_ref[...], aq)).astype(BF16)
    do = do_ref[...]
    own_k = (fk_ref[...].astype(F32) + dot_nn(t_ref[...], ak)).astype(BF16)
    own_v = (fv_ref[...].astype(F32) + dot_nn(t_ref[...], av)).astype(BF16)
    keys = [own_k[:rows], own_k[rows:]] + [ref[...] for ref in k_refs]
    values = [own_v[:rows], own_v[rows:]] + [ref[...] for ref in v_refs]
    count = len(keys)
    scores = [dot_nt(keys[b], query) * SCALE + bias_ref[b] for b in range(count)]
    top = functools.reduce(jnp.maximum, scores)
    top = jnp.max(top, axis=0, keepdims=True)
    shifted = [jnp.exp(s - top) for s in scores]
    total = jnp.sum(functools.reduce(jnp.add, shifted), axis=0, keepdims=True)
    inverse = 1.0 / total
    probs = [s * inverse for s in shifted]
    lows = [p.astype(BF16) for p in probs]
    attended = functools.reduce(jnp.add, [dot_tn(lows[b], values[b]) for b in range(count)])
    attended = attended.astype(BF16).astype(F32)
    delta = jnp.sum((do.astype(F32) * attended).T, axis=0, keepdims=True)
    grads = [
        (probs[b] * (dot_nt(values[b], do) - delta)).astype(BF16) for b in range(count)
    ]
    dq = functools.reduce(jnp.add, [dot_tn(grads[b], keys[b]) for b in range(count)])
    dq = (dq * SCALE).astype(BF16)
    gq_ref[...] = dot_tn(tr_ref[...], dq)
    lowq_ref[...] += dot_nt(dq, aq)
    both = jnp.concatenate([ak, av], axis=1)
    for b in range(count):
        dk = (dot_nn(grads[b], query) * SCALE).astype(BF16)
        dv = dot_nn(lows[b], do).astype(BF16)
        part = jnp.concatenate([dk, dv], axis=1)
        low_ref[b * rows : (b + 1) * rows, :] += dot_nt(part, both)
        out = dot_nn(tt_ref[:, b * rows : (b + 1) * rows], part)
        if b == 0:
            total_part = out
        else:
            total_part += out
    gk_ref[...] = total_part[:, :DH]
    gv_ref[...] = total_part[:, DH:]


def attention(bias, fq, do, fk, fv, t, tr, tt, aq, ak, av, payloads):
    rows, width = fq.shape
    heads = width // DH
    rank = t.shape[1]
    blocks = len(payloads)
    count = blocks + 2

    def col(r):
        return pl.BlockSpec((r, DH), lambda h: (0, h))

    def whole(shape):
        return pl.BlockSpec(shape, lambda h: (0, 0))

    return pl.pallas_call(
        functools.partial(attention_kernel, blocks),
        grid=(heads,),
        out_shape=[
            jax.ShapeDtypeStruct((rank, width), F32),
            jax.ShapeDtypeStruct((rank, width), F32),
            jax.ShapeDtypeStruct((rank, width), F32),
            jax.ShapeDtypeStruct((rows, rank), F32),
            jax.ShapeDtypeStruct((count * rows, rank), F32),
        ],
        in_specs=[pl.BlockSpec(memory_space=pltpu.SMEM)]
        + [col(rows), col(rows), col(2 * rows), col(2 * rows)]
        + [whole(t.shape), whole(tr.shape), whole(tt.shape)]
        + [col(rank)] * 3
        + [col(rows)] * blocks
        + [pl.BlockSpec((rows, DH), lambda h: (0, heads + h))] * blocks,
        out_specs=[col(rank)] * 3 + [whole((rows, rank)), whole((count * rows, rank))],
        compiler_params=pltpu.CompilerParams(vmem_limit_bytes=32 * 1024 * 1024),
    )(bias, fq, do, fk, fv, t, tr, tt, aq, ak, av, *payloads, *payloads)


def sum_rows(part, frame_idx, half_idx, frames):
    rows, width = part.shape
    half = width // 2
    keep = lax.dynamic_slice_in_dim(part, half_idx * half, half, 1)
    give = lax.dynamic_slice_in_dim(part, (1 - half_idx) * half, half, 1)
    mine = keep + swap(give, "rep")
    if frames & (frames - 1) or rows % frames or frames > REACH + 1:
        total = lax.psum(mine, "tm").astype(BF16)
    else:
        chunk = rows // frames
        low = mine.astype(BF16)
        acc = lax.dynamic_slice_in_dim(mine, frame_idx * chunk, chunk, 0)
        for m in range(1, frames):
            give = lax.dynamic_slice_in_dim(low, (frame_idx ^ m) * chunk, chunk, 0)
            acc = acc + lax.ppermute(give, "tm", [(i, i ^ m) for i in range(frames)]).astype(F32)
        acc = acc.astype(BF16)
        total = jnp.zeros((rows, half), BF16)
        total = lax.dynamic_update_slice_in_dim(total, acc, frame_idx * chunk, 0)
        for m in range(1, frames):
            got = lax.ppermute(acc, "tm", [(i, i ^ m) for i in range(frames)])
            total = lax.dynamic_update_slice_in_dim(total, got, (frame_idx ^ m) * chunk, 0)
    other = swap(total, "rep")
    first = jnp.where(half_idx == 0, total, other)
    second = jnp.where(half_idx == 0, other, total)
    return jnp.concatenate([first, second], axis=1).astype(F32)


def window_plan(
    frozen_query,
    frozen_key,
    frozen_value,
    token_adapter_input,
    query_adapter_out,
    key_adapter_out,
    value_adapter_out,
    out_grad,
    band_width,
):
    rows, width = frozen_query.shape
    rank = token_adapter_input.shape[1]
    frames = band_width.shape[0]
    frame_idx = lax.axis_index("tm")
    half_idx = lax.axis_index("rep")
    t = token_adapter_input
    tr = lax.dynamic_slice_in_dim(t, half_idx * rows, rows, 0)

    def tile_rows_of(frozen, adapter):
        own = lax.dynamic_slice_in_dim(frozen, half_idx * rows, rows, 0)
        return (own.astype(F32) + dot_nn(tr, adapter)).astype(BF16)

    payload = jnp.concatenate(
        [tile_rows_of(frozen_key, key_adapter_out), tile_rows_of(frozen_value, value_adapter_out), tr],
        axis=1,
    )

    frame_ids = jnp.arange(frames)
    band_row = jnp.sum(jnp.where((frame_ids == frame_idx)[:, None], band_width, 0), axis=0)

    def band_at(offsets):
        seen = functools.reduce(jnp.logical_or, [frame_ids == frame_idx + o for o in offsets])
        return jnp.sum(jnp.where(seen, band_row, 0))

    own_band = band_at((0,))
    allowed = [jnp.abs(half_idx - tile) < own_band for tile in range(2)]
    payloads = []
    plan = routes(frames)
    for d, offsets in plan:
        got = lax.ppermute(payload, "tm", pairs(frames, offsets))
        band = band_at(offsets)
        payloads.append(got)
        allowed.append(band > 0)
        if d <= NEAR:
            payloads.append(swap(got, "rep"))
            allowed.append(band > 1)
    bias = jnp.where(jnp.stack(allowed), 0.0, -jnp.inf).astype(F32)
    tt = jnp.concatenate([t] + [p[:, 2 * width :] for p in payloads], axis=0).T

    gq, gk, gv, low_q, low_b = attention(
        bias, frozen_query, out_grad, frozen_key, frozen_value, t, tr, tt,
        query_adapter_out, key_adapter_out, value_adapter_out, payloads,
    )

    own = low_b[: 2 * rows]
    same = lax.dynamic_slice_in_dim(own, half_idx * rows, rows, 0) + low_q
    other = lax.dynamic_slice_in_dim(own, (1 - half_idx) * rows, rows, 0)
    start = 2 * rows
    for d, offsets in plan:
        size = 2 * rows if d <= NEAR else rows
        back = [(target, source) for source, target in pairs(frames, offsets)]
        got = lax.ppermute(low_b[start : start + size], "tm", back)
        start += size
        same = same + got[:rows]
        if d <= NEAR:
            other = other + got[rows:]
    low = jnp.where(
        half_idx == 0,
        jnp.concatenate([same, other], axis=0),
        jnp.concatenate([other, same], axis=0),
    )
    low = low + swap(low, "rep")
    low = low + swap(low, "head")

    grads = sum_rows(jnp.concatenate([gq, gk, gv], axis=0), frame_idx, half_idx, frames)
    return grads[:rank], grads[rank : 2 * rank], grads[2 * rank :], low


def head_table(heads, frames):
    base, extra = divmod(heads, frames)
    lead = (frames - extra) // 2
    counts = [base + (1 if lead <= j < lead + extra else 0) for j in range(frames)]
    return [sum(counts[:j]) for j in range(frames)], counts


def lookup(table, index):
    value = jnp.int32(table[0])
    for j in range(1, len(table)):
        value = jnp.where(index == j, jnp.int32(table[j]), value)
    return value


def column(head):
    return pl.ds(pl.multiple_of(head * DH, DH), DH)


def vmem(count):
    return [pl.BlockSpec(memory_space=pltpu.VMEM)] * count


def pack_kernel(frames, outputs, fq_ref, do_ref, fk_ref, fv_ref, t_ref, *refs):
    outs, (q_in, do_in, k_in, v_in, k2_in, v2_in, t_in, sems) = refs[:-8], refs[-8:]
    wanted = {what for parts in outputs for _, _, what in parts}
    me, half = lax.axis_index("tm"), lax.axis_index("rep")
    rows = fq_ref.shape[0]
    mine = pl.ds(pl.multiple_of(half * rows, rows), rows)
    rest = pl.ds(pl.multiple_of((1 - half) * rows, rows), rows)
    moves = [
        (fq_ref, q_in), (do_ref, do_in), (fk_ref.at[mine, :], k_in), (fv_ref.at[mine, :], v_in), (t_ref, t_in)
    ]
    if "other" in wanted:
        moves += [(fk_ref.at[rest, :], k2_in), (fv_ref.at[rest, :], v2_in)]
    copies = [pltpu.make_async_copy(a, b, sems.at[n]) for n, (a, b) in enumerate(moves)]
    for copy in copies:
        copy.start()
    for copy in copies:
        copy.wait()
    for out, parts in zip(outs, outputs):
        at = 0
        for table, m, what in parts:
            if what in ("t", "other t"):
                blocks = [t_in[mine if what == "t" else rest, :]]
            else:
                cols = column(lookup(table, me ^ m))
                sources = (q_in, do_in, k_in, v_in) if what == "mine" else (k2_in, v2_in)
                blocks = [ref[:, cols] for ref in sources]
            for block in blocks:
                out[:, at : at + block.shape[1]] = block
                at += block.shape[1]


def pack(frames, outputs, limit, fq, do, fk, fv, t):
    rows, width = fq.shape
    size = {"mine": 4 * DH, "other": 2 * DH, "t": t.shape[1], "other t": t.shape[1]}
    return pl.pallas_call(
        functools.partial(pack_kernel, frames, outputs),
        in_specs=[pl.BlockSpec(memory_space=pltpu.HBM)] * 5,
        out_specs=vmem(len(outputs)),
        out_shape=[
            jax.ShapeDtypeStruct((rows, sum(size[what] for _, _, what in parts)), BF16)
            for parts in outputs
        ],
        scratch_shapes=[pltpu.VMEM((rows, width), BF16)] * 6
        + [pltpu.VMEM(t.shape, BF16), pltpu.SemaphoreType.DMA((7,))],
        compiler_params=pltpu.CompilerParams(vmem_limit_bytes=limit * 1024 * 1024),
    )(fq, do, fk, fv, t)


def pick_kernel(spans, groups, *refs):
    n = 0
    for out, count in zip(refs[-len(groups) :], groups):
        for at in range(count):
            start, size = spans[n]
            out[:, at * size : (at + 1) * size] = refs[n][:, start : start + size]
            n += 1


def pick(parts, size, groups, after=()):
    arrays = [array for array, _ in parts]
    rows, dtype = arrays[0].shape[0], arrays[0].dtype
    return pl.pallas_call(
        functools.partial(pick_kernel, [(start, size) for _, start in parts], groups),
        in_specs=vmem(len(arrays)) + [pl.BlockSpec(memory_space=pl.ANY)] * len(after),
        out_specs=vmem(len(groups)),
        out_shape=[jax.ShapeDtypeStruct((rows, size * count), dtype) for count in groups],
        compiler_params=SMALL,
    )(*arrays, *after)


def one_head(frames, bands, q, do, frozen_k, frozen_v, tokens, aq, ak, av):
    flat = q.shape[0]
    rows = flat // frames
    t_same = tokens[:flat]

    def adapted(frozen, rows_of, adapter):
        return (frozen.astype(F32) + dot_nn(rows_of, adapter)).astype(BF16)

    query = adapted(q, t_same, aq)
    keys, values = adapted(frozen_k, tokens, ak), adapted(frozen_v, tokens, av)
    do_t, keys_t, values_t = do.T, keys.T, values.T

    def bias(i, b):
        j, need = (b, 0) if b < frames else (b - frames, 1)
        value = jnp.where(bands[i, j] > need, 0.0, -jnp.inf).astype(F32)
        return jnp.full((1, rows), value, F32)

    span = 2 if frames % 2 == 0 else 1
    wide = span * rows
    groups = [range(first, first + span) for first in range(0, frames, span)]
    seen = [
        list(range(frames))
        + [frames + j for j in range(frames) if any(abs(i - j) <= NEAR for i in mine)]
        for mine in groups
    ]
    here = [slice(mine[0] * rows, mine[0] * rows + wide) for mine in groups]
    pairs_of = range(len(groups))

    def gather(whole, g, axis):
        parts = [
            whole[b * rows : (b + 1) * rows] if axis == 0 else whole[:, b * rows : (b + 1) * rows]
            for b in seen[g]
        ]
        return jnp.concatenate(parts, axis=axis)

    def block(whole, n):
        return whole[n * rows : (n + 1) * rows]

    def softmax(g, raw):
        scores = [
            block(raw, n) * SCALE_2 + jnp.concatenate([bias(i, b) for i in groups[g]], axis=1)
            for n, b in enumerate(seen[g])
        ]
        top = jnp.max(functools.reduce(jnp.maximum, scores), axis=0, keepdims=True)
        shifted = [jnp.exp2(s - top) for s in scores]
        inverse = 1.0 / jnp.sum(functools.reduce(jnp.add, shifted), axis=0, keepdims=True)
        return [s * inverse for s in shifted]

    raws = [dot_nt(gather(keys, g, 0), query[here[g]]) for g in pairs_of]
    prob_grads = [dot_nt(gather(values, g, 0), do[here[g]]) for g in pairs_of]
    probs = [softmax(g, raws[g]) for g in pairs_of]
    lows = [jnp.concatenate([p.astype(BF16) for p in probs[g]], axis=0) for g in pairs_of]
    grads = []
    for g in pairs_of:
        attended = dot_nn(gather(values_t, g, 1), lows[g]).astype(BF16).astype(F32)
        delta = jnp.sum(do_t[:, here[g]].astype(F32) * attended, axis=0, keepdims=True)
        parts = [
            (probs[g][n] * (block(prob_grads[g], n) - delta)).astype(BF16) for n in range(len(seen[g]))
        ]
        grads.append(jnp.concatenate(parts, axis=0))
    dvs, dks = [None] * (2 * frames), [None] * (2 * frames)

    def add(sums, g, whole):
        for n, b in enumerate(seen[g]):
            sums[b] = block(whole, n) if sums[b] is None else sums[b] + block(whole, n)

    for g in pairs_of:
        add(dvs, g, dot_nn(lows[g], do[here[g]]))
    for g in pairs_of:
        add(dks, g, dot_nn(grads[g], query[here[g]]))
    dqs = [(dot_nn(gather(keys_t, g, 1), grads[g]) * SCALE).astype(BF16).T for g in pairs_of]
    dq = jnp.concatenate(dqs, axis=0)
    dk = (jnp.concatenate(dks, axis=0) * SCALE).astype(BF16)
    dv = jnp.concatenate(dvs, axis=0).astype(BF16)
    both = jnp.concatenate([dk, dv], axis=1)
    sums = dot_tn(tokens, both)
    grads = jnp.concatenate([dot_tn(t_same, dq), sums[:, :DH], sums[:, DH:]], axis=0)
    lows = dot_nt(both, jnp.concatenate([ak, av], axis=1))
    return grads, lows[:flat] + dot_nt(dq, aq), lows[flat:]


def group_kernel(heads, frames, chained, waits, sides, count, *refs):
    refs = list(refs)

    def take(count):
        taken = refs[:count]
        del refs[:count]
        return taken

    (bands,) = take(1)
    arrays, adapters = take(count), take(3)
    before = take(2) if chained else None
    take(waits)
    keep_ref, *give_refs = take(1 + GIVES if chained else 2)
    low_refs = [] if chained else take(2)
    q, do, k, v, tokens = refs
    me, half = lax.axis_index("tm"), lax.axis_index("rep")
    rows = arrays[0].shape[0]
    flat = frames * rows
    cut = 3 * tokens.shape[1] // 2
    first = half == 0
    same_at = [pl.ds(pl.multiple_of((me ^ m) * rows, rows), rows) for m in range(frames)]
    other_at = [pl.ds(pl.multiple_of(flat + (me ^ m) * rows, rows), rows) for m in range(frames)]

    def put(targets, places, rows_at):
        for m, (n, start) in enumerate(places):
            for c, target in enumerate(targets):
                target[rows_at[m], :] = arrays[n][:, start + c * DH : start + (c + 1) * DH]

    put([tokens], sides[0][0], same_at)
    put([tokens], sides[0][1], other_at)

    def run(n, table):
        put([q, do, k, v], sides[1 + n][0], same_at)
        put([k, v], sides[1 + n][1], other_at)
        cols = column(lookup(table, me))
        grads, low_same, low_other = one_head(
            frames, bands, q[...], do[...], k[...], v[...], tokens[...], *[a[:, cols] for a in adapters]
        )
        keep = jnp.where(first, grads[:cut], grads[cut:])
        give = jnp.where(first, grads[cut:], grads[:cut])
        return keep, give, low_same, low_other

    if chained:
        keep, give, low_same, low_other = run(0, heads[0][0])
        keep_ref[:cut, :] = keep
        keep_ref[cut:, :] = before[0][...] + low_same
        give = jnp.concatenate([give, before[1][...] + low_other], axis=0)
        size = give.shape[0] // GIVES
        for n, ref in enumerate(give_refs):
            ref[...] = give[n * size : (n + 1) * size].astype(ref.dtype)
        return
    for n, (table, counts) in enumerate(heads):
        here = slice(n * cut, (n + 1) * cut)

        def body():
            keep, give, low_same, low_other = run(n, table)
            keep_ref[here, :] = keep
            give_refs[0][here, :] = give.astype(BF16)
            if n == 0:
                low_refs[0][...] = low_same
                low_refs[1][...] = low_other
            else:
                low_refs[0][...] += low_same
                low_refs[1][...] += low_other

        if min(counts) > 0:
            body()
        else:
            live = lookup(counts, me) > 0
            pl.when(live)(body)

            @pl.when(jnp.logical_not(live))
            def _():
                keep_ref[here, :] = jnp.zeros((cut, DH), F32)
                give_refs[0][here, :] = jnp.zeros((cut, DH), BF16)


def head_group(heads, bands, sides, adapters, before=(), after=()):
    frames = len(sides[0][0])
    arrays, places = [], []
    for side in sides:
        found = []
        for pairs_of in side:
            found.append([])
            for array, start in pairs_of:
                known = [n for n, a in enumerate(arrays) if a is array]
                if not known:
                    arrays.append(array)
                found[-1].append((known[0] if known else len(arrays) - 1, start))
        places.append(found)
    rows, rank = arrays[0].shape[0], adapters[0].shape[0]
    flat = frames * rows
    size = len(heads) * 3 * rank // 2
    chained = len(before) > 0
    args = [bands, *arrays, *adapters, *before, *after]
    specs = [pl.BlockSpec(memory_space=pltpu.SMEM)] + vmem(len(arrays) + 3 + len(before))
    specs += [pl.BlockSpec(memory_space=pl.ANY)] * len(after)
    low = jax.ShapeDtypeStruct((flat, rank), F32)
    if chained:
        part = jax.ShapeDtypeStruct(((size + flat) // GIVES, rank), BF16)
        shapes = [jax.ShapeDtypeStruct((size + flat, rank), F32)] + [part] * GIVES
    else:
        edge = jax.ShapeDtypeStruct((size, rank), F32)
        shapes = [edge, jax.ShapeDtypeStruct((size, rank), BF16), low, low]
    return pl.pallas_call(
        functools.partial(
            group_kernel, heads, frames, chained, len(after), places, len(arrays)
        ),
        in_specs=specs,
        out_specs=vmem(len(shapes)),
        out_shape=shapes,
        scratch_shapes=[pltpu.VMEM((flat, DH), BF16)] * 2
        + [pltpu.VMEM((2 * flat, DH), BF16)] * 2
        + [pltpu.VMEM((2 * flat, rank), BF16)],
        compiler_params=pltpu.CompilerParams(vmem_limit_bytes=40 * 1024 * 1024),
    )(*args)


def hand_out_kernel(frames, size, parts, keep_ref, *refs):
    gots, (own_ref, *sends, total) = refs[:parts], refs[-frames - 1 :]
    me = lax.axis_index("tm")
    rows = own_ref.shape[0]
    total[...] = keep_ref[...] + jnp.concatenate([got[...].astype(F32) for got in gots], axis=0)
    for m in range(frames):
        low = total[pl.ds(pl.multiple_of(size + (me ^ m) * rows, 8), rows), :]
        if m == 0:
            own_ref[...] = low
        else:
            sends[m - 1][:rows, :] = low.astype(BF16)
            sends[m - 1][rows:, :] = total[:size, :].astype(BF16)


def hand_out(frames, rows, keep, gots, after):
    size, rank = keep.shape[0] - frames * rows, keep.shape[1]
    own, *sends = pl.pallas_call(
        functools.partial(hand_out_kernel, frames, size, len(gots)),
        in_specs=vmem(1 + len(gots)) + [pl.BlockSpec(memory_space=pl.ANY)] * len(after),
        out_specs=vmem(frames),
        out_shape=[jax.ShapeDtypeStruct((rows, rank), F32)]
        + [jax.ShapeDtypeStruct((rows + size, rank), BF16)] * (frames - 1),
        scratch_shapes=[pltpu.VMEM(keep.shape, F32)],
        compiler_params=SMALL,
    )(keep, *gots, *after)
    return own, sends


def relay_kernel(wide, piece, facing, lead_ref, rest_ref):
    size = lead_ref.shape[0]
    middle = lookup(wide, lax.axis_index("tm")) > 0
    lead_ref[...] = jnp.where(middle, facing[:size, :], piece[:size, :])
    rest_ref[...] = facing[size:, :]


def relay(wide, piece, facing):
    half = jax.ShapeDtypeStruct((piece.shape[0] // 2, piece.shape[1]), piece.dtype)
    return pl.pallas_call(
        functools.partial(relay_kernel, wide),
        in_specs=vmem(2),
        out_specs=vmem(2),
        out_shape=[half, half],
        compiler_params=SMALL,
    )(piece, facing)


def collect_kernel(wide, own_low, own, near, third, last, piece, pair, facing, lead_far, rest_far, *outs):
    out_ref, low_ref = outs
    rows = own_low.shape[0]
    size = own.shape[0] - rows
    low = own_low[...]
    for got in (near, third, last):
        low = low + got[:rows, :].astype(F32)
    out_ref[:rows, :] = low.astype(BF16)
    low_ref[...] = low.astype(BF16)
    middle = lookup(wide, lax.axis_index("tm")) > 0
    blocks = [ref[rows:, :] for ref in (own, near, third, last)]
    blocks += [piece[:size, :], pair[:size, :], lead_far[...], facing[:size, :]]
    blocks.append(jnp.where(middle, piece[size:, :], pair[size:, :]))
    blocks.append(jnp.where(middle, facing[size:, :], rest_far[...]))
    for n, block in enumerate(blocks):
        out_ref[rows + n * size : rows + (n + 1) * size, :] = block


def collect(wide, own_low, own, gots, *pieces):
    (rows, rank), size = own_low.shape, pieces[0].shape[0] // 2
    return pl.pallas_call(
        functools.partial(collect_kernel, wide),
        in_specs=vmem(2 + len(gots) + len(pieces)),
        out_specs=vmem(2),
        out_shape=[
            jax.ShapeDtypeStruct((rows + 10 * size, rank), BF16),
            jax.ShapeDtypeStruct((rows, rank), BF16),
        ],
        compiler_params=SMALL,
    )(own_low, own, *gots, *pieces)


def place_kernel(frames, lead, late, rest, tail, tail2, low_head, low_diag, *refs):
    outs, filled, sems = refs[:4], refs[4:8], refs[8]
    me, half = lax.axis_index("tm"), lax.axis_index("rep")
    first = half == 0
    rank = filled[0].shape[0]
    cut = 3 * rank // 2
    rows = low_head.shape[0]
    side = me // 2
    places = [lookup(late, me ^ m) for m in range(frames)] + [lookup(lead, me ^ m) for m in range(frames)]
    places += [lookup(rest, 1 + side), lookup(rest, 2 - side)]
    copies = [pltpu.make_async_copy(filled[o], outs[o], sems.at[o]) for o in range(4)]

    def rows_of(ref, n, start, stop):
        return ref[rows + n * cut + start : rows + n * cut + stop, :].astype(F32)

    for o in range(3):
        for n, head in enumerate(places):
            parts = []
            for owner, low_end, high_end in ((0, 0, cut), (1, cut, 2 * cut)):
                start, stop = max(o * rank, low_end), min((o + 1) * rank, high_end)
                if start < stop:
                    mine, its = (rows_of(ref, n, start - low_end, stop - low_end) for ref in (tail, tail2))
                    parts.append(jnp.where(first, mine, its) if owner == 0 else jnp.where(first, its, mine))
            filled[o][:, column(head)] = parts[0] if len(parts) == 1 else jnp.concatenate(parts, axis=0)
        copies[o].start()
    same = tail[:rows, :].astype(F32) + low_head[...].astype(F32)
    other = tail2[:rows, :].astype(F32) + low_diag[...].astype(F32)
    filled[3][:rows, :] = jnp.where(first, same, other)
    filled[3][rows:, :] = jnp.where(first, other, same)
    copies[3].start()
    for copy in copies:
        copy.wait()


def place(frames, lead, late, rest, tail, tail2, low_head, low_diag, rank, width):
    rows = low_head.shape[0]
    shapes = [(rank, width)] * 3 + [(2 * rows, rank)]
    return pl.pallas_call(
        functools.partial(place_kernel, frames, lead, late, rest),
        in_specs=vmem(4),
        out_specs=[pl.BlockSpec(memory_space=pl.ANY)] * 4,
        out_shape=[jax.ShapeDtypeStruct(shape, F32) for shape in shapes],
        scratch_shapes=[pltpu.VMEM(shape, F32) for shape in shapes] + [pltpu.SemaphoreType.DMA((4,))],
        compiler_params=SMALL,
    )(tail, tail2, low_head, low_diag)


def exchange_plan(
    frozen_query,
    frozen_key,
    frozen_value,
    token_adapter_input,
    query_adapter_out,
    key_adapter_out,
    value_adapter_out,
    out_grad,
    band_width,
):
    rows, width = frozen_query.shape
    rank = token_adapter_input.shape[1]
    frames = band_width.shape[0]
    heads = width // DH
    starts, counts = head_table(heads, frames)
    most = max(counts)
    columns = [[min(starts[j] + s, heads - 1) for j in range(frames)] for s in range(most)]
    numbers = [[int(s < counts[j]) for j in range(frames)] for s in range(most)]
    slots = list(zip(columns, numbers))
    lead, late, rest = slots[0], slots[1], slots[2]
    wide = [j for j in range(frames) if counts[j] == most]
    adapters = [query_adapter_out, key_adapter_out, value_adapter_out]
    arrays = (frozen_query, out_grad, frozen_key, frozen_value, token_adapter_input)

    def meet(name, block, m, targets=range(frames)):
        with jax.named_scope(f"{name}_over_tm"):
            return lax.ppermute(block, "tm", [(j ^ m, j) for j in targets])

    def swap_in_chip(name, block):
        with jax.named_scope(f"{name}_in_chip"):
            return swap(block, "rep")

    def mine(slot, m):
        return (slot[0], m, "mine")

    sent, kept, sent_late = [], [], []
    for m in range(1, frames):
        first = [mine(lead, m), (None, m, "t")]
        if m == 1:
            sent.append(first + [mine(rest, m), mine(late, m)])
        else:
            sent += [first, [mine(rest, m)]]
            sent_late.append([mine(late, m)])
    for slot in (lead, rest, late):
        kept += [[mine(slot, 0)], [(slot[0], 0, "other")]]
    kept += [[(None, 0, "t")], [(None, 0, "other t")]]
    packed = pack(frames, sent, 56, *arrays)
    packed_late = pack(frames, sent_late + kept, 16, *arrays)
    kept = packed_late[len(sent_late) :]
    block = meet("nearest", packed[0], 1)
    lead_got, rest_got, late_got = [(block, 0)], [(block, 4 * DH + rank)], [(block, 8 * DH + rank)]
    for m in range(2, frames):
        lead_got.append((meet("lead", packed[2 * m - 3], m), 0))
        rest_got.append((meet("rest", packed[2 * m - 2], m, wide), 0))
        late_got.append((meet("late", packed_late[m - 2], m), 0))

    def sides(name, n, got, wide_t, groups, skip, after=()):
        size = 4 * DH - skip + (rank if wide_t else 0)
        picked = pick([(a, start + skip) for a, start in got], size, groups, after)
        cross = [swap_in_chip(name, block) for block in picked]
        where = 2 * DH - skip
        cross = [(block, at * size + where) for block, count in zip(cross, groups) for at in range(count)]
        rows_here = [(kept[2 * n], 0)] + got
        rows_there = [(kept[2 * n + 1], 0)] + cross
        return rows_here, rows_there, cross

    *lead_side, cross = sides("lead", 0, lead_got, True, (3,), 2 * DH, kept[:1])
    t_side = (
        [(kept[6], 0)] + [(a, start + 4 * DH) for a, start in lead_got],
        [(kept[7], 0)] + [(block, start + 2 * DH) for block, start in cross],
    )
    *rest_side, _ = sides("rest", 1, rest_got, False, (3,), 2 * DH)
    early = [lead, rest]
    keep, give, *low = head_group(early, band_width, [t_side, lead_side, rest_side], adapters)
    got = swap_in_chip("early_gradients", give)
    piece = (keep + got.astype(F32)).astype(BF16)
    *late_side, _ = sides("late", 2, late_got, False, (3,), 0, [got])
    pair = meet("early_gradients", piece, 1)
    facing = meet("early_gradients", piece, 3)
    keep, *gives = head_group([late], band_width, [t_side, late_side], adapters, low, [piece])
    gives = [swap_in_chip("late_sums", g) for g in gives]
    own_low, sends = hand_out(frames, rows, keep, gives, [pair])
    gots = [meet("late_sums", block, m) for m, block in enumerate(sends, 1)]
    lead_far, rest_far = relay(rest[1], piece, facing)
    with jax.named_scope("relayed_over_tm"):
        outward = [(1, 0), (2, 3)]
        lead_far = lax.ppermute(lead_far, "tm", [(0, 2), (3, 1), *outward])
        rest_far = lax.ppermute(rest_far, "tm", outward)
    tail, low = collect(rest[1], own_low, sends[2], gots, piece, pair, facing, lead_far, rest_far)
    diag = [(0, 3), (1, 2), (2, 1), (3, 0)]
    with jax.named_scope("low_over_head"):
        low_head, low_diag = swap(low, "head"), lax.ppermute(low, ("head", "rep"), diag)
    outs = place(
        frames, lead[0], late[0], rest[0], tail, swap_in_chip("tail", tail), low_head, low_diag, rank, width
    )
    return tuple(outs)


def on_device(frozen_query, *rest):
    frames = rest[-1].shape[0]
    heads = frozen_query.shape[1] // DH
    whole_reach = frames == 4 and heads == 2 * frames + 2
    return (exchange_plan if whole_reach else window_plan)(frozen_query, *rest)


def solution(mesh):
    in_specs = (
        P(("groups", "tm", "rep"), "head"),
        P(("groups", "tm"), "head"),
        P(("groups", "tm"), "head"),
        P(("groups", "tm"), None),
        P(None, "head"),
        P(None, "head"),
        P(None, "head"),
        P(("groups", "tm", "rep"), "head"),
        P(),
    )
    out_specs = (
        P("groups", "head"),
        P("groups", "head"),
        P("groups", "head"),
        P(("groups", "tm"), None),
    )
    return jax.shard_map(
        on_device, mesh=mesh, in_specs=in_specs, out_specs=out_specs, check_vma=False
    )
```

```python
import functools
import math

import jax
import jax.numpy as jnp
from jax import lax
from jax.experimental import pallas as pl
from jax.experimental.pallas import tpu as pltpu
from jax.sharding import PartitionSpec as P

DH = 128
NEAR = 1
REACH = 4
SCALE = DH ** (-0.5)
SCALE_2 = SCALE * math.log2(math.e)
F32 = jnp.float32
BF16 = jnp.bfloat16
GIVES = 2
SMALL = pltpu.CompilerParams(vmem_limit_bytes=16 * 1024 * 1024)


def dot_nn(left, right):
    return lax.dot_general(left, right, (((1,), (0,)), ((), ())), preferred_element_type=F32)


def dot_nt(left, right):
    return lax.dot_general(left, right, (((1,), (1,)), ((), ())), preferred_element_type=F32)


def dot_tn(left, right):
    return lax.dot_general(left, right, (((0,), (0,)), ((), ())), preferred_element_type=F32)


def routes(count):
    found = []
    for d in range(1, min(REACH, count - 1) + 1):
        if 2 * d >= count:
            found.append((d, (-d, d)))
        else:
            found.append((d, (-d,)))
            found.append((d, (d,)))
    return found


def pairs(count, offsets):
    return [(i + o, i) for o in offsets for i in range(count) if 0 <= i + o < count]


def swap(block, axis):
    return lax.ppermute(block, axis, [(0, 1), (1, 0)])


def attention_kernel(
    blocks, bias_ref, fq_ref, do_ref, fk_ref, fv_ref, t_ref, tr_ref, tt_ref, aq_ref, ak_ref, av_ref, *refs
):
    k_refs = refs[:blocks]
    v_refs = refs[blocks : 2 * blocks]
    gq_ref, gk_ref, gv_ref, lowq_ref, low_ref = refs[2 * blocks :]
    rows = fq_ref.shape[0]

    @pl.when(pl.program_id(0) == 0)
    def _():
        lowq_ref[...] = jnp.zeros_like(lowq_ref)
        low_ref[...] = jnp.zeros_like(low_ref)

    aq, ak, av = aq_ref[...], ak_ref[...], av_ref[...]
    query = (fq_ref[...].astype(F32) + dot_nn(tr_ref[...], aq)).astype(BF16)
    do = do_ref[...]
    own_k = (fk_ref[...].astype(F32) + dot_nn(t_ref[...], ak)).astype(BF16)
    own_v = (fv_ref[...].astype(F32) + dot_nn(t_ref[...], av)).astype(BF16)
    keys = [own_k[:rows], own_k[rows:]] + [ref[...] for ref in k_refs]
    values = [own_v[:rows], own_v[rows:]] + [ref[...] for ref in v_refs]
    count = len(keys)
    scores = [dot_nt(keys[b], query) * SCALE + bias_ref[b] for b in range(count)]
    top = functools.reduce(jnp.maximum, scores)
    top = jnp.max(top, axis=0, keepdims=True)
    shifted = [jnp.exp(s - top) for s in scores]
    total = jnp.sum(functools.reduce(jnp.add, shifted), axis=0, keepdims=True)
    inverse = 1.0 / total
    probs = [s * inverse for s in shifted]
    lows = [p.astype(BF16) for p in probs]
    attended = functools.reduce(jnp.add, [dot_tn(lows[b], values[b]) for b in range(count)])
    attended = attended.astype(BF16).astype(F32)
    delta = jnp.sum((do.astype(F32) * attended).T, axis=0, keepdims=True)
    grads = [
        (probs[b] * (dot_nt(values[b], do) - delta)).astype(BF16) for b in range(count)
    ]
    dq = functools.reduce(jnp.add, [dot_tn(grads[b], keys[b]) for b in range(count)])
    dq = (dq * SCALE).astype(BF16)
    gq_ref[...] = dot_tn(tr_ref[...], dq)
    lowq_ref[...] += dot_nt(dq, aq)
    both = jnp.concatenate([ak, av], axis=1)
    for b in range(count):
        dk = (dot_nn(grads[b], query) * SCALE).astype(BF16)
        dv = dot_nn(lows[b], do).astype(BF16)
        part = jnp.concatenate([dk, dv], axis=1)
        low_ref[b * rows : (b + 1) * rows, :] += dot_nt(part, both)
        out = dot_nn(tt_ref[:, b * rows : (b + 1) * rows], part)
        if b == 0:
            total_part = out
        else:
            total_part += out
    gk_ref[...] = total_part[:, :DH]
    gv_ref[...] = total_part[:, DH:]


def attention(bias, fq, do, fk, fv, t, tr, tt, aq, ak, av, payloads):
    rows, width = fq.shape
    heads = width // DH
    rank = t.shape[1]
    blocks = len(payloads)
    count = blocks + 2

    def col(r):
        return pl.BlockSpec((r, DH), lambda h: (0, h))

    def whole(shape):
        return pl.BlockSpec(shape, lambda h: (0, 0))

    return pl.pallas_call(
        functools.partial(attention_kernel, blocks),
        grid=(heads,),
        out_shape=[
            jax.ShapeDtypeStruct((rank, width), F32),
            jax.ShapeDtypeStruct((rank, width), F32),
            jax.ShapeDtypeStruct((rank, width), F32),
            jax.ShapeDtypeStruct((rows, rank), F32),
            jax.ShapeDtypeStruct((count * rows, rank), F32),
        ],
        in_specs=[pl.BlockSpec(memory_space=pltpu.SMEM)]
        + [col(rows), col(rows), col(2 * rows), col(2 * rows)]
        + [whole(t.shape), whole(tr.shape), whole(tt.shape)]
        + [col(rank)] * 3
        + [col(rows)] * blocks
        + [pl.BlockSpec((rows, DH), lambda h: (0, heads + h))] * blocks,
        out_specs=[col(rank)] * 3 + [whole((rows, rank)), whole((count * rows, rank))],
        compiler_params=pltpu.CompilerParams(vmem_limit_bytes=32 * 1024 * 1024),
    )(bias, fq, do, fk, fv, t, tr, tt, aq, ak, av, *payloads, *payloads)


def sum_rows(part, frame_idx, half_idx, frames):
    rows, width = part.shape
    half = width // 2
    keep = lax.dynamic_slice_in_dim(part, half_idx * half, half, 1)
    give = lax.dynamic_slice_in_dim(part, (1 - half_idx) * half, half, 1)
    mine = keep + swap(give, "rep")
    if frames & (frames - 1) or rows % frames or frames > REACH + 1:
        total = lax.psum(mine, "tm").astype(BF16)
    else:
        chunk = rows // frames
        low = mine.astype(BF16)
        acc = lax.dynamic_slice_in_dim(mine, frame_idx * chunk, chunk, 0)
        for m in range(1, frames):
            give = lax.dynamic_slice_in_dim(low, (frame_idx ^ m) * chunk, chunk, 0)
            acc = acc + lax.ppermute(give, "tm", [(i, i ^ m) for i in range(frames)]).astype(F32)
        acc = acc.astype(BF16)
        total = jnp.zeros((rows, half), BF16)
        total = lax.dynamic_update_slice_in_dim(total, acc, frame_idx * chunk, 0)
        for m in range(1, frames):
            got = lax.ppermute(acc, "tm", [(i, i ^ m) for i in range(frames)])
            total = lax.dynamic_update_slice_in_dim(total, got, (frame_idx ^ m) * chunk, 0)
    other = swap(total, "rep")
    first = jnp.where(half_idx == 0, total, other)
    second = jnp.where(half_idx == 0, other, total)
    return jnp.concatenate([first, second], axis=1).astype(F32)


def window_plan(
    frozen_query,
    frozen_key,
    frozen_value,
    token_adapter_input,
    query_adapter_out,
    key_adapter_out,
    value_adapter_out,
    out_grad,
    band_width,
):
    rows, width = frozen_query.shape
    rank = token_adapter_input.shape[1]
    frames = band_width.shape[0]
    frame_idx = lax.axis_index("tm")
    half_idx = lax.axis_index("rep")
    t = token_adapter_input
    tr = lax.dynamic_slice_in_dim(t, half_idx * rows, rows, 0)

    def tile_rows_of(frozen, adapter):
        own = lax.dynamic_slice_in_dim(frozen, half_idx * rows, rows, 0)
        return (own.astype(F32) + dot_nn(tr, adapter)).astype(BF16)

    payload = jnp.concatenate(
        [tile_rows_of(frozen_key, key_adapter_out), tile_rows_of(frozen_value, value_adapter_out), tr],
        axis=1,
    )

    frame_ids = jnp.arange(frames)
    band_row = jnp.sum(jnp.where((frame_ids == frame_idx)[:, None], band_width, 0), axis=0)

    def band_at(offsets):
        seen = functools.reduce(jnp.logical_or, [frame_ids == frame_idx + o for o in offsets])
        return jnp.sum(jnp.where(seen, band_row, 0))

    own_band = band_at((0,))
    allowed = [jnp.abs(half_idx - tile) < own_band for tile in range(2)]
    payloads = []
    plan = routes(frames)
    for d, offsets in plan:
        got = lax.ppermute(payload, "tm", pairs(frames, offsets))
        band = band_at(offsets)
        payloads.append(got)
        allowed.append(band > 0)
        if d <= NEAR:
            payloads.append(swap(got, "rep"))
            allowed.append(band > 1)
    bias = jnp.where(jnp.stack(allowed), 0.0, -jnp.inf).astype(F32)
    tt = jnp.concatenate([t] + [p[:, 2 * width :] for p in payloads], axis=0).T

    gq, gk, gv, low_q, low_b = attention(
        bias, frozen_query, out_grad, frozen_key, frozen_value, t, tr, tt,
        query_adapter_out, key_adapter_out, value_adapter_out, payloads,
    )

    own = low_b[: 2 * rows]
    same = lax.dynamic_slice_in_dim(own, half_idx * rows, rows, 0) + low_q
    other = lax.dynamic_slice_in_dim(own, (1 - half_idx) * rows, rows, 0)
    start = 2 * rows
    for d, offsets in plan:
        size = 2 * rows if d <= NEAR else rows
        back = [(target, source) for source, target in pairs(frames, offsets)]
        got = lax.ppermute(low_b[start : start + size], "tm", back)
        start += size
        same = same + got[:rows]
        if d <= NEAR:
            other = other + got[rows:]
    low = jnp.where(
        half_idx == 0,
        jnp.concatenate([same, other], axis=0),
        jnp.concatenate([other, same], axis=0),
    )
    low = low + swap(low, "rep")
    low = low + swap(low, "head")

    grads = sum_rows(jnp.concatenate([gq, gk, gv], axis=0), frame_idx, half_idx, frames)
    return grads[:rank], grads[rank : 2 * rank], grads[2 * rank :], low


def head_table(heads, frames):
    base, extra = divmod(heads, frames)
    lead = (frames - extra) // 2
    counts = [base + (1 if lead <= j < lead + extra else 0) for j in range(frames)]
    return [sum(counts[:j]) for j in range(frames)], counts


def lookup(table, index):
    value = jnp.int32(table[0])
    for j in range(1, len(table)):
        value = jnp.where(index == j, jnp.int32(table[j]), value)
    return value


def column(head):
    return pl.ds(pl.multiple_of(head * DH, DH), DH)


def vmem(count):
    return [pl.BlockSpec(memory_space=pltpu.VMEM)] * count


def pack_kernel(frames, outputs, fq_ref, do_ref, fk_ref, fv_ref, t_ref, *refs):
    outs, (q_in, do_in, k_in, v_in, k2_in, v2_in, t_in, sems) = refs[:-8], refs[-8:]
    wanted = {what for parts in outputs for _, _, what in parts}
    me, half = lax.axis_index("tm"), lax.axis_index("rep")
    rows = fq_ref.shape[0]
    mine = pl.ds(pl.multiple_of(half * rows, rows), rows)
    rest = pl.ds(pl.multiple_of((1 - half) * rows, rows), rows)
    moves = [
        (fq_ref, q_in), (do_ref, do_in), (fk_ref.at[mine, :], k_in), (fv_ref.at[mine, :], v_in), (t_ref, t_in)
    ]
    if "other" in wanted:
        moves += [(fk_ref.at[rest, :], k2_in), (fv_ref.at[rest, :], v2_in)]
    copies = [pltpu.make_async_copy(a, b, sems.at[n]) for n, (a, b) in enumerate(moves)]
    for copy in copies:
        copy.start()
    for copy in copies:
        copy.wait()
    for out, parts in zip(outs, outputs):
        at = 0
        for table, m, what in parts:
            if what in ("t", "other t"):
                blocks = [t_in[mine if what == "t" else rest, :]]
            else:
                cols = column(lookup(table, me ^ m))
                sources = (q_in, do_in, k_in, v_in) if what == "mine" else (k2_in, v2_in)
                blocks = [ref[:, cols] for ref in sources]
            for block in blocks:
                out[:, at : at + block.shape[1]] = block
                at += block.shape[1]


def pack(frames, outputs, limit, fq, do, fk, fv, t):
    rows, width = fq.shape
    size = {"mine": 4 * DH, "other": 2 * DH, "t": t.shape[1], "other t": t.shape[1]}
    return pl.pallas_call(
        functools.partial(pack_kernel, frames, outputs),
        in_specs=[pl.BlockSpec(memory_space=pltpu.HBM)] * 5,
        out_specs=vmem(len(outputs)),
        out_shape=[
            jax.ShapeDtypeStruct((rows, sum(size[what] for _, _, what in parts)), BF16)
            for parts in outputs
        ],
        scratch_shapes=[pltpu.VMEM((rows, width), BF16)] * 6
        + [pltpu.VMEM(t.shape, BF16), pltpu.SemaphoreType.DMA((7,))],
        compiler_params=pltpu.CompilerParams(vmem_limit_bytes=limit * 1024 * 1024),
    )(fq, do, fk, fv, t)


def pick_kernel(spans, groups, *refs):
    n = 0
    for out, count in zip(refs[-len(groups) :], groups):
        for at in range(count):
            start, size = spans[n]
            out[:, at * size : (at + 1) * size] = refs[n][:, start : start + size]
            n += 1


def pick(parts, size, groups, after=()):
    arrays = [array for array, _ in parts]
    rows, dtype = arrays[0].shape[0], arrays[0].dtype
    return pl.pallas_call(
        functools.partial(pick_kernel, [(start, size) for _, start in parts], groups),
        in_specs=vmem(len(arrays)) + [pl.BlockSpec(memory_space=pl.ANY)] * len(after),
        out_specs=vmem(len(groups)),
        out_shape=[jax.ShapeDtypeStruct((rows, size * count), dtype) for count in groups],
        compiler_params=SMALL,
    )(*arrays, *after)


def one_head(frames, bands, q, do, frozen_k, frozen_v, tokens, aq, ak, av):
    flat = q.shape[0]
    rows = flat // frames
    t_same = tokens[:flat]

    def adapted(frozen, rows_of, adapter):
        return (frozen.astype(F32) + dot_nn(rows_of, adapter)).astype(BF16)

    query = adapted(q, t_same, aq)
    keys, values = adapted(frozen_k, tokens, ak), adapted(frozen_v, tokens, av)
    do_t, keys_t, values_t = do.T, keys.T, values.T

    def bias(i, b):
        j, need = (b, 0) if b < frames else (b - frames, 1)
        value = jnp.where(bands[i, j] > need, 0.0, -jnp.inf).astype(F32)
        return jnp.full((1, rows), value, F32)

    span = 2 if frames % 2 == 0 else 1
    wide = span * rows
    groups = [range(first, first + span) for first in range(0, frames, span)]
    seen = [
        list(range(frames))
        + [frames + j for j in range(frames) if any(abs(i - j) <= NEAR for i in mine)]
        for mine in groups
    ]
    here = [slice(mine[0] * rows, mine[0] * rows + wide) for mine in groups]
    pairs_of = range(len(groups))

    def gather(whole, g, axis):
        parts = [
            whole[b * rows : (b + 1) * rows] if axis == 0 else whole[:, b * rows : (b + 1) * rows]
            for b in seen[g]
        ]
        return jnp.concatenate(parts, axis=axis)

    def block(whole, n):
        return whole[n * rows : (n + 1) * rows]

    def softmax(g, raw):
        scores = [
            block(raw, n) * SCALE_2 + jnp.concatenate([bias(i, b) for i in groups[g]], axis=1)
            for n, b in enumerate(seen[g])
        ]
        top = jnp.max(functools.reduce(jnp.maximum, scores), axis=0, keepdims=True)
        shifted = [jnp.exp2(s - top) for s in scores]
        inverse = 1.0 / jnp.sum(functools.reduce(jnp.add, shifted), axis=0, keepdims=True)
        return [s * inverse for s in shifted]

    raws = [dot_nt(gather(keys, g, 0), query[here[g]]) for g in pairs_of]
    prob_grads = [dot_nt(gather(values, g, 0), do[here[g]]) for g in pairs_of]
    probs = [softmax(g, raws[g]) for g in pairs_of]
    lows = [jnp.concatenate([p.astype(BF16) for p in probs[g]], axis=0) for g in pairs_of]
    grads = []
    for g in pairs_of:
        attended = dot_nn(gather(values_t, g, 1), lows[g]).astype(BF16).astype(F32)
        delta = jnp.sum(do_t[:, here[g]].astype(F32) * attended, axis=0, keepdims=True)
        parts = [
            (probs[g][n] * (block(prob_grads[g], n) - delta)).astype(BF16) for n in range(len(seen[g]))
        ]
        grads.append(jnp.concatenate(parts, axis=0))
    dvs, dks = [None] * (2 * frames), [None] * (2 * frames)

    def add(sums, g, whole):
        for n, b in enumerate(seen[g]):
            sums[b] = block(whole, n) if sums[b] is None else sums[b] + block(whole, n)

    for g in pairs_of:
        add(dvs, g, dot_nn(lows[g], do[here[g]]))
    for g in pairs_of:
        add(dks, g, dot_nn(grads[g], query[here[g]]))
    dqs = [(dot_nn(gather(keys_t, g, 1), grads[g]) * SCALE).astype(BF16).T for g in pairs_of]
    dq = jnp.concatenate(dqs, axis=0)
    dk = (jnp.concatenate(dks, axis=0) * SCALE).astype(BF16)
    dv = jnp.concatenate(dvs, axis=0).astype(BF16)
    both = jnp.concatenate([dk, dv], axis=1)
    sums = dot_tn(tokens, both)
    grads = jnp.concatenate([dot_tn(t_same, dq), sums[:, :DH], sums[:, DH:]], axis=0)
    lows = dot_nt(both, jnp.concatenate([ak, av], axis=1))
    return grads, lows[:flat] + dot_nt(dq, aq), lows[flat:]


def group_kernel(heads, frames, chained, waits, sides, count, *refs):
    refs = list(refs)

    def take(count):
        taken = refs[:count]
        del refs[:count]
        return taken

    (bands,) = take(1)
    arrays, adapters = take(count), take(3)
    before = take(2) if chained else None
    take(waits)
    keep_ref, *give_refs = take(1 + GIVES if chained else 2)
    low_refs = [] if chained else take(2)
    q, do, k, v, tokens = refs
    me, half = lax.axis_index("tm"), lax.axis_index("rep")
    rows = arrays[0].shape[0]
    flat = frames * rows
    cut = 3 * tokens.shape[1] // 2
    first = half == 0
    same_at = [pl.ds(pl.multiple_of((me ^ m) * rows, rows), rows) for m in range(frames)]
    other_at = [pl.ds(pl.multiple_of(flat + (me ^ m) * rows, rows), rows) for m in range(frames)]

    def put(targets, places, rows_at):
        for m, (n, start) in enumerate(places):
            for c, target in enumerate(targets):
                target[rows_at[m], :] = arrays[n][:, start + c * DH : start + (c + 1) * DH]

    put([tokens], sides[0][0], same_at)
    put([tokens], sides[0][1], other_at)

    def run(n, table):
        put([q, do, k, v], sides[1 + n][0], same_at)
        put([k, v], sides[1 + n][1], other_at)
        cols = column(lookup(table, me))
        grads, low_same, low_other = one_head(
            frames, bands, q[...], do[...], k[...], v[...], tokens[...], *[a[:, cols] for a in adapters]
        )
        keep = jnp.where(first, grads[:cut], grads[cut:])
        give = jnp.where(first, grads[cut:], grads[:cut])
        return keep, give, low_same, low_other

    if chained:
        keep, give, low_same, low_other = run(0, heads[0][0])
        keep_ref[:cut, :] = keep
        keep_ref[cut:, :] = before[0][...] + low_same
        give = jnp.concatenate([give, before[1][...] + low_other], axis=0)
        size = give.shape[0] // GIVES
        for n, ref in enumerate(give_refs):
            ref[...] = give[n * size : (n + 1) * size].astype(ref.dtype)
        return
    for n, (table, counts) in enumerate(heads):
        here = slice(n * cut, (n + 1) * cut)

        def body():
            keep, give, low_same, low_other = run(n, table)
            keep_ref[here, :] = keep
            give_refs[0][here, :] = give.astype(BF16)
            if n == 0:
                low_refs[0][...] = low_same
                low_refs[1][...] = low_other
            else:
                low_refs[0][...] += low_same
                low_refs[1][...] += low_other

        if min(counts) > 0:
            body()
        else:
            live = lookup(counts, me) > 0
            pl.when(live)(body)

            @pl.when(jnp.logical_not(live))
            def _():
                keep_ref[here, :] = jnp.zeros((cut, DH), F32)
                give_refs[0][here, :] = jnp.zeros((cut, DH), BF16)


def head_group(heads, bands, sides, adapters, before=(), after=()):
    frames = len(sides[0][0])
    arrays, places = [], []
    for side in sides:
        found = []
        for pairs_of in side:
            found.append([])
            for array, start in pairs_of:
                known = [n for n, a in enumerate(arrays) if a is array]
                if not known:
                    arrays.append(array)
                found[-1].append((known[0] if known else len(arrays) - 1, start))
        places.append(found)
    rows, rank = arrays[0].shape[0], adapters[0].shape[0]
    flat = frames * rows
    size = len(heads) * 3 * rank // 2
    chained = len(before) > 0
    args = [bands, *arrays, *adapters, *before, *after]
    specs = [pl.BlockSpec(memory_space=pltpu.SMEM)] + vmem(len(arrays) + 3 + len(before))
    specs += [pl.BlockSpec(memory_space=pl.ANY)] * len(after)
    low = jax.ShapeDtypeStruct((flat, rank), F32)
    if chained:
        part = jax.ShapeDtypeStruct(((size + flat) // GIVES, rank), BF16)
        shapes = [jax.ShapeDtypeStruct((size + flat, rank), F32)] + [part] * GIVES
    else:
        edge = jax.ShapeDtypeStruct((size, rank), F32)
        shapes = [edge, jax.ShapeDtypeStruct((size, rank), BF16), low, low]
    return pl.pallas_call(
        functools.partial(
            group_kernel, heads, frames, chained, len(after), places, len(arrays)
        ),
        in_specs=specs,
        out_specs=vmem(len(shapes)),
        out_shape=shapes,
        scratch_shapes=[pltpu.VMEM((flat, DH), BF16)] * 2
        + [pltpu.VMEM((2 * flat, DH), BF16)] * 2
        + [pltpu.VMEM((2 * flat, rank), BF16)],
        compiler_params=pltpu.CompilerParams(vmem_limit_bytes=40 * 1024 * 1024),
    )(*args)


def hand_out_kernel(frames, size, parts, keep_ref, *refs):
    gots, facing = refs[:parts], refs[parts]
    own_low, own_late, near, low_third, low_last, total = refs[-6:]
    me = lax.axis_index("tm")
    rows = own_low.shape[0]
    total[...] = keep_ref[...] + jnp.concatenate([got[...].astype(F32) for got in gots], axis=0)

    def low(m):
        return total[pl.ds(pl.multiple_of(size + (me ^ m) * rows, 8), rows), :]

    late = total[:size, :].astype(BF16)
    own_low[...] = low(0)
    own_late[...] = late
    near[:rows, :] = low(1).astype(BF16)
    near[rows : rows + size, :] = late
    near[rows + size :, :] = facing[...]
    low_third[...] = low(2).astype(BF16)
    low_last[...] = low(3).astype(BF16)


def hand_out(frames, rows, keep, gots, facing, after):
    size, rank = keep.shape[0] - frames * rows, keep.shape[1]
    return pl.pallas_call(
        functools.partial(hand_out_kernel, frames, size, len(gots)),
        in_specs=vmem(2 + len(gots)) + [pl.BlockSpec(memory_space=pl.ANY)] * len(after),
        out_specs=vmem(5),
        out_shape=[jax.ShapeDtypeStruct((rows, rank), F32)]
        + [jax.ShapeDtypeStruct((n, rank), BF16) for n in (size, rows + 3 * size, rows, rows)],
        scratch_shapes=[pltpu.VMEM(keep.shape, F32)],
        compiler_params=SMALL,
    )(keep, *gots, facing, *after)


def hold_kernel(late, piece, *refs):
    late_out, lead_out = refs[-2:]
    late_out[...] = late[...]
    lead_out[...] = piece[: lead_out.shape[0], :]


def hold(late, piece, after):
    return pl.pallas_call(
        hold_kernel,
        in_specs=vmem(2) + [pl.BlockSpec(memory_space=pl.ANY)] * len(after),
        out_specs=vmem(2),
        out_shape=[jax.ShapeDtypeStruct(late.shape, late.dtype)] * 2,
        compiler_params=SMALL,
    )(late, piece, *after)


def sum_low_kernel(own, near, third, last, out):
    rows = own.shape[0]
    low = own[...] + near[:rows, :].astype(F32) + third[...].astype(F32) + last[...].astype(F32)
    out[...] = low.astype(BF16)


def sum_low(own, near, third, last):
    return pl.pallas_call(
        sum_low_kernel,
        in_specs=vmem(4),
        out_specs=pl.BlockSpec(memory_space=pltpu.VMEM),
        out_shape=jax.ShapeDtypeStruct(own.shape, BF16),
        compiler_params=SMALL,
    )(own, near, third, last)


def collect_kernel(wide, low, low_head, own, near, third, last, piece, pair, far, facing, out_ref):
    rows, size = low.shape[0], own.shape[0]
    out_ref[:rows, :] = (low[...].astype(F32) + low_head[...].astype(F32)).astype(BF16)
    middle = lookup(wide, lax.axis_index("tm")) > 0

    def part(n):
        return near[rows + n * size : rows + (n + 1) * size, :]

    blocks = [own[...], part(0), third[...], last[...], piece[:size, :], pair[:size, :]]
    blocks += [jnp.where(middle, far[...], part(1)), facing[:size, :]]
    blocks.append(jnp.where(middle, piece[size:, :], pair[size:, :]))
    blocks.append(jnp.where(middle, facing[size:, :], part(2)))
    for n, block in enumerate(blocks):
        out_ref[rows + n * size : rows + (n + 1) * size, :] = block


def collect(wide, low, low_head, *pieces):
    (rows, rank), size = low.shape, pieces[0].shape[0]
    return pl.pallas_call(
        functools.partial(collect_kernel, wide),
        in_specs=vmem(2 + len(pieces)),
        out_specs=pl.BlockSpec(memory_space=pltpu.VMEM),
        out_shape=jax.ShapeDtypeStruct((rows + 10 * size, rank), BF16),
        compiler_params=SMALL,
    )(low, low_head, *pieces)


def place_kernel(frames, lead, late, rest, tail, tail2, *outs):
    me, half = lax.axis_index("tm"), lax.axis_index("rep")
    first = half == 0
    rank = outs[0].shape[0]
    cut = 3 * rank // 2
    rows = outs[3].shape[0] // 2

    def both(here):
        a, b = tail[here, :].astype(F32), tail2[here, :].astype(F32)
        return jnp.concatenate([jnp.where(first, a, b), jnp.where(first, b, a)], axis=0)

    outs[3][...] = both(slice(0, rows))
    side = me // 2
    places = [lookup(late, me ^ m) for m in range(frames)] + [lookup(lead, me ^ m) for m in range(frames)]
    places += [lookup(rest, 1 + side), lookup(rest, 2 - side)]
    for n, head in enumerate(places):
        whole = both(slice(rows + n * cut, rows + (n + 1) * cut))
        for o in range(3):
            outs[o][:, column(head)] = whole[o * rank : (o + 1) * rank]


def place(frames, lead, late, rest, tail, tail2, rows, rank, width):
    return pl.pallas_call(
        functools.partial(place_kernel, frames, lead, late, rest),
        in_specs=vmem(2),
        out_specs=vmem(4),
        out_shape=[jax.ShapeDtypeStruct((rank, width), F32)] * 3
        + [jax.ShapeDtypeStruct((2 * rows, rank), F32)],
        compiler_params=SMALL,
    )(tail, tail2)


def exchange_plan(
    frozen_query,
    frozen_key,
    frozen_value,
    token_adapter_input,
    query_adapter_out,
    key_adapter_out,
    value_adapter_out,
    out_grad,
    band_width,
):
    rows, width = frozen_query.shape
    rank = token_adapter_input.shape[1]
    frames = band_width.shape[0]
    heads = width // DH
    starts, counts = head_table(heads, frames)
    most = max(counts)
    columns = [[min(starts[j] + s, heads - 1) for j in range(frames)] for s in range(most)]
    numbers = [[int(s < counts[j]) for j in range(frames)] for s in range(most)]
    slots = list(zip(columns, numbers))
    lead, late, rest = slots[0], slots[1], slots[2]
    wide = [j for j in range(frames) if counts[j] == most]
    adapters = [query_adapter_out, key_adapter_out, value_adapter_out]
    arrays = (frozen_query, out_grad, frozen_key, frozen_value, token_adapter_input)

    def meet(name, block, m, targets=range(frames)):
        with jax.named_scope(f"{name}_over_tm"):
            return lax.ppermute(block, "tm", [(j ^ m, j) for j in targets])

    def swap_in_chip(name, block):
        with jax.named_scope(f"{name}_in_chip"):
            return swap(block, "rep")

    def mine(slot, m):
        return (slot[0], m, "mine")

    sent, kept, sent_late = [], [], []
    for m in range(1, frames):
        first = [mine(lead, m), (None, m, "t")]
        if m == 1:
            sent.append(first + [mine(rest, m), mine(late, m)])
        else:
            sent += [first, [mine(rest, m)]]
            sent_late.append([mine(late, m)])
    for slot in (lead, rest, late):
        kept += [[mine(slot, 0)], [(slot[0], 0, "other")]]
    kept += [[(None, 0, "t")], [(None, 0, "other t")]]
    packed = pack(frames, sent, 56, *arrays)
    packed_late = pack(frames, sent_late + kept, 16, *arrays)
    kept = packed_late[len(sent_late) :]
    block = meet("nearest", packed[0], 1)
    lead_got, rest_got, late_got = [(block, 0)], [(block, 4 * DH + rank)], [(block, 8 * DH + rank)]
    for m in range(2, frames):
        lead_got.append((meet("lead", packed[2 * m - 3], m), 0))
        rest_got.append((meet("rest", packed[2 * m - 2], m, wide), 0))
        late_got.append((meet("late", packed_late[m - 2], m), 0))

    def sides(name, n, got, wide_t, groups, skip, after=()):
        size = 4 * DH - skip + (rank if wide_t else 0)
        picked = pick([(a, start + skip) for a, start in got], size, groups, after)
        cross = [swap_in_chip(name, block) for block in picked]
        where = 2 * DH - skip
        cross = [(block, at * size + where) for block, count in zip(cross, groups) for at in range(count)]
        rows_here = [(kept[2 * n], 0)] + got
        rows_there = [(kept[2 * n + 1], 0)] + cross
        return rows_here, rows_there, cross

    *lead_side, cross = sides("lead", 0, lead_got, True, (3,), 2 * DH, kept[:1])
    t_side = (
        [(kept[6], 0)] + [(a, start + 4 * DH) for a, start in lead_got],
        [(kept[7], 0)] + [(block, start + 2 * DH) for block, start in cross],
    )
    *rest_side, _ = sides("rest", 1, rest_got, False, (3,), 2 * DH)
    early = [lead, rest]
    keep, give, *low = head_group(early, band_width, [t_side, lead_side, rest_side], adapters)
    got = swap_in_chip("early_gradients", give)
    piece = (keep + got.astype(F32)).astype(BF16)
    *late_side, _ = sides("late", 2, late_got, False, (3,), 0, [got])
    pair = meet("early_gradients", piece, 1)
    facing = meet("early_gradients", piece, 3)
    keep, *gives = head_group([late], band_width, [t_side, late_side], adapters, low, [piece])
    gives = [swap_in_chip("late_sums", g) for g in gives]
    own_low, own, near, low_third, low_last = hand_out(frames, rows, keep, gives, facing, [pair])
    near = meet("late_sums", near, 1)
    low_third, low_last = meet("low", low_third, 2), meet("low", low_last, 3)
    held, lead_held = hold(own, piece, [low_third, low_last])
    third, last = meet("late_gradients", held, 2), meet("late_gradients", held, 3)
    with jax.named_scope("early_lead_over_tm"):
        far = lax.ppermute(lead_held, "tm", [(0, 2), (3, 1)])
    low = sum_low(own_low, near, low_third, low_last)
    with jax.named_scope("low_over_head"):
        low_head = swap(low, "head")
    tail = collect(rest[1], low, low_head, own, near, third, last, piece, pair, far, facing)
    outs = place(
        frames, lead[0], late[0], rest[0], tail, swap_in_chip("tail", tail), rows, rank, width
    )
    return tuple(outs)


def on_device(frozen_query, *rest):
    frames = rest[-1].shape[0]
    heads = frozen_query.shape[1] // DH
    whole_reach = frames == 4 and heads == 2 * frames + 2
    return (exchange_plan if whole_reach else window_plan)(frozen_query, *rest)


def solution(mesh):
    in_specs = (
        P(("groups", "tm", "rep"), "head"),
        P(("groups", "tm"), "head"),
        P(("groups", "tm"), "head"),
        P(("groups", "tm"), None),
        P(None, "head"),
        P(None, "head"),
        P(None, "head"),
        P(("groups", "tm", "rep"), "head"),
        P(),
    )
    out_specs = (
        P("groups", "head"),
        P("groups", "head"),
        P("groups", "head"),
        P(("groups", "tm"), None),
    )
    return jax.shard_map(
        on_device, mesh=mesh, in_specs=in_specs, out_specs=out_specs, check_vma=False
    )
```

```python
import functools
import math

import jax
import jax.numpy as jnp
from jax import lax
from jax.experimental import pallas as pl
from jax.experimental.pallas import tpu as pltpu
from jax.sharding import PartitionSpec as P

DH = 128
NEAR = 1
REACH = 4
SCALE = DH ** (-0.5)
SCALE_2 = SCALE * math.log2(math.e)
F32 = jnp.float32
BF16 = jnp.bfloat16
GIVES = 2
SMALL = pltpu.CompilerParams(vmem_limit_bytes=16 * 1024 * 1024)


def dot_nn(left, right):
    return lax.dot_general(left, right, (((1,), (0,)), ((), ())), preferred_element_type=F32)


def dot_nt(left, right):
    return lax.dot_general(left, right, (((1,), (1,)), ((), ())), preferred_element_type=F32)


def dot_tn(left, right):
    return lax.dot_general(left, right, (((0,), (0,)), ((), ())), preferred_element_type=F32)


def routes(count):
    found = []
    for d in range(1, min(REACH, count - 1) + 1):
        if 2 * d >= count:
            found.append((d, (-d, d)))
        else:
            found.append((d, (-d,)))
            found.append((d, (d,)))
    return found


def pairs(count, offsets):
    return [(i + o, i) for o in offsets for i in range(count) if 0 <= i + o < count]


def swap(block, axis):
    return lax.ppermute(block, axis, [(0, 1), (1, 0)])


def attention_kernel(
    blocks, bias_ref, fq_ref, do_ref, fk_ref, fv_ref, t_ref, tr_ref, tt_ref, aq_ref, ak_ref, av_ref, *refs
):
    k_refs = refs[:blocks]
    v_refs = refs[blocks : 2 * blocks]
    gq_ref, gk_ref, gv_ref, lowq_ref, low_ref = refs[2 * blocks :]
    rows = fq_ref.shape[0]

    @pl.when(pl.program_id(0) == 0)
    def _():
        lowq_ref[...] = jnp.zeros_like(lowq_ref)
        low_ref[...] = jnp.zeros_like(low_ref)

    aq, ak, av = aq_ref[...], ak_ref[...], av_ref[...]
    query = (fq_ref[...].astype(F32) + dot_nn(tr_ref[...], aq)).astype(BF16)
    do = do_ref[...]
    own_k = (fk_ref[...].astype(F32) + dot_nn(t_ref[...], ak)).astype(BF16)
    own_v = (fv_ref[...].astype(F32) + dot_nn(t_ref[...], av)).astype(BF16)
    keys = [own_k[:rows], own_k[rows:]] + [ref[...] for ref in k_refs]
    values = [own_v[:rows], own_v[rows:]] + [ref[...] for ref in v_refs]
    count = len(keys)
    scores = [dot_nt(keys[b], query) * SCALE + bias_ref[b] for b in range(count)]
    top = functools.reduce(jnp.maximum, scores)
    top = jnp.max(top, axis=0, keepdims=True)
    shifted = [jnp.exp(s - top) for s in scores]
    total = jnp.sum(functools.reduce(jnp.add, shifted), axis=0, keepdims=True)
    inverse = 1.0 / total
    probs = [s * inverse for s in shifted]
    lows = [p.astype(BF16) for p in probs]
    attended = functools.reduce(jnp.add, [dot_tn(lows[b], values[b]) for b in range(count)])
    attended = attended.astype(BF16).astype(F32)
    delta = jnp.sum((do.astype(F32) * attended).T, axis=0, keepdims=True)
    grads = [
        (probs[b] * (dot_nt(values[b], do) - delta)).astype(BF16) for b in range(count)
    ]
    dq = functools.reduce(jnp.add, [dot_tn(grads[b], keys[b]) for b in range(count)])
    dq = (dq * SCALE).astype(BF16)
    gq_ref[...] = dot_tn(tr_ref[...], dq)
    lowq_ref[...] += dot_nt(dq, aq)
    both = jnp.concatenate([ak, av], axis=1)
    for b in range(count):
        dk = (dot_nn(grads[b], query) * SCALE).astype(BF16)
        dv = dot_nn(lows[b], do).astype(BF16)
        part = jnp.concatenate([dk, dv], axis=1)
        low_ref[b * rows : (b + 1) * rows, :] += dot_nt(part, both)
        out = dot_nn(tt_ref[:, b * rows : (b + 1) * rows], part)
        if b == 0:
            total_part = out
        else:
            total_part += out
    gk_ref[...] = total_part[:, :DH]
    gv_ref[...] = total_part[:, DH:]


def attention(bias, fq, do, fk, fv, t, tr, tt, aq, ak, av, payloads):
    rows, width = fq.shape
    heads = width // DH
    rank = t.shape[1]
    blocks = len(payloads)
    count = blocks + 2

    def col(r):
        return pl.BlockSpec((r, DH), lambda h: (0, h))

    def whole(shape):
        return pl.BlockSpec(shape, lambda h: (0, 0))

    return pl.pallas_call(
        functools.partial(attention_kernel, blocks),
        grid=(heads,),
        out_shape=[
            jax.ShapeDtypeStruct((rank, width), F32),
            jax.ShapeDtypeStruct((rank, width), F32),
            jax.ShapeDtypeStruct((rank, width), F32),
            jax.ShapeDtypeStruct((rows, rank), F32),
            jax.ShapeDtypeStruct((count * rows, rank), F32),
        ],
        in_specs=[pl.BlockSpec(memory_space=pltpu.SMEM)]
        + [col(rows), col(rows), col(2 * rows), col(2 * rows)]
        + [whole(t.shape), whole(tr.shape), whole(tt.shape)]
        + [col(rank)] * 3
        + [col(rows)] * blocks
        + [pl.BlockSpec((rows, DH), lambda h: (0, heads + h))] * blocks,
        out_specs=[col(rank)] * 3 + [whole((rows, rank)), whole((count * rows, rank))],
        compiler_params=pltpu.CompilerParams(vmem_limit_bytes=32 * 1024 * 1024),
    )(bias, fq, do, fk, fv, t, tr, tt, aq, ak, av, *payloads, *payloads)


def sum_rows(part, frame_idx, half_idx, frames):
    rows, width = part.shape
    half = width // 2
    keep = lax.dynamic_slice_in_dim(part, half_idx * half, half, 1)
    give = lax.dynamic_slice_in_dim(part, (1 - half_idx) * half, half, 1)
    mine = keep + swap(give, "rep")
    if frames & (frames - 1) or rows % frames or frames > REACH + 1:
        total = lax.psum(mine, "tm").astype(BF16)
    else:
        chunk = rows // frames
        low = mine.astype(BF16)
        acc = lax.dynamic_slice_in_dim(mine, frame_idx * chunk, chunk, 0)
        for m in range(1, frames):
            give = lax.dynamic_slice_in_dim(low, (frame_idx ^ m) * chunk, chunk, 0)
            acc = acc + lax.ppermute(give, "tm", [(i, i ^ m) for i in range(frames)]).astype(F32)
        acc = acc.astype(BF16)
        total = jnp.zeros((rows, half), BF16)
        total = lax.dynamic_update_slice_in_dim(total, acc, frame_idx * chunk, 0)
        for m in range(1, frames):
            got = lax.ppermute(acc, "tm", [(i, i ^ m) for i in range(frames)])
            total = lax.dynamic_update_slice_in_dim(total, got, (frame_idx ^ m) * chunk, 0)
    other = swap(total, "rep")
    first = jnp.where(half_idx == 0, total, other)
    second = jnp.where(half_idx == 0, other, total)
    return jnp.concatenate([first, second], axis=1).astype(F32)


def window_plan(
    frozen_query,
    frozen_key,
    frozen_value,
    token_adapter_input,
    query_adapter_out,
    key_adapter_out,
    value_adapter_out,
    out_grad,
    band_width,
):
    rows, width = frozen_query.shape
    rank = token_adapter_input.shape[1]
    frames = band_width.shape[0]
    frame_idx = lax.axis_index("tm")
    half_idx = lax.axis_index("rep")
    t = token_adapter_input
    tr = lax.dynamic_slice_in_dim(t, half_idx * rows, rows, 0)

    def tile_rows_of(frozen, adapter):
        own = lax.dynamic_slice_in_dim(frozen, half_idx * rows, rows, 0)
        return (own.astype(F32) + dot_nn(tr, adapter)).astype(BF16)

    payload = jnp.concatenate(
        [tile_rows_of(frozen_key, key_adapter_out), tile_rows_of(frozen_value, value_adapter_out), tr],
        axis=1,
    )

    frame_ids = jnp.arange(frames)
    band_row = jnp.sum(jnp.where((frame_ids == frame_idx)[:, None], band_width, 0), axis=0)

    def band_at(offsets):
        seen = functools.reduce(jnp.logical_or, [frame_ids == frame_idx + o for o in offsets])
        return jnp.sum(jnp.where(seen, band_row, 0))

    own_band = band_at((0,))
    allowed = [jnp.abs(half_idx - tile) < own_band for tile in range(2)]
    payloads = []
    plan = routes(frames)
    for d, offsets in plan:
        got = lax.ppermute(payload, "tm", pairs(frames, offsets))
        band = band_at(offsets)
        payloads.append(got)
        allowed.append(band > 0)
        if d <= NEAR:
            payloads.append(swap(got, "rep"))
            allowed.append(band > 1)
    bias = jnp.where(jnp.stack(allowed), 0.0, -jnp.inf).astype(F32)
    tt = jnp.concatenate([t] + [p[:, 2 * width :] for p in payloads], axis=0).T

    gq, gk, gv, low_q, low_b = attention(
        bias, frozen_query, out_grad, frozen_key, frozen_value, t, tr, tt,
        query_adapter_out, key_adapter_out, value_adapter_out, payloads,
    )

    own = low_b[: 2 * rows]
    same = lax.dynamic_slice_in_dim(own, half_idx * rows, rows, 0) + low_q
    other = lax.dynamic_slice_in_dim(own, (1 - half_idx) * rows, rows, 0)
    start = 2 * rows
    for d, offsets in plan:
        size = 2 * rows if d <= NEAR else rows
        back = [(target, source) for source, target in pairs(frames, offsets)]
        got = lax.ppermute(low_b[start : start + size], "tm", back)
        start += size
        same = same + got[:rows]
        if d <= NEAR:
            other = other + got[rows:]
    low = jnp.where(
        half_idx == 0,
        jnp.concatenate([same, other], axis=0),
        jnp.concatenate([other, same], axis=0),
    )
    low = low + swap(low, "rep")
    low = low + swap(low, "head")

    grads = sum_rows(jnp.concatenate([gq, gk, gv], axis=0), frame_idx, half_idx, frames)
    return grads[:rank], grads[rank : 2 * rank], grads[2 * rank :], low


def head_table(heads, frames):
    base, extra = divmod(heads, frames)
    lead = (frames - extra) // 2
    counts = [base + (1 if lead <= j < lead + extra else 0) for j in range(frames)]
    return [sum(counts[:j]) for j in range(frames)], counts


def lookup(table, index):
    value = jnp.int32(table[0])
    for j in range(1, len(table)):
        value = jnp.where(index == j, jnp.int32(table[j]), value)
    return value


def column(head):
    return pl.ds(pl.multiple_of(head * DH, DH), DH)


def vmem(count):
    return [pl.BlockSpec(memory_space=pltpu.VMEM)] * count


def pack_kernel(frames, outputs, fq_ref, do_ref, fk_ref, fv_ref, t_ref, *refs):
    outs, (q_in, do_in, k_in, v_in, k2_in, v2_in, t_in, sems) = refs[:-8], refs[-8:]
    wanted = {what for parts in outputs for _, _, what in parts}
    me, half = lax.axis_index("tm"), lax.axis_index("rep")
    rows = fq_ref.shape[0]
    mine = pl.ds(pl.multiple_of(half * rows, rows), rows)
    rest = pl.ds(pl.multiple_of((1 - half) * rows, rows), rows)
    moves = [
        (fq_ref, q_in), (do_ref, do_in), (fk_ref.at[mine, :], k_in), (fv_ref.at[mine, :], v_in), (t_ref, t_in)
    ]
    if "other" in wanted:
        moves += [(fk_ref.at[rest, :], k2_in), (fv_ref.at[rest, :], v2_in)]
    copies = [pltpu.make_async_copy(a, b, sems.at[n]) for n, (a, b) in enumerate(moves)]
    for copy in copies:
        copy.start()
    for copy in copies:
        copy.wait()
    for out, parts in zip(outs, outputs):
        at = 0
        for table, m, what in parts:
            if what in ("t", "other t"):
                blocks = [t_in[mine if what == "t" else rest, :]]
            else:
                cols = column(lookup(table, me ^ m))
                sources = (q_in, do_in, k_in, v_in) if what == "mine" else (k2_in, v2_in)
                blocks = [ref[:, cols] for ref in sources]
            for block in blocks:
                out[:, at : at + block.shape[1]] = block
                at += block.shape[1]


def pack(frames, outputs, limit, fq, do, fk, fv, t):
    rows, width = fq.shape
    size = {"mine": 4 * DH, "other": 2 * DH, "t": t.shape[1], "other t": t.shape[1]}
    return pl.pallas_call(
        functools.partial(pack_kernel, frames, outputs),
        in_specs=[pl.BlockSpec(memory_space=pltpu.HBM)] * 5,
        out_specs=vmem(len(outputs)),
        out_shape=[
            jax.ShapeDtypeStruct((rows, sum(size[what] for _, _, what in parts)), BF16)
            for parts in outputs
        ],
        scratch_shapes=[pltpu.VMEM((rows, width), BF16)] * 6
        + [pltpu.VMEM(t.shape, BF16), pltpu.SemaphoreType.DMA((7,))],
        compiler_params=pltpu.CompilerParams(vmem_limit_bytes=limit * 1024 * 1024),
    )(fq, do, fk, fv, t)


def pick_kernel(spans, groups, *refs):
    n = 0
    for out, count in zip(refs[-len(groups) :], groups):
        for at in range(count):
            start, size = spans[n]
            out[:, at * size : (at + 1) * size] = refs[n][:, start : start + size]
            n += 1


def pick(parts, size, groups, after=()):
    arrays = [array for array, _ in parts]
    rows, dtype = arrays[0].shape[0], arrays[0].dtype
    return pl.pallas_call(
        functools.partial(pick_kernel, [(start, size) for _, start in parts], groups),
        in_specs=vmem(len(arrays)) + [pl.BlockSpec(memory_space=pl.ANY)] * len(after),
        out_specs=vmem(len(groups)),
        out_shape=[jax.ShapeDtypeStruct((rows, size * count), dtype) for count in groups],
        compiler_params=SMALL,
    )(*arrays, *after)


def one_head(frames, bands, q, do, frozen_k, frozen_v, tokens, aq, ak, av):
    flat = q.shape[0]
    rows = flat // frames
    t_same = tokens[:flat]

    def adapted(frozen, rows_of, adapter):
        return (frozen.astype(F32) + dot_nn(rows_of, adapter)).astype(BF16)

    query = adapted(q, t_same, aq)
    keys, values = adapted(frozen_k, tokens, ak), adapted(frozen_v, tokens, av)
    do_t, keys_t, values_t = do.T, keys.T, values.T

    def bias(i, b):
        j, need = (b, 0) if b < frames else (b - frames, 1)
        value = jnp.where(bands[i, j] > need, 0.0, -jnp.inf).astype(F32)
        return jnp.full((1, rows), value, F32)

    span = 2 if frames % 2 == 0 else 1
    wide = span * rows
    groups = [range(first, first + span) for first in range(0, frames, span)]
    seen = [
        list(range(frames))
        + [frames + j for j in range(frames) if any(abs(i - j) <= NEAR for i in mine)]
        for mine in groups
    ]
    here = [slice(mine[0] * rows, mine[0] * rows + wide) for mine in groups]
    pairs_of = range(len(groups))

    def gather(whole, g, axis):
        parts = [
            whole[b * rows : (b + 1) * rows] if axis == 0 else whole[:, b * rows : (b + 1) * rows]
            for b in seen[g]
        ]
        return jnp.concatenate(parts, axis=axis)

    def block(whole, n):
        return whole[n * rows : (n + 1) * rows]

    def softmax(g, raw):
        scores = [
            block(raw, n) * SCALE_2 + jnp.concatenate([bias(i, b) for i in groups[g]], axis=1)
            for n, b in enumerate(seen[g])
        ]
        top = jnp.max(functools.reduce(jnp.maximum, scores), axis=0, keepdims=True)
        shifted = [jnp.exp2(s - top) for s in scores]
        inverse = 1.0 / jnp.sum(functools.reduce(jnp.add, shifted), axis=0, keepdims=True)
        return [s * inverse for s in shifted]

    raws = [dot_nt(gather(keys, g, 0), query[here[g]]) for g in pairs_of]
    prob_grads = [dot_nt(gather(values, g, 0), do[here[g]]) for g in pairs_of]
    probs = [softmax(g, raws[g]) for g in pairs_of]
    lows = [jnp.concatenate([p.astype(BF16) for p in probs[g]], axis=0) for g in pairs_of]
    grads = []
    for g in pairs_of:
        attended = dot_nn(gather(values_t, g, 1), lows[g]).astype(BF16).astype(F32)
        delta = jnp.sum(do_t[:, here[g]].astype(F32) * attended, axis=0, keepdims=True)
        parts = [
            (probs[g][n] * (block(prob_grads[g], n) - delta)).astype(BF16) for n in range(len(seen[g]))
        ]
        grads.append(jnp.concatenate(parts, axis=0))
    dvs, dks = [None] * (2 * frames), [None] * (2 * frames)

    def add(sums, g, whole):
        for n, b in enumerate(seen[g]):
            sums[b] = block(whole, n) if sums[b] is None else sums[b] + block(whole, n)

    for g in pairs_of:
        add(dvs, g, dot_nn(lows[g], do[here[g]]))
    for g in pairs_of:
        add(dks, g, dot_nn(grads[g], query[here[g]]))
    dqs = [(dot_nn(gather(keys_t, g, 1), grads[g]) * SCALE).astype(BF16).T for g in pairs_of]
    dq = jnp.concatenate(dqs, axis=0)
    dk = (jnp.concatenate(dks, axis=0) * SCALE).astype(BF16)
    dv = jnp.concatenate(dvs, axis=0).astype(BF16)
    both = jnp.concatenate([dk, dv], axis=1)
    sums = dot_tn(tokens, both)
    grads = jnp.concatenate([dot_tn(t_same, dq), sums[:, :DH], sums[:, DH:]], axis=0)
    lows = dot_nt(both, jnp.concatenate([ak, av], axis=1))
    return grads, lows[:flat] + dot_nt(dq, aq), lows[flat:]


def group_kernel(heads, frames, chained, waits, sides, count, *refs):
    refs = list(refs)

    def take(count):
        taken = refs[:count]
        del refs[:count]
        return taken

    (bands,) = take(1)
    arrays, adapters = take(count), take(3)
    before = take(2) if chained else None
    take(waits)
    keep_ref, *give_refs = take(1 + GIVES if chained else 2)
    low_refs = [] if chained else take(2)
    q, do, k, v, tokens = refs
    me, half = lax.axis_index("tm"), lax.axis_index("rep")
    rows = arrays[0].shape[0]
    flat = frames * rows
    cut = 3 * tokens.shape[1] // 2
    first = half == 0
    same_at = [pl.ds(pl.multiple_of((me ^ m) * rows, rows), rows) for m in range(frames)]
    other_at = [pl.ds(pl.multiple_of(flat + (me ^ m) * rows, rows), rows) for m in range(frames)]

    def put(targets, places, rows_at):
        for m, (n, start) in enumerate(places):
            for c, target in enumerate(targets):
                target[rows_at[m], :] = arrays[n][:, start + c * DH : start + (c + 1) * DH]

    put([tokens], sides[0][0], same_at)
    put([tokens], sides[0][1], other_at)

    def run(n, table):
        put([q, do, k, v], sides[1 + n][0], same_at)
        put([k, v], sides[1 + n][1], other_at)
        cols = column(lookup(table, me))
        grads, low_same, low_other = one_head(
            frames, bands, q[...], do[...], k[...], v[...], tokens[...], *[a[:, cols] for a in adapters]
        )
        keep = jnp.where(first, grads[:cut], grads[cut:])
        give = jnp.where(first, grads[cut:], grads[:cut])
        return keep, give, low_same, low_other

    if chained:
        keep, give, low_same, low_other = run(0, heads[0][0])
        keep_ref[:cut, :] = keep
        keep_ref[cut:, :] = before[0][...] + low_same
        give = jnp.concatenate([give, before[1][...] + low_other], axis=0)
        size = give.shape[0] // GIVES
        for n, ref in enumerate(give_refs):
            ref[...] = give[n * size : (n + 1) * size].astype(ref.dtype)
        return
    for n, (table, counts) in enumerate(heads):
        here = slice(n * cut, (n + 1) * cut)

        def body():
            keep, give, low_same, low_other = run(n, table)
            keep_ref[here, :] = keep
            give_refs[0][here, :] = give.astype(BF16)
            if n == 0:
                low_refs[0][...] = low_same
                low_refs[1][...] = low_other
            else:
                low_refs[0][...] += low_same
                low_refs[1][...] += low_other

        if min(counts) > 0:
            body()
        else:
            live = lookup(counts, me) > 0
            pl.when(live)(body)

            @pl.when(jnp.logical_not(live))
            def _():
                keep_ref[here, :] = jnp.zeros((cut, DH), F32)
                give_refs[0][here, :] = jnp.zeros((cut, DH), BF16)


def head_group(heads, bands, sides, adapters, before=(), after=()):
    frames = len(sides[0][0])
    arrays, places = [], []
    for side in sides:
        found = []
        for pairs_of in side:
            found.append([])
            for array, start in pairs_of:
                known = [n for n, a in enumerate(arrays) if a is array]
                if not known:
                    arrays.append(array)
                found[-1].append((known[0] if known else len(arrays) - 1, start))
        places.append(found)
    rows, rank = arrays[0].shape[0], adapters[0].shape[0]
    flat = frames * rows
    size = len(heads) * 3 * rank // 2
    chained = len(before) > 0
    args = [bands, *arrays, *adapters, *before, *after]
    specs = [pl.BlockSpec(memory_space=pltpu.SMEM)] + vmem(len(arrays) + 3 + len(before))
    specs += [pl.BlockSpec(memory_space=pl.ANY)] * len(after)
    low = jax.ShapeDtypeStruct((flat, rank), F32)
    if chained:
        part = jax.ShapeDtypeStruct(((size + flat) // GIVES, rank), BF16)
        shapes = [jax.ShapeDtypeStruct((size + flat, rank), F32)] + [part] * GIVES
    else:
        edge = jax.ShapeDtypeStruct((size, rank), F32)
        shapes = [edge, jax.ShapeDtypeStruct((size, rank), BF16), low, low]
    return pl.pallas_call(
        functools.partial(
            group_kernel, heads, frames, chained, len(after), places, len(arrays)
        ),
        in_specs=specs,
        out_specs=vmem(len(shapes)),
        out_shape=shapes,
        scratch_shapes=[pltpu.VMEM((flat, DH), BF16)] * 2
        + [pltpu.VMEM((2 * flat, DH), BF16)] * 2
        + [pltpu.VMEM((2 * flat, rank), BF16)],
        compiler_params=pltpu.CompilerParams(vmem_limit_bytes=40 * 1024 * 1024),
    )(*args)


def hand_out_kernel(frames, size, parts, keep_ref, *refs):
    gots, facing, (own_ref, *sends, total) = refs[:parts], refs[parts], refs[-frames - 1 :]
    me = lax.axis_index("tm")
    rows = own_ref.shape[0]
    total[...] = keep_ref[...] + jnp.concatenate([got[...].astype(F32) for got in gots], axis=0)
    for m in range(frames):
        low = total[pl.ds(pl.multiple_of(size + (me ^ m) * rows, 8), rows), :]
        if m == 0:
            own_ref[...] = low
        else:
            sends[m - 1][:rows, :] = low.astype(BF16)
            sends[m - 1][rows : rows + size, :] = total[:size, :].astype(BF16)
    sends[0][rows + size :, :] = facing[...]


def hand_out(frames, rows, keep, gots, facing, after):
    size, rank = keep.shape[0] - frames * rows, keep.shape[1]
    own, *sends = pl.pallas_call(
        functools.partial(hand_out_kernel, frames, size, len(gots)),
        in_specs=vmem(2 + len(gots)) + [pl.BlockSpec(memory_space=pl.ANY)] * len(after),
        out_specs=vmem(frames),
        out_shape=[jax.ShapeDtypeStruct((rows, rank), F32)]
        + [jax.ShapeDtypeStruct((rows + size * n, rank), BF16) for n in (3, 1, 1)],
        scratch_shapes=[pltpu.VMEM(keep.shape, F32)],
        compiler_params=SMALL,
    )(keep, *gots, facing, *after)
    return own, sends


def collect_kernel(wide, own_low, own, near, third, last, piece, pair, far, facing, out_ref, low_ref):
    rows = own_low.shape[0]
    size = own.shape[0] - rows
    low = own_low[...]
    for got in (near, third, last):
        low = low + got[:rows, :].astype(F32)
    out_ref[:rows, :] = low.astype(BF16)
    low_ref[...] = low.astype(BF16)
    middle = lookup(wide, lax.axis_index("tm")) > 0

    def part(ref, n):
        return ref[rows + n * size : rows + (n + 1) * size, :]

    blocks = [part(ref, 0) for ref in (own, near, third, last)]
    blocks += [piece[:size, :], pair[:size, :]]
    blocks += [jnp.where(middle, far[...], part(near, 1)), facing[:size, :]]
    blocks.append(jnp.where(middle, piece[size:, :], pair[size:, :]))
    blocks.append(jnp.where(middle, facing[size:, :], part(near, 2)))
    for n, block in enumerate(blocks):
        out_ref[rows + n * size : rows + (n + 1) * size, :] = block


def collect(wide, own_low, own, gots, *pieces):
    (rows, rank), size = own_low.shape, pieces[0].shape[0] // 2
    return pl.pallas_call(
        functools.partial(collect_kernel, wide),
        in_specs=vmem(2 + len(gots) + len(pieces)),
        out_specs=vmem(2),
        out_shape=[
            jax.ShapeDtypeStruct((rows + 10 * size, rank), BF16),
            jax.ShapeDtypeStruct((rows, rank), BF16),
        ],
        compiler_params=SMALL,
    )(own_low, own, *gots, *pieces)


def place_kernel(frames, lead, late, rest, tail, tail2, low_head, low_diag, *refs):
    outs, filled, sems = refs[:4], refs[4:8], refs[8]
    me, half = lax.axis_index("tm"), lax.axis_index("rep")
    first = half == 0
    rank = filled[0].shape[0]
    cut = 3 * rank // 2
    rows = low_head.shape[0]
    side = me // 2
    places = [lookup(late, me ^ m) for m in range(frames)] + [lookup(lead, me ^ m) for m in range(frames)]
    places += [lookup(rest, 1 + side), lookup(rest, 2 - side)]
    copies = [pltpu.make_async_copy(filled[o], outs[o], sems.at[o]) for o in range(4)]

    def rows_of(ref, n, start, stop):
        return ref[rows + n * cut + start : rows + n * cut + stop, :].astype(F32)

    for o in range(3):
        for n, head in enumerate(places):
            parts = []
            for owner, low_end, high_end in ((0, 0, cut), (1, cut, 2 * cut)):
                start, stop = max(o * rank, low_end), min((o + 1) * rank, high_end)
                if start < stop:
                    mine, its = (rows_of(ref, n, start - low_end, stop - low_end) for ref in (tail, tail2))
                    parts.append(jnp.where(first, mine, its) if owner == 0 else jnp.where(first, its, mine))
            filled[o][:, column(head)] = parts[0] if len(parts) == 1 else jnp.concatenate(parts, axis=0)
        copies[o].start()
    same = tail[:rows, :].astype(F32) + low_head[...].astype(F32)
    other = tail2[:rows, :].astype(F32) + low_diag[...].astype(F32)
    filled[3][:rows, :] = jnp.where(first, same, other)
    filled[3][rows:, :] = jnp.where(first, other, same)
    copies[3].start()
    for copy in copies:
        copy.wait()


def place(frames, lead, late, rest, tail, tail2, low_head, low_diag, rank, width):
    rows = low_head.shape[0]
    shapes = [(rank, width)] * 3 + [(2 * rows, rank)]
    return pl.pallas_call(
        functools.partial(place_kernel, frames, lead, late, rest),
        in_specs=vmem(4),
        out_specs=[pl.BlockSpec(memory_space=pl.ANY)] * 4,
        out_shape=[jax.ShapeDtypeStruct(shape, F32) for shape in shapes],
        scratch_shapes=[pltpu.VMEM(shape, F32) for shape in shapes] + [pltpu.SemaphoreType.DMA((4,))],
        compiler_params=SMALL,
    )(tail, tail2, low_head, low_diag)


def exchange_plan(
    frozen_query,
    frozen_key,
    frozen_value,
    token_adapter_input,
    query_adapter_out,
    key_adapter_out,
    value_adapter_out,
    out_grad,
    band_width,
):
    rows, width = frozen_query.shape
    rank = token_adapter_input.shape[1]
    frames = band_width.shape[0]
    heads = width // DH
    starts, counts = head_table(heads, frames)
    most = max(counts)
    columns = [[min(starts[j] + s, heads - 1) for j in range(frames)] for s in range(most)]
    numbers = [[int(s < counts[j]) for j in range(frames)] for s in range(most)]
    slots = list(zip(columns, numbers))
    lead, late, rest = slots[0], slots[1], slots[2]
    wide = [j for j in range(frames) if counts[j] == most]
    adapters = [query_adapter_out, key_adapter_out, value_adapter_out]
    arrays = (frozen_query, out_grad, frozen_key, frozen_value, token_adapter_input)

    def meet(name, block, m, targets=range(frames)):
        with jax.named_scope(f"{name}_over_tm"):
            return lax.ppermute(block, "tm", [(j ^ m, j) for j in targets])

    def swap_in_chip(name, block):
        with jax.named_scope(f"{name}_in_chip"):
            return swap(block, "rep")

    def mine(slot, m):
        return (slot[0], m, "mine")

    sent, kept, sent_late = [], [], []
    for m in range(1, frames):
        first = [mine(lead, m), (None, m, "t")]
        if m == 1:
            sent.append(first + [mine(rest, m), mine(late, m)])
        else:
            sent += [first, [mine(rest, m)]]
            sent_late.append([mine(late, m)])
    for slot in (lead, rest, late):
        kept += [[mine(slot, 0)], [(slot[0], 0, "other")]]
    kept += [[(None, 0, "t")], [(None, 0, "other t")]]
    packed = pack(frames, sent, 56, *arrays)
    packed_late = pack(frames, sent_late + kept, 16, *arrays)
    kept = packed_late[len(sent_late) :]
    block = meet("nearest", packed[0], 1)
    lead_got, rest_got, late_got = [(block, 0)], [(block, 4 * DH + rank)], [(block, 8 * DH + rank)]
    for m in range(2, frames):
        lead_got.append((meet("lead", packed[2 * m - 3], m), 0))
        rest_got.append((meet("rest", packed[2 * m - 2], m, wide), 0))
        late_got.append((meet("late", packed_late[m - 2], m), 0))

    def sides(name, n, got, wide_t, groups, skip, after=()):
        size = 4 * DH - skip + (rank if wide_t else 0)
        picked = pick([(a, start + skip) for a, start in got], size, groups, after)
        cross = [swap_in_chip(name, block) for block in picked]
        where = 2 * DH - skip
        cross = [(block, at * size + where) for block, count in zip(cross, groups) for at in range(count)]
        rows_here = [(kept[2 * n], 0)] + got
        rows_there = [(kept[2 * n + 1], 0)] + cross
        return rows_here, rows_there, cross

    *lead_side, cross = sides("lead", 0, lead_got, True, (3,), 2 * DH, kept[:1])
    t_side = (
        [(kept[6], 0)] + [(a, start + 4 * DH) for a, start in lead_got],
        [(kept[7], 0)] + [(block, start + 2 * DH) for block, start in cross],
    )
    *rest_side, _ = sides("rest", 1, rest_got, False, (3,), 2 * DH)
    early = [lead, rest]
    keep, give, *low = head_group(early, band_width, [t_side, lead_side, rest_side], adapters)
    got = swap_in_chip("early_gradients", give)
    piece = (keep + got.astype(F32)).astype(BF16)
    *late_side, _ = sides("late", 2, late_got, False, (3,), 2 * DH, [got])
    cut = 3 * rank // 2
    pair = meet("early_gradients", piece, 1)
    facing = meet("early_gradients", piece, 3)
    with jax.named_scope("early_lead_over_tm"):
        far = lax.ppermute(piece[:cut], "tm", [(0, 2), (3, 1)])
    keep, *gives = head_group([late], band_width, [t_side, late_side], adapters, low, [piece])
    gives = [swap_in_chip("late_sums", g) for g in gives]
    own_low, sends = hand_out(frames, rows, keep, gives, facing, [pair])
    gots = [meet("late_sums", block, m) for m, block in enumerate(sends, 1)]
    tail, low = collect(rest[1], own_low, sends[2], gots, piece, pair, far, facing)
    diag = [(0, 3), (1, 2), (2, 1), (3, 0)]
    with jax.named_scope("low_over_head"):
        low_head, low_diag = swap(low, "head"), lax.ppermute(low, ("head", "rep"), diag)
    outs = place(
        frames, lead[0], late[0], rest[0], tail, swap_in_chip("tail", tail), low_head, low_diag, rank, width
    )
    return tuple(outs)


def on_device(frozen_query, *rest):
    frames = rest[-1].shape[0]
    heads = frozen_query.shape[1] // DH
    whole_reach = frames == 4 and heads == 2 * frames + 2
    return (exchange_plan if whole_reach else window_plan)(frozen_query, *rest)


def solution(mesh):
    in_specs = (
        P(("groups", "tm", "rep"), "head"),
        P(("groups", "tm"), "head"),
        P(("groups", "tm"), "head"),
        P(("groups", "tm"), None),
        P(None, "head"),
        P(None, "head"),
        P(None, "head"),
        P(("groups", "tm", "rep"), "head"),
        P(),
    )
    out_specs = (
        P("groups", "head"),
        P("groups", "head"),
        P("groups", "head"),
        P(("groups", "tm"), None),
    )
    return jax.shard_map(
        on_device, mesh=mesh, in_specs=in_specs, out_specs=out_specs, check_vma=False
    )
```

```python
import functools
import math

import jax
import jax.numpy as jnp
from jax import lax
from jax.experimental import pallas as pl
from jax.experimental.pallas import tpu as pltpu
from jax.sharding import PartitionSpec as P

DH = 128
NEAR = 1
REACH = 4
SCALE = DH ** (-0.5)
SCALE_2 = SCALE * math.log2(math.e)
F32 = jnp.float32
BF16 = jnp.bfloat16
GIVES = 2
SMALL = pltpu.CompilerParams(vmem_limit_bytes=16 * 1024 * 1024)


def dot_nn(left, right):
    return lax.dot_general(left, right, (((1,), (0,)), ((), ())), preferred_element_type=F32)


def dot_nt(left, right):
    return lax.dot_general(left, right, (((1,), (1,)), ((), ())), preferred_element_type=F32)


def dot_tn(left, right):
    return lax.dot_general(left, right, (((0,), (0,)), ((), ())), preferred_element_type=F32)


def routes(count):
    found = []
    for d in range(1, min(REACH, count - 1) + 1):
        if 2 * d >= count:
            found.append((d, (-d, d)))
        else:
            found.append((d, (-d,)))
            found.append((d, (d,)))
    return found


def pairs(count, offsets):
    return [(i + o, i) for o in offsets for i in range(count) if 0 <= i + o < count]


def swap(block, axis):
    return lax.ppermute(block, axis, [(0, 1), (1, 0)])


def attention_kernel(
    blocks, bias_ref, fq_ref, do_ref, fk_ref, fv_ref, t_ref, tr_ref, tt_ref, aq_ref, ak_ref, av_ref, *refs
):
    k_refs = refs[:blocks]
    v_refs = refs[blocks : 2 * blocks]
    gq_ref, gk_ref, gv_ref, lowq_ref, low_ref = refs[2 * blocks :]
    rows = fq_ref.shape[0]

    @pl.when(pl.program_id(0) == 0)
    def _():
        lowq_ref[...] = jnp.zeros_like(lowq_ref)
        low_ref[...] = jnp.zeros_like(low_ref)

    aq, ak, av = aq_ref[...], ak_ref[...], av_ref[...]
    query = (fq_ref[...].astype(F32) + dot_nn(tr_ref[...], aq)).astype(BF16)
    do = do_ref[...]
    own_k = (fk_ref[...].astype(F32) + dot_nn(t_ref[...], ak)).astype(BF16)
    own_v = (fv_ref[...].astype(F32) + dot_nn(t_ref[...], av)).astype(BF16)
    keys = [own_k[:rows], own_k[rows:]] + [ref[...] for ref in k_refs]
    values = [own_v[:rows], own_v[rows:]] + [ref[...] for ref in v_refs]
    count = len(keys)
    scores = [dot_nt(keys[b], query) * SCALE + bias_ref[b] for b in range(count)]
    top = functools.reduce(jnp.maximum, scores)
    top = jnp.max(top, axis=0, keepdims=True)
    shifted = [jnp.exp(s - top) for s in scores]
    total = jnp.sum(functools.reduce(jnp.add, shifted), axis=0, keepdims=True)
    inverse = 1.0 / total
    probs = [s * inverse for s in shifted]
    lows = [p.astype(BF16) for p in probs]
    attended = functools.reduce(jnp.add, [dot_tn(lows[b], values[b]) for b in range(count)])
    attended = attended.astype(BF16).astype(F32)
    delta = jnp.sum((do.astype(F32) * attended).T, axis=0, keepdims=True)
    grads = [
        (probs[b] * (dot_nt(values[b], do) - delta)).astype(BF16) for b in range(count)
    ]
    dq = functools.reduce(jnp.add, [dot_tn(grads[b], keys[b]) for b in range(count)])
    dq = (dq * SCALE).astype(BF16)
    gq_ref[...] = dot_tn(tr_ref[...], dq)
    lowq_ref[...] += dot_nt(dq, aq)
    both = jnp.concatenate([ak, av], axis=1)
    for b in range(count):
        dk = (dot_nn(grads[b], query) * SCALE).astype(BF16)
        dv = dot_nn(lows[b], do).astype(BF16)
        part = jnp.concatenate([dk, dv], axis=1)
        low_ref[b * rows : (b + 1) * rows, :] += dot_nt(part, both)
        out = dot_nn(tt_ref[:, b * rows : (b + 1) * rows], part)
        if b == 0:
            total_part = out
        else:
            total_part += out
    gk_ref[...] = total_part[:, :DH]
    gv_ref[...] = total_part[:, DH:]


def attention(bias, fq, do, fk, fv, t, tr, tt, aq, ak, av, payloads):
    rows, width = fq.shape
    heads = width // DH
    rank = t.shape[1]
    blocks = len(payloads)
    count = blocks + 2

    def col(r):
        return pl.BlockSpec((r, DH), lambda h: (0, h))

    def whole(shape):
        return pl.BlockSpec(shape, lambda h: (0, 0))

    return pl.pallas_call(
        functools.partial(attention_kernel, blocks),
        grid=(heads,),
        out_shape=[
            jax.ShapeDtypeStruct((rank, width), F32),
            jax.ShapeDtypeStruct((rank, width), F32),
            jax.ShapeDtypeStruct((rank, width), F32),
            jax.ShapeDtypeStruct((rows, rank), F32),
            jax.ShapeDtypeStruct((count * rows, rank), F32),
        ],
        in_specs=[pl.BlockSpec(memory_space=pltpu.SMEM)]
        + [col(rows), col(rows), col(2 * rows), col(2 * rows)]
        + [whole(t.shape), whole(tr.shape), whole(tt.shape)]
        + [col(rank)] * 3
        + [col(rows)] * blocks
        + [pl.BlockSpec((rows, DH), lambda h: (0, heads + h))] * blocks,
        out_specs=[col(rank)] * 3 + [whole((rows, rank)), whole((count * rows, rank))],
        compiler_params=pltpu.CompilerParams(vmem_limit_bytes=32 * 1024 * 1024),
    )(bias, fq, do, fk, fv, t, tr, tt, aq, ak, av, *payloads, *payloads)


def sum_rows(part, frame_idx, half_idx, frames):
    rows, width = part.shape
    half = width // 2
    keep = lax.dynamic_slice_in_dim(part, half_idx * half, half, 1)
    give = lax.dynamic_slice_in_dim(part, (1 - half_idx) * half, half, 1)
    mine = keep + swap(give, "rep")
    if frames & (frames - 1) or rows % frames or frames > REACH + 1:
        total = lax.psum(mine, "tm").astype(BF16)
    else:
        chunk = rows // frames
        low = mine.astype(BF16)
        acc = lax.dynamic_slice_in_dim(mine, frame_idx * chunk, chunk, 0)
        for m in range(1, frames):
            give = lax.dynamic_slice_in_dim(low, (frame_idx ^ m) * chunk, chunk, 0)
            acc = acc + lax.ppermute(give, "tm", [(i, i ^ m) for i in range(frames)]).astype(F32)
        acc = acc.astype(BF16)
        total = jnp.zeros((rows, half), BF16)
        total = lax.dynamic_update_slice_in_dim(total, acc, frame_idx * chunk, 0)
        for m in range(1, frames):
            got = lax.ppermute(acc, "tm", [(i, i ^ m) for i in range(frames)])
            total = lax.dynamic_update_slice_in_dim(total, got, (frame_idx ^ m) * chunk, 0)
    other = swap(total, "rep")
    first = jnp.where(half_idx == 0, total, other)
    second = jnp.where(half_idx == 0, other, total)
    return jnp.concatenate([first, second], axis=1).astype(F32)


def window_plan(
    frozen_query,
    frozen_key,
    frozen_value,
    token_adapter_input,
    query_adapter_out,
    key_adapter_out,
    value_adapter_out,
    out_grad,
    band_width,
):
    rows, width = frozen_query.shape
    rank = token_adapter_input.shape[1]
    frames = band_width.shape[0]
    frame_idx = lax.axis_index("tm")
    half_idx = lax.axis_index("rep")
    t = token_adapter_input
    tr = lax.dynamic_slice_in_dim(t, half_idx * rows, rows, 0)

    def tile_rows_of(frozen, adapter):
        own = lax.dynamic_slice_in_dim(frozen, half_idx * rows, rows, 0)
        return (own.astype(F32) + dot_nn(tr, adapter)).astype(BF16)

    payload = jnp.concatenate(
        [tile_rows_of(frozen_key, key_adapter_out), tile_rows_of(frozen_value, value_adapter_out), tr],
        axis=1,
    )

    frame_ids = jnp.arange(frames)
    band_row = jnp.sum(jnp.where((frame_ids == frame_idx)[:, None], band_width, 0), axis=0)

    def band_at(offsets):
        seen = functools.reduce(jnp.logical_or, [frame_ids == frame_idx + o for o in offsets])
        return jnp.sum(jnp.where(seen, band_row, 0))

    own_band = band_at((0,))
    allowed = [jnp.abs(half_idx - tile) < own_band for tile in range(2)]
    payloads = []
    plan = routes(frames)
    for d, offsets in plan:
        got = lax.ppermute(payload, "tm", pairs(frames, offsets))
        band = band_at(offsets)
        payloads.append(got)
        allowed.append(band > 0)
        if d <= NEAR:
            payloads.append(swap(got, "rep"))
            allowed.append(band > 1)
    bias = jnp.where(jnp.stack(allowed), 0.0, -jnp.inf).astype(F32)
    tt = jnp.concatenate([t] + [p[:, 2 * width :] for p in payloads], axis=0).T

    gq, gk, gv, low_q, low_b = attention(
        bias, frozen_query, out_grad, frozen_key, frozen_value, t, tr, tt,
        query_adapter_out, key_adapter_out, value_adapter_out, payloads,
    )

    own = low_b[: 2 * rows]
    same = lax.dynamic_slice_in_dim(own, half_idx * rows, rows, 0) + low_q
    other = lax.dynamic_slice_in_dim(own, (1 - half_idx) * rows, rows, 0)
    start = 2 * rows
    for d, offsets in plan:
        size = 2 * rows if d <= NEAR else rows
        back = [(target, source) for source, target in pairs(frames, offsets)]
        got = lax.ppermute(low_b[start : start + size], "tm", back)
        start += size
        same = same + got[:rows]
        if d <= NEAR:
            other = other + got[rows:]
    low = jnp.where(
        half_idx == 0,
        jnp.concatenate([same, other], axis=0),
        jnp.concatenate([other, same], axis=0),
    )
    low = low + swap(low, "rep")
    low = low + swap(low, "head")

    grads = sum_rows(jnp.concatenate([gq, gk, gv], axis=0), frame_idx, half_idx, frames)
    return grads[:rank], grads[rank : 2 * rank], grads[2 * rank :], low


def head_table(heads, frames):
    base, extra = divmod(heads, frames)
    lead = (frames - extra) // 2
    counts = [base + (1 if lead <= j < lead + extra else 0) for j in range(frames)]
    return [sum(counts[:j]) for j in range(frames)], counts


def lookup(table, index):
    value = jnp.int32(table[0])
    for j in range(1, len(table)):
        value = jnp.where(index == j, jnp.int32(table[j]), value)
    return value


def column(head):
    return pl.ds(pl.multiple_of(head * DH, DH), DH)


def vmem(count):
    return [pl.BlockSpec(memory_space=pltpu.VMEM)] * count


def pack_kernel(frames, outputs, fq_ref, do_ref, fk_ref, fv_ref, t_ref, *refs):
    outs, (q_in, do_in, k_in, v_in, k2_in, v2_in, t_in, sems) = refs[:-8], refs[-8:]
    wanted = {what for parts in outputs for _, _, what in parts}
    me, half = lax.axis_index("tm"), lax.axis_index("rep")
    rows = fq_ref.shape[0]
    mine = pl.ds(pl.multiple_of(half * rows, rows), rows)
    rest = pl.ds(pl.multiple_of((1 - half) * rows, rows), rows)
    moves = [
        (fq_ref, q_in), (do_ref, do_in), (fk_ref.at[mine, :], k_in), (fv_ref.at[mine, :], v_in), (t_ref, t_in)
    ]
    if "other" in wanted:
        moves += [(fk_ref.at[rest, :], k2_in), (fv_ref.at[rest, :], v2_in)]
    copies = [pltpu.make_async_copy(a, b, sems.at[n]) for n, (a, b) in enumerate(moves)]
    for copy in copies:
        copy.start()
    for copy in copies:
        copy.wait()
    for out, parts in zip(outs, outputs):
        at = 0
        for table, m, what in parts:
            if what in ("t", "other t"):
                blocks = [t_in[mine if what == "t" else rest, :]]
            else:
                cols = column(lookup(table, me ^ m))
                sources = (q_in, do_in, k_in, v_in) if what == "mine" else (k2_in, v2_in)
                blocks = [ref[:, cols] for ref in sources]
            for block in blocks:
                out[:, at : at + block.shape[1]] = block
                at += block.shape[1]


def pack(frames, outputs, limit, fq, do, fk, fv, t):
    rows, width = fq.shape
    size = {"mine": 4 * DH, "other": 2 * DH, "t": t.shape[1], "other t": t.shape[1]}
    return pl.pallas_call(
        functools.partial(pack_kernel, frames, outputs),
        in_specs=[pl.BlockSpec(memory_space=pltpu.HBM)] * 5,
        out_specs=vmem(len(outputs)),
        out_shape=[
            jax.ShapeDtypeStruct((rows, sum(size[what] for _, _, what in parts)), BF16)
            for parts in outputs
        ],
        scratch_shapes=[pltpu.VMEM((rows, width), BF16)] * 6
        + [pltpu.VMEM(t.shape, BF16), pltpu.SemaphoreType.DMA((7,))],
        compiler_params=pltpu.CompilerParams(vmem_limit_bytes=limit * 1024 * 1024),
    )(fq, do, fk, fv, t)


def pick_kernel(spans, groups, *refs):
    n = 0
    for out, count in zip(refs[-len(groups) :], groups):
        for at in range(count):
            start, size = spans[n]
            out[:, at * size : (at + 1) * size] = refs[n][:, start : start + size]
            n += 1


def pick(parts, size, groups, after=()):
    arrays = [array for array, _ in parts]
    rows, dtype = arrays[0].shape[0], arrays[0].dtype
    return pl.pallas_call(
        functools.partial(pick_kernel, [(start, size) for _, start in parts], groups),
        in_specs=vmem(len(arrays)) + [pl.BlockSpec(memory_space=pl.ANY)] * len(after),
        out_specs=vmem(len(groups)),
        out_shape=[jax.ShapeDtypeStruct((rows, size * count), dtype) for count in groups],
        compiler_params=SMALL,
    )(*arrays, *after)


def one_head(frames, bands, q, do, frozen_k, frozen_v, tokens, aq, ak, av):
    flat = q.shape[0]
    rows = flat // frames
    t_same = tokens[:flat]

    def adapted(frozen, rows_of, adapter):
        return (frozen.astype(F32) + dot_nn(rows_of, adapter)).astype(BF16)

    query = adapted(q, t_same, aq)
    keys, values = adapted(frozen_k, tokens, ak), adapted(frozen_v, tokens, av)
    do_t, keys_t, values_t = do.T, keys.T, values.T

    def bias(i, b):
        j, need = (b, 0) if b < frames else (b - frames, 1)
        value = jnp.where(bands[i, j] > need, 0.0, -jnp.inf).astype(F32)
        return jnp.full((1, rows), value, F32)

    span = 2 if frames % 2 == 0 else 1
    wide = span * rows
    groups = [range(first, first + span) for first in range(0, frames, span)]
    seen = [
        list(range(frames))
        + [frames + j for j in range(frames) if any(abs(i - j) <= NEAR for i in mine)]
        for mine in groups
    ]
    here = [slice(mine[0] * rows, mine[0] * rows + wide) for mine in groups]
    pairs_of = range(len(groups))

    def gather(whole, g, axis):
        parts = [
            whole[b * rows : (b + 1) * rows] if axis == 0 else whole[:, b * rows : (b + 1) * rows]
            for b in seen[g]
        ]
        return jnp.concatenate(parts, axis=axis)

    def block(whole, n):
        return whole[n * rows : (n + 1) * rows]

    def softmax(g, raw):
        scores = [
            block(raw, n) * SCALE_2 + jnp.concatenate([bias(i, b) for i in groups[g]], axis=1)
            for n, b in enumerate(seen[g])
        ]
        top = jnp.max(functools.reduce(jnp.maximum, scores), axis=0, keepdims=True)
        shifted = [jnp.exp2(s - top) for s in scores]
        inverse = 1.0 / jnp.sum(functools.reduce(jnp.add, shifted), axis=0, keepdims=True)
        return [s * inverse for s in shifted]

    raws = [dot_nt(gather(keys, g, 0), query[here[g]]) for g in pairs_of]
    prob_grads = [dot_nt(gather(values, g, 0), do[here[g]]) for g in pairs_of]
    probs = [softmax(g, raws[g]) for g in pairs_of]
    lows = [jnp.concatenate([p.astype(BF16) for p in probs[g]], axis=0) for g in pairs_of]
    grads = []
    for g in pairs_of:
        attended = dot_nn(gather(values_t, g, 1), lows[g]).astype(BF16).astype(F32)
        delta = jnp.sum(do_t[:, here[g]].astype(F32) * attended, axis=0, keepdims=True)
        parts = [
            (probs[g][n] * (block(prob_grads[g], n) - delta)).astype(BF16) for n in range(len(seen[g]))
        ]
        grads.append(jnp.concatenate(parts, axis=0))
    dvs, dks = [None] * (2 * frames), [None] * (2 * frames)

    def add(sums, g, whole):
        for n, b in enumerate(seen[g]):
            sums[b] = block(whole, n) if sums[b] is None else sums[b] + block(whole, n)

    for g in pairs_of:
        add(dvs, g, dot_nn(lows[g], do[here[g]]))
    for g in pairs_of:
        add(dks, g, dot_nn(grads[g], query[here[g]]))
    dqs = [(dot_nn(gather(keys_t, g, 1), grads[g]) * SCALE).astype(BF16).T for g in pairs_of]
    dq = jnp.concatenate(dqs, axis=0)
    dk = (jnp.concatenate(dks, axis=0) * SCALE).astype(BF16)
    dv = jnp.concatenate(dvs, axis=0).astype(BF16)
    both = jnp.concatenate([dk, dv], axis=1)
    sums = dot_tn(tokens, both)
    grads = jnp.concatenate([dot_tn(t_same, dq), sums[:, :DH], sums[:, DH:]], axis=0)
    lows = dot_nt(both, jnp.concatenate([ak, av], axis=1))
    return grads, lows[:flat] + dot_nt(dq, aq), lows[flat:]


def group_kernel(heads, frames, chained, waits, sides, count, *refs):
    refs = list(refs)

    def take(count):
        taken = refs[:count]
        del refs[:count]
        return taken

    (bands,) = take(1)
    arrays, adapters = take(count), take(3)
    before = take(2) if chained else None
    take(waits)
    keep_ref, *give_refs = take(1 + GIVES if chained else 2)
    low_refs = [] if chained else take(2)
    q, do, k, v, tokens = refs
    me, half = lax.axis_index("tm"), lax.axis_index("rep")
    rows = arrays[0].shape[0]
    flat = frames * rows
    cut = 3 * tokens.shape[1] // 2
    first = half == 0
    same_at = [pl.ds(pl.multiple_of((me ^ m) * rows, rows), rows) for m in range(frames)]
    other_at = [pl.ds(pl.multiple_of(flat + (me ^ m) * rows, rows), rows) for m in range(frames)]

    def put(targets, places, rows_at):
        for m, (n, start) in enumerate(places):
            for c, target in enumerate(targets):
                target[rows_at[m], :] = arrays[n][:, start + c * DH : start + (c + 1) * DH]

    put([tokens], sides[0][0], same_at)
    put([tokens], sides[0][1], other_at)

    def run(n, table):
        put([q, do, k, v], sides[1 + n][0], same_at)
        put([k, v], sides[1 + n][1], other_at)
        cols = column(lookup(table, me))
        grads, low_same, low_other = one_head(
            frames, bands, q[...], do[...], k[...], v[...], tokens[...], *[a[:, cols] for a in adapters]
        )
        keep = jnp.where(first, grads[:cut], grads[cut:])
        give = jnp.where(first, grads[cut:], grads[:cut])
        return keep, give, low_same, low_other

    if chained:
        keep, give, low_same, low_other = run(0, heads[0][0])
        keep_ref[:cut, :] = keep
        keep_ref[cut:, :] = before[0][...] + low_same
        give = jnp.concatenate([give, before[1][...] + low_other], axis=0)
        size = give.shape[0] // GIVES
        for n, ref in enumerate(give_refs):
            ref[...] = give[n * size : (n + 1) * size].astype(ref.dtype)
        return
    for n, (table, counts) in enumerate(heads):
        here = slice(n * cut, (n + 1) * cut)

        def body():
            keep, give, low_same, low_other = run(n, table)
            keep_ref[here, :] = keep
            give_refs[0][here, :] = give.astype(BF16)
            if n == 0:
                low_refs[0][...] = low_same
                low_refs[1][...] = low_other
            else:
                low_refs[0][...] += low_same
                low_refs[1][...] += low_other

        if min(counts) > 0:
            body()
        else:
            live = lookup(counts, me) > 0
            pl.when(live)(body)

            @pl.when(jnp.logical_not(live))
            def _():
                keep_ref[here, :] = jnp.zeros((cut, DH), F32)
                give_refs[0][here, :] = jnp.zeros((cut, DH), BF16)


def head_group(heads, bands, sides, adapters, before=(), after=()):
    frames = len(sides[0][0])
    arrays, places = [], []
    for side in sides:
        found = []
        for pairs_of in side:
            found.append([])
            for array, start in pairs_of:
                known = [n for n, a in enumerate(arrays) if a is array]
                if not known:
                    arrays.append(array)
                found[-1].append((known[0] if known else len(arrays) - 1, start))
        places.append(found)
    rows, rank = arrays[0].shape[0], adapters[0].shape[0]
    flat = frames * rows
    size = len(heads) * 3 * rank // 2
    chained = len(before) > 0
    args = [bands, *arrays, *adapters, *before, *after]
    specs = [pl.BlockSpec(memory_space=pltpu.SMEM)] + vmem(len(arrays) + 3 + len(before))
    specs += [pl.BlockSpec(memory_space=pl.ANY)] * len(after)
    low = jax.ShapeDtypeStruct((flat, rank), F32)
    if chained:
        part = jax.ShapeDtypeStruct(((size + flat) // GIVES, rank), BF16)
        shapes = [jax.ShapeDtypeStruct((size + flat, rank), F32)] + [part] * GIVES
    else:
        edge = jax.ShapeDtypeStruct((size, rank), F32)
        shapes = [edge, jax.ShapeDtypeStruct((size, rank), BF16), low, low]
    return pl.pallas_call(
        functools.partial(
            group_kernel, heads, frames, chained, len(after), places, len(arrays)
        ),
        in_specs=specs,
        out_specs=vmem(len(shapes)),
        out_shape=shapes,
        scratch_shapes=[pltpu.VMEM((flat, DH), BF16)] * 2
        + [pltpu.VMEM((2 * flat, DH), BF16)] * 2
        + [pltpu.VMEM((2 * flat, rank), BF16)],
        compiler_params=pltpu.CompilerParams(vmem_limit_bytes=40 * 1024 * 1024),
    )(*args)


def hand_out_kernel(frames, size, parts, keep_ref, *refs):
    gots, facing, (own_ref, *sends, total) = refs[:parts], refs[-frames - 2], refs[-frames - 1 :]
    me = lax.axis_index("tm")
    rows = own_ref.shape[0]
    total[...] = keep_ref[...] + jnp.concatenate([got[...].astype(F32) for got in gots], axis=0)
    for m in range(frames):
        low = total[pl.ds(pl.multiple_of(size + (me ^ m) * rows, 8), rows), :]
        if m == 0:
            own_ref[...] = low
        else:
            sends[m - 1][:rows, :] = low.astype(BF16)
            sends[m - 1][rows : rows + size, :] = total[:size, :].astype(BF16)
    sends[0][rows + size :, :] = facing[...]


def hand_out(frames, rows, keep, gots, facing, after):
    size, rank = keep.shape[0] - frames * rows, keep.shape[1]
    own, *sends = pl.pallas_call(
        functools.partial(hand_out_kernel, frames, size, len(gots)),
        in_specs=vmem(1 + len(gots)) + [pl.BlockSpec(memory_space=pl.ANY)] * len(after) + vmem(1),
        out_specs=vmem(frames),
        out_shape=[jax.ShapeDtypeStruct((rows, rank), F32)]
        + [jax.ShapeDtypeStruct((rows + size * n, rank), BF16) for n in (3, 1, 1)],
        scratch_shapes=[pltpu.VMEM(keep.shape, F32)],
        compiler_params=SMALL,
    )(keep, *gots, *after, facing)
    return own, sends


def collect_kernel(wide, own_low, own, near, third, last, piece, pair, far, facing, out_ref, low_ref):
    rows = own_low.shape[0]
    size = own.shape[0] - rows
    low = own_low[...]
    for got in (near, third, last):
        low = low + got[:rows, :].astype(F32)
    out_ref[:rows, :] = low.astype(BF16)
    low_ref[...] = low.astype(BF16)
    middle = lookup(wide, lax.axis_index("tm")) > 0

    def part(ref, n):
        return ref[rows + n * size : rows + (n + 1) * size, :]

    blocks = [part(ref, 0) for ref in (own, near, third, last)]
    blocks += [piece[:size, :], pair[:size, :]]
    blocks += [jnp.where(middle, far[...], part(near, 1)), facing[:size, :]]
    blocks.append(jnp.where(middle, piece[size:, :], pair[size:, :]))
    blocks.append(jnp.where(middle, facing[size:, :], part(near, 2)))
    for n, block in enumerate(blocks):
        out_ref[rows + n * size : rows + (n + 1) * size, :] = block


def collect(wide, own_low, own, gots, *pieces):
    (rows, rank), size = own_low.shape, pieces[0].shape[0] // 2
    return pl.pallas_call(
        functools.partial(collect_kernel, wide),
        in_specs=vmem(2 + len(gots) + len(pieces)),
        out_specs=vmem(2),
        out_shape=[
            jax.ShapeDtypeStruct((rows + 10 * size, rank), BF16),
            jax.ShapeDtypeStruct((rows, rank), BF16),
        ],
        compiler_params=SMALL,
    )(own_low, own, *gots, *pieces)


def place_kernel(frames, lead, late, rest, tail, tail2, low_head, low_diag, *refs):
    outs, filled, sems = refs[:4], refs[4:8], refs[8]
    me, half = lax.axis_index("tm"), lax.axis_index("rep")
    first = half == 0
    rank = filled[0].shape[0]
    cut = 3 * rank // 2
    rows = low_head.shape[0]
    side = me // 2
    places = [lookup(late, me ^ m) for m in range(frames)] + [lookup(lead, me ^ m) for m in range(frames)]
    places += [lookup(rest, 1 + side), lookup(rest, 2 - side)]
    copies = [pltpu.make_async_copy(filled[o], outs[o], sems.at[o]) for o in range(4)]

    def rows_of(ref, n, start, stop):
        return ref[rows + n * cut + start : rows + n * cut + stop, :].astype(F32)

    for o in range(3):
        for n, head in enumerate(places):
            parts = []
            for owner, low_end, high_end in ((0, 0, cut), (1, cut, 2 * cut)):
                start, stop = max(o * rank, low_end), min((o + 1) * rank, high_end)
                if start < stop:
                    mine, its = (rows_of(ref, n, start - low_end, stop - low_end) for ref in (tail, tail2))
                    parts.append(jnp.where(first, mine, its) if owner == 0 else jnp.where(first, its, mine))
            filled[o][:, column(head)] = parts[0] if len(parts) == 1 else jnp.concatenate(parts, axis=0)
        copies[o].start()
    same = tail[:rows, :].astype(F32) + low_head[...].astype(F32)
    other = tail2[:rows, :].astype(F32) + low_diag[...].astype(F32)
    filled[3][:rows, :] = jnp.where(first, same, other)
    filled[3][rows:, :] = jnp.where(first, other, same)
    copies[3].start()
    for copy in copies:
        copy.wait()


def place(frames, lead, late, rest, tail, tail2, low_head, low_diag, rank, width):
    rows = low_head.shape[0]
    shapes = [(rank, width)] * 3 + [(2 * rows, rank)]
    return pl.pallas_call(
        functools.partial(place_kernel, frames, lead, late, rest),
        in_specs=vmem(4),
        out_specs=[pl.BlockSpec(memory_space=pl.ANY)] * 4,
        out_shape=[jax.ShapeDtypeStruct(shape, F32) for shape in shapes],
        scratch_shapes=[pltpu.VMEM(shape, F32) for shape in shapes] + [pltpu.SemaphoreType.DMA((4,))],
        compiler_params=SMALL,
    )(tail, tail2, low_head, low_diag)


def exchange_plan(
    frozen_query,
    frozen_key,
    frozen_value,
    token_adapter_input,
    query_adapter_out,
    key_adapter_out,
    value_adapter_out,
    out_grad,
    band_width,
):
    rows, width = frozen_query.shape
    rank = token_adapter_input.shape[1]
    frames = band_width.shape[0]
    heads = width // DH
    starts, counts = head_table(heads, frames)
    most = max(counts)
    columns = [[min(starts[j] + s, heads - 1) for j in range(frames)] for s in range(most)]
    numbers = [[int(s < counts[j]) for j in range(frames)] for s in range(most)]
    slots = list(zip(columns, numbers))
    lead, late, rest = slots[0], slots[1], slots[2]
    wide = [j for j in range(frames) if counts[j] == most]
    adapters = [query_adapter_out, key_adapter_out, value_adapter_out]
    arrays = (frozen_query, out_grad, frozen_key, frozen_value, token_adapter_input)

    def meet(name, block, m, targets=range(frames)):
        with jax.named_scope(f"{name}_over_tm"):
            return lax.ppermute(block, "tm", [(j ^ m, j) for j in targets])

    def swap_in_chip(name, block):
        with jax.named_scope(f"{name}_in_chip"):
            return swap(block, "rep")

    def mine(slot, m):
        return (slot[0], m, "mine")

    sent, kept, sent_late = [], [], []
    for m in range(1, frames):
        first = [mine(lead, m), (None, m, "t")]
        if m == 1:
            sent.append(first + [mine(rest, m), mine(late, m)])
        else:
            sent += [first, [mine(rest, m)]]
            sent_late.append([mine(late, m)])
    for slot in (lead, rest, late):
        kept += [[mine(slot, 0)], [(slot[0], 0, "other")]]
    kept += [[(None, 0, "t")], [(None, 0, "other t")]]
    packed = pack(frames, sent, 56, *arrays)
    packed_late = pack(frames, sent_late + kept, 16, *arrays)
    kept = packed_late[len(sent_late) :]
    block = meet("nearest", packed[0], 1)
    lead_got, rest_got, late_got = [(block, 0)], [(block, 4 * DH + rank)], [(block, 8 * DH + rank)]
    for m in range(2, frames):
        lead_got.append((meet("lead", packed[2 * m - 3], m), 0))
        rest_got.append((meet("rest", packed[2 * m - 2], m, wide), 0))
        late_got.append((meet("late", packed_late[m - 2], m), 0))

    def sides(name, n, got, wide_t, groups, skip, after=()):
        size = 4 * DH - skip + (rank if wide_t else 0)
        picked = pick([(a, start + skip) for a, start in got], size, groups, after)
        cross = [swap_in_chip(name, block) for block in picked]
        where = 2 * DH - skip
        cross = [(block, at * size + where) for block, count in zip(cross, groups) for at in range(count)]
        rows_here = [(kept[2 * n], 0)] + got
        rows_there = [(kept[2 * n + 1], 0)] + cross
        return rows_here, rows_there, cross

    *lead_side, cross = sides("lead", 0, lead_got, True, (3,), 2 * DH, kept[:1])
    t_side = (
        [(kept[6], 0)] + [(a, start + 4 * DH) for a, start in lead_got],
        [(kept[7], 0)] + [(block, start + 2 * DH) for block, start in cross],
    )
    *rest_side, _ = sides("rest", 1, rest_got, False, (3,), 2 * DH)
    early = [lead, rest]
    keep, give, *low = head_group(early, band_width, [t_side, lead_side, rest_side], adapters)
    got = swap_in_chip("early_gradients", give)
    piece = (keep + got.astype(F32)).astype(BF16)
    *late_side, _ = sides("late", 2, late_got, False, (3,), 2 * DH, [got])
    cut = 3 * rank // 2
    pair = meet("early_pair", piece, 1)
    facing = meet("early_facing", piece, 3)
    with jax.named_scope("early_lead_over_tm"):
        far = lax.ppermute(piece[:cut], "tm", [(0, 2), (3, 1)])
    keep, *gives = head_group([late], band_width, [t_side, late_side], adapters, low, [piece])
    gives = [swap_in_chip("late_sums", g) for g in gives]
    own_low, sends = hand_out(frames, rows, keep, gives, facing, [pair])
    gots = [meet("late_sums", block, m) for m, block in enumerate(sends, 1)]
    tail, low = collect(rest[1], own_low, sends[2], gots, piece, pair, far, facing)
    diag = [(0, 3), (1, 2), (2, 1), (3, 0)]
    with jax.named_scope("low_over_head"):
        low_head, low_diag = swap(low, "head"), lax.ppermute(low, ("head", "rep"), diag)
    outs = place(
        frames, lead[0], late[0], rest[0], tail, swap_in_chip("tail", tail), low_head, low_diag, rank, width
    )
    return tuple(outs)


def on_device(frozen_query, *rest):
    frames = rest[-1].shape[0]
    heads = frozen_query.shape[1] // DH
    whole_reach = frames == 4 and heads == 2 * frames + 2
    return (exchange_plan if whole_reach else window_plan)(frozen_query, *rest)


def solution(mesh):
    in_specs = (
        P(("groups", "tm", "rep"), "head"),
        P(("groups", "tm"), "head"),
        P(("groups", "tm"), "head"),
        P(("groups", "tm"), None),
        P(None, "head"),
        P(None, "head"),
        P(None, "head"),
        P(("groups", "tm", "rep"), "head"),
        P(),
    )
    out_specs = (
        P("groups", "head"),
        P("groups", "head"),
        P("groups", "head"),
        P(("groups", "tm"), None),
    )
    return jax.shard_map(
        on_device, mesh=mesh, in_specs=in_specs, out_specs=out_specs, check_vma=False
    )
```

```python
import functools
import math

import jax
import jax.numpy as jnp
from jax import lax
from jax.experimental import pallas as pl
from jax.experimental.pallas import tpu as pltpu
from jax.sharding import PartitionSpec as P

DH = 128
NEAR = 1
REACH = 4
SCALE = DH ** (-0.5)
SCALE_2 = SCALE * math.log2(math.e)
F32 = jnp.float32
BF16 = jnp.bfloat16
GIVES = 2
SMALL = pltpu.CompilerParams(vmem_limit_bytes=16 * 1024 * 1024)


def dot_nn(left, right):
    return lax.dot_general(left, right, (((1,), (0,)), ((), ())), preferred_element_type=F32)


def dot_nt(left, right):
    return lax.dot_general(left, right, (((1,), (1,)), ((), ())), preferred_element_type=F32)


def dot_tn(left, right):
    return lax.dot_general(left, right, (((0,), (0,)), ((), ())), preferred_element_type=F32)


def routes(count):
    found = []
    for d in range(1, min(REACH, count - 1) + 1):
        if 2 * d >= count:
            found.append((d, (-d, d)))
        else:
            found.append((d, (-d,)))
            found.append((d, (d,)))
    return found


def pairs(count, offsets):
    return [(i + o, i) for o in offsets for i in range(count) if 0 <= i + o < count]


def swap(block, axis):
    return lax.ppermute(block, axis, [(0, 1), (1, 0)])


def attention_kernel(
    blocks, bias_ref, fq_ref, do_ref, fk_ref, fv_ref, t_ref, tr_ref, tt_ref, aq_ref, ak_ref, av_ref, *refs
):
    k_refs = refs[:blocks]
    v_refs = refs[blocks : 2 * blocks]
    gq_ref, gk_ref, gv_ref, lowq_ref, low_ref = refs[2 * blocks :]
    rows = fq_ref.shape[0]

    @pl.when(pl.program_id(0) == 0)
    def _():
        lowq_ref[...] = jnp.zeros_like(lowq_ref)
        low_ref[...] = jnp.zeros_like(low_ref)

    aq, ak, av = aq_ref[...], ak_ref[...], av_ref[...]
    query = (fq_ref[...].astype(F32) + dot_nn(tr_ref[...], aq)).astype(BF16)
    do = do_ref[...]
    own_k = (fk_ref[...].astype(F32) + dot_nn(t_ref[...], ak)).astype(BF16)
    own_v = (fv_ref[...].astype(F32) + dot_nn(t_ref[...], av)).astype(BF16)
    keys = [own_k[:rows], own_k[rows:]] + [ref[...] for ref in k_refs]
    values = [own_v[:rows], own_v[rows:]] + [ref[...] for ref in v_refs]
    count = len(keys)
    scores = [dot_nt(keys[b], query) * SCALE + bias_ref[b] for b in range(count)]
    top = functools.reduce(jnp.maximum, scores)
    top = jnp.max(top, axis=0, keepdims=True)
    shifted = [jnp.exp(s - top) for s in scores]
    total = jnp.sum(functools.reduce(jnp.add, shifted), axis=0, keepdims=True)
    inverse = 1.0 / total
    probs = [s * inverse for s in shifted]
    lows = [p.astype(BF16) for p in probs]
    attended = functools.reduce(jnp.add, [dot_tn(lows[b], values[b]) for b in range(count)])
    attended = attended.astype(BF16).astype(F32)
    delta = jnp.sum((do.astype(F32) * attended).T, axis=0, keepdims=True)
    grads = [
        (probs[b] * (dot_nt(values[b], do) - delta)).astype(BF16) for b in range(count)
    ]
    dq = functools.reduce(jnp.add, [dot_tn(grads[b], keys[b]) for b in range(count)])
    dq = (dq * SCALE).astype(BF16)
    gq_ref[...] = dot_tn(tr_ref[...], dq)
    lowq_ref[...] += dot_nt(dq, aq)
    both = jnp.concatenate([ak, av], axis=1)
    for b in range(count):
        dk = (dot_nn(grads[b], query) * SCALE).astype(BF16)
        dv = dot_nn(lows[b], do).astype(BF16)
        part = jnp.concatenate([dk, dv], axis=1)
        low_ref[b * rows : (b + 1) * rows, :] += dot_nt(part, both)
        out = dot_nn(tt_ref[:, b * rows : (b + 1) * rows], part)
        if b == 0:
            total_part = out
        else:
            total_part += out
    gk_ref[...] = total_part[:, :DH]
    gv_ref[...] = total_part[:, DH:]


def attention(bias, fq, do, fk, fv, t, tr, tt, aq, ak, av, payloads):
    rows, width = fq.shape
    heads = width // DH
    rank = t.shape[1]
    blocks = len(payloads)
    count = blocks + 2

    def col(r):
        return pl.BlockSpec((r, DH), lambda h: (0, h))

    def whole(shape):
        return pl.BlockSpec(shape, lambda h: (0, 0))

    return pl.pallas_call(
        functools.partial(attention_kernel, blocks),
        grid=(heads,),
        out_shape=[
            jax.ShapeDtypeStruct((rank, width), F32),
            jax.ShapeDtypeStruct((rank, width), F32),
            jax.ShapeDtypeStruct((rank, width), F32),
            jax.ShapeDtypeStruct((rows, rank), F32),
            jax.ShapeDtypeStruct((count * rows, rank), F32),
        ],
        in_specs=[pl.BlockSpec(memory_space=pltpu.SMEM)]
        + [col(rows), col(rows), col(2 * rows), col(2 * rows)]
        + [whole(t.shape), whole(tr.shape), whole(tt.shape)]
        + [col(rank)] * 3
        + [col(rows)] * blocks
        + [pl.BlockSpec((rows, DH), lambda h: (0, heads + h))] * blocks,
        out_specs=[col(rank)] * 3 + [whole((rows, rank)), whole((count * rows, rank))],
        compiler_params=pltpu.CompilerParams(vmem_limit_bytes=32 * 1024 * 1024),
    )(bias, fq, do, fk, fv, t, tr, tt, aq, ak, av, *payloads, *payloads)


def sum_rows(part, frame_idx, half_idx, frames):
    rows, width = part.shape
    half = width // 2
    keep = lax.dynamic_slice_in_dim(part, half_idx * half, half, 1)
    give = lax.dynamic_slice_in_dim(part, (1 - half_idx) * half, half, 1)
    mine = keep + swap(give, "rep")
    if frames & (frames - 1) or rows % frames or frames > REACH + 1:
        total = lax.psum(mine, "tm").astype(BF16)
    else:
        chunk = rows // frames
        low = mine.astype(BF16)
        acc = lax.dynamic_slice_in_dim(mine, frame_idx * chunk, chunk, 0)
        for m in range(1, frames):
            give = lax.dynamic_slice_in_dim(low, (frame_idx ^ m) * chunk, chunk, 0)
            acc = acc + lax.ppermute(give, "tm", [(i, i ^ m) for i in range(frames)]).astype(F32)
        acc = acc.astype(BF16)
        total = jnp.zeros((rows, half), BF16)
        total = lax.dynamic_update_slice_in_dim(total, acc, frame_idx * chunk, 0)
        for m in range(1, frames):
            got = lax.ppermute(acc, "tm", [(i, i ^ m) for i in range(frames)])
            total = lax.dynamic_update_slice_in_dim(total, got, (frame_idx ^ m) * chunk, 0)
    other = swap(total, "rep")
    first = jnp.where(half_idx == 0, total, other)
    second = jnp.where(half_idx == 0, other, total)
    return jnp.concatenate([first, second], axis=1).astype(F32)


def window_plan(
    frozen_query,
    frozen_key,
    frozen_value,
    token_adapter_input,
    query_adapter_out,
    key_adapter_out,
    value_adapter_out,
    out_grad,
    band_width,
):
    rows, width = frozen_query.shape
    rank = token_adapter_input.shape[1]
    frames = band_width.shape[0]
    frame_idx = lax.axis_index("tm")
    half_idx = lax.axis_index("rep")
    t = token_adapter_input
    tr = lax.dynamic_slice_in_dim(t, half_idx * rows, rows, 0)

    def tile_rows_of(frozen, adapter):
        own = lax.dynamic_slice_in_dim(frozen, half_idx * rows, rows, 0)
        return (own.astype(F32) + dot_nn(tr, adapter)).astype(BF16)

    payload = jnp.concatenate(
        [tile_rows_of(frozen_key, key_adapter_out), tile_rows_of(frozen_value, value_adapter_out), tr],
        axis=1,
    )

    frame_ids = jnp.arange(frames)
    band_row = jnp.sum(jnp.where((frame_ids == frame_idx)[:, None], band_width, 0), axis=0)

    def band_at(offsets):
        seen = functools.reduce(jnp.logical_or, [frame_ids == frame_idx + o for o in offsets])
        return jnp.sum(jnp.where(seen, band_row, 0))

    own_band = band_at((0,))
    allowed = [jnp.abs(half_idx - tile) < own_band for tile in range(2)]
    payloads = []
    plan = routes(frames)
    for d, offsets in plan:
        got = lax.ppermute(payload, "tm", pairs(frames, offsets))
        band = band_at(offsets)
        payloads.append(got)
        allowed.append(band > 0)
        if d <= NEAR:
            payloads.append(swap(got, "rep"))
            allowed.append(band > 1)
    bias = jnp.where(jnp.stack(allowed), 0.0, -jnp.inf).astype(F32)
    tt = jnp.concatenate([t] + [p[:, 2 * width :] for p in payloads], axis=0).T

    gq, gk, gv, low_q, low_b = attention(
        bias, frozen_query, out_grad, frozen_key, frozen_value, t, tr, tt,
        query_adapter_out, key_adapter_out, value_adapter_out, payloads,
    )

    own = low_b[: 2 * rows]
    same = lax.dynamic_slice_in_dim(own, half_idx * rows, rows, 0) + low_q
    other = lax.dynamic_slice_in_dim(own, (1 - half_idx) * rows, rows, 0)
    start = 2 * rows
    for d, offsets in plan:
        size = 2 * rows if d <= NEAR else rows
        back = [(target, source) for source, target in pairs(frames, offsets)]
        got = lax.ppermute(low_b[start : start + size], "tm", back)
        start += size
        same = same + got[:rows]
        if d <= NEAR:
            other = other + got[rows:]
    low = jnp.where(
        half_idx == 0,
        jnp.concatenate([same, other], axis=0),
        jnp.concatenate([other, same], axis=0),
    )
    low = low + swap(low, "rep")
    low = low + swap(low, "head")

    grads = sum_rows(jnp.concatenate([gq, gk, gv], axis=0), frame_idx, half_idx, frames)
    return grads[:rank], grads[rank : 2 * rank], grads[2 * rank :], low


def head_table(heads, frames):
    base, extra = divmod(heads, frames)
    lead = (frames - extra) // 2
    counts = [base + (1 if lead <= j < lead + extra else 0) for j in range(frames)]
    return [sum(counts[:j]) for j in range(frames)], counts


def lookup(table, index):
    value = jnp.int32(table[0])
    for j in range(1, len(table)):
        value = jnp.where(index == j, jnp.int32(table[j]), value)
    return value


def column(head):
    return pl.ds(pl.multiple_of(head * DH, DH), DH)


def vmem(count):
    return [pl.BlockSpec(memory_space=pltpu.VMEM)] * count


def pack_kernel(frames, outputs, fq_ref, do_ref, fk_ref, fv_ref, t_ref, *refs):
    outs, (q_in, do_in, k_in, v_in, k2_in, v2_in, t_in, sems) = refs[:-8], refs[-8:]
    wanted = {what for parts in outputs for _, _, what in parts}
    me, half = lax.axis_index("tm"), lax.axis_index("rep")
    rows = fq_ref.shape[0]
    mine = pl.ds(pl.multiple_of(half * rows, rows), rows)
    rest = pl.ds(pl.multiple_of((1 - half) * rows, rows), rows)
    moves = [
        (fq_ref, q_in), (do_ref, do_in), (fk_ref.at[mine, :], k_in), (fv_ref.at[mine, :], v_in), (t_ref, t_in)
    ]
    if "other" in wanted:
        moves += [(fk_ref.at[rest, :], k2_in), (fv_ref.at[rest, :], v2_in)]
    copies = [pltpu.make_async_copy(a, b, sems.at[n]) for n, (a, b) in enumerate(moves)]
    for copy in copies:
        copy.start()
    for copy in copies:
        copy.wait()
    for out, parts in zip(outs, outputs):
        at = 0
        for table, m, what in parts:
            if what in ("t", "other t"):
                blocks = [t_in[mine if what == "t" else rest, :]]
            else:
                cols = column(lookup(table, me ^ m))
                sources = (q_in, do_in, k_in, v_in) if what == "mine" else (k2_in, v2_in)
                blocks = [ref[:, cols] for ref in sources]
            for block in blocks:
                out[:, at : at + block.shape[1]] = block
                at += block.shape[1]


def pack(frames, outputs, limit, fq, do, fk, fv, t):
    rows, width = fq.shape
    size = {"mine": 4 * DH, "other": 2 * DH, "t": t.shape[1], "other t": t.shape[1]}
    return pl.pallas_call(
        functools.partial(pack_kernel, frames, outputs),
        in_specs=[pl.BlockSpec(memory_space=pltpu.HBM)] * 5,
        out_specs=vmem(len(outputs)),
        out_shape=[
            jax.ShapeDtypeStruct((rows, sum(size[what] for _, _, what in parts)), BF16)
            for parts in outputs
        ],
        scratch_shapes=[pltpu.VMEM((rows, width), BF16)] * 6
        + [pltpu.VMEM(t.shape, BF16), pltpu.SemaphoreType.DMA((7,))],
        compiler_params=pltpu.CompilerParams(vmem_limit_bytes=limit * 1024 * 1024),
    )(fq, do, fk, fv, t)


def pick_kernel(spans, groups, *refs):
    n = 0
    for out, count in zip(refs[-len(groups) :], groups):
        for at in range(count):
            start, size = spans[n]
            out[:, at * size : (at + 1) * size] = refs[n][:, start : start + size]
            n += 1


def pick(parts, size, groups, after=()):
    arrays = [array for array, _ in parts]
    rows, dtype = arrays[0].shape[0], arrays[0].dtype
    return pl.pallas_call(
        functools.partial(pick_kernel, [(start, size) for _, start in parts], groups),
        in_specs=vmem(len(arrays)) + [pl.BlockSpec(memory_space=pl.ANY)] * len(after),
        out_specs=vmem(len(groups)),
        out_shape=[jax.ShapeDtypeStruct((rows, size * count), dtype) for count in groups],
        compiler_params=SMALL,
    )(*arrays, *after)


def one_head(frames, bands, q, do, frozen_k, frozen_v, tokens, aq, ak, av):
    flat = q.shape[0]
    rows = flat // frames
    t_same = tokens[:flat]

    def adapted(frozen, rows_of, adapter):
        return (frozen.astype(F32) + dot_nn(rows_of, adapter)).astype(BF16)

    query = adapted(q, t_same, aq)
    keys, values = adapted(frozen_k, tokens, ak), adapted(frozen_v, tokens, av)
    do_t, keys_t, values_t = do.T, keys.T, values.T

    def bias(i, b):
        j, need = (b, 0) if b < frames else (b - frames, 1)
        value = jnp.where(bands[i, j] > need, 0.0, -jnp.inf).astype(F32)
        return jnp.full((1, rows), value, F32)

    span = 2 if frames % 2 == 0 else 1
    wide = span * rows
    groups = [range(first, first + span) for first in range(0, frames, span)]
    seen = [
        list(range(frames))
        + [frames + j for j in range(frames) if any(abs(i - j) <= NEAR for i in mine)]
        for mine in groups
    ]
    here = [slice(mine[0] * rows, mine[0] * rows + wide) for mine in groups]
    pairs_of = range(len(groups))

    def gather(whole, g, axis):
        parts = [
            whole[b * rows : (b + 1) * rows] if axis == 0 else whole[:, b * rows : (b + 1) * rows]
            for b in seen[g]
        ]
        return jnp.concatenate(parts, axis=axis)

    def block(whole, n):
        return whole[n * rows : (n + 1) * rows]

    def softmax(g, raw):
        scores = [
            block(raw, n) * SCALE_2 + jnp.concatenate([bias(i, b) for i in groups[g]], axis=1)
            for n, b in enumerate(seen[g])
        ]
        top = jnp.max(functools.reduce(jnp.maximum, scores), axis=0, keepdims=True)
        shifted = [jnp.exp2(s - top) for s in scores]
        inverse = 1.0 / jnp.sum(functools.reduce(jnp.add, shifted), axis=0, keepdims=True)
        return [s * inverse for s in shifted]

    raws = [dot_nt(gather(keys, g, 0), query[here[g]]) for g in pairs_of]
    prob_grads = [dot_nt(gather(values, g, 0), do[here[g]]) for g in pairs_of]
    probs = [softmax(g, raws[g]) for g in pairs_of]
    lows = [jnp.concatenate([p.astype(BF16) for p in probs[g]], axis=0) for g in pairs_of]
    grads = []
    for g in pairs_of:
        attended = dot_nn(gather(values_t, g, 1), lows[g]).astype(BF16).astype(F32)
        delta = jnp.sum(do_t[:, here[g]].astype(F32) * attended, axis=0, keepdims=True)
        parts = [
            (probs[g][n] * (block(prob_grads[g], n) - delta)).astype(BF16) for n in range(len(seen[g]))
        ]
        grads.append(jnp.concatenate(parts, axis=0))
    dvs, dks = [None] * (2 * frames), [None] * (2 * frames)

    def add(sums, g, whole):
        for n, b in enumerate(seen[g]):
            sums[b] = block(whole, n) if sums[b] is None else sums[b] + block(whole, n)

    for g in pairs_of:
        add(dvs, g, dot_nn(lows[g], do[here[g]]))
    for g in pairs_of:
        add(dks, g, dot_nn(grads[g], query[here[g]]))
    dqs = [(dot_nn(gather(keys_t, g, 1), grads[g]) * SCALE).astype(BF16).T for g in pairs_of]
    dq = jnp.concatenate(dqs, axis=0)
    dk = (jnp.concatenate(dks, axis=0) * SCALE).astype(BF16)
    dv = jnp.concatenate(dvs, axis=0).astype(BF16)
    both = jnp.concatenate([dk, dv], axis=1)
    sums = dot_tn(tokens, both)
    grads = jnp.concatenate([dot_tn(t_same, dq), sums[:, :DH], sums[:, DH:]], axis=0)
    lows = dot_nt(both, jnp.concatenate([ak, av], axis=1))
    return grads, lows[:flat] + dot_nt(dq, aq), lows[flat:]


def group_kernel(heads, frames, chained, waits, sides, count, *refs):
    refs = list(refs)

    def take(count):
        taken = refs[:count]
        del refs[:count]
        return taken

    (bands,) = take(1)
    arrays, adapters = take(count), take(3)
    before = take(2) if chained else None
    take(waits)
    keep_ref, *give_refs = take(1 + GIVES if chained else 2)
    low_refs = [] if chained else take(2)
    q, do, k, v, tokens = refs
    me, half = lax.axis_index("tm"), lax.axis_index("rep")
    rows = arrays[0].shape[0]
    flat = frames * rows
    cut = 3 * tokens.shape[1] // 2
    first = half == 0
    same_at = [pl.ds(pl.multiple_of((me ^ m) * rows, rows), rows) for m in range(frames)]
    other_at = [pl.ds(pl.multiple_of(flat + (me ^ m) * rows, rows), rows) for m in range(frames)]

    def put(targets, places, rows_at):
        for m, (n, start) in enumerate(places):
            for c, target in enumerate(targets):
                target[rows_at[m], :] = arrays[n][:, start + c * DH : start + (c + 1) * DH]

    put([tokens], sides[0][0], same_at)
    put([tokens], sides[0][1], other_at)

    def run(n, table):
        put([q, do, k, v], sides[1 + n][0], same_at)
        put([k, v], sides[1 + n][1], other_at)
        cols = column(lookup(table, me))
        grads, low_same, low_other = one_head(
            frames, bands, q[...], do[...], k[...], v[...], tokens[...], *[a[:, cols] for a in adapters]
        )
        keep = jnp.where(first, grads[:cut], grads[cut:])
        give = jnp.where(first, grads[cut:], grads[:cut])
        return keep, give, low_same, low_other

    if chained:
        keep, give, low_same, low_other = run(0, heads[0][0])
        keep_ref[:cut, :] = keep
        keep_ref[cut:, :] = before[0][...] + low_same
        give = jnp.concatenate([give, before[1][...] + low_other], axis=0)
        size = give.shape[0] // GIVES
        for n, ref in enumerate(give_refs):
            ref[...] = give[n * size : (n + 1) * size].astype(ref.dtype)
        return
    for n, (table, counts) in enumerate(heads):
        here = slice(n * cut, (n + 1) * cut)

        def body():
            keep, give, low_same, low_other = run(n, table)
            keep_ref[here, :] = keep
            give_refs[0][here, :] = give.astype(BF16)
            if n == 0:
                low_refs[0][...] = low_same
                low_refs[1][...] = low_other
            else:
                low_refs[0][...] += low_same
                low_refs[1][...] += low_other

        if min(counts) > 0:
            body()
        else:
            live = lookup(counts, me) > 0
            pl.when(live)(body)

            @pl.when(jnp.logical_not(live))
            def _():
                keep_ref[here, :] = jnp.zeros((cut, DH), F32)
                give_refs[0][here, :] = jnp.zeros((cut, DH), BF16)


def head_group(heads, bands, sides, adapters, before=(), after=()):
    frames = len(sides[0][0])
    arrays, places = [], []
    for side in sides:
        found = []
        for pairs_of in side:
            found.append([])
            for array, start in pairs_of:
                known = [n for n, a in enumerate(arrays) if a is array]
                if not known:
                    arrays.append(array)
                found[-1].append((known[0] if known else len(arrays) - 1, start))
        places.append(found)
    rows, rank = arrays[0].shape[0], adapters[0].shape[0]
    flat = frames * rows
    size = len(heads) * 3 * rank // 2
    chained = len(before) > 0
    args = [bands, *arrays, *adapters, *before, *after]
    specs = [pl.BlockSpec(memory_space=pltpu.SMEM)] + vmem(len(arrays) + 3 + len(before))
    specs += [pl.BlockSpec(memory_space=pl.ANY)] * len(after)
    low = jax.ShapeDtypeStruct((flat, rank), F32)
    if chained:
        part = jax.ShapeDtypeStruct(((size + flat) // GIVES, rank), BF16)
        shapes = [jax.ShapeDtypeStruct((size + flat, rank), F32)] + [part] * GIVES
    else:
        edge = jax.ShapeDtypeStruct((size, rank), F32)
        shapes = [edge, jax.ShapeDtypeStruct((size, rank), BF16), low, low]
    return pl.pallas_call(
        functools.partial(
            group_kernel, heads, frames, chained, len(after), places, len(arrays)
        ),
        in_specs=specs,
        out_specs=vmem(len(shapes)),
        out_shape=shapes,
        scratch_shapes=[pltpu.VMEM((flat, DH), BF16)] * 2
        + [pltpu.VMEM((2 * flat, DH), BF16)] * 2
        + [pltpu.VMEM((2 * flat, rank), BF16)],
        compiler_params=pltpu.CompilerParams(vmem_limit_bytes=40 * 1024 * 1024),
    )(*args)


def hand_out_kernel(frames, size, parts, keep_ref, *refs):
    gots, facing, (own_ref, *sends, total) = refs[:parts], refs[-frames - 2], refs[-frames - 1 :]
    me = lax.axis_index("tm")
    rows = own_ref.shape[0]
    total[...] = keep_ref[...] + jnp.concatenate([got[...].astype(F32) for got in gots], axis=0)
    for m in range(frames):
        low = total[pl.ds(pl.multiple_of(size + (me ^ m) * rows, 8), rows), :]
        if m == 0:
            own_ref[...] = low
        else:
            sends[m - 1][:rows, :] = low.astype(BF16)
            sends[m - 1][rows : rows + size, :] = total[:size, :].astype(BF16)
    sends[0][rows + size :, :] = facing[...]


def hand_out(frames, rows, keep, gots, facing, after):
    size, rank = keep.shape[0] - frames * rows, keep.shape[1]
    own, *sends = pl.pallas_call(
        functools.partial(hand_out_kernel, frames, size, len(gots)),
        in_specs=vmem(1 + len(gots)) + [pl.BlockSpec(memory_space=pl.ANY)] * len(after) + vmem(1),
        out_specs=vmem(frames),
        out_shape=[jax.ShapeDtypeStruct((rows, rank), F32)]
        + [jax.ShapeDtypeStruct((rows + size * n, rank), BF16) for n in (3, 1, 1)],
        scratch_shapes=[pltpu.VMEM(keep.shape, F32)],
        compiler_params=SMALL,
    )(keep, *gots, *after, facing)
    return own, sends


def collect_kernel(wide, own_low, own, near, third, last, piece, pair, far, facing, out_ref, low_ref):
    rows = own_low.shape[0]
    size = own.shape[0] - rows
    low = own_low[...]
    for got in (near, third, last):
        low = low + got[:rows, :].astype(F32)
    out_ref[:rows, :] = low.astype(BF16)
    low_ref[...] = low.astype(BF16)
    middle = lookup(wide, lax.axis_index("tm")) > 0

    def part(ref, n):
        return ref[rows + n * size : rows + (n + 1) * size, :]

    blocks = [part(ref, 0) for ref in (own, near, third, last)]
    blocks += [piece[:size, :], pair[:size, :]]
    blocks += [jnp.where(middle, far[...], part(near, 1)), facing[:size, :]]
    blocks.append(jnp.where(middle, piece[size:, :], pair[size:, :]))
    blocks.append(jnp.where(middle, facing[size:, :], part(near, 2)))
    for n, block in enumerate(blocks):
        out_ref[rows + n * size : rows + (n + 1) * size, :] = block


def collect(wide, own_low, own, gots, *pieces):
    (rows, rank), size = own_low.shape, pieces[0].shape[0] // 2
    return pl.pallas_call(
        functools.partial(collect_kernel, wide),
        in_specs=vmem(2 + len(gots) + len(pieces)),
        out_specs=vmem(2),
        out_shape=[
            jax.ShapeDtypeStruct((rows + 10 * size, rank), BF16),
            jax.ShapeDtypeStruct((rows, rank), BF16),
        ],
        compiler_params=SMALL,
    )(own_low, own, *gots, *pieces)


def place_kernel(frames, lead, late, rest, tail, tail2, low_diag, low_head, *refs):
    outs, filled, sems = refs[:4], refs[4:8], refs[8]
    me, half = lax.axis_index("tm"), lax.axis_index("rep")
    first = half == 0
    rank = filled[0].shape[0]
    cut = 3 * rank // 2
    rows = low_head.shape[0]
    side = me // 2
    places = [lookup(late, me ^ m) for m in range(frames)] + [lookup(lead, me ^ m) for m in range(frames)]
    places += [lookup(rest, 1 + side), lookup(rest, 2 - side)]
    copies = [pltpu.make_async_copy(filled[o], outs[o], sems.at[o]) for o in range(4)]

    def rows_of(ref, n, start, stop):
        return ref[rows + n * cut + start : rows + n * cut + stop, :].astype(F32)

    for o in range(3):
        for n, head in enumerate(places):
            parts = []
            for owner, low_end, high_end in ((0, 0, cut), (1, cut, 2 * cut)):
                start, stop = max(o * rank, low_end), min((o + 1) * rank, high_end)
                if start < stop:
                    mine, its = (rows_of(ref, n, start - low_end, stop - low_end) for ref in (tail, tail2))
                    parts.append(jnp.where(first, mine, its) if owner == 0 else jnp.where(first, its, mine))
            filled[o][:, column(head)] = parts[0] if len(parts) == 1 else jnp.concatenate(parts, axis=0)
        copies[o].start()
    same = tail[:rows, :].astype(F32) + low_head[...].astype(F32)
    other = tail2[:rows, :].astype(F32) + low_diag[...].astype(F32)
    filled[3][:rows, :] = jnp.where(first, same, other)
    filled[3][rows:, :] = jnp.where(first, other, same)
    copies[3].start()
    for copy in copies:
        copy.wait()


def place(frames, lead, late, rest, tail, tail2, low_head, low_diag, rank, width):
    rows = low_head.shape[0]
    shapes = [(rank, width)] * 3 + [(2 * rows, rank)]
    return pl.pallas_call(
        functools.partial(place_kernel, frames, lead, late, rest),
        in_specs=vmem(4),
        out_specs=[pl.BlockSpec(memory_space=pl.ANY)] * 4,
        out_shape=[jax.ShapeDtypeStruct(shape, F32) for shape in shapes],
        scratch_shapes=[pltpu.VMEM(shape, F32) for shape in shapes] + [pltpu.SemaphoreType.DMA((4,))],
        compiler_params=SMALL,
    )(tail, tail2, low_diag, low_head)


def exchange_plan(
    frozen_query,
    frozen_key,
    frozen_value,
    token_adapter_input,
    query_adapter_out,
    key_adapter_out,
    value_adapter_out,
    out_grad,
    band_width,
):
    rows, width = frozen_query.shape
    rank = token_adapter_input.shape[1]
    frames = band_width.shape[0]
    heads = width // DH
    starts, counts = head_table(heads, frames)
    most = max(counts)
    columns = [[min(starts[j] + s, heads - 1) for j in range(frames)] for s in range(most)]
    numbers = [[int(s < counts[j]) for j in range(frames)] for s in range(most)]
    slots = list(zip(columns, numbers))
    lead, late, rest = slots[0], slots[1], slots[2]
    wide = [j for j in range(frames) if counts[j] == most]
    adapters = [query_adapter_out, key_adapter_out, value_adapter_out]
    arrays = (frozen_query, out_grad, frozen_key, frozen_value, token_adapter_input)

    def meet(name, block, m, targets=range(frames)):
        with jax.named_scope(f"{name}_over_tm"):
            return lax.ppermute(block, "tm", [(j ^ m, j) for j in targets])

    def swap_in_chip(name, block):
        with jax.named_scope(f"{name}_in_chip"):
            return swap(block, "rep")

    def mine(slot, m):
        return (slot[0], m, "mine")

    sent, kept, sent_late = [], [], []
    for m in range(1, frames):
        first = [mine(lead, m), (None, m, "t")]
        if m == 1:
            sent.append(first + [mine(rest, m), mine(late, m)])
        else:
            sent += [first, [mine(rest, m)]]
            sent_late.append([mine(late, m)])
    for slot in (lead, rest, late):
        kept += [[mine(slot, 0)], [(slot[0], 0, "other")]]
    kept += [[(None, 0, "t")], [(None, 0, "other t")]]
    packed = pack(frames, sent, 56, *arrays)
    packed_late = pack(frames, sent_late + kept, 16, *arrays)
    kept = packed_late[len(sent_late) :]
    block = meet("nearest", packed[0], 1)
    lead_got, rest_got, late_got = [(block, 0)], [(block, 4 * DH + rank)], [(block, 8 * DH + rank)]
    for m in range(2, frames):
        lead_got.append((meet("lead", packed[2 * m - 3], m), 0))
        rest_got.append((meet("rest", packed[2 * m - 2], m, wide), 0))
        late_got.append((meet("late", packed_late[m - 2], m), 0))

    def sides(name, n, got, wide_t, groups, skip, after=()):
        size = 4 * DH - skip + (rank if wide_t else 0)
        picked = pick([(a, start + skip) for a, start in got], size, groups, after)
        cross = [swap_in_chip(name, block) for block in picked]
        where = 2 * DH - skip
        cross = [(block, at * size + where) for block, count in zip(cross, groups) for at in range(count)]
        rows_here = [(kept[2 * n], 0)] + got
        rows_there = [(kept[2 * n + 1], 0)] + cross
        return rows_here, rows_there, cross

    *lead_side, cross = sides("lead", 0, lead_got, True, (3,), 2 * DH, kept[:1])
    t_side = (
        [(kept[6], 0)] + [(a, start + 4 * DH) for a, start in lead_got],
        [(kept[7], 0)] + [(block, start + 2 * DH) for block, start in cross],
    )
    *rest_side, _ = sides("rest", 1, rest_got, False, (3,), 2 * DH)
    early = [lead, rest]
    keep, give, *low = head_group(early, band_width, [t_side, lead_side, rest_side], adapters)
    got = swap_in_chip("early_gradients", give)
    piece = (keep + got.astype(F32)).astype(BF16)
    *late_side, _ = sides("late", 2, late_got, False, (3,), 2 * DH, [got])
    cut = 3 * rank // 2
    pair = meet("early_pair", piece, 1)
    facing = meet("early_facing", piece, 3)
    with jax.named_scope("early_lead_over_tm"):
        far = lax.ppermute(piece[:cut], "tm", [(0, 2), (3, 1)])
    keep, *gives = head_group([late], band_width, [t_side, late_side], adapters, low, [piece])
    gives = [swap_in_chip("late_sums", g) for g in gives]
    own_low, sends = hand_out(frames, rows, keep, gives, facing, [pair])
    gots = [meet("late_sums", block, m) for m, block in enumerate(sends, 1)]
    tail, low = collect(rest[1], own_low, sends[2], gots, piece, pair, far, facing)
    diag = [(0, 3), (1, 2), (2, 1), (3, 0)]
    with jax.named_scope("low_over_head"):
        low_head, low_diag = swap(low, "head"), lax.ppermute(low, ("head", "rep"), diag)
    outs = place(
        frames, lead[0], late[0], rest[0], tail, swap_in_chip("tail", tail), low_head, low_diag, rank, width
    )
    return tuple(outs)


def on_device(frozen_query, *rest):
    frames = rest[-1].shape[0]
    heads = frozen_query.shape[1] // DH
    whole_reach = frames == 4 and heads == 2 * frames + 2
    return (exchange_plan if whole_reach else window_plan)(frozen_query, *rest)


def solution(mesh):
    in_specs = (
        P(("groups", "tm", "rep"), "head"),
        P(("groups", "tm"), "head"),
        P(("groups", "tm"), "head"),
        P(("groups", "tm"), None),
        P(None, "head"),
        P(None, "head"),
        P(None, "head"),
        P(("groups", "tm", "rep"), "head"),
        P(),
    )
    out_specs = (
        P("groups", "head"),
        P("groups", "head"),
        P("groups", "head"),
        P(("groups", "tm"), None),
    )
    return jax.shard_map(
        on_device, mesh=mesh, in_specs=in_specs, out_specs=out_specs, check_vma=False
    )
```

```python
import functools
import math

import jax
import jax.numpy as jnp
from jax import lax
from jax.experimental import pallas as pl
from jax.experimental.pallas import tpu as pltpu
from jax.sharding import PartitionSpec as P

DH = 128
NEAR = 1
REACH = 4
SCALE = DH ** (-0.5)
SCALE_2 = SCALE * math.log2(math.e)
F32 = jnp.float32
BF16 = jnp.bfloat16
GIVES = 4
SMALL = pltpu.CompilerParams(vmem_limit_bytes=16 * 1024 * 1024)


def dot_nn(left, right):
    return lax.dot_general(left, right, (((1,), (0,)), ((), ())), preferred_element_type=F32)


def dot_nt(left, right):
    return lax.dot_general(left, right, (((1,), (1,)), ((), ())), preferred_element_type=F32)


def dot_tn(left, right):
    return lax.dot_general(left, right, (((0,), (0,)), ((), ())), preferred_element_type=F32)


def routes(count):
    found = []
    for d in range(1, min(REACH, count - 1) + 1):
        if 2 * d >= count:
            found.append((d, (-d, d)))
        else:
            found.append((d, (-d,)))
            found.append((d, (d,)))
    return found


def pairs(count, offsets):
    return [(i + o, i) for o in offsets for i in range(count) if 0 <= i + o < count]


def swap(block, axis):
    return lax.ppermute(block, axis, [(0, 1), (1, 0)])


def attention_kernel(
    blocks, bias_ref, fq_ref, do_ref, fk_ref, fv_ref, t_ref, tr_ref, tt_ref, aq_ref, ak_ref, av_ref, *refs
):
    k_refs = refs[:blocks]
    v_refs = refs[blocks : 2 * blocks]
    gq_ref, gk_ref, gv_ref, lowq_ref, low_ref = refs[2 * blocks :]
    rows = fq_ref.shape[0]

    @pl.when(pl.program_id(0) == 0)
    def _():
        lowq_ref[...] = jnp.zeros_like(lowq_ref)
        low_ref[...] = jnp.zeros_like(low_ref)

    aq, ak, av = aq_ref[...], ak_ref[...], av_ref[...]
    query = (fq_ref[...].astype(F32) + dot_nn(tr_ref[...], aq)).astype(BF16)
    do = do_ref[...]
    own_k = (fk_ref[...].astype(F32) + dot_nn(t_ref[...], ak)).astype(BF16)
    own_v = (fv_ref[...].astype(F32) + dot_nn(t_ref[...], av)).astype(BF16)
    keys = [own_k[:rows], own_k[rows:]] + [ref[...] for ref in k_refs]
    values = [own_v[:rows], own_v[rows:]] + [ref[...] for ref in v_refs]
    count = len(keys)
    scores = [dot_nt(keys[b], query) * SCALE + bias_ref[b] for b in range(count)]
    top = functools.reduce(jnp.maximum, scores)
    top = jnp.max(top, axis=0, keepdims=True)
    shifted = [jnp.exp(s - top) for s in scores]
    total = jnp.sum(functools.reduce(jnp.add, shifted), axis=0, keepdims=True)
    inverse = 1.0 / total
    probs = [s * inverse for s in shifted]
    lows = [p.astype(BF16) for p in probs]
    attended = functools.reduce(jnp.add, [dot_tn(lows[b], values[b]) for b in range(count)])
    attended = attended.astype(BF16).astype(F32)
    delta = jnp.sum((do.astype(F32) * attended).T, axis=0, keepdims=True)
    grads = [
        (probs[b] * (dot_nt(values[b], do) - delta)).astype(BF16) for b in range(count)
    ]
    dq = functools.reduce(jnp.add, [dot_tn(grads[b], keys[b]) for b in range(count)])
    dq = (dq * SCALE).astype(BF16)
    gq_ref[...] = dot_tn(tr_ref[...], dq)
    lowq_ref[...] += dot_nt(dq, aq)
    both = jnp.concatenate([ak, av], axis=1)
    for b in range(count):
        dk = (dot_nn(grads[b], query) * SCALE).astype(BF16)
        dv = dot_nn(lows[b], do).astype(BF16)
        part = jnp.concatenate([dk, dv], axis=1)
        low_ref[b * rows : (b + 1) * rows, :] += dot_nt(part, both)
        out = dot_nn(tt_ref[:, b * rows : (b + 1) * rows], part)
        if b == 0:
            total_part = out
        else:
            total_part += out
    gk_ref[...] = total_part[:, :DH]
    gv_ref[...] = total_part[:, DH:]


def attention(bias, fq, do, fk, fv, t, tr, tt, aq, ak, av, payloads):
    rows, width = fq.shape
    heads = width // DH
    rank = t.shape[1]
    blocks = len(payloads)
    count = blocks + 2

    def col(r):
        return pl.BlockSpec((r, DH), lambda h: (0, h))

    def whole(shape):
        return pl.BlockSpec(shape, lambda h: (0, 0))

    return pl.pallas_call(
        functools.partial(attention_kernel, blocks),
        grid=(heads,),
        out_shape=[
            jax.ShapeDtypeStruct((rank, width), F32),
            jax.ShapeDtypeStruct((rank, width), F32),
            jax.ShapeDtypeStruct((rank, width), F32),
            jax.ShapeDtypeStruct((rows, rank), F32),
            jax.ShapeDtypeStruct((count * rows, rank), F32),
        ],
        in_specs=[pl.BlockSpec(memory_space=pltpu.SMEM)]
        + [col(rows), col(rows), col(2 * rows), col(2 * rows)]
        + [whole(t.shape), whole(tr.shape), whole(tt.shape)]
        + [col(rank)] * 3
        + [col(rows)] * blocks
        + [pl.BlockSpec((rows, DH), lambda h: (0, heads + h))] * blocks,
        out_specs=[col(rank)] * 3 + [whole((rows, rank)), whole((count * rows, rank))],
        compiler_params=pltpu.CompilerParams(vmem_limit_bytes=32 * 1024 * 1024),
    )(bias, fq, do, fk, fv, t, tr, tt, aq, ak, av, *payloads, *payloads)


def sum_rows(part, frame_idx, half_idx, frames):
    rows, width = part.shape
    half = width // 2
    keep = lax.dynamic_slice_in_dim(part, half_idx * half, half, 1)
    give = lax.dynamic_slice_in_dim(part, (1 - half_idx) * half, half, 1)
    mine = keep + swap(give, "rep")
    if frames & (frames - 1) or rows % frames or frames > REACH + 1:
        total = lax.psum(mine, "tm").astype(BF16)
    else:
        chunk = rows // frames
        low = mine.astype(BF16)
        acc = lax.dynamic_slice_in_dim(mine, frame_idx * chunk, chunk, 0)
        for m in range(1, frames):
            give = lax.dynamic_slice_in_dim(low, (frame_idx ^ m) * chunk, chunk, 0)
            acc = acc + lax.ppermute(give, "tm", [(i, i ^ m) for i in range(frames)]).astype(F32)
        acc = acc.astype(BF16)
        total = jnp.zeros((rows, half), BF16)
        total = lax.dynamic_update_slice_in_dim(total, acc, frame_idx * chunk, 0)
        for m in range(1, frames):
            got = lax.ppermute(acc, "tm", [(i, i ^ m) for i in range(frames)])
            total = lax.dynamic_update_slice_in_dim(total, got, (frame_idx ^ m) * chunk, 0)
    other = swap(total, "rep")
    first = jnp.where(half_idx == 0, total, other)
    second = jnp.where(half_idx == 0, other, total)
    return jnp.concatenate([first, second], axis=1).astype(F32)


def window_plan(
    frozen_query,
    frozen_key,
    frozen_value,
    token_adapter_input,
    query_adapter_out,
    key_adapter_out,
    value_adapter_out,
    out_grad,
    band_width,
):
    rows, width = frozen_query.shape
    rank = token_adapter_input.shape[1]
    frames = band_width.shape[0]
    frame_idx = lax.axis_index("tm")
    half_idx = lax.axis_index("rep")
    t = token_adapter_input
    tr = lax.dynamic_slice_in_dim(t, half_idx * rows, rows, 0)

    def tile_rows_of(frozen, adapter):
        own = lax.dynamic_slice_in_dim(frozen, half_idx * rows, rows, 0)
        return (own.astype(F32) + dot_nn(tr, adapter)).astype(BF16)

    payload = jnp.concatenate(
        [tile_rows_of(frozen_key, key_adapter_out), tile_rows_of(frozen_value, value_adapter_out), tr],
        axis=1,
    )

    frame_ids = jnp.arange(frames)
    band_row = jnp.sum(jnp.where((frame_ids == frame_idx)[:, None], band_width, 0), axis=0)

    def band_at(offsets):
        seen = functools.reduce(jnp.logical_or, [frame_ids == frame_idx + o for o in offsets])
        return jnp.sum(jnp.where(seen, band_row, 0))

    own_band = band_at((0,))
    allowed = [jnp.abs(half_idx - tile) < own_band for tile in range(2)]
    payloads = []
    plan = routes(frames)
    for d, offsets in plan:
        got = lax.ppermute(payload, "tm", pairs(frames, offsets))
        band = band_at(offsets)
        payloads.append(got)
        allowed.append(band > 0)
        if d <= NEAR:
            payloads.append(swap(got, "rep"))
            allowed.append(band > 1)
    bias = jnp.where(jnp.stack(allowed), 0.0, -jnp.inf).astype(F32)
    tt = jnp.concatenate([t] + [p[:, 2 * width :] for p in payloads], axis=0).T

    gq, gk, gv, low_q, low_b = attention(
        bias, frozen_query, out_grad, frozen_key, frozen_value, t, tr, tt,
        query_adapter_out, key_adapter_out, value_adapter_out, payloads,
    )

    own = low_b[: 2 * rows]
    same = lax.dynamic_slice_in_dim(own, half_idx * rows, rows, 0) + low_q
    other = lax.dynamic_slice_in_dim(own, (1 - half_idx) * rows, rows, 0)
    start = 2 * rows
    for d, offsets in plan:
        size = 2 * rows if d <= NEAR else rows
        back = [(target, source) for source, target in pairs(frames, offsets)]
        got = lax.ppermute(low_b[start : start + size], "tm", back)
        start += size
        same = same + got[:rows]
        if d <= NEAR:
            other = other + got[rows:]
    low = jnp.where(
        half_idx == 0,
        jnp.concatenate([same, other], axis=0),
        jnp.concatenate([other, same], axis=0),
    )
    low = low + swap(low, "rep")
    low = low + swap(low, "head")

    grads = sum_rows(jnp.concatenate([gq, gk, gv], axis=0), frame_idx, half_idx, frames)
    return grads[:rank], grads[rank : 2 * rank], grads[2 * rank :], low


def head_table(heads, frames):
    base, extra = divmod(heads, frames)
    lead = (frames - extra) // 2
    counts = [base + (1 if lead <= j < lead + extra else 0) for j in range(frames)]
    return [sum(counts[:j]) for j in range(frames)], counts


def lookup(table, index):
    value = jnp.int32(table[0])
    for j in range(1, len(table)):
        value = jnp.where(index == j, jnp.int32(table[j]), value)
    return value


def column(head):
    return pl.ds(pl.multiple_of(head * DH, DH), DH)


def vmem(count):
    return [pl.BlockSpec(memory_space=pltpu.VMEM)] * count


def pack_kernel(frames, outputs, fq_ref, do_ref, fk_ref, fv_ref, t_ref, *refs):
    outs, (q_in, do_in, k_in, v_in, k2_in, v2_in, t_in, sems) = refs[:-8], refs[-8:]
    wanted = {what for parts in outputs for _, _, what in parts}
    me, half = lax.axis_index("tm"), lax.axis_index("rep")
    rows = fq_ref.shape[0]
    mine = pl.ds(pl.multiple_of(half * rows, rows), rows)
    rest = pl.ds(pl.multiple_of((1 - half) * rows, rows), rows)
    moves = [
        (fq_ref, q_in), (do_ref, do_in), (fk_ref.at[mine, :], k_in), (fv_ref.at[mine, :], v_in), (t_ref, t_in)
    ]
    if "other" in wanted:
        moves += [(fk_ref.at[rest, :], k2_in), (fv_ref.at[rest, :], v2_in)]
    copies = [pltpu.make_async_copy(a, b, sems.at[n]) for n, (a, b) in enumerate(moves)]
    for copy in copies:
        copy.start()
    for copy in copies:
        copy.wait()
    for out, parts in zip(outs, outputs):
        at = 0
        for table, m, what in parts:
            if what in ("t", "other t"):
                blocks = [t_in[mine if what == "t" else rest, :]]
            else:
                cols = column(lookup(table, me ^ m))
                sources = (q_in, do_in, k_in, v_in) if what == "mine" else (k2_in, v2_in)
                blocks = [ref[:, cols] for ref in sources]
            for block in blocks:
                out[:, at : at + block.shape[1]] = block
                at += block.shape[1]


def pack(frames, outputs, limit, fq, do, fk, fv, t):
    rows, width = fq.shape
    size = {"mine": 4 * DH, "other": 2 * DH, "t": t.shape[1], "other t": t.shape[1]}
    return pl.pallas_call(
        functools.partial(pack_kernel, frames, outputs),
        in_specs=[pl.BlockSpec(memory_space=pltpu.HBM)] * 5,
        out_specs=vmem(len(outputs)),
        out_shape=[
            jax.ShapeDtypeStruct((rows, sum(size[what] for _, _, what in parts)), BF16)
            for parts in outputs
        ],
        scratch_shapes=[pltpu.VMEM((rows, width), BF16)] * 6
        + [pltpu.VMEM(t.shape, BF16), pltpu.SemaphoreType.DMA((7,))],
        compiler_params=pltpu.CompilerParams(vmem_limit_bytes=limit * 1024 * 1024),
    )(fq, do, fk, fv, t)


def pick_kernel(spans, groups, *refs):
    n = 0
    for out, count in zip(refs[-len(groups) :], groups):
        for at in range(count):
            start, size = spans[n]
            out[:, at * size : (at + 1) * size] = refs[n][:, start : start + size]
            n += 1


def pick(parts, size, groups, after=()):
    arrays = [array for array, _ in parts]
    rows, dtype = arrays[0].shape[0], arrays[0].dtype
    return pl.pallas_call(
        functools.partial(pick_kernel, [(start, size) for _, start in parts], groups),
        in_specs=vmem(len(arrays)) + [pl.BlockSpec(memory_space=pl.ANY)] * len(after),
        out_specs=vmem(len(groups)),
        out_shape=[jax.ShapeDtypeStruct((rows, size * count), dtype) for count in groups],
        compiler_params=SMALL,
    )(*arrays, *after)


def one_head(frames, bands, q, do, frozen_k, frozen_v, tokens, aq, ak, av):
    flat = q.shape[0]
    rows = flat // frames
    t_same = tokens[:flat]

    def adapted(frozen, rows_of, adapter):
        return (frozen.astype(F32) + dot_nn(rows_of, adapter)).astype(BF16)

    query = adapted(q, t_same, aq)
    keys, values = adapted(frozen_k, tokens, ak), adapted(frozen_v, tokens, av)
    do_t, keys_t, values_t = do.T, keys.T, values.T

    def bias(i, b):
        j, need = (b, 0) if b < frames else (b - frames, 1)
        value = jnp.where(bands[i, j] > need, 0.0, -jnp.inf).astype(F32)
        return jnp.full((1, rows), value, F32)

    span = 2 if frames % 2 == 0 else 1
    wide = span * rows
    groups = [range(first, first + span) for first in range(0, frames, span)]
    seen = [
        list(range(frames))
        + [frames + j for j in range(frames) if any(abs(i - j) <= NEAR for i in mine)]
        for mine in groups
    ]
    here = [slice(mine[0] * rows, mine[0] * rows + wide) for mine in groups]
    pairs_of = range(len(groups))

    def gather(whole, g, axis):
        parts = [
            whole[b * rows : (b + 1) * rows] if axis == 0 else whole[:, b * rows : (b + 1) * rows]
            for b in seen[g]
        ]
        return jnp.concatenate(parts, axis=axis)

    def block(whole, n):
        return whole[n * rows : (n + 1) * rows]

    def softmax(g, raw):
        scores = [
            block(raw, n) * SCALE_2 + jnp.concatenate([bias(i, b) for i in groups[g]], axis=1)
            for n, b in enumerate(seen[g])
        ]
        top = jnp.max(functools.reduce(jnp.maximum, scores), axis=0, keepdims=True)
        shifted = [jnp.exp2(s - top) for s in scores]
        inverse = 1.0 / jnp.sum(functools.reduce(jnp.add, shifted), axis=0, keepdims=True)
        return [s * inverse for s in shifted]

    raws = [dot_nt(gather(keys, g, 0), query[here[g]]) for g in pairs_of]
    prob_grads = [dot_nt(gather(values, g, 0), do[here[g]]) for g in pairs_of]
    probs = [softmax(g, raws[g]) for g in pairs_of]
    lows = [jnp.concatenate([p.astype(BF16) for p in probs[g]], axis=0) for g in pairs_of]
    grads = []
    for g in pairs_of:
        attended = dot_nn(gather(values_t, g, 1), lows[g]).astype(BF16).astype(F32)
        delta = jnp.sum(do_t[:, here[g]].astype(F32) * attended, axis=0, keepdims=True)
        parts = [
            (probs[g][n] * (block(prob_grads[g], n) - delta)).astype(BF16) for n in range(len(seen[g]))
        ]
        grads.append(jnp.concatenate(parts, axis=0))
    dvs, dks = [None] * (2 * frames), [None] * (2 * frames)

    def add(sums, g, whole):
        for n, b in enumerate(seen[g]):
            sums[b] = block(whole, n) if sums[b] is None else sums[b] + block(whole, n)

    for g in pairs_of:
        add(dvs, g, dot_nn(lows[g], do[here[g]]))
    for g in pairs_of:
        add(dks, g, dot_nn(grads[g], query[here[g]]))
    dqs = [(dot_nn(gather(keys_t, g, 1), grads[g]) * SCALE).astype(BF16).T for g in pairs_of]
    dq = jnp.concatenate(dqs, axis=0)
    dk = (jnp.concatenate(dks, axis=0) * SCALE).astype(BF16)
    dv = jnp.concatenate(dvs, axis=0).astype(BF16)
    both = jnp.concatenate([dk, dv], axis=1)
    sums = dot_tn(tokens, both)
    grads = jnp.concatenate([dot_tn(t_same, dq), sums[:, :DH], sums[:, DH:]], axis=0)
    lows = dot_nt(both, jnp.concatenate([ak, av], axis=1))
    return grads, lows[:flat] + dot_nt(dq, aq), lows[flat:]


def group_kernel(heads, frames, chained, waits, sides, count, *refs):
    refs = list(refs)

    def take(count):
        taken = refs[:count]
        del refs[:count]
        return taken

    (bands,) = take(1)
    arrays, adapters = take(count), take(3)
    before = take(2) if chained else None
    take(waits)
    keep_ref, *give_refs = take(1 + GIVES if chained else 2)
    low_refs = [] if chained else take(2)
    q, do, k, v, tokens = refs
    me, half = lax.axis_index("tm"), lax.axis_index("rep")
    rows = arrays[0].shape[0]
    flat = frames * rows
    cut = 3 * tokens.shape[1] // 2
    first = half == 0
    same_at = [pl.ds(pl.multiple_of((me ^ m) * rows, rows), rows) for m in range(frames)]
    other_at = [pl.ds(pl.multiple_of(flat + (me ^ m) * rows, rows), rows) for m in range(frames)]

    def put(targets, places, rows_at):
        for m, (n, start) in enumerate(places):
            for c, target in enumerate(targets):
                target[rows_at[m], :] = arrays[n][:, start + c * DH : start + (c + 1) * DH]

    put([tokens], sides[0][0], same_at)
    put([tokens], sides[0][1], other_at)

    def run(n, table):
        put([q, do, k, v], sides[1 + n][0], same_at)
        put([k, v], sides[1 + n][1], other_at)
        cols = column(lookup(table, me))
        grads, low_same, low_other = one_head(
            frames, bands, q[...], do[...], k[...], v[...], tokens[...], *[a[:, cols] for a in adapters]
        )
        keep = jnp.where(first, grads[:cut], grads[cut:])
        give = jnp.where(first, grads[cut:], grads[:cut])
        return keep, give, low_same, low_other

    if chained:
        keep, give, low_same, low_other = run(0, heads[0][0])
        keep_ref[:cut, :] = keep
        keep_ref[cut:, :] = before[0][...] + low_same
        give = jnp.concatenate([give, before[1][...] + low_other], axis=0)
        size = give.shape[0] // GIVES
        for n, ref in enumerate(give_refs):
            ref[...] = give[n * size : (n + 1) * size].astype(ref.dtype)
        return
    for n, (table, counts) in enumerate(heads):
        here = slice(n * cut, (n + 1) * cut)

        def body():
            keep, give, low_same, low_other = run(n, table)
            keep_ref[here, :] = keep
            give_refs[0][here, :] = give.astype(BF16)
            if n == 0:
                low_refs[0][...] = low_same
                low_refs[1][...] = low_other
            else:
                low_refs[0][...] += low_same
                low_refs[1][...] += low_other

        if min(counts) > 0:
            body()
        else:
            live = lookup(counts, me) > 0
            pl.when(live)(body)

            @pl.when(jnp.logical_not(live))
            def _():
                keep_ref[here, :] = jnp.zeros((cut, DH), F32)
                give_refs[0][here, :] = jnp.zeros((cut, DH), BF16)


def head_group(heads, bands, sides, adapters, before=(), after=()):
    frames = len(sides[0][0])
    arrays, places = [], []
    for side in sides:
        found = []
        for pairs_of in side:
            found.append([])
            for array, start in pairs_of:
                known = [n for n, a in enumerate(arrays) if a is array]
                if not known:
                    arrays.append(array)
                found[-1].append((known[0] if known else len(arrays) - 1, start))
        places.append(found)
    rows, rank = arrays[0].shape[0], adapters[0].shape[0]
    flat = frames * rows
    size = len(heads) * 3 * rank // 2
    chained = len(before) > 0
    args = [bands, *arrays, *adapters, *before, *after]
    specs = [pl.BlockSpec(memory_space=pltpu.SMEM)] + vmem(len(arrays) + 3 + len(before))
    specs += [pl.BlockSpec(memory_space=pl.ANY)] * len(after)
    low = jax.ShapeDtypeStruct((flat, rank), F32)
    if chained:
        part = jax.ShapeDtypeStruct(((size + flat) // GIVES, rank), BF16)
        shapes = [jax.ShapeDtypeStruct((size + flat, rank), F32)] + [part] * GIVES
    else:
        edge = jax.ShapeDtypeStruct((size, rank), F32)
        shapes = [edge, jax.ShapeDtypeStruct((size, rank), BF16), low, low]
    return pl.pallas_call(
        functools.partial(
            group_kernel, heads, frames, chained, len(after), places, len(arrays)
        ),
        in_specs=specs,
        out_specs=vmem(len(shapes)),
        out_shape=shapes,
        scratch_shapes=[pltpu.VMEM((flat, DH), BF16)] * 2
        + [pltpu.VMEM((2 * flat, DH), BF16)] * 2
        + [pltpu.VMEM((2 * flat, rank), BF16)],
        compiler_params=pltpu.CompilerParams(vmem_limit_bytes=40 * 1024 * 1024),
    )(*args)


def hand_out_kernel(frames, size, parts, keep_ref, *refs):
    gots, facing, (own_ref, *sends, total) = refs[:parts], refs[parts], refs[-frames - 1 :]
    me = lax.axis_index("tm")
    rows = own_ref.shape[0]
    total[...] = keep_ref[...] + jnp.concatenate([got[...].astype(F32) for got in gots], axis=0)
    for m in range(frames):
        low = total[pl.ds(pl.multiple_of(size + (me ^ m) * rows, 8), rows), :]
        if m == 0:
            own_ref[...] = low
        else:
            sends[m - 1][:rows, :] = low.astype(BF16)
            sends[m - 1][rows : rows + size, :] = total[:size, :].astype(BF16)
    sends[0][rows + size :, :] = facing[...]


def hand_out(frames, rows, keep, gots, facing, after):
    size, rank = keep.shape[0] - frames * rows, keep.shape[1]
    own, *sends = pl.pallas_call(
        functools.partial(hand_out_kernel, frames, size, len(gots)),
        in_specs=vmem(2 + len(gots)) + [pl.BlockSpec(memory_space=pl.ANY)] * len(after),
        out_specs=vmem(frames),
        out_shape=[jax.ShapeDtypeStruct((rows, rank), F32)]
        + [jax.ShapeDtypeStruct((rows + size * n, rank), BF16) for n in (3, 1, 1)],
        scratch_shapes=[pltpu.VMEM(keep.shape, F32)],
        compiler_params=SMALL,
    )(keep, *gots, facing, *after)
    return own, sends


def collect_kernel(wide, own_low, own, near, third, last, piece, pair, far, facing, out_ref, low_ref):
    rows = own_low.shape[0]
    size = own.shape[0] - rows
    low = own_low[...]
    for got in (near, third, last):
        low = low + got[:rows, :].astype(F32)
    out_ref[:rows, :] = low.astype(BF16)
    low_ref[...] = low.astype(BF16)
    middle = lookup(wide, lax.axis_index("tm")) > 0

    def part(ref, n):
        return ref[rows + n * size : rows + (n + 1) * size, :]

    blocks = [part(ref, 0) for ref in (own, near, third, last)]
    blocks += [piece[:size, :], pair[:size, :]]
    blocks += [jnp.where(middle, far[...], part(near, 1)), facing[:size, :]]
    blocks.append(jnp.where(middle, piece[size:, :], pair[size:, :]))
    blocks.append(jnp.where(middle, facing[size:, :], part(near, 2)))
    for n, block in enumerate(blocks):
        out_ref[rows + n * size : rows + (n + 1) * size, :] = block


def collect(wide, own_low, own, gots, *pieces):
    (rows, rank), size = own_low.shape, pieces[0].shape[0] // 2
    return pl.pallas_call(
        functools.partial(collect_kernel, wide),
        in_specs=vmem(2 + len(gots) + len(pieces)),
        out_specs=vmem(2),
        out_shape=[
            jax.ShapeDtypeStruct((rows + 10 * size, rank), BF16),
            jax.ShapeDtypeStruct((rows, rank), BF16),
        ],
        compiler_params=SMALL,
    )(own_low, own, *gots, *pieces)


def place_kernel(frames, lead, late, rest, tail, tail2, low_head, low_diag, *refs):
    outs, filled, sems = refs[:4], refs[4:8], refs[8]
    me, half = lax.axis_index("tm"), lax.axis_index("rep")
    first = half == 0
    rank = filled[0].shape[0]
    cut = 3 * rank // 2
    rows = low_head.shape[0]
    side = me // 2
    places = [lookup(late, me ^ m) for m in range(frames)] + [lookup(lead, me ^ m) for m in range(frames)]
    places += [lookup(rest, 1 + side), lookup(rest, 2 - side)]
    copies = [pltpu.make_async_copy(filled[o], outs[o], sems.at[o]) for o in range(4)]

    def rows_of(ref, n, start, stop):
        return ref[rows + n * cut + start : rows + n * cut + stop, :].astype(F32)

    for o in range(3):
        for n, head in enumerate(places):
            parts = []
            for owner, low_end, high_end in ((0, 0, cut), (1, cut, 2 * cut)):
                start, stop = max(o * rank, low_end), min((o + 1) * rank, high_end)
                if start < stop:
                    mine, its = (rows_of(ref, n, start - low_end, stop - low_end) for ref in (tail, tail2))
                    parts.append(jnp.where(first, mine, its) if owner == 0 else jnp.where(first, its, mine))
            filled[o][:, column(head)] = parts[0] if len(parts) == 1 else jnp.concatenate(parts, axis=0)
        copies[o].start()
    same = tail[:rows, :].astype(F32) + low_head[...].astype(F32)
    other = tail2[:rows, :].astype(F32) + low_diag[...].astype(F32)
    filled[3][:rows, :] = jnp.where(first, same, other)
    filled[3][rows:, :] = jnp.where(first, other, same)
    copies[3].start()
    for copy in copies:
        copy.wait()


def place(frames, lead, late, rest, tail, tail2, low_head, low_diag, rank, width):
    rows = low_head.shape[0]
    shapes = [(rank, width)] * 3 + [(2 * rows, rank)]
    return pl.pallas_call(
        functools.partial(place_kernel, frames, lead, late, rest),
        in_specs=vmem(4),
        out_specs=[pl.BlockSpec(memory_space=pl.ANY)] * 4,
        out_shape=[jax.ShapeDtypeStruct(shape, F32) for shape in shapes],
        scratch_shapes=[pltpu.VMEM(shape, F32) for shape in shapes] + [pltpu.SemaphoreType.DMA((4,))],
        compiler_params=SMALL,
    )(tail, tail2, low_head, low_diag)


def exchange_plan(
    frozen_query,
    frozen_key,
    frozen_value,
    token_adapter_input,
    query_adapter_out,
    key_adapter_out,
    value_adapter_out,
    out_grad,
    band_width,
):
    rows, width = frozen_query.shape
    rank = token_adapter_input.shape[1]
    frames = band_width.shape[0]
    heads = width // DH
    starts, counts = head_table(heads, frames)
    most = max(counts)
    columns = [[min(starts[j] + s, heads - 1) for j in range(frames)] for s in range(most)]
    numbers = [[int(s < counts[j]) for j in range(frames)] for s in range(most)]
    slots = list(zip(columns, numbers))
    lead, late, rest = slots[0], slots[1], slots[2]
    wide = [j for j in range(frames) if counts[j] == most]
    adapters = [query_adapter_out, key_adapter_out, value_adapter_out]
    arrays = (frozen_query, out_grad, frozen_key, frozen_value, token_adapter_input)

    def meet(name, block, m, targets=range(frames)):
        with jax.named_scope(f"{name}_over_tm"):
            return lax.ppermute(block, "tm", [(j ^ m, j) for j in targets])

    def swap_in_chip(name, block):
        with jax.named_scope(f"{name}_in_chip"):
            return swap(block, "rep")

    def mine(slot, m):
        return (slot[0], m, "mine")

    sent, kept, sent_late = [], [], []
    for m in range(1, frames):
        first = [mine(lead, m), (None, m, "t")]
        if m == 1:
            sent.append(first + [mine(rest, m), mine(late, m)])
        else:
            sent += [first, [mine(rest, m)]]
            sent_late.append([mine(late, m)])
    for slot in (lead, rest, late):
        kept += [[mine(slot, 0)], [(slot[0], 0, "other")]]
    kept += [[(None, 0, "t")], [(None, 0, "other t")]]
    packed = pack(frames, sent, 56, *arrays)
    packed_late = pack(frames, sent_late + kept, 16, *arrays)
    kept = packed_late[len(sent_late) :]
    block = meet("nearest", packed[0], 1)
    lead_got, rest_got, late_got = [(block, 0)], [(block, 4 * DH + rank)], [(block, 8 * DH + rank)]
    for m in range(2, frames):
        lead_got.append((meet("lead", packed[2 * m - 3], m), 0))
        rest_got.append((meet("rest", packed[2 * m - 2], m, wide), 0))
        late_got.append((meet("late", packed_late[m - 2], m), 0))

    def sides(name, n, got, wide_t, groups, skip, after=()):
        size = 4 * DH - skip + (rank if wide_t else 0)
        picked = pick([(a, start + skip) for a, start in got], size, groups, after)
        cross = [swap_in_chip(name, block) for block in picked]
        where = 2 * DH - skip
        cross = [(block, at * size + where) for block, count in zip(cross, groups) for at in range(count)]
        rows_here = [(kept[2 * n], 0)] + got
        rows_there = [(kept[2 * n + 1], 0)] + cross
        return rows_here, rows_there, cross

    *lead_side, cross = sides("lead", 0, lead_got, True, (3,), 2 * DH, kept[:1])
    t_side = (
        [(kept[6], 0)] + [(a, start + 4 * DH) for a, start in lead_got],
        [(kept[7], 0)] + [(block, start + 2 * DH) for block, start in cross],
    )
    *rest_side, _ = sides("rest", 1, rest_got, False, (3,), 2 * DH)
    early = [lead, rest]
    keep, give, *low = head_group(early, band_width, [t_side, lead_side, rest_side], adapters)
    got = swap_in_chip("early_gradients", give)
    piece = (keep + got.astype(F32)).astype(BF16)
    *late_side, _ = sides("late", 2, late_got, False, (3,), 0, [got])
    cut = 3 * rank // 2
    pair = meet("early_gradients", piece, 1)
    facing = meet("early_gradients", piece, 3)
    with jax.named_scope("early_lead_over_tm"):
        far = lax.ppermute(piece[:cut], "tm", [(0, 2), (3, 1)])
    keep, *gives = head_group([late], band_width, [t_side, late_side], adapters, low, [piece])
    gives = [swap_in_chip("late_sums", g) for g in gives]
    own_low, sends = hand_out(frames, rows, keep, gives, facing, [pair, far])
    gots = [meet("late_sums", block, m) for m, block in enumerate(sends, 1)]
    tail, low = collect(rest[1], own_low, sends[2], gots, piece, pair, far, facing)
    diag = [(0, 3), (1, 2), (2, 1), (3, 0)]
    with jax.named_scope("low_over_head"):
        low_head, low_diag = swap(low, "head"), lax.ppermute(low, ("head", "rep"), diag)
    outs = place(
        frames, lead[0], late[0], rest[0], tail, swap_in_chip("tail", tail), low_head, low_diag, rank, width
    )
    return tuple(outs)


def on_device(frozen_query, *rest):
    frames = rest[-1].shape[0]
    heads = frozen_query.shape[1] // DH
    whole_reach = frames == 4 and heads == 2 * frames + 2
    return (exchange_plan if whole_reach else window_plan)(frozen_query, *rest)


def solution(mesh):
    in_specs = (
        P(("groups", "tm", "rep"), "head"),
        P(("groups", "tm"), "head"),
        P(("groups", "tm"), "head"),
        P(("groups", "tm"), None),
        P(None, "head"),
        P(None, "head"),
        P(None, "head"),
        P(("groups", "tm", "rep"), "head"),
        P(),
    )
    out_specs = (
        P("groups", "head"),
        P("groups", "head"),
        P("groups", "head"),
        P(("groups", "tm"), None),
    )
    return jax.shard_map(
        on_device, mesh=mesh, in_specs=in_specs, out_specs=out_specs, check_vma=False
    )
```
